32 devices in a mesh: section: 2 (over core), head: 16 (over z, y, x).
Axes of the slice: x: 2, y: 2, z: 4, core: 2. Of those that a mesh axis runs over, the one named last changes fastest.
Arguments:
- inputs: bfloat16 [2, 1024, 2048], P(None, 'head'), may hold values from -6 to 6
- cotangent: bfloat16 [2, 1024, 2048], P(None, 'head'), may hold values from -6 to 6
- valid_lengths: int32 [2, 4], replicated, may hold values from 0 to 1024, as said below
- proj_in: float32 [2, 2048, 8256], P('section', None, 'head'), may hold values from -0.125 to 0.125
- proj_in_m: float32 [2, 2048, 8256], P('section', None, 'head'), may hold values from -1.2 to 1.2
- proj_in_v: float32 [2, 2048, 8256], P('section', None, 'head'), may hold values from 0.04 to 0.16
- proj_state: float32 [2, 2048, 256], P('section'), may hold values from -0.125 to 0.125
- proj_state_m: float32 [2, 2048, 256], P('section'), may hold values from -1.2 to 1.2
- proj_state_v: float32 [2, 2048, 256], P('section'), may hold values from 0.04 to 0.16
- proj_out: float32 [2, 4096, 2048], P('section', 'head'), may hold values from -0.09375 to 0.09375
- proj_out_m: float32 [2, 4096, 2048], P('section', 'head'), may hold values from -1.2 to 1.2
- proj_out_v: float32 [2, 4096, 2048], P('section', 'head'), may hold values from 0.04 to 0.16
- head_params: float32 [2, 64, 387], P('section', 'head')
- head_m: float32 [2, 64, 387], P('section', 'head'), may hold values from -2.4 to 2.4
- head_v: float32 [2, 64, 387], P('section', 'head'), may hold values from 0.16 to 0.64
- shared_params: float32 [2, 3328], P('section')
- shared_m: float32 [2, 3328], P('section'), may hold values from -2.4 to 2.4
- shared_v: float32 [2, 3328], P('section'), may hold values from 0.16 to 0.64
Outputs:
- layer_outputs: bfloat16 [2, 2, 1024, 2048], P('section', None, 'head')
- input_grads: float32 [2, 2, 1024, 2048], P('section', None, 'head')
- grad_norm: float32 [], replicated
- proj_in_new: float32 [2, 2048, 8256], P('section', None, 'head')
- proj_in_m_new: float32 [2, 2048, 8256], P('section', None, 'head')
- proj_in_v_new: float32 [2, 2048, 8256], P('section', None, 'head')
- proj_in_low: bfloat16 [2, 2048, 8256], P('section', None, 'head')
- proj_state_new: float32 [2, 2048, 256], P('section')
- proj_state_m_new: float32 [2, 2048, 256], P('section')
- proj_state_v_new: float32 [2, 2048, 256], P('section')
- proj_state_low: bfloat16 [2, 2048, 256], P('section')
- proj_out_new: float32 [2, 4096, 2048], P('section', 'head')
- proj_out_m_new: float32 [2, 4096, 2048], P('section', 'head')
- proj_out_v_new: float32 [2, 4096, 2048], P('section', 'head')
- proj_out_low: bfloat16 [2, 4096, 2048], P('section', 'head')
- head_new: float32 [2, 64, 387], P('section', 'head')
- head_m_new: float32 [2, 64, 387], P('section', 'head')
- head_v_new: float32 [2, 64, 387], P('section', 'head')
- shared_new: float32 [2, 3328], P('section')
- shared_m_new: float32 [2, 3328], P('section')
- shared_v_new: float32 [2, 3328], P('section')
The draws below stay inside these ranges and needn't reach their ends.
Inputs may be any that keep to these rules, and one draw needn't show every extreme that they name: `valid_lengths`: entry c of a micro-batch's row is nonzero exactly where a sequence's padded span begins at block c; block 0 always begins one; a span runs to the next beginning or to the micro-batch's end. Outside the last micro-batch every span holds 1024 tokens or more and its valid length exceeds its span minus 256; the last micro-batch holds one sequence of 1024 valid tokens.
All inputs are finite; a program needn't handle non-finite values.
Results may differ from the reference program's by a relative error of at most 0.023.
The reference program's roundings to bfloat16 on the way count: a program that leaves them out, or rounds other values in their place, can miss the bound.
Values may be sent and summed in bfloat16 or wider, within the bound.
A program may use at most 384 MiB of HBM per device.

```python
import math
import jax
import jax.numpy as jnp
from jax import lax

D = 2048
HEADS = 64
HDIM = 64
NSTATE = 128
CONV = 4
STRETCH = 256
MICRO = 2
SHORT_SPAN = 1024
ADAM_STEP = 5
MB_TOK = 1024
HK = 387
SK = 3328
PARAMS = 51698560
N_SECTION = 2


def draw_valid_lengths(key, part):
    key = jax.random.fold_in(key, 11)
    span_key, trim_key = jax.random.split(key)
    block_count = MB_TOK // STRETCH
    least = SHORT_SPAN // STRETCH
    block_idx = jnp.arange(block_count, dtype=jnp.int32)
    spans = jax.random.randint(span_key, (MICRO, block_count), least, 2 * least + 1, dtype=jnp.int32)
    ends = jnp.cumsum(spans, axis=1)
    begins = ends - spans
    usable = begins + least <= block_count
    hits = (begins[:, :, None] == block_idx[None, None, :]) & usable[:, :, None]
    is_start = jnp.any(hits, axis=1)
    later = is_start[:, None, :] & (block_idx[None, None, :] > block_idx[None, :, None])
    following = jnp.min(jnp.where(later, block_idx[None, None, :], block_count), axis=2)
    span_tokens = (following - block_idx[None, :]) * STRETCH
    trimmed = jax.random.randint(trim_key, (MICRO, block_count), 0, STRETCH, dtype=jnp.int32)
    short_rows = jnp.where(is_start, span_tokens - trimmed, 0)
    long_row = jnp.where(block_idx == 0, MB_TOK, 0)
    micro_idx = jnp.arange(MICRO, dtype=jnp.int32)[:, None]
    return jnp.where(micro_idx == MICRO - 1, long_row[None, :], short_rows).astype(jnp.int32)


def draw_head_params(key, part):
    key = jax.random.fold_in(key, 23)
    subkeys = jax.random.split(key, 6)
    conv_part = jax.random.uniform(subkeys[0], (2, HEADS, CONV * HDIM), jnp.float32, -0.5, 0.5)
    channel = jnp.arange(2 * HEADS * HDIM, dtype=jnp.float32).reshape(2, HEADS, HDIM)
    gain_part = (0.6 + 1.2 * channel / (2 * HEADS * HDIM)) * jax.random.uniform(subkeys[1], (2, HEADS, HDIM), jnp.float32, 0.8, 1.2)
    bias_part = jax.random.uniform(subkeys[2], (2, HEADS, HDIM), jnp.float32, -0.3, 0.3)
    step_bias = jax.random.uniform(subkeys[3], (2, HEADS, 1), jnp.float32, -1.0, 0.5)
    decay_log = jax.random.uniform(subkeys[4], (2, HEADS, 1), jnp.float32, math.log(0.0015), math.log(0.045))
    skip_part = jax.random.uniform(subkeys[5], (2, HEADS, 1), jnp.float32, 0.5, 1.5)
    return jnp.concatenate([conv_part, gain_part, bias_part, step_bias, decay_log, skip_part], axis=2)


def draw_shared_params(key, part):
    key = jax.random.fold_in(key, 37)
    subkeys = jax.random.split(key, 3)
    conv_part = jax.random.uniform(subkeys[0], (2, CONV * 2 * NSTATE), jnp.float32, -0.5, 0.5)
    bias_part = jax.random.uniform(subkeys[1], (2, 2 * NSTATE), jnp.float32, -0.3, 0.3)
    gain_part = 1.0 + jax.random.uniform(subkeys[2], (2, D), jnp.float32, -0.15, 0.15)
    return jnp.concatenate([conv_part, bias_part, gain_part], axis=1)


def shard_levels(own_key, dims, cuts, low, high):
    loudness, own = 1.0, jax.random.fold_in(own_key, 6)
    for dim, shards_of in cuts:
        steps = jnp.exp(jax.random.uniform(jax.random.fold_in(own, dim), (shards_of,), jnp.float32, low / len(cuts), high / len(cuts)))
        loudness = loudness * jnp.repeat(steps, dims[dim] // shards_of).reshape([-1 if axis == dim else 1 for axis in range(len(dims))])
    return loudness


def scatter_about(stream_key, extent, scale, bound, cuts=(), held_as=jnp.bfloat16):
    entries = jax.random.normal(stream_key, extent, jnp.float32) * scale
    if len(cuts) > 0:
        entries = shard_levels(stream_key, extent, cuts, -0.22, 0.18) * entries
    return jnp.clip(entries, min=-bound, max=bound).astype(held_as)


def setup_inputs(seed: int = 0) -> dict:
    seeds = jax.random.split(jax.random.key(seed), 19)
    return {
        "inputs": scatter_about(seeds[0], (MICRO, MB_TOK, D), 1.0, 6.0, ((1, 16),)),
        "cotangent": scatter_about(seeds[1], (MICRO, MB_TOK, D), 1.0, 6.0, ((1, 16),)),
        "valid_lengths": draw_valid_lengths(jax.random.fold_in(seeds[18], 71), 0),
        "proj_in": scatter_about(seeds[3], (N_SECTION, D, HEADS * (2 * HDIM + 1)), D ** -0.5, 0.125, ((0, 2), (2, 16)), jnp.float32),
        "proj_in_m": scatter_about(seeds[4], (N_SECTION, D, HEADS * (2 * HDIM + 1)), 0.2, 1.2, ((0, 2), (2, 16)), jnp.float32),
        "proj_in_v": jnp.clip(jnp.exp(math.log(0.16) - 1.3862944 * jax.random.uniform(seeds[5], (N_SECTION, D, HEADS * (2 * HDIM + 1)), jnp.float32) ** shard_levels(seeds[5], (N_SECTION, D, HEADS * (2 * HDIM + 1)), ((0, 2), (2, 16)), -0.2, 0.2)), 0.04, 0.16),
        "proj_state": scatter_about(seeds[6], (N_SECTION, D, 2 * NSTATE), D ** -0.5, 0.125, ((0, 2),), jnp.float32),
        "proj_state_m": scatter_about(seeds[7], (N_SECTION, D, 2 * NSTATE), 0.2, 1.2, ((0, 2),), jnp.float32),
        "proj_state_v": jnp.clip(jnp.exp(math.log(0.16) - 1.3862944 * jax.random.uniform(seeds[8], (N_SECTION, D, 2 * NSTATE), jnp.float32) ** shard_levels(seeds[8], (N_SECTION, D, 2 * NSTATE), ((0, 2),), -0.2, 0.2)), 0.04, 0.16),
        "proj_out": scatter_about(seeds[9], (N_SECTION, HEADS * HDIM, D), (HEADS * HDIM) ** -0.5, 0.09375, ((0, 2), (1, 16)), jnp.float32),
        "proj_out_m": scatter_about(seeds[10], (N_SECTION, HEADS * HDIM, D), 0.2, 1.2, ((0, 2), (1, 16)), jnp.float32),
        "proj_out_v": jnp.clip(jnp.exp(math.log(0.16) - 1.3862944 * jax.random.uniform(seeds[11], (N_SECTION, HEADS * HDIM, D), jnp.float32) ** shard_levels(seeds[11], (N_SECTION, HEADS * HDIM, D), ((0, 2), (1, 16)), -0.2, 0.2)), 0.04, 0.16),
        "head_params": draw_head_params(jax.random.fold_in(seeds[18], 71), 0),
        "head_m": scatter_about(seeds[13], (N_SECTION, HEADS, HK), 0.4, 2.4, ((0, 2), (1, 16)), jnp.float32),
        "head_v": jnp.clip(jnp.exp(math.log(0.64) - 1.3862944 * jax.random.uniform(seeds[14], (N_SECTION, HEADS, HK), jnp.float32) ** shard_levels(seeds[14], (N_SECTION, HEADS, HK), ((0, 2), (1, 16)), -0.2, 0.2)), 0.16, 0.64),
        "shared_params": draw_shared_params(jax.random.fold_in(seeds[18], 71), 0),
        "shared_m": scatter_about(seeds[16], (N_SECTION, SK), 0.4, 2.4, ((0, 2),), jnp.float32),
        "shared_v": jnp.clip(jnp.exp(math.log(0.64) - 1.3862944 * jax.random.uniform(seeds[17], (N_SECTION, SK), jnp.float32) ** shard_levels(seeds[17], (N_SECTION, SK), ((0, 2),), -0.2, 0.2)), 0.16, 0.64),
    }


HIGH = lax.Precision.HIGHEST
EPS_NORM = 1e-05
ADAM_EPS = 1e-08
BETA_ONE = 0.5
BETA_TWO = 0.5
CLIP_COEF = 0.2
LEARN_MATRIX = 0.02
LEARN_VECTOR = 0.2
WEIGHT_DECAY = 0.1

@jax.custom_vjp
def low(v):
    return lax.optimization_barrier(v.astype(jnp.bfloat16)).astype(jnp.float32)

@jax.custom_vjp
def low_back(v):
    return v

def low_keep(v):
    return (low(v), None)

def low_pass(kept, grad):
    return (grad,)

def back_keep(v):
    return (v, None)

def back_low(kept, grad):
    return (low(grad),)
low.defvjp(low_keep, low_pass)
low_back.defvjp(back_keep, back_low)

def seq_layout(lengths_row):
    block_count = lengths_row.shape[0]
    block_idx = jnp.arange(block_count, dtype=jnp.int32)
    starts = lengths_row > 0
    start_block = lax.cummax(jnp.where(starts, block_idx, 0), axis=0)
    owner_mask = (start_block[:, None] == block_idx[None, :]).astype(jnp.int32)
    seq_length = lax.optimization_barrier(jnp.sum(owner_mask * lengths_row[None, :], axis=1))
    token_idx = jnp.arange(block_count * STRETCH, dtype=jnp.int32)
    position = token_idx - jnp.repeat(start_block, STRETCH) * STRETCH
    live_mask = (position < jnp.repeat(seq_length, STRETCH)).astype(jnp.float32)
    return (position, live_mask, starts.astype(jnp.float32))

def causal_conv(values, conv_taps, conv_bias, position):
    running = conv_bias + conv_taps[0] * values
    for offset in range(1, CONV):
        pad_rows = jnp.zeros((offset,) + values.shape[1:], jnp.float32)
        shifted = jnp.concatenate([pad_rows, values[:-offset]], axis=0)
        in_seq = (position >= offset).astype(jnp.float32).reshape((-1,) + (1,) * (values.ndim - 1))
        running = running + conv_taps[offset] * shifted * in_seq
    return running

def block_scan(inner_act, step_size, decay_rate, writer, reader, resets):
    token_count, head_count, width = inner_act.shape
    blocks = token_count // STRETCH

    def advance(carry_state, pieces):
        block_inner, block_step, block_writer, block_reader, block_reset = pieces
        carry_state = carry_state * (1.0 - block_reset)
        log_decay = jnp.cumsum(block_step * decay_rate[None, :], axis=0)
        intersection = jnp.dot(block_reader, block_writer.T, precision=HIGH)
        causal_mask = jnp.arange(STRETCH)[:, None] >= jnp.arange(STRETCH)[None, :]
        log_gap = log_decay[:, None, :] - log_decay[None, :, :]
        decays = jnp.exp(jnp.where(causal_mask[:, :, None], log_gap, -jnp.inf))
        block_weights = intersection[:, :, None] * decays * block_step[None, :, :]
        within = jnp.einsum('ijh,jhp->ihp', block_weights, block_inner, precision=HIGH)
        carried = jnp.exp(log_decay)[:, :, None] * jnp.einsum('in,hpn->ihp', block_reader, carry_state, precision=HIGH)
        tail_weight = jnp.exp(log_decay[-1][None, :] - log_decay) * block_step
        added_state = jnp.einsum('jh,jhp,jn->hpn', tail_weight, block_inner, block_writer, precision=HIGH)
        new_state = jnp.exp(log_decay[-1])[:, None, None] * carry_state + added_state
        return (new_state, within + carried)
    start_state = jnp.zeros((head_count, width, NSTATE), jnp.float32)
    pieces = (inner_act.reshape(blocks, STRETCH, head_count, width), step_size.reshape(blocks, STRETCH, head_count), writer.reshape(blocks, STRETCH, NSTATE), reader.reshape(blocks, STRETCH, NSTATE), resets)
    final_state, outputs = lax.scan(jax.checkpoint(advance), start_state, pieces)
    return outputs.reshape(token_count, head_count, width)

def mixer_core(projected, state_raw, head_part, shared_conv, position, resets):
    token_count = projected.shape[0]
    head_count = head_part.shape[0]
    columns = projected.reshape(token_count, head_count, 2 * HDIM + 1)
    gate_raw = columns[:, :, :HDIM]
    inner_raw = columns[:, :, HDIM:2 * HDIM]
    step_raw = columns[:, :, 2 * HDIM]
    conv_taps = head_part[:, :CONV * HDIM].reshape(head_count, CONV, HDIM).transpose(1, 0, 2)
    conv_bias = head_part[:, (CONV + 1) * HDIM:(CONV + 2) * HDIM]
    step_bias = head_part[:, -3]
    decay_log = head_part[:, -2]
    skip_gain = head_part[:, -1]
    inner_act = jax.nn.silu(causal_conv(inner_raw, conv_taps, conv_bias, position))
    state_taps = shared_conv[:CONV * 2 * NSTATE].reshape(CONV, 2 * NSTATE)
    state_bias = shared_conv[CONV * 2 * NSTATE:]
    state_in = jax.nn.silu(causal_conv(state_raw, state_taps, state_bias, position))
    step_size = jax.nn.softplus(step_raw + step_bias[None, :])
    decay_rate = -jnp.exp(decay_log)
    scanned = block_scan(inner_act, step_size, decay_rate, state_in[:, :NSTATE], state_in[:, NSTATE:], resets)
    mixed_out = scanned + skip_gain[None, :, None] * inner_act
    gated_out = (mixed_out * jax.nn.silu(gate_raw)).reshape(token_count, head_count * HDIM)
    squares = lax.optimization_barrier(jnp.sum(gated_out * gated_out, axis=1))
    return (gated_out, squares)

def mixer_layer(residual, weight_in, weight_state, weight_out, head_part, shared_part, position, live_mask, resets):
    conv_length = 2 * CONV * NSTATE + 2 * NSTATE
    in_gain = shared_part[conv_length:]
    normed = residual * lax.rsqrt(lax.optimization_barrier(jnp.mean(residual * residual, axis=1, keepdims=True)) + EPS_NORM) * in_gain
    lowered = low(normed)
    projected = low_back(jnp.dot(lowered, low(weight_in), precision=HIGH))
    state_raw = low(low_back(jnp.dot(lowered, low(weight_state), precision=HIGH)))
    gated_out, squares = mixer_core(projected, state_raw, head_part, shared_part[:conv_length], position, resets)
    out_gain = head_part[:, CONV * HDIM:(CONV + 1) * HDIM].reshape(-1)
    scaled = low(gated_out * lax.rsqrt(squares / (HEADS * HDIM) + EPS_NORM)[:, None] * out_gain)
    branch = low_back(jnp.dot(scaled, low(weight_out), precision=HIGH))
    return residual + live_mask[:, None] * branch

def layer_grads(weights, layer_inputs, upstreams, position, live_mask, resets):

    def step_micro(running, pieces):
        layer_in, upstream, pos_row, live_row, reset_row = pieces

        def apply_layer(residual, weight_in, weight_state, weight_out, head_part, shared_part):
            return mixer_layer(residual, weight_in, weight_state, weight_out, head_part, shared_part, pos_row, live_row, reset_row)
        result, pullback = jax.vjp(apply_layer, layer_in, *weights)
        gradients = pullback(upstream)
        running = tuple((summed + gradient for summed, gradient in zip(running, gradients[1:])))
        return (running, (result, gradients[0]))
    zero_init = tuple((jnp.zeros_like(weight) for weight in weights))
    return lax.scan(step_micro, zero_init, (layer_inputs, upstreams, position, live_mask, resets))

def adam_update(weight, moment, second, gradient, rate, decay):
    moment_new = BETA_ONE * moment + (1.0 - BETA_ONE) * gradient
    second_new = BETA_TWO * second + (1.0 - BETA_TWO) * gradient * gradient
    corrected = moment_new / (1.0 - BETA_ONE ** ADAM_STEP)
    corrected_sq = second_new / (1.0 - BETA_TWO ** ADAM_STEP)
    weight_new = weight - rate * (corrected / (jnp.sqrt(corrected_sq) + ADAM_EPS) + decay * weight)
    return (weight_new, moment_new, second_new)

def reference(inputs, cotangent, valid_lengths, proj_in, proj_in_m, proj_in_v, proj_state, proj_state_m, proj_state_v, proj_out, proj_out_m, proj_out_v, head_params, head_m, head_v, shared_params, shared_m, shared_v):
    position, live_mask, resets = jax.vmap(seq_layout)(valid_lengths)
    masters = (proj_in, proj_state, proj_out, head_params, shared_params)
    lower_weights = tuple((master[0] for master in masters))
    upper_weights = tuple((master[1] for master in masters))
    first_inputs = inputs.astype(jnp.float32)

    def lower_forward(pieces):
        layer_in, pos_row, live_row, reset_row = pieces
        return mixer_layer(layer_in, *lower_weights, pos_row, live_row, reset_row)
    hidden = lax.map(lower_forward, (first_inputs, position, live_mask, resets))
    upper_sums, (upper_out, hidden_grad) = layer_grads(upper_weights, low(hidden), cotangent.astype(jnp.float32), position, live_mask, resets)
    lower_sums, (lower_out, input_grad) = layer_grads(lower_weights, first_inputs, low(hidden_grad), position, live_mask, resets)
    gradients = tuple((jnp.stack([lower_grad, upper_grad]) for lower_grad, upper_grad in zip(lower_sums, upper_sums)))
    norm_sq = jnp.float32(0.0)
    for gradient in gradients:
        norm_sq = norm_sq + jnp.sum(gradient * gradient)
    grad_norm = jnp.sqrt(norm_sq)
    threshold = CLIP_COEF * PARAMS ** 0.5
    clip_scale = threshold / jnp.maximum(grad_norm, threshold)
    moments = (proj_in_m, proj_state_m, proj_out_m, head_m, shared_m)
    seconds = (proj_in_v, proj_state_v, proj_out_v, head_v, shared_v)
    updated = []
    for index_group in range(5):
        rate = LEARN_MATRIX if index_group < 3 else LEARN_VECTOR
        decay = WEIGHT_DECAY if index_group < 3 else 0.0
        updated.append(adam_update(masters[index_group], moments[index_group], seconds[index_group], clip_scale * gradients[index_group], rate, decay))
    layer_outputs = jnp.stack([hidden, upper_out]).astype(jnp.bfloat16)
    input_grads = jnp.stack([input_grad, hidden_grad])
    return (layer_outputs, input_grads, grad_norm, updated[0][0], updated[0][1], updated[0][2], updated[0][0].astype(jnp.bfloat16), updated[1][0], updated[1][1], updated[1][2], updated[1][0].astype(jnp.bfloat16), updated[2][0], updated[2][1], updated[2][2], updated[2][0].astype(jnp.bfloat16), updated[3][0], updated[3][1], updated[3][2], updated[4][0], updated[4][1], updated[4][2])
```

```python
import itertools

import jax
import jax.numpy as jnp
import numpy as np
from jax import lax
from jax.experimental import pallas as pl
from jax.experimental.pallas import tpu as pltpu
from jax.sharding import PartitionSpec as P

HEADS = 64
HDIM = 64
NSTATE = 128
CONV = 4
STRETCH = 256
ADAM_STEP = 5
PARAMS = 51698560

HIGH = lax.Precision.HIGHEST
EPS_NORM = 1e-05
ADAM_EPS = 1e-08
BETA_ONE = 0.5
BETA_TWO = 0.5
CLIP_COEF = 0.2
LEARN_MATRIX = 0.02
LEARN_VECTOR = 0.2
WEIGHT_DECAY = 0.1

F32 = jnp.float32
BF16 = jnp.bfloat16
MESH = pl.DeviceIdType.MESH
LANES = 128
CHUNK = 128
COLS = HDIM * 2 + 1
GAIN_ROW = 9
VMEM_LIMIT = 56 << 20


def seq_layout(lengths_row):
    block_count = lengths_row.shape[0]
    block_idx = jnp.arange(block_count, dtype=jnp.int32)
    starts = lengths_row > 0
    start_block = lax.cummax(jnp.where(starts, block_idx, 0), axis=0)
    owner_mask = (start_block[:, None] == block_idx[None, :]).astype(jnp.int32)
    seq_length = jnp.sum(owner_mask * lengths_row[None, :], axis=1)
    return (start_block, seq_length, starts.astype(jnp.float32))


def chip_dims(count):
    side = 4 if count % 64 == 0 else 2
    if count % (side * side) != 0:
        return (count, 1, 1)
    return (count // (side * side), side, side)


def place(dims):
    me = lax.axis_index("head")
    return (me // (dims[1] * dims[2]), (me // dims[2]) % dims[1], me % dims[2])


def linear(dims, spot):
    return (spot[0] * dims[1] + spot[1]) * dims[2] + spot[2]


def moved(dims, spot, shifts):
    return tuple(s if d == 0 else (s + d) % n for s, d, n in zip(spot, shifts, dims))


def shift_of(order, offsets):
    out = [0, 0, 0]
    for axis, off in zip(order, offsets):
        out[axis] = off
    return out


def greet_axes(dims, spot):
    barrier = pltpu.get_barrier_semaphore()
    count = 0
    for axis in range(3):
        for off in range(1, dims[axis]):
            peer = linear(dims, moved(dims, spot, shift_of((axis,), (off,))))
            pl.semaphore_signal(
                barrier, inc=1, device_id={"head": peer}, device_id_type=MESH
            )
            count += 1
    if count:
        pl.semaphore_wait(barrier, count)


def greet_all(count):
    barrier = pltpu.get_barrier_semaphore()
    me = lax.axis_index("head")
    for off in range(1, count):
        pl.semaphore_signal(
            barrier, inc=1, device_id={"head": (me + off) % count}, device_id_type=MESH
        )
    if count > 1:
        pl.semaphore_wait(barrier, count - 1)


def rows_at(shard, rows):
    return pl.ds(pl.multiple_of(shard * rows, rows), rows)


def column_parts(width):
    tiles = width // LANES
    late = max(tiles // 8, 0)
    early = (tiles - 2 * late) // 2
    sizes = [early, tiles - 2 * late - early, late, late]
    orders = [(0, 2, 1), (0, 1, 2), (2, 1, 0), (1, 2, 0)]
    parts, start = [], 0
    for size, order in zip(sizes, orders):
        if size:
            parts.append((start, size * LANES, order))
            start += size * LANES
    return parts


def guarded(preds, action):
    preds = [pred for pred in preds if pred is not None]
    if not preds:
        action()
        return
    cond = preds[0]()
    for pred in preds[1:]:
        cond = jnp.logical_and(cond, pred())
    pl.when(cond)(action)


def gather_steps(dims, parts, rows, own_ref, all_ref, send_sem, recv_sem):
    spot = place(dims)
    me = linear(dims, spot)
    waits = []
    counter = [0] * len(parts)

    def lined(axis):
        return axis == 0 and dims[0] > 2 and dims[1] == 2

    def above(axis, dist):
        return lambda: spot[axis] + dist < dims[axis]

    def below(axis, dist):
        return lambda: spot[axis] >= dist

    def sources(part, pos):
        axis = parts[part][2][pos]
        if not lined(axis):
            return [(off, None) for off in range(1, dims[axis])]
        out = []
        for dist in range(1, dims[axis]):
            out.append((dist, above(axis, dist)))
            out.append((-dist, below(axis, dist)))
        return out

    def block(part, offsets):
        start, width, order = parts[part]
        shard = linear(dims, moved(dims, spot, shift_of(order, offsets)))
        return shard, all_ref.at[rows_at(shard, rows), pl.ds(start, width)]

    def push(part, offsets, pos, preds, src, came):
        axis = parts[part][2][pos]
        shard, dst = block(part, offsets)
        up, down = (1, above(axis, 1)), (-1, below(axis, 1))
        if lined(axis):
            targets = [up, down] if came == 0 else [down] if came > 0 else [up]
        else:
            targets = [(off, None) for off in range(1, dims[axis])] if came == 0 else []
        for off, pred in targets:
            peer = linear(dims, moved(dims, spot, shift_of((axis,), (off,))))
            number = counter[part]
            counter[part] += 1

            def begin(peer=peer, number=number):
                pltpu.make_async_remote_copy(
                    src_ref=dst if src is None else src,
                    dst_ref=dst,
                    send_sem=send_sem.at[part, number],
                    recv_sem=recv_sem.at[part, shard],
                    device_id={"head": peer},
                    device_id_type=MESH,
                ).start()

            guarded([pred], begin)
            waits.append((preds + [pred], part, number))

    def visit(part, offsets, preds, pos, came):
        def body():
            shard, dst = block(part, offsets)
            pltpu.make_async_remote_copy(
                src_ref=dst,
                dst_ref=dst,
                send_sem=send_sem.at[part, 0],
                recv_sem=recv_sem.at[part, shard],
                device_id={"head": me},
                device_id_type=MESH,
            ).wait_recv()
            push(part, offsets, pos, preds, None, came)
            for later in range(pos + 1, 3):
                push(part, offsets, later, preds, None, 0)

        guarded(preds, body)

    for pos in range(3):
        for part, (start, width, _) in enumerate(parts):
            push(part, (0, 0, 0), pos, [], own_ref.at[:, pl.ds(start, width)], 0)
    todo = []
    for part in range(len(parts)):
        first, second, third = (sources(part, pos) for pos in range(3))
        for k, (oa, pa) in enumerate(first):
            todo.append(((0, k, part), part, (oa, 0, 0), [pa], 0, oa))
        for ka, (oa, pa) in enumerate([(0, None)] + first):
            for k, (ob, pb) in enumerate(second):
                todo.append(((1, ka + k, part), part, (oa, ob, 0), [pa, pb], 1, ob))
            for kb, (ob, pb) in enumerate([(0, None)] + second):
                for k, (oc, pc) in enumerate(third):
                    todo.append(
                        ((2, ka + kb + k, part), part, (oa, ob, oc), [pa, pb, pc], 2, oc)
                    )
    todo.sort(key=lambda entry: entry[0])
    for _, part, offsets, preds, pos, came in todo:
        visit(part, offsets, preds, pos, came)
    for preds, part, number in waits:

        def settle(part=part, number=number):
            start, width, _ = parts[part]
            ref = own_ref.at[:, pl.ds(start, width)]
            pltpu.make_async_remote_copy(
                src_ref=ref,
                dst_ref=ref,
                send_sem=send_sem.at[part, number],
                recv_sem=recv_sem.at[part, 0],
                device_id={"head": me},
                device_id_type=MESH,
            ).wait_send()

        guarded(preds, settle)


def gather_sends(dims):
    return 3 * dims[0] * dims[1] * dims[2]


def scatter_steps(dims, parts, rows, in_ref, out_ref, box_ref, send_sem, recv_sem):
    spot = place(dims)
    me = linear(dims, spot)
    sends = []
    big = max(dims)

    def size(part, pos):
        return dims[parts[part][2][pos]]

    def slot_one(part, ea, ob, oc):
        return ((ea - 1) * size(part, 1) + ob) * size(part, 2) + oc

    def slot_two(part, eb, oc):
        base = (size(part, 0) - 1) * size(part, 1) * size(part, 2)
        return base + (eb - 1) * size(part, 2) + oc

    def slot_three(part, ec):
        return slot_two(part, size(part, 1), 0) + ec - 1

    def cols(part):
        return pl.ds(parts[part][0], parts[part][1])

    def mine(part, offsets):
        shard = linear(dims, moved(dims, spot, shift_of(parts[part][2], offsets)))
        return in_ref.at[rows_at(shard, rows), cols(part)]

    def send(part, src, pos, off, slot):
        peer = linear(dims, moved(dims, spot, shift_of((parts[part][2][pos],), (off,))))
        copy = pltpu.make_async_remote_copy(
            src_ref=src,
            dst_ref=box_ref.at[slot, :, cols(part)],
            send_sem=send_sem.at[part, slot],
            recv_sem=recv_sem.at[part, slot],
            device_id={"head": peer},
            device_id_type=MESH,
        )
        copy.start()
        sends.append(copy)

    def arrived(part, slot):
        ref = box_ref.at[slot, :, cols(part)]
        pltpu.make_async_remote_copy(
            src_ref=ref,
            dst_ref=ref,
            send_sem=send_sem.at[part, slot],
            recv_sem=recv_sem.at[part, slot],
            device_id={"head": me},
            device_id_type=MESH,
        ).wait_recv()
        return ref[...].astype(F32)

    every = range(len(parts))
    ranks = sorted(
        itertools.product(range(big), range(big)), key=lambda t: (t[0] == 0, t[1] == 0)
    )
    for ob, oc in ranks:
        for off in range(1, big):
            for part in every:
                if off < size(part, 0) and ob < size(part, 1) and oc < size(part, 2):
                    slot = slot_one(part, size(part, 0) - off, ob, oc)
                    send(part, mine(part, (off, ob, oc)), 0, off, slot)
    for ob, oc in ranks:
        for part in every:
            if ob == 0 or ob >= size(part, 1) or oc >= size(part, 2):
                continue
            total = mine(part, (0, ob, oc))[...].astype(F32)
            for ea in range(1, size(part, 0)):
                total = total + arrived(part, slot_one(part, ea, ob, oc))
            hold = mine(part, (0, ob, oc))
            if size(part, 0) > 1:
                hold = box_ref.at[slot_one(part, 1, ob, oc), :, cols(part)]
                hold[...] = total.astype(box_ref.dtype)
            send(part, hold, 1, ob, slot_two(part, size(part, 1) - ob, oc))
    for oc in list(range(1, big)) + [0]:
        for part in every:
            if oc >= size(part, 2):
                continue
            total = mine(part, (0, 0, oc))[...].astype(F32)
            for ea in range(1, size(part, 0)):
                total = total + arrived(part, slot_one(part, ea, 0, oc))
            for eb in range(1, size(part, 1)):
                total = total + arrived(part, slot_two(part, eb, oc))
            if oc == 0:
                for ec in range(1, size(part, 2)):
                    total = total + arrived(part, slot_three(part, ec))
                out_ref[:, cols(part)] = total
                continue
            hold = mine(part, (0, 0, oc))
            if size(part, 0) > 1:
                hold = box_ref.at[slot_one(part, 1, 0, oc), :, cols(part)]
            elif size(part, 1) > 1:
                hold = box_ref.at[slot_two(part, 1, oc), :, cols(part)]
            if size(part, 0) > 1 or size(part, 1) > 1:
                hold[...] = total.astype(box_ref.dtype)
            send(part, hold, 2, oc, slot_three(part, size(part, 2) - oc))
    return sends


def start_direct(count, own_ref_of, box_ref, send_sem, recv_sem):
    me = lax.axis_index("head")
    copies = []
    for off in range(1, count):
        peer = (me + off) % count
        copy = pltpu.make_async_remote_copy(
            src_ref=own_ref_of(peer),
            dst_ref=box_ref.at[me],
            send_sem=send_sem.at[off],
            recv_sem=recv_sem.at[count - off],
            device_id={"head": peer},
            device_id_type=MESH,
        )
        copy.start()
        copies.append(copy)
    return copies


def wait_direct(count, box_ref, copies, recv_sem, send_sem):
    me = lax.axis_index("head")
    for off in range(1, count):
        ref = box_ref.at[(me + off) % count]
        pltpu.make_async_remote_copy(
            src_ref=ref,
            dst_ref=ref,
            send_sem=send_sem.at[off],
            recv_sem=recv_sem.at[off],
            device_id={"head": me},
            device_id_type=MESH,
        ).wait_recv()
    for copy in copies:
        copy.wait_send()


VMEM_SPEC = pl.BlockSpec(memory_space=pltpu.VMEM)
ANY_SPEC = pl.BlockSpec(memory_space=pl.ANY)
DMA = pltpu.SemaphoreType.DMA


def gather_rows(count, own, stats, collective_id):
    dims = chip_dims(count)
    rows, width = own.shape
    parts = column_parts(width)

    def kernel(*refs):
        if stats is None:
            own_ref, all_ref, send_sem, recv_sem, local_sem = refs
        else:
            (own_ref, stat_ref, all_ref, box_ref, send_sem, recv_sem, local_sem) = refs[:7]
            small_send, small_recv = refs[7:]
        spot = place(dims)
        me = linear(dims, spot)
        if stats is None:
            greet_axes(dims, spot)
        else:
            greet_all(count)
        local = pltpu.make_async_copy(own_ref, all_ref.at[rows_at(me, rows)], local_sem)
        local.start()
        if stats is not None:
            copies = start_direct(count, lambda peer: stat_ref, box_ref, small_send, small_recv)
            box_ref[me] = stat_ref[...]
        gather_steps(dims, parts, rows, own_ref, all_ref, send_sem, recv_sem)
        if stats is not None:
            wait_direct(count, box_ref, copies, small_recv, small_send)
        local.wait()

    out_shape = [jax.ShapeDtypeStruct((count * rows, width), own.dtype)]
    out_specs = [ANY_SPEC]
    scratch = [
        DMA((len(parts), gather_sends(dims))),
        DMA((len(parts), count)),
        DMA,
    ]
    operands = [own]
    if stats is not None:
        out_shape.append(jax.ShapeDtypeStruct((count,) + stats.shape, stats.dtype))
        out_specs.append(VMEM_SPEC)
        scratch += [DMA((count,)), DMA((count,))]
        operands.append(stats)
    return pl.pallas_call(
        kernel,
        out_shape=out_shape,
        in_specs=[VMEM_SPEC] * len(operands),
        out_specs=out_specs,
        scratch_shapes=scratch,
        compiler_params=pltpu.CompilerParams(
            collective_id=collective_id, has_side_effects=True, vmem_limit_bytes=VMEM_LIMIT
        ),
        name="gather_rows",
    )(*operands)


def scatter_rows(count, partial, small, collective_id):
    dims = chip_dims(count)
    width = partial.shape[1]
    rows = partial.shape[0] // count
    parts = [(s, w, tuple(reversed(order))) for s, w, order in column_parts(width)]

    def kernel(*refs):
        if small is None:
            in_ref, out_ref, box_ref, send_sem, recv_sem = refs
        else:
            in_ref, small_ref, out_ref, sums_ref, box_ref, send_sem, recv_sem = refs[:7]
            small_send, small_recv = refs[7:]
        me = lax.axis_index("head")
        spot = place(dims)
        if small is None:
            greet_axes(dims, spot)
        else:
            greet_all(count)
            copies = start_direct(
                count, lambda peer: small_ref.at[peer], sums_ref, small_send, small_recv
            )
            sums_ref[me] = small_ref[me]
        sends = scatter_steps(dims, parts, rows, in_ref, out_ref, box_ref, send_sem, recv_sem)
        if small is not None:
            wait_direct(count, sums_ref, copies, small_recv, small_send)
        for copy in sends:
            copy.wait_send()

    out_shape = [jax.ShapeDtypeStruct((rows, width), F32)]
    scratch = [
        pltpu.VMEM((max(count - 1, 1), rows, width), partial.dtype),
        DMA((len(parts), max(count - 1, 1))),
        DMA((len(parts), max(count - 1, 1))),
    ]
    operands = [partial]
    if small is not None:
        out_shape.append(jax.ShapeDtypeStruct(small.shape, small.dtype))
        scratch += [DMA((count,)), DMA((count,))]
        operands.append(small)
    return pl.pallas_call(
        kernel,
        out_shape=out_shape,
        in_specs=[VMEM_SPEC] * len(operands),
        out_specs=[VMEM_SPEC] * len(out_shape),
        scratch_shapes=scratch,
        compiler_params=pltpu.CompilerParams(
            collective_id=collective_id, has_side_effects=True, vmem_limit_bytes=VMEM_LIMIT
        ),
        name="scatter_rows",
    )(*operands)


def gather_small(count, block, collective_id):
    def kernel(in_ref, box_ref, send_sem, recv_sem):
        greet_all(count)
        copies = start_direct(count, lambda peer: in_ref, box_ref, send_sem, recv_sem)
        box_ref[lax.axis_index("head")] = in_ref[...]
        wait_direct(count, box_ref, copies, recv_sem, send_sem)

    return pl.pallas_call(
        kernel,
        out_shape=jax.ShapeDtypeStruct((count,) + block.shape, block.dtype),
        in_specs=[VMEM_SPEC],
        out_specs=VMEM_SPEC,
        scratch_shapes=[DMA((count,)), DMA((count,))],
        compiler_params=pltpu.CompilerParams(
            collective_id=collective_id, has_side_effects=True
        ),
        name="gather_small",
    )(block)


def greet_other():
    barrier = pltpu.get_barrier_semaphore()
    other = 1 - lax.axis_index("section")
    pl.semaphore_signal(barrier, inc=1, device_id={"section": other}, device_id_type=MESH)
    pl.semaphore_wait(barrier, 1)
    return other


def both_sections(arrays, collective_id):
    number = len(arrays)

    def kernel(*refs):
        ins, outs = refs[:number], refs[number : 2 * number]
        send_sem, recv_sem, local_sem = refs[2 * number :]
        section = lax.axis_index("section")
        locals_ = [
            pltpu.make_async_copy(ins[k], outs[k].at[section], local_sem.at[k])
            for k in range(number)
        ]
        for local in locals_:
            local.start()
        other = greet_other()
        copies = []
        for k in range(number):
            locals_[k].wait()
            copy = pltpu.make_async_remote_copy(
                src_ref=outs[k].at[section],
                dst_ref=outs[k].at[section],
                send_sem=send_sem.at[k],
                recv_sem=recv_sem.at[k],
                device_id={"section": other},
                device_id_type=MESH,
            )
            copy.start()
            copies.append(copy)
        for copy in copies:
            copy.wait()

    return pl.pallas_call(
        kernel,
        out_shape=[jax.ShapeDtypeStruct((2,) + a.shape, a.dtype) for a in arrays],
        in_specs=[ANY_SPEC] * number,
        out_specs=[VMEM_SPEC] * number,
        scratch_shapes=[DMA((number,))] * 3,
        compiler_params=pltpu.CompilerParams(
            collective_id=collective_id, has_side_effects=True, vmem_limit_bytes=VMEM_LIMIT
        ),
        name="both_sections",
    )(*arrays)


def trade_sections(sums, stacks, collective_id):
    pairs = sums + stacks
    number, summed = len(pairs), len(sums)

    def kernel(*refs):
        ins, outs = refs[: 2 * number], refs[2 * number : 3 * number]
        boxes = refs[3 * number : 3 * number + summed]
        send_sem, recv_sem = refs[3 * number + summed :]
        section = lax.axis_index("section")
        other = greet_other()

        def go(mine, theirs):
            copies = []
            for k in range(number):
                copy = pltpu.make_async_remote_copy(
                    src_ref=theirs[k],
                    dst_ref=boxes[k] if k < summed else outs[k].at[section],
                    send_sem=send_sem.at[k],
                    recv_sem=recv_sem.at[k],
                    device_id={"section": other},
                    device_id_type=MESH,
                )
                copy.start()
                copies.append(copy)
            for k in range(summed, number):
                outs[k][section] = mine[k][...]
            for k in range(number):
                copies[k].wait()
                if k < summed:
                    outs[k][...] = mine[k][...].astype(F32) + boxes[k][...].astype(F32)

        pl.when(section == 0)(lambda: go(ins[0::2], ins[1::2]))
        pl.when(section == 1)(lambda: go(ins[1::2], ins[0::2]))

    shapes = [jax.ShapeDtypeStruct(a.shape, F32) for a, _ in sums]
    shapes += [jax.ShapeDtypeStruct((2,) + a.shape, a.dtype) for a, _ in stacks]
    return pl.pallas_call(
        kernel,
        out_shape=shapes,
        in_specs=[VMEM_SPEC] * (2 * number),
        out_specs=[VMEM_SPEC] * number,
        scratch_shapes=[pltpu.VMEM(a.shape, a.dtype) for a, _ in sums] + [DMA((number,))] * 2,
        compiler_params=pltpu.CompilerParams(
            collective_id=collective_id, has_side_effects=True, vmem_limit_bytes=VMEM_LIMIT
        ),
        name="trade_sections",
    )(*[a for pair in pairs for a in pair])


class Sizes:
    def __init__(self, heads, tokens, width):
        self.heads = heads
        self.padded = heads + heads % 2
        self.channels = self.padded * HDIM
        self.conv = self.channels + 2 * NSTATE
        self.cols = 2 * self.channels + 2 * NSTATE + LANES
        self.dt = 2 * self.channels + 2 * NSTATE
        self.master = heads * COLS
        self.master_pad = -(-self.master // LANES) * LANES
        self.grad_rows = self.master_pad + 2 * NSTATE
        self.tokens = tokens
        self.width = width
        self.blocks = tokens // STRETCH

    def order(self):
        table = np.zeros((self.grad_rows, self.cols), np.float32)
        for head in range(self.heads):
            for j in range(HDIM):
                table[head * COLS + j, head * HDIM + j] = 1
                table[head * COLS + HDIM + j, self.channels + head * HDIM + j] = 1
            table[head * COLS + 2 * HDIM, self.dt + head] = 1
        for j in range(2 * NSTATE):
            table[self.master_pad + j, 2 * self.channels + j] = 1
        return jnp.asarray(table, BF16)

    def head_sum(self):
        table = np.zeros((self.channels, LANES), np.float32)
        for head in range(self.padded):
            table[head * HDIM : (head + 1) * HDIM, head] = 1
        return jnp.asarray(table, F32)


def nt(left, right, precision=None):
    return lax.dot_general(
        left, right, (((1,), (1,)), ((), ())), precision=precision, preferred_element_type=F32
    )


def tn(left, right, precision=None):
    return lax.dot_general(
        left, right, (((0,), (0,)), ((), ())), precision=precision, preferred_element_type=F32
    )


def nn(left, right, precision=None):
    return jnp.dot(left, right, precision=precision, preferred_element_type=F32)


def softplus(value):
    return jnp.maximum(value, 0.0) + jnp.log1p(jnp.exp(-jnp.abs(value)))


def sigmoid(value):
    return 1.0 / (1.0 + jnp.exp(-value))


def halves(left, right):
    rows = left.shape[0]
    lane = lax.broadcasted_iota(jnp.int32, (rows, LANES), 1)
    return jnp.where(lane < HDIM, left, right)


def lower_mask(size):
    row = lax.broadcasted_iota(jnp.int32, (size, size), 0)
    col = lax.broadcasted_iota(jnp.int32, (size, size), 1)
    return row >= col


def step_rows(log_decay, step):
    lane = lax.broadcasted_iota(jnp.int32, log_decay.shape, 1)
    both = jnp.where(lane < 8, log_decay, pltpu.roll(step, 8, 1))
    return jnp.transpose(jnp.where(lane < 16, both, 0.0))


def prepare_weights(sz, proj_in, proj_state, order):
    rows = min(256, sz.width)

    def kernel(in_ref, state_ref, order_ref, out_ref):
        low = in_ref[...].astype(BF16)
        table = order_ref[: sz.master, :]
        out_ref[...] = nn(low, table).astype(BF16)
        out_ref[:, 2 * sz.channels : sz.dt] = state_ref[...].astype(BF16)

    return pl.pallas_call(
        kernel,
        out_shape=jax.ShapeDtypeStruct((sz.width, sz.cols), BF16),
        grid=(sz.width // rows,),
        in_specs=[
            pl.BlockSpec((rows, sz.master), lambda i: (i, 0)),
            pl.BlockSpec((rows, 2 * NSTATE), lambda i: (i, 0)),
            pl.BlockSpec((sz.grad_rows, sz.cols), lambda i: (0, 0)),
        ],
        out_specs=pl.BlockSpec((rows, sz.cols), lambda i: (i, 0)),
        compiler_params=pltpu.CompilerParams(vmem_limit_bytes=VMEM_LIMIT),
        name="prepare_weights",
    )(proj_in, proj_state, order)


def pack_params(sz, head_part, shared_part):
    heads = sz.heads
    pad = ((0, 0), (0, sz.channels - heads * HDIM))
    taps = head_part[:, : CONV * HDIM].reshape(heads, CONV, HDIM).transpose(1, 0, 2)
    taps = jnp.pad(taps.reshape(CONV, heads * HDIM), pad)
    bias = head_part[:, (CONV + 1) * HDIM : (CONV + 2) * HDIM].reshape(1, -1)
    gain = head_part[:, CONV * HDIM : (CONV + 1) * HDIM].reshape(1, -1)
    skip = jnp.repeat(head_part[:, -1], HDIM).reshape(1, -1)
    state_taps = shared_part[: CONV * 2 * NSTATE].reshape(CONV, 2 * NSTATE)
    state_bias = shared_part[CONV * 2 * NSTATE : (CONV + 1) * 2 * NSTATE].reshape(1, -1)
    in_gain = shared_part[(CONV + 1) * 2 * NSTATE :].reshape(1, -1)

    def row(value):
        return jnp.pad(value, ((0, 0), (0, sz.width - value.shape[1])))

    rows = [
        row(jnp.concatenate([taps, state_taps], axis=1)),
        row(jnp.concatenate([jnp.pad(bias, pad), state_bias], axis=1)),
        row(gain),
        row(skip),
        row(head_part[:, -3].reshape(1, -1)),
        row(-jnp.exp(head_part[:, -2]).reshape(1, -1)),
        in_gain,
        jnp.zeros((16 - GAIN_ROW - 1, sz.width), F32),
    ]
    return jnp.concatenate(rows, axis=0)


def forward_core(sz, layer, resets, gathered, weights, weight_out, pack, rows):
    block, chunk, chans = STRETCH, CHUNK, sz.channels
    subs = block // chunk
    shards = block // rows

    def kernel(
        reset_ref, h_ref, w_ref, wo_ref, pk_ref, part_ref, sq_ref, p_ref, y_ref, s_ref,
        conv_ref, state_ref,
    ):
        c = pl.program_id(0)
        keep = 1.0 - reset_ref[c]

        @pl.when(c == 0)
        def _():
            conv_ref[...] = jnp.zeros_like(conv_ref)
            state_ref[...] = jnp.zeros_like(state_ref)

        p_ref[...] = nn(h_ref[...], w_ref[...])
        inner = p_ref[:, chans : 2 * chans]
        state_raw = p_ref[:, 2 * chans : sz.dt].astype(BF16).astype(F32)
        conv_ref[0:8, :] = conv_ref[block : block + 8, :] * keep
        conv_ref[8 : 8 + block, :chans] = inner
        conv_ref[8 : 8 + block, chans:] = state_raw
        pre = pk_ref[CONV : CONV + 1, : sz.conv] + pk_ref[0:1, : sz.conv] * conv_ref[8 : 8 + block, :]
        for tap in range(1, CONV):
            pre = pre + pk_ref[tap : tap + 1, : sz.conv] * conv_ref[8 - tap : 8 - tap + block, :]
        act = pre * sigmoid(pre)
        step = softplus(p_ref[:, sz.dt :] + pk_ref[7:8, :LANES])
        decay = step * pk_ref[8:9, :LANES]
        mask = lower_mask(chunk)
        lower = mask.astype(F32)
        lane = lax.broadcasted_iota(jnp.int32, (chunk, LANES), 1)
        for sub in range(subs):
            span = slice(sub * chunk, (sub + 1) * chunk)
            if sub == 0:
                state_ref[...] = state_ref[...] * keep
            s_ref[sub] = state_ref[...]
            dt = step[span]
            log_decay = nn(lower, decay[span], HIGH)
            flat = step_rows(log_decay, dt)
            writer = act[span, chans : chans + NSTATE].astype(BF16)
            reader = act[span, chans + NSTATE :].astype(BF16)
            cross = nt(reader, writer)
            for pair in range(sz.padded // 2):
                cols = slice(pair * LANES, (pair + 1) * LANES)
                x = act[span, cols]
                total = jnp.zeros((chunk, LANES), F32)
                for side in range(2):
                    head = 2 * pair + side
                    gap = log_decay[:, head : head + 1] - flat[head : head + 1, :]
                    weight = cross * jnp.exp(jnp.where(mask, gap, -1e30)) * flat[8 + head : 9 + head, :]
                    part = jnp.where((lane < HDIM) == (side == 0), x, 0.0).astype(BF16)
                    total = total + nn(weight.astype(BF16), part)
                logs = halves(log_decay[:, 2 * pair : 2 * pair + 1], log_decay[:, 2 * pair + 1 : 2 * pair + 2])
                dts = halves(dt[:, 2 * pair : 2 * pair + 1], dt[:, 2 * pair + 1 : 2 * pair + 2])
                old = state_ref[:, cols]
                total = total + jnp.exp(logs) * nn(reader, old.astype(BF16))
                last = logs[chunk - 1 : chunk, :]
                moved_in = (x * jnp.exp(last - logs) * dts).astype(BF16)
                state_ref[:, cols] = jnp.exp(last) * old + tn(writer, moved_in)
                y_ref[span, cols] = total + pk_ref[6:7, cols] * x
        z = p_ref[:, :chans]
        gated = y_ref[...] * z * sigmoid(z)
        square = nt(jnp.ones((8, chans), F32), gated * gated, HIGH)
        for k in range(shards):
            sq_ref[k] = square[:, k * rows : (k + 1) * rows]
        low = (gated * pk_ref[5:6, :chans]).astype(BF16)
        part_ref[...] = nn(low, wo_ref[...]).astype(BF16)

    width = sz.width
    return pl.pallas_call(
        kernel,
        grid=(sz.blocks,),
        out_shape=[
            jax.ShapeDtypeStruct((sz.tokens, width), BF16),
            jax.ShapeDtypeStruct((sz.tokens // rows, 8, rows), F32),
            jax.ShapeDtypeStruct((sz.tokens, sz.cols), F32),
            jax.ShapeDtypeStruct((sz.tokens, chans), F32),
            jax.ShapeDtypeStruct((sz.tokens // chunk, NSTATE, chans), F32),
        ],
        in_specs=[
            pl.BlockSpec(memory_space=pltpu.SMEM),
            pl.BlockSpec((block, width), lambda c: (c, 0)),
            pl.BlockSpec((None, width, sz.cols), lambda c: (layer, 0, 0)),
            pl.BlockSpec((None, chans, width), lambda c: (layer, 0, 0)),
            pl.BlockSpec((None, 16, width), lambda c: (layer, 0, 0)),
        ],
        out_specs=[
            pl.BlockSpec((block, width), lambda c: (c, 0)),
            pl.BlockSpec((shards, 8, rows), lambda c: (c, 0, 0)),
            pl.BlockSpec((block, sz.cols), lambda c: (c, 0)),
            pl.BlockSpec((block, chans), lambda c: (c, 0)),
            pl.BlockSpec((subs, NSTATE, chans), lambda c: (c, 0, 0)),
        ],
        scratch_shapes=[
            pltpu.VMEM((block + 8, sz.conv), F32),
            pltpu.VMEM((NSTATE, chans), F32),
        ],
        compiler_params=pltpu.CompilerParams(vmem_limit_bytes=VMEM_LIMIT),
        name="forward_core",
    )(resets, gathered, weights, weight_out, pack)


def backward_core(sz, layer, resets, grads, proj, mixed, states, stats, weights, weight_out, pack, order):
    block, chunk, chans = STRETCH, CHUNK, sz.channels
    subs = block // chunk
    blocks = sz.blocks

    def kernel(
        reset_ref, g_ref, p_ref, halo_ref, y_ref, s_ref, st_ref, w_ref, wo_ref, pk_ref, order_ref, sum_ref,
        gh_ref, gt_ref, q_ref, acc_ref,
        conv_ref, dpre_ref, dact_ref, dlog_ref, ddt_ref, dstate_ref,
    ):
        i = pl.program_id(0)
        c = blocks - 1 - i
        keep = 1.0 - reset_ref[c]
        after = 1.0 - reset_ref[jnp.minimum(c + 1, blocks - 1)]

        @pl.when(i == 0)
        def _():
            dpre_ref[...] = jnp.zeros_like(dpre_ref)
            dstate_ref[...] = jnp.zeros_like(dstate_ref)
            acc_ref[...] = jnp.zeros_like(acc_ref)

        conv_ref[0:8, :chans] = halo_ref[:, chans : 2 * chans] * keep
        conv_ref[0:8, chans:] = halo_ref[:, 2 * chans : sz.dt].astype(BF16).astype(F32) * keep
        conv_ref[8 : 8 + block, :chans] = p_ref[:, chans : 2 * chans]
        conv_ref[8 : 8 + block, chans:] = p_ref[:, 2 * chans : sz.dt].astype(BF16).astype(F32)
        pre = pk_ref[CONV : CONV + 1, : sz.conv] + pk_ref[0:1, : sz.conv] * conv_ref[8 : 8 + block, :]
        for tap in range(1, CONV):
            pre = pre + pk_ref[tap : tap + 1, : sz.conv] * conv_ref[8 - tap : 8 - tap + block, :]
        gate = sigmoid(pre)
        act = pre * gate
        slope = gate * (1.0 + pre * (1.0 - gate))
        step_in = p_ref[:, sz.dt :] + pk_ref[7:8, :LANES]
        step = softplus(step_in)
        rate = pk_ref[8:9, :LANES]
        decay = step * rate
        z = p_ref[:, :chans]
        zgate = sigmoid(z)
        zsilu = z * zgate
        y = y_ref[...]
        gated = y * zsilu
        gain = pk_ref[5:6, :chans]
        skip = pk_ref[6:7, :chans]
        scale = st_ref[:, 0:1]
        along = st_ref[:, 1:2]
        grad_q = nt(g_ref[...], wo_ref[...])
        q_ref[...] = (gated * scale * gain).astype(BF16)
        acc_ref[5:6, :chans] += jnp.sum(grad_q * gated * scale, axis=0, keepdims=True)
        dgated = grad_q * gain * scale - gated * (scale * scale * along * (1.0 / (HEADS * HDIM)))
        dy = dgated * zsilu
        dz = dgated * y * zgate * (1.0 + z * (1.0 - zgate))
        x_all = act[:, :chans]
        acc_ref[6:7, :chans] += jnp.sum(dy * x_all, axis=0, keepdims=True)
        scan_dot = nn(dy * (y - skip * x_all), sum_ref[...], HIGH)
        mask = lower_mask(chunk)
        lower = mask.astype(F32)
        lane = lax.broadcasted_iota(jnp.int32, (chunk, LANES), 1)
        for sub in reversed(range(subs)):
            span = slice(sub * chunk, (sub + 1) * chunk)
            dt = step[span]
            log_decay = nn(lower, decay[span], HIGH)
            flat = step_rows(log_decay, dt)
            writer = act[span, chans : chans + NSTATE].astype(BF16)
            reader = act[span, chans + NSTATE :].astype(BF16)
            cross = nt(reader, writer)
            cross_grad = jnp.zeros((chunk, chunk), F32)
            dreader = jnp.zeros((chunk, NSTATE), F32)
            dwriter = jnp.zeros((chunk, NSTATE), F32)
            fall = jnp.zeros((LANES, chunk), F32)
            row = lax.broadcasted_iota(jnp.int32, (LANES, chunk), 0)
            reach = []
            carried = []
            for pair in range(sz.padded // 2):
                cols = slice(pair * LANES, (pair + 1) * LANES)
                x = act[span, cols]
                g = dy[span, cols]
                logs = halves(log_decay[:, 2 * pair : 2 * pair + 1], log_decay[:, 2 * pair + 1 : 2 * pair + 2])
                dts = halves(dt[:, 2 * pair : 2 * pair + 1], dt[:, 2 * pair + 1 : 2 * pair + 2])
                last = logs[chunk - 1 : chunk, :]
                old = s_ref[sub, :, cols]
                dnew = dstate_ref[:, cols]
                old_low, dnew_low = old.astype(BF16), dnew.astype(BF16)
                faded = (g * jnp.exp(logs)).astype(BF16)
                tail = jnp.exp(last - logs)
                dreader = dreader + nt(faded, old_low)
                ahead = nn(writer, dnew_low)
                dx = g * skip[:, cols] + ahead * tail * dts
                dwriter = dwriter + nt((x * tail * dts).astype(BF16), dnew_low)
                reach.append(x * ahead * tail)
                carried.append(jnp.sum(old * dnew, axis=0, keepdims=True) * jnp.exp(last))
                dstate_ref[:, cols] = jnp.exp(last) * dnew + tn(reader, faded)
                x_low = x.astype(BF16)
                for side in range(2):
                    head = 2 * pair + side
                    own = (lane < HDIM) == (side == 0)
                    g_own = jnp.where(own, g, 0.0).astype(BF16)
                    gap = log_decay[:, head : head + 1] - flat[head : head + 1, :]
                    decays = jnp.exp(jnp.where(mask, gap, -1e30))
                    steps = flat[8 + head : 9 + head, :]
                    spread = nt(g_own, x_low) * decays
                    weight = cross * decays * steps
                    dx = dx + tn(weight.astype(BF16), g_own)
                    cross_grad = cross_grad + spread * steps
                    sums = jnp.sum(spread * cross, axis=0, keepdims=True)
                    fall = fall + jnp.where(row == head, sums, 0.0)
                dact_ref[span, cols] = dx
            cross_low = cross_grad.astype(BF16)
            dact_ref[span, chans : chans + NSTATE] = dwriter + tn(cross_low, reader)
            dact_ref[span, chans + NSTATE :] = dreader + nn(cross_low, writer)
            reach = nn(jnp.concatenate(reach, axis=1), sum_ref[...], HIGH)
            carried = nn(jnp.concatenate(carried, axis=1), sum_ref[...], HIGH)
            direct = jnp.transpose(fall) + reach
            given = dt * reach
            dlog = scan_dot[span] - dt * direct
            ends = jnp.sum(given, axis=0, keepdims=True) + carried
            at_end = lax.broadcasted_iota(jnp.int32, (chunk, LANES), 0) == chunk - 1
            dlog = dlog + jnp.where(at_end, ends, 0.0)
            ddecay = tn(lower, dlog, HIGH)
            ddt_ref[span, :] = direct + ddecay * rate
            acc_ref[8:9, :LANES] += jnp.sum(ddecay * dt, axis=0, keepdims=True)
        dstate_ref[...] = dstate_ref[...] * keep
        ddt_raw = ddt_ref[...] * sigmoid(step_in)
        acc_ref[7:8, :LANES] += jnp.sum(ddt_raw, axis=0, keepdims=True)
        dpre_ref[block : block + 8, :] = dpre_ref[0:8, :] * after
        dpre_ref[0:block, :] = dact_ref[...] * slope
        raw = conv_ref[8 : 8 + block, :]
        acc_ref[CONV : CONV + 1, : sz.conv] += jnp.sum(dpre_ref[0:block, :], axis=0, keepdims=True)
        draw = jnp.zeros((block, sz.conv), F32)
        for tap in range(CONV):
            later = dpre_ref[tap : tap + block, :]
            draw = draw + pk_ref[tap : tap + 1, : sz.conv] * later
            acc_ref[tap : tap + 1, : sz.conv] += jnp.sum(raw * later, axis=0, keepdims=True)
        low = jnp.concatenate(
            [dz.astype(BF16), draw.astype(BF16), ddt_raw.astype(BF16)], axis=1
        )
        gh_ref[...] = nt(low, w_ref[...]).astype(BF16)
        gt_ref[...] = nt(order_ref[...], low).astype(BF16)

    width = sz.width
    back = blocks - 1
    per = block // 8
    return pl.pallas_call(
        kernel,
        grid=(blocks,),
        out_shape=[
            jax.ShapeDtypeStruct((sz.tokens, width), BF16),
            jax.ShapeDtypeStruct((sz.grad_rows, sz.tokens), BF16),
            jax.ShapeDtypeStruct((sz.tokens, chans), BF16),
            jax.ShapeDtypeStruct((16, width), F32),
        ],
        in_specs=[
            pl.BlockSpec(memory_space=pltpu.SMEM),
            pl.BlockSpec((block, width), lambda i: (back - i, 0)),
            pl.BlockSpec((block, sz.cols), lambda i: (back - i, 0)),
            pl.BlockSpec((8, sz.cols), lambda i: (jnp.maximum((back - i) * per - 1, 0), 0)),
            pl.BlockSpec((block, chans), lambda i: (back - i, 0)),
            pl.BlockSpec((subs, NSTATE, chans), lambda i: (back - i, 0, 0)),
            pl.BlockSpec((block, LANES), lambda i: (back - i, 0)),
            pl.BlockSpec((None, width, sz.cols), lambda i: (layer, 0, 0)),
            pl.BlockSpec((None, chans, width), lambda i: (layer, 0, 0)),
            pl.BlockSpec((None, 16, width), lambda i: (layer, 0, 0)),
            pl.BlockSpec((sz.grad_rows, sz.cols), lambda i: (0, 0)),
            pl.BlockSpec((chans, LANES), lambda i: (0, 0)),
        ],
        out_specs=[
            pl.BlockSpec((block, width), lambda i: (back - i, 0)),
            pl.BlockSpec((sz.grad_rows, block), lambda i: (0, back - i)),
            pl.BlockSpec((block, chans), lambda i: (back - i, 0)),
            pl.BlockSpec((16, width), lambda i: (0, 0)),
        ],
        scratch_shapes=[
            pltpu.VMEM((block + 8, sz.conv), F32),
            pltpu.VMEM((block + 8, sz.conv), F32),
            pltpu.VMEM((block, sz.conv), F32),
            pltpu.VMEM((chunk, LANES), F32),
            pltpu.VMEM((block, LANES), F32),
            pltpu.VMEM((NSTATE, chans), F32),
        ],
        compiler_params=pltpu.CompilerParams(vmem_limit_bytes=VMEM_LIMIT),
        name="backward_core",
    )(resets, grads, proj, proj, mixed, states, stats, weights, weight_out, pack, order, sz.head_sum())


def weight_grads(sz, grads_t, gathered, scaled, out_grads):
    cols = 256

    def kernel(gt_ref, h_ref, q_ref, g_ref, in_ref, out_ref):
        in_ref[...] = nn(gt_ref[...], h_ref[...]).astype(BF16)
        out_ref[...] = tn(q_ref[...], g_ref[...]).astype(BF16)

    tokens, width, chans = sz.tokens, sz.width, sz.channels
    return pl.pallas_call(
        kernel,
        grid=(width // cols,),
        out_shape=[
            jax.ShapeDtypeStruct((sz.grad_rows, width), BF16),
            jax.ShapeDtypeStruct((chans, width), BF16),
        ],
        in_specs=[
            pl.BlockSpec((sz.grad_rows, tokens), lambda i: (0, 0)),
            pl.BlockSpec((tokens, cols), lambda i: (0, i)),
            pl.BlockSpec((tokens, chans), lambda i: (0, 0)),
            pl.BlockSpec((tokens, cols), lambda i: (0, i)),
        ],
        out_specs=[
            pl.BlockSpec((sz.grad_rows, cols), lambda i: (0, i)),
            pl.BlockSpec((chans, cols), lambda i: (0, i)),
        ],
        compiler_params=pltpu.CompilerParams(vmem_limit_bytes=VMEM_LIMIT),
        name="weight_grads",
    )(grads_t, gathered, scaled, out_grads)


def input_norm(residual, in_gain):
    return (
        residual
        * lax.rsqrt(jnp.mean(residual * residual, axis=1, keepdims=True) + EPS_NORM)
        * in_gain
    )


def adam_update(weight, moment, second, gradient, rate, decay):
    moment_new = BETA_ONE * moment + (1.0 - BETA_ONE) * gradient
    second_new = BETA_TWO * second + (1.0 - BETA_TWO) * gradient * gradient
    corrected = moment_new / (1.0 - BETA_ONE**ADAM_STEP)
    corrected_sq = second_new / (1.0 - BETA_TWO**ADAM_STEP)
    weight_new = weight - rate * (corrected / (jnp.sqrt(corrected_sq) + ADAM_EPS) + decay * weight)
    return (weight_new, moment_new, second_new)


def shards(
    inputs,
    cotangent,
    valid_lengths,
    proj_in,
    proj_in_m,
    proj_in_v,
    proj_state,
    proj_state_m,
    proj_state_v,
    proj_out,
    proj_out_m,
    proj_out_v,
    head_params,
    head_m,
    head_v,
    shared_params,
    shared_m,
    shared_v,
):
    section = lax.axis_index("section")
    head_idx = lax.axis_index("head")
    count = lax.axis_size("head")
    rows, width = inputs.shape[1], inputs.shape[2]
    heads = head_params.shape[1]
    tokens = rows * count
    sz = Sizes(heads, tokens, width)
    order = sz.order()
    start_block, seq_length, resets = seq_layout(
        lax.dynamic_index_in_dim(valid_lengths, section, 0, keepdims=False)
    )
    token = head_idx * rows + jnp.arange(rows, dtype=jnp.int32)
    own_block = token // STRETCH
    position = token - start_block[own_block] * STRETCH
    live = (position < seq_length[own_block]).astype(F32)[:, None]
    first_in = lax.dynamic_index_in_dim(inputs, section, 0, keepdims=False).astype(F32)
    last_grad = lax.dynamic_index_in_dim(cotangent, section, 0, keepdims=False).astype(F32)
    own_weights = prepare_weights(sz, proj_in[0], proj_state[0], order)
    own_out = proj_out[0].astype(BF16)
    own_out = jnp.pad(own_out, ((0, sz.channels - own_out.shape[0]), (0, 0)))
    own_pack = pack_params(sz, head_params[0], shared_params[0])
    weights, weight_out, pack = both_sections([own_weights, own_out, own_pack], 0)

    kept = []
    residual = first_in
    for layer in range(2):
        in_gain = pack[layer, GAIN_ROW]
        normed = input_norm(residual, in_gain).astype(BF16)
        (gathered,) = gather_rows(count, normed, None, 1)
        partial, squares, proj, mixed, states = forward_core(
            sz, layer, resets, gathered, weights, weight_out, pack, rows
        )
        summed, all_squares = scatter_rows(count, partial, squares, 2)
        scale = lax.rsqrt(jnp.sum(all_squares, axis=0)[0] / (HEADS * HDIM) + EPS_NORM)
        branch = summed * scale[:, None]
        result = (residual + live * branch).astype(BF16)
        kept.append((residual, in_gain, gathered, proj, mixed, states, scale, branch, result))
        residual = result.astype(F32)

    upstream = last_grad
    made = [None, None]
    input_grads = [None, None]
    for layer in (1, 0):
        residual, in_gain, gathered, proj, mixed, states, scale, branch, _ = kept[layer]
        out_grad = (live * upstream).astype(BF16)
        along = jnp.sum(out_grad.astype(F32) * branch, axis=1)
        stats = jnp.stack([scale, along])
        stats = jnp.pad(stats, ((0, 6), (0, LANES - rows)))
        out_grads, all_stats = gather_rows(count, out_grad, stats, 3)
        all_stats = all_stats[:, :2, :rows].transpose(0, 2, 1).reshape(tokens, 2)
        all_stats = jnp.pad(all_stats, ((0, 0), (0, LANES - 2)))
        grad_rows, grads_t, scaled, small = backward_core(
            sz, layer, resets, out_grads, proj, mixed, states, all_stats, weights, weight_out, pack, order
        )
        (grad_normed,) = scatter_rows(count, grad_rows, None, 4)
        in_t, out_w = weight_grads(sz, grads_t, gathered, scaled, out_grads)
        _, in_pull = jax.vjp(input_norm, residual, in_gain)
        grad_res, grad_in_gain = in_pull(grad_normed)
        small = jnp.concatenate(
            [small[:GAIN_ROW], grad_in_gain[None], small[GAIN_ROW + 1 :]], axis=0
        )
        made[layer] = [in_t, out_w, small]
        grad_res = grad_res + upstream
        input_grads[layer] = grad_res
        upstream = grad_res.astype(BF16).astype(F32)

    sum_t, sum_out, small, layer_outs, grad_buffer = trade_sections(
        list(zip(made[0], made[1])),
        [(kept[0][8], kept[1][8]), (input_grads[0], input_grads[1])],
        5,
    )
    grad_in = sum_t[: sz.master].T
    grad_out = sum_out[: heads * HDIM]

    state_part = sum_t[sz.master_pad :].astype(BF16)
    share_rows = 16 * count
    (state_own,) = scatter_rows(count, state_part.reshape(share_rows, -1), None, 6)
    (state_all,) = gather_rows(count, state_own.astype(BF16), None, 7)
    grad_state = state_all.reshape(state_part.shape).astype(F32).T
    chans = heads * HDIM
    conv_rows = small[: CONV + 1, sz.channels : sz.conv].reshape(-1)
    shared_own = jnp.concatenate([conv_rows, small[GAIN_ROW]])
    shared_rows = -(-shared_own.shape[0] // (8 * LANES)) * 8
    shared_own = jnp.pad(shared_own, (0, shared_rows * LANES - shared_own.shape[0]))
    shared_all = gather_small(count, shared_own.reshape(shared_rows, LANES), 8)
    grad_shared = jnp.sum(shared_all, axis=0).reshape(-1)[: shared_params.shape[1]]
    head_part = head_params[0]
    taps = small[:CONV, :chans].reshape(CONV, heads, HDIM).transpose(1, 0, 2).reshape(heads, -1)
    grad_head = jnp.concatenate(
        [
            taps,
            small[5, :chans].reshape(heads, HDIM),
            small[CONV, :chans].reshape(heads, HDIM),
            small[7, :heads][:, None],
            (small[8, :heads] * -jnp.exp(head_part[:, -2]))[:, None],
            jnp.sum(small[6, :chans].reshape(heads, HDIM), axis=1)[:, None],
        ],
        axis=1,
    )
    local_sq = (
        jnp.sum(sum_t[: sz.master] ** 2) + jnp.sum(grad_out * grad_out) + jnp.sum(grad_head * grad_head)
    )
    local_sq = local_sq + (jnp.sum(grad_state * grad_state) + jnp.sum(grad_shared * grad_shared)) / count
    sums = gather_small(count, jnp.full((8, LANES), local_sq, F32), 9)
    section_sq = jnp.sum(sums[:, 0, 0])
    norm_sq = section_sq + lax.ppermute(section_sq, "section", [(0, 1), (1, 0)])
    grad_norm = jnp.sqrt(norm_sq)
    threshold = CLIP_COEF * PARAMS**0.5
    clip_scale = threshold / jnp.maximum(grad_norm, threshold)
    new_in = adam_update(
        proj_in[0], proj_in_m[0], proj_in_v[0], clip_scale * grad_in, LEARN_MATRIX, WEIGHT_DECAY
    )
    new_state = adam_update(
        proj_state[0], proj_state_m[0], proj_state_v[0], clip_scale * grad_state, LEARN_MATRIX, WEIGHT_DECAY
    )
    new_out = adam_update(
        proj_out[0], proj_out_m[0], proj_out_v[0], clip_scale * grad_out, LEARN_MATRIX, WEIGHT_DECAY
    )
    new_head = adam_update(
        head_part, head_m[0], head_v[0], clip_scale * grad_head, LEARN_VECTOR, 0.0
    )
    new_shared = adam_update(
        shared_params[0], shared_m[0], shared_v[0], clip_scale * grad_shared, LEARN_VECTOR, 0.0
    )
    return (
        layer_outs[None],
        grad_buffer[None],
        grad_norm,
        new_in[0][None],
        new_in[1][None],
        new_in[2][None],
        new_in[0][None].astype(BF16),
        new_state[0][None],
        new_state[1][None],
        new_state[2][None],
        new_state[0][None].astype(BF16),
        new_out[0][None],
        new_out[1][None],
        new_out[2][None],
        new_out[0][None].astype(BF16),
        new_head[0][None],
        new_head[1][None],
        new_head[2][None],
        new_shared[0][None],
        new_shared[1][None],
        new_shared[2][None],
    )


def solution(mesh):
    in_specs = (
        P(None, "head", None),
        P(None, "head", None),
        P(),
        P("section", None, "head"),
        P("section", None, "head"),
        P("section", None, "head"),
        P("section", None, None),
        P("section", None, None),
        P("section", None, None),
        P("section", "head", None),
        P("section", "head", None),
        P("section", "head", None),
        P("section", "head", None),
        P("section", "head", None),
        P("section", "head", None),
        P("section", None),
        P("section", None),
        P("section", None),
    )
    out_specs = (
        P("section", None, "head", None),
        P("section", None, "head", None),
        P(),
        P("section", None, "head"),
        P("section", None, "head"),
        P("section", None, "head"),
        P("section", None, "head"),
        P("section", None, None),
        P("section", None, None),
        P("section", None, None),
        P("section", None, None),
        P("section", "head", None),
        P("section", "head", None),
        P("section", "head", None),
        P("section", "head", None),
        P("section", "head", None),
        P("section", "head", None),
        P("section", "head", None),
        P("section", None),
        P("section", None),
        P("section", None),
    )
    return jax.shard_map(shards, mesh=mesh, in_specs=in_specs, out_specs=out_specs, check_vma=False)
```

```python
import itertools

import jax
import jax.numpy as jnp
import numpy as np
from jax import lax
from jax.experimental import pallas as pl
from jax.experimental.pallas import tpu as pltpu
from jax.sharding import PartitionSpec as P

HEADS = 64
HDIM = 64
NSTATE = 128
CONV = 4
STRETCH = 256
ADAM_STEP = 5
PARAMS = 51698560

HIGH = lax.Precision.HIGHEST
EPS_NORM = 1e-05
ADAM_EPS = 1e-08
BETA_ONE = 0.5
BETA_TWO = 0.5
CLIP_COEF = 0.2
LEARN_MATRIX = 0.02
LEARN_VECTOR = 0.2
WEIGHT_DECAY = 0.1

F32 = jnp.float32
BF16 = jnp.bfloat16
MESH = pl.DeviceIdType.MESH
LANES = 128
CHUNK = 128
COLS = HDIM * 2 + 1
GAIN_ROW = 9
VMEM_LIMIT = 56 << 20


def seq_layout(lengths_row):
    block_count = lengths_row.shape[0]
    block_idx = jnp.arange(block_count, dtype=jnp.int32)
    starts = lengths_row > 0
    start_block = lax.cummax(jnp.where(starts, block_idx, 0), axis=0)
    owner_mask = (start_block[:, None] == block_idx[None, :]).astype(jnp.int32)
    seq_length = jnp.sum(owner_mask * lengths_row[None, :], axis=1)
    return (start_block, seq_length, starts.astype(jnp.float32))


def chip_dims(count):
    side = 4 if count % 64 == 0 else 2
    if count % (side * side) != 0:
        return (count, 1, 1)
    return (count // (side * side), side, side)


def place(dims):
    me = lax.axis_index("head")
    return (me // (dims[1] * dims[2]), (me // dims[2]) % dims[1], me % dims[2])


def linear(dims, spot):
    return (spot[0] * dims[1] + spot[1]) * dims[2] + spot[2]


def moved(dims, spot, shifts):
    return tuple(s if d == 0 else (s + d) % n for s, d, n in zip(spot, shifts, dims))


def shift_of(order, offsets):
    out = [0, 0, 0]
    for axis, off in zip(order, offsets):
        out[axis] = off
    return out


def greet_axes(dims, spot):
    barrier = pltpu.get_barrier_semaphore()
    count = 0
    for axis in range(3):
        for off in range(1, dims[axis]):
            peer = linear(dims, moved(dims, spot, shift_of((axis,), (off,))))
            pl.semaphore_signal(
                barrier, inc=1, device_id={"head": peer}, device_id_type=MESH
            )
            count += 1
    if count:
        pl.semaphore_wait(barrier, count)


def greet_all(count):
    barrier = pltpu.get_barrier_semaphore()
    me = lax.axis_index("head")
    for off in range(1, count):
        pl.semaphore_signal(
            barrier, inc=1, device_id={"head": (me + off) % count}, device_id_type=MESH
        )
    if count > 1:
        pl.semaphore_wait(barrier, count - 1)


def rows_at(shard, rows):
    return pl.ds(pl.multiple_of(shard * rows, rows), rows)


def column_parts(width, shares):
    tiles = width // LANES
    parts, start, taken = [], 0, 0
    for share, order, group in shares:
        taken += share
        stop = tiles * taken // 16 * LANES
        if stop > start:
            parts.append((start, stop - start, order, group))
            start = stop
    return parts


GATHER = ((2, (2, 1, 0), 0), (2, (1, 2, 0), 0), (6, (0, 2, 1), 0), (6, (0, 1, 2), 0))
GATHER_SMALL = ((8, (0, 2, 1), 0), (8, (0, 1, 2), 0))
SCATTER = (
    (1, (2, 0, 1), 0), (1, (1, 0, 2), 0), (1, (0, 1, 2), 0), (1, (0, 2, 1), 0),
    (3, (2, 1, 0), 0), (3, (1, 2, 0), 0), (3, (2, 1, 0), 1), (3, (1, 2, 0), 1),
)
SCATTER_SMALL = ((8, (2, 1, 0), 0), (8, (1, 2, 0), 0))
SCATTER_PACE = (0.3, 0.9, 0.7, 2.0)


def guarded(preds, action):
    preds = [pred for pred in preds if pred is not None]
    if not preds:
        action()
        return
    cond = preds[0]()
    for pred in preds[1:]:
        cond = jnp.logical_and(cond, pred())
    pl.when(cond)(action)


def gather_steps(dims, parts, rows, own_ref, all_ref, send_sem, recv_sem):
    spot = place(dims)
    me = linear(dims, spot)
    waits = []
    counter = [0] * len(parts)

    def lined(axis):
        return axis == 0 and dims[0] > 2 and dims[1] == 2

    def above(axis, dist):
        return lambda: spot[axis] + dist < dims[axis]

    def below(axis, dist):
        return lambda: spot[axis] >= dist

    def sources(part, pos):
        axis = parts[part][2][pos]
        if not lined(axis):
            return [(off, None) for off in range(1, dims[axis])]
        out = []
        for dist in range(1, dims[axis]):
            out.append((dist, above(axis, dist)))
            out.append((-dist, below(axis, dist)))
        return out

    def block(part, offsets):
        start, width, order, _ = parts[part]
        shard = linear(dims, moved(dims, spot, shift_of(order, offsets)))
        return shard, all_ref.at[rows_at(shard, rows), pl.ds(start, width)]

    def push(part, offsets, pos, preds, src, came):
        axis = parts[part][2][pos]
        shard, dst = block(part, offsets)
        up, down = (1, above(axis, 1)), (-1, below(axis, 1))
        if lined(axis):
            targets = [up, down] if came == 0 else [down] if came > 0 else [up]
        else:
            targets = [(off, None) for off in range(1, dims[axis])] if came == 0 else []
        for off, pred in targets:
            peer = linear(dims, moved(dims, spot, shift_of((axis,), (off,))))
            number = counter[part]
            counter[part] += 1

            def begin(peer=peer, number=number):
                pltpu.make_async_remote_copy(
                    src_ref=dst if src is None else src,
                    dst_ref=dst,
                    send_sem=send_sem.at[part, number],
                    recv_sem=recv_sem.at[part, shard],
                    device_id={"head": peer},
                    device_id_type=MESH,
                ).start()

            guarded([pred], begin)
            waits.append((preds + [pred], part, number))

    def visit(part, offsets, preds, pos, came):
        def body():
            shard, dst = block(part, offsets)
            pltpu.make_async_remote_copy(
                src_ref=dst,
                dst_ref=dst,
                send_sem=send_sem.at[part, 0],
                recv_sem=recv_sem.at[part, shard],
                device_id={"head": me},
                device_id_type=MESH,
            ).wait_recv()
            push(part, offsets, pos, preds, None, came)
            for later in range(pos + 1, 3):
                push(part, offsets, later, preds, None, 0)

        guarded(preds, body)

    for pos in range(3):
        for part, (start, width, _, _) in enumerate(parts):
            push(part, (0, 0, 0), pos, [], own_ref.at[:, pl.ds(start, width)], 0)
    todo = []
    for part in range(len(parts)):
        first, second, third = (sources(part, pos) for pos in range(3))
        for k, (oa, pa) in enumerate(first):
            todo.append(((0, k, part), part, (oa, 0, 0), [pa], 0, oa))
        for ka, (oa, pa) in enumerate([(0, None)] + first):
            for k, (ob, pb) in enumerate(second):
                todo.append(((1, ka + k, part), part, (oa, ob, 0), [pa, pb], 1, ob))
            for kb, (ob, pb) in enumerate([(0, None)] + second):
                for k, (oc, pc) in enumerate(third):
                    todo.append(
                        ((2, ka + kb + k, part), part, (oa, ob, oc), [pa, pb, pc], 2, oc)
                    )
    todo.sort(key=lambda entry: (sum(abs(off) for off in entry[2]), entry[0]))
    for _, part, offsets, preds, pos, came in todo:
        visit(part, offsets, preds, pos, came)
    for preds, part, number in waits:

        def settle(part=part, number=number):
            start, width, _, _ = parts[part]
            ref = own_ref.at[:, pl.ds(start, width)]
            pltpu.make_async_remote_copy(
                src_ref=ref,
                dst_ref=ref,
                send_sem=send_sem.at[part, number],
                recv_sem=recv_sem.at[part, 0],
                device_id={"head": me},
                device_id_type=MESH,
            ).wait_send()

        guarded(preds, settle)


def gather_sends(dims):
    return 3 * dims[0] * dims[1] * dims[2]


def scatter_steps(dims, parts, rows, in_ref, out_ref, box_ref, send_sem, recv_sem):
    spot = place(dims)
    me = linear(dims, spot)
    sends = []

    def size(part, pos):
        return dims[parts[part][2][pos]]

    def slot_one(part, ea, ob, oc):
        return ((ea - 1) * size(part, 1) + ob) * size(part, 2) + oc

    def slot_two(part, eb, oc):
        base = (size(part, 0) - 1) * size(part, 1) * size(part, 2)
        return base + (eb - 1) * size(part, 2) + oc

    def slot_three(part, ec):
        return slot_two(part, size(part, 1), 0) + ec - 1

    def cols(part):
        return pl.ds(parts[part][0], parts[part][1])

    def mine(part, offsets):
        shard = linear(dims, moved(dims, spot, shift_of(parts[part][2], offsets)))
        return in_ref.at[rows_at(shard, rows), cols(part)]

    def send(part, src, pos, off, slot):
        peer = linear(dims, moved(dims, spot, shift_of((parts[part][2][pos],), (off,))))
        copy = pltpu.make_async_remote_copy(
            src_ref=src,
            dst_ref=box_ref.at[slot, :, cols(part)],
            send_sem=send_sem.at[part, slot],
            recv_sem=recv_sem.at[part, slot],
            device_id={"head": peer},
            device_id_type=MESH,
        )
        copy.start()
        sends.append(copy)

    def arrived(part, slot):
        ref = box_ref.at[slot, :, cols(part)]
        pltpu.make_async_remote_copy(
            src_ref=ref,
            dst_ref=ref,
            send_sem=send_sem.at[part, slot],
            recv_sem=recv_sem.at[part, slot],
            device_id={"head": me},
            device_id_type=MESH,
        ).wait_recv()
        return ref[...].astype(F32)

    def combined(part, ob, oc, stages):
        total = mine(part, (0, ob, oc))[...].astype(F32)
        for ea in range(1, size(part, 0)):
            total = total + arrived(part, slot_one(part, ea, ob, oc))
        for eb in range(1, size(part, 1)) if stages > 1 else ():
            total = total + arrived(part, slot_two(part, eb, oc))
        for ec in range(1, size(part, 2)) if stages > 2 else ():
            total = total + arrived(part, slot_three(part, ec))
        return total

    def put_by(part, ob, oc, total):
        if size(part, 0) > 1:
            hold = box_ref.at[slot_one(part, 1, ob, oc), :, cols(part)]
        elif size(part, 1) > 1 and ob == 0:
            hold = box_ref.at[slot_two(part, 1, oc), :, cols(part)]
        else:
            return mine(part, (0, ob, oc))
        hold[...] = total.astype(box_ref.dtype)
        return hold

    def first(part, ob, oc, off):
        slot = slot_one(part, size(part, 0) - off, ob, oc)
        send(part, mine(part, (off, ob, oc)), 0, off, slot)

    def second(part, ob, oc, _):
        hold = put_by(part, ob, oc, combined(part, ob, oc, 1))
        send(part, hold, 1, ob, slot_two(part, size(part, 1) - ob, oc))

    def third(part, _, oc, __):
        hold = put_by(part, 0, oc, combined(part, 0, oc, 2))
        send(part, hold, 2, oc, slot_three(part, size(part, 2) - oc))

    def last(part, _, __, ___):
        out_ref[:, cols(part)] = combined(part, 0, 0, 3)

    lag, rest, turn, end = SCATTER_PACE
    program = []
    for part, (_, _, _, group) in enumerate(parts):
        for ob, oc in itertools.product(range(size(part, 1)), range(size(part, 2))):
            for off in range(1, size(part, 0)):
                rank = (0.0 if ob else rest) + group * lag
                program.append((rank, oc == 0, off, part, first, ob, oc))
            if ob:
                program.append((turn + group * lag, oc == 0, 0, part, second, ob, oc))
        for oc in range(1, size(part, 2)):
            program.append((end + group * lag, False, 0, part, third, 0, oc))
        program.append((3.0 + group * lag, True, 0, part, last, 0, 0))
    program.sort(key=lambda step: step[:4])
    for _, _, off, part, action, ob, oc in program:
        action(part, ob, oc, off)
    return sends


def start_direct(count, own_ref_of, box_ref, send_sem, recv_sem):
    me = lax.axis_index("head")
    copies = []
    for off in range(1, count):
        peer = (me + off) % count
        copy = pltpu.make_async_remote_copy(
            src_ref=own_ref_of(peer),
            dst_ref=box_ref.at[me],
            send_sem=send_sem.at[off],
            recv_sem=recv_sem.at[count - off],
            device_id={"head": peer},
            device_id_type=MESH,
        )
        copy.start()
        copies.append(copy)
    return copies


def wait_direct(count, box_ref, copies, recv_sem, send_sem):
    me = lax.axis_index("head")
    for off in range(1, count):
        ref = box_ref.at[(me + off) % count]
        pltpu.make_async_remote_copy(
            src_ref=ref,
            dst_ref=ref,
            send_sem=send_sem.at[off],
            recv_sem=recv_sem.at[off],
            device_id={"head": me},
            device_id_type=MESH,
        ).wait_recv()
    for copy in copies:
        copy.wait_send()


VMEM_SPEC = pl.BlockSpec(memory_space=pltpu.VMEM)
ANY_SPEC = pl.BlockSpec(memory_space=pl.ANY)
DMA = pltpu.SemaphoreType.DMA


def params(collective_id):
    return pltpu.CompilerParams(
        collective_id=collective_id, has_side_effects=True, vmem_limit_bytes=VMEM_LIMIT
    )


def gather_scratch(parts, dims, count):
    return [DMA((len(parts), gather_sends(dims))), DMA((len(parts), count)), DMA]


def run_gather(count, parts, own_ref, all_ref, sems, stat=None):
    dims = chip_dims(count)
    rows = own_ref.shape[0]
    me = lax.axis_index("head")
    send_sem, recv_sem, local_sem = sems
    local = pltpu.make_async_copy(own_ref, all_ref.at[rows_at(me, rows)], local_sem)
    local.start()
    if stat is not None:
        stat_ref, box_ref, small_send, small_recv = stat
        copies = start_direct(count, lambda peer: stat_ref, box_ref, small_send, small_recv)
        box_ref[me] = stat_ref[...]
    gather_steps(dims, parts, rows, own_ref, all_ref, send_sem, recv_sem)
    if stat is not None:
        wait_direct(count, box_ref, copies, small_recv, small_send)
    local.wait()


def gather_rows(count, own, stats, collective_id):
    dims = chip_dims(count)
    rows, width = own.shape
    parts = column_parts(width, GATHER_SMALL)

    def kernel(own_ref, stat_ref, all_ref, box_ref, *sems):
        greet_all(count)
        run_gather(count, parts, own_ref, all_ref, sems[:3], (stat_ref, box_ref) + sems[3:])

    return pl.pallas_call(
        kernel,
        out_shape=[
            jax.ShapeDtypeStruct((count * rows, width), own.dtype),
            jax.ShapeDtypeStruct((count,) + stats.shape, stats.dtype),
        ],
        in_specs=[VMEM_SPEC] * 2,
        out_specs=[ANY_SPEC, VMEM_SPEC],
        scratch_shapes=gather_scratch(parts, dims, count) + [DMA((count,)), DMA((count,))],
        compiler_params=params(collective_id),
        name="gather_rows",
    )(own, stats)


def scatter_scratch(parts, count, rows, width):
    slots = max(count - 1, 1)
    return [pltpu.VMEM((slots, rows, width), BF16), DMA((len(parts), slots)), DMA((len(parts), slots))]


def scatter_rows(count, partial, small, collective_id):
    dims = chip_dims(count)
    width = partial.shape[1]
    rows = partial.shape[0] // count
    parts = column_parts(width, SCATTER_SMALL)

    def kernel(in_ref, small_ref, out_ref, sums_ref, box_ref, send_sem, recv_sem, small_send, small_recv):
        me = lax.axis_index("head")
        greet_all(count)
        copies = start_direct(
            count, lambda peer: small_ref.at[peer], sums_ref, small_send, small_recv
        )
        sums_ref[me] = small_ref[me]
        sends = scatter_steps(dims, parts, rows, in_ref, out_ref, box_ref, send_sem, recv_sem)
        wait_direct(count, sums_ref, copies, small_recv, small_send)
        for copy in sends:
            copy.wait_send()

    return pl.pallas_call(
        kernel,
        out_shape=[
            jax.ShapeDtypeStruct((rows, width), F32),
            jax.ShapeDtypeStruct(small.shape, small.dtype),
        ],
        in_specs=[VMEM_SPEC] * 2,
        out_specs=[VMEM_SPEC] * 2,
        scratch_shapes=scatter_scratch(parts, count, rows, width) + [DMA((count,)), DMA((count,))],
        compiler_params=params(collective_id),
        name="scatter_rows",
    )(partial, small)


def norm_rows(value, gain):
    mean = jnp.mean(value * value, axis=1, keepdims=True)
    return value * lax.rsqrt(mean + EPS_NORM) * gain


def norm_rows_back(value, gain, grad):
    width = value.shape[1]
    scale = lax.rsqrt(jnp.mean(value * value, axis=1, keepdims=True) + EPS_NORM)
    scaled = grad * gain
    dot = jnp.sum(scaled * value, axis=1, keepdims=True)
    back = scaled * scale - value * (scale * scale * scale * dot * (1.0 / width))
    return back, jnp.sum(grad * value * scale, axis=0, keepdims=True)


def opening(count, sz, own_weights, own_out, own_pack, first, collective_id):
    dims = chip_dims(count)
    rows, width = first.shape
    parts = column_parts(width, GATHER)

    def kernel(w_ref, wo_ref, pk_ref, x_ref, ws_ref, wos_ref, pks_ref, all_ref, own_ref, *sems):
        section = lax.axis_index("section")
        other = 1 - section
        barrier = pltpu.get_barrier_semaphore()
        pl.semaphore_signal(barrier, inc=1, device_id={"section": other}, device_id_type=MESH)
        me = lax.axis_index("head")
        for off in range(1, count):
            pl.semaphore_signal(
                barrier, inc=1, device_id={"head": (me + off) % count}, device_id_type=MESH
            )
        pl.semaphore_wait(barrier, count)
        pair_send, pair_recv, pair_local = sems[3:]
        copies = []
        for k, (src, dst) in enumerate(((pk_ref, pks_ref), (w_ref, ws_ref), (wo_ref, wos_ref))):
            copy = pltpu.make_async_remote_copy(
                src_ref=src,
                dst_ref=dst.at[section],
                send_sem=pair_send.at[k],
                recv_sem=pair_recv.at[k],
                device_id={"section": other},
                device_id_type=MESH,
            )
            copy.start()
            copies.append(copy)
            if k > 0:
                local = pltpu.make_async_copy(src, dst.at[section], pair_local.at[k])
                local.start()
                copies.append(local)
        pks_ref[section] = pk_ref[...]
        copies[0].wait()
        gain = pks_ref[0, GAIN_ROW : GAIN_ROW + 1, :]
        own_ref[...] = norm_rows(x_ref[...].astype(F32), gain).astype(BF16)
        run_gather(count, parts, own_ref, all_ref, sems[:3])
        for copy in copies[1:]:
            copy.wait()

    return pl.pallas_call(
        kernel,
        out_shape=[
            jax.ShapeDtypeStruct((2,) + own_weights.shape, BF16),
            jax.ShapeDtypeStruct((2,) + own_out.shape, BF16),
            jax.ShapeDtypeStruct((2,) + own_pack.shape, F32),
            jax.ShapeDtypeStruct((count * rows, width), BF16),
        ],
        in_specs=[VMEM_SPEC] * 4,
        out_specs=[ANY_SPEC, ANY_SPEC, VMEM_SPEC, ANY_SPEC],
        scratch_shapes=[pltpu.VMEM((rows, width), BF16)]
        + gather_scratch(parts, dims, count)
        + [DMA((3,))] * 3,
        compiler_params=params(collective_id),
        name="opening",
    )(own_weights, own_out, own_pack, first)


def column_of(tile, rows):
    row = lax.broadcasted_iota(jnp.int32, (rows, rows), 0)
    lane = lax.broadcasted_iota(jnp.int32, (rows, rows), 1)
    return nt((row == lane).astype(F32), tile, HIGH)[:, 0:1]


def write_stats(stat_ref, squares, out_grad, branch, rows):
    dot = nt(jnp.ones((8, branch.shape[1]), F32), out_grad * branch, HIGH)
    scale = lax.rsqrt(squares / (HEADS * HDIM) + EPS_NORM)
    row = lax.broadcasted_iota(jnp.int32, (8, rows), 0)
    stat_ref[...] = jnp.zeros_like(stat_ref)
    stat_ref[:, :rows] = jnp.where(row == 0, scale, jnp.where(row == 1, dot, 0.0))


def after_forward(count, sz, layer, partial, squares, residual, live, pack, cotangent, collective_id):
    dims = chip_dims(count)
    rows, width = residual.shape
    parts, back = column_parts(width, GATHER), column_parts(width, SCATTER)
    turn = cotangent is not None

    def kernel(*refs):
        refs = list(refs)
        in_ref, sq_ref, u_ref, live_ref, pk_ref = (refs.pop(0) for _ in range(5))
        cot_ref = refs.pop(0) if turn else None
        result_ref, branch_ref, total_ref, all_ref = (refs.pop(0) for _ in range(4))
        stats_ref = refs.pop(0) if turn else None
        sums_ref, own_ref, box_ref, rs_send, rs_recv = (refs.pop(0) for _ in range(5))
        ag_sems = [refs.pop(0) for _ in range(3)]
        small_send, small_recv = refs.pop(0), refs.pop(0)
        me = lax.axis_index("head")
        greet_all(count)
        copies = start_direct(count, lambda peer: sq_ref.at[peer], sums_ref, small_send, small_recv)
        sums_ref[me] = sq_ref[me]
        sends = scatter_steps(dims, back, rows, in_ref, branch_ref, box_ref, rs_send, rs_recv)
        wait_direct(count, sums_ref, copies, small_recv, small_send)
        total = jnp.sum(sums_ref[...], axis=0)
        total_ref[...] = total
        scale = lax.rsqrt(column_of(total, rows) / (HEADS * HDIM) + EPS_NORM)
        branch = branch_ref[...] * scale
        branch_ref[...] = branch
        live_col = live_ref[:, 0:1]
        result = (u_ref[...].astype(F32) + live_col * branch).astype(BF16)
        result_ref[...] = result
        stat = None
        if turn:
            stat_ref, stat_send, stat_recv = refs
            out_grad = (live_col * cot_ref[...].astype(F32)).astype(BF16)
            own_ref[...] = out_grad
            write_stats(stat_ref, total, out_grad.astype(F32), branch, rows)
            stat = (stat_ref, stats_ref, stat_send, stat_recv)
        else:
            gain = pk_ref[layer + 1, GAIN_ROW : GAIN_ROW + 1, :]
            own_ref[...] = norm_rows(result.astype(F32), gain).astype(BF16)
        run_gather(count, parts, own_ref, all_ref, ag_sems, stat)
        for copy in sends:
            copy.wait_send()

    out_shape = [
        jax.ShapeDtypeStruct((rows, width), BF16),
        jax.ShapeDtypeStruct((rows, width), F32),
        jax.ShapeDtypeStruct((8, rows), F32),
        jax.ShapeDtypeStruct((count * rows, width), BF16),
    ]
    out_specs = [VMEM_SPEC, VMEM_SPEC, VMEM_SPEC, ANY_SPEC]
    scratch = [pltpu.VMEM((count, 8, rows), F32), pltpu.VMEM((rows, width), BF16)]
    scratch += scatter_scratch(back, count, rows, width) + gather_scratch(parts, dims, count)
    scratch += [DMA((count,))] * 2
    operands = [partial, squares, residual, live, pack]
    if turn:
        out_shape.append(jax.ShapeDtypeStruct((count, 8, LANES), F32))
        out_specs.append(VMEM_SPEC)
        scratch += [pltpu.VMEM((8, LANES), F32)] + [DMA((count,))] * 2
        operands.append(cotangent)
    return pl.pallas_call(
        kernel,
        out_shape=out_shape,
        in_specs=[VMEM_SPEC] * len(operands),
        out_specs=out_specs,
        scratch_shapes=scratch,
        compiler_params=params(collective_id),
        name="after_forward",
    )(*operands)


def after_backward(count, sz, layer, partial, residual, upstream, live, pack, below, collective_id):
    dims = chip_dims(count)
    rows, width = residual.shape
    parts, back = column_parts(width, GATHER), column_parts(width, SCATTER)
    more = below is not None

    def kernel(*refs):
        refs = list(refs)
        in_ref, u_ref, up_ref, live_ref, pk_ref = (refs.pop(0) for _ in range(5))
        if more:
            branch_ref, total_ref = refs.pop(0), refs.pop(0)
        grad_ref, low_ref, gain_ref = (refs.pop(0) for _ in range(3))
        if more:
            all_ref, stats_ref = refs.pop(0), refs.pop(0)
        box_ref, rs_send, rs_recv = (refs.pop(0) for _ in range(3))
        greet_all(count) if more else greet_axes(dims, place(dims))
        sends = scatter_steps(dims, back, rows, in_ref, grad_ref, box_ref, rs_send, rs_recv)
        gain = pk_ref[layer, GAIN_ROW : GAIN_ROW + 1, :]
        grad, gain_grad = norm_rows_back(u_ref[...].astype(F32), gain, grad_ref[...])
        grad = grad + up_ref[...].astype(F32)
        grad_ref[...] = grad
        low_ref[...] = grad.astype(BF16)
        gain_ref[...] = gain_grad
        if more:
            own_ref, stat_ref, stat_send, stat_recv = (refs.pop(0) for _ in range(4))
            out_grad = (live_ref[:, 0:1] * grad.astype(BF16).astype(F32)).astype(BF16)
            own_ref[...] = out_grad
            write_stats(stat_ref, total_ref[...], out_grad.astype(F32), branch_ref[...], rows)
            run_gather(count, parts, own_ref, all_ref, refs, (stat_ref, stats_ref, stat_send, stat_recv))
        for copy in sends:
            copy.wait_send()

    out_shape = [
        jax.ShapeDtypeStruct((rows, width), F32),
        jax.ShapeDtypeStruct((rows, width), BF16),
        jax.ShapeDtypeStruct((1, width), F32),
    ]
    out_specs = [VMEM_SPEC] * 3
    scratch = scatter_scratch(back, count, rows, width)
    operands = [partial, residual, upstream, live, pack]
    if more:
        out_shape += [
            jax.ShapeDtypeStruct((count * rows, width), BF16),
            jax.ShapeDtypeStruct((count, 8, LANES), F32),
        ]
        out_specs += [ANY_SPEC, VMEM_SPEC]
        scratch += [pltpu.VMEM((rows, width), BF16), pltpu.VMEM((8, LANES), F32)]
        scratch += [DMA((count,))] * 2 + gather_scratch(parts, dims, count)
        operands += list(below)
    return pl.pallas_call(
        kernel,
        out_shape=out_shape,
        in_specs=[VMEM_SPEC] * len(operands),
        out_specs=out_specs,
        scratch_shapes=scratch,
        compiler_params=params(collective_id),
        name="after_backward",
    )(*operands)


def greet_other():
    barrier = pltpu.get_barrier_semaphore()
    other = 1 - lax.axis_index("section")
    pl.semaphore_signal(barrier, inc=1, device_id={"section": other}, device_id_type=MESH)
    pl.semaphore_wait(barrier, 1)
    return other


def add_up(out_ref, mine_ref, got_ref, squares_ref):
    rows, width = out_ref.shape
    step = 16 if rows % 16 == 0 else rows

    def body(i, carry):
        span = pl.ds(pl.multiple_of(i * step, step), step)
        total = mine_ref[span, :].astype(F32) + got_ref[span, :].astype(F32)
        out_ref[span, :] = total
        if squares_ref is not None:
            part = total * total
            for k in range(0, step, 8):
                squares_ref[...] += part[k : k + 8]
        return carry

    lax.fori_loop(0, rows // step, body, 0)


def trade_sections(sums, stacks, squared, collective_id):
    pairs = sums + stacks
    number, summed = len(pairs), len(sums)

    def kernel(*refs):
        ins, outs = refs[: 2 * number], refs[2 * number : 3 * number]
        squares_ref = refs[3 * number]
        boxes = refs[3 * number + 1 : 3 * number + 1 + summed]
        send_sem, recv_sem = refs[3 * number + 1 + summed :]
        squares_ref[...] = jnp.zeros_like(squares_ref)
        section = lax.axis_index("section")
        other = greet_other()

        def go(mine, theirs):
            copies = []
            for k in range(number):
                copy = pltpu.make_async_remote_copy(
                    src_ref=theirs[k],
                    dst_ref=boxes[k] if k < summed else outs[k].at[section],
                    send_sem=send_sem.at[k],
                    recv_sem=recv_sem.at[k],
                    device_id={"section": other},
                    device_id_type=MESH,
                )
                copy.start()
                copies.append(copy)
            for k in range(summed, number):
                outs[k][section] = mine[k][...]
            for k in range(number):
                copies[k].wait()
                if k < summed:
                    add_up(outs[k], mine[k], boxes[k], squares_ref if k < squared else None)

        pl.when(section == 0)(lambda: go(ins[0::2], ins[1::2]))
        pl.when(section == 1)(lambda: go(ins[1::2], ins[0::2]))

    shapes = [jax.ShapeDtypeStruct(a.shape, F32) for a, _ in sums]
    shapes += [jax.ShapeDtypeStruct((2,) + a.shape, a.dtype) for a, _ in stacks]
    shapes.append(jax.ShapeDtypeStruct((8, sums[0][0].shape[1]), F32))
    return pl.pallas_call(
        kernel,
        out_shape=shapes,
        in_specs=[VMEM_SPEC] * (2 * number),
        out_specs=[VMEM_SPEC] * len(shapes),
        scratch_shapes=[pltpu.VMEM(a.shape, a.dtype) for a, _ in sums] + [DMA((number,))] * 2,
        compiler_params=pltpu.CompilerParams(
            collective_id=collective_id, has_side_effects=True, vmem_limit_bytes=VMEM_LIMIT
        ),
        name="trade_sections",
    )(*[a for pair in pairs for a in pair])


class Sizes:
    def __init__(self, heads, tokens, width):
        self.heads = heads
        self.padded = heads + heads % 2
        self.channels = self.padded * HDIM
        self.conv = self.channels + 2 * NSTATE
        self.cols = 2 * self.channels + 2 * NSTATE + LANES
        self.dt = 2 * self.channels + 2 * NSTATE
        self.master = heads * COLS
        self.master_pad = -(-self.master // LANES) * LANES
        self.grad_rows = self.master_pad + 2 * NSTATE
        self.tokens = tokens
        self.width = width
        self.blocks = tokens // STRETCH

    def order(self):
        table = np.zeros((self.grad_rows, self.cols), np.float32)
        for head in range(self.heads):
            for j in range(HDIM):
                table[head * COLS + j, head * HDIM + j] = 1
                table[head * COLS + HDIM + j, self.channels + head * HDIM + j] = 1
            table[head * COLS + 2 * HDIM, self.dt + head] = 1
        for j in range(2 * NSTATE):
            table[self.master_pad + j, 2 * self.channels + j] = 1
        return jnp.asarray(table, BF16)

    def head_sum(self):
        table = np.zeros((self.channels, LANES), np.float32)
        for head in range(self.padded):
            table[head * HDIM : (head + 1) * HDIM, head] = 1
        return jnp.asarray(table, F32)


def nt(left, right, precision=None):
    return lax.dot_general(
        left, right, (((1,), (1,)), ((), ())), precision=precision, preferred_element_type=F32
    )


def tn(left, right, precision=None):
    return lax.dot_general(
        left, right, (((0,), (0,)), ((), ())), precision=precision, preferred_element_type=F32
    )


def nn(left, right, precision=None):
    return jnp.dot(left, right, precision=precision, preferred_element_type=F32)


def split(value):
    high = value.astype(BF16)
    return high, (value - high.astype(F32)).astype(BF16)


def fine(dot, left, right, left_axis, right_axis):
    left_high, left_low = split(left)
    right_high, right_low = split(right)
    return dot(
        jnp.concatenate([left_high, left_low, left_high], axis=left_axis),
        jnp.concatenate([right_high, right_high, right_low], axis=right_axis),
    )


def nt3(left, right):
    return fine(nt, left, right, 1, 1)


def tn3(left, right):
    return fine(tn, left, right, 0, 0)


def nn3(left, right):
    return fine(nn, left, right, 1, 0)


def softplus(value):
    return jnp.maximum(value, 0.0) + jnp.log1p(jnp.exp(-jnp.abs(value)))


def sigmoid(value):
    return 1.0 / (1.0 + jnp.exp(-value))


def halves(left, right):
    rows = left.shape[0]
    lane = lax.broadcasted_iota(jnp.int32, (rows, LANES), 1)
    return jnp.where(lane < HDIM, left, right)


def lower_mask(size):
    row = lax.broadcasted_iota(jnp.int32, (size, size), 0)
    col = lax.broadcasted_iota(jnp.int32, (size, size), 1)
    return row >= col


def step_rows(log_decay, step):
    lane = lax.broadcasted_iota(jnp.int32, log_decay.shape, 1)
    both = jnp.where(lane < 8, log_decay, pltpu.roll(step, 8, 1))
    return jnp.transpose(jnp.where(lane < 16, both, 0.0))


def prepare_weights(sz, proj_in_t, proj_state, order):
    cols = 256
    full = sz.master // 16 * 16

    def kernel(in_ref, state_ref, order_ref, out_ref, low_ref):
        low_ref[:full, :] = in_ref[:full, 0, :].astype(BF16)
        if full < sz.master_pad:
            low_ref[full:, :] = jnp.zeros((sz.master_pad - full, cols), BF16)
        if full < sz.master:
            low_ref[full : full + 16, :] = jnp.concatenate(
                [in_ref[full : sz.master, 0, :], jnp.zeros((full + 16 - sz.master, cols), F32)], axis=0
            ).astype(BF16)
        table = order_ref[: sz.master_pad, :]
        out_ref[...] = tn(table, low_ref[...]).astype(BF16)
        row = lax.broadcasted_iota(jnp.int32, (2 * NSTATE, 2 * NSTATE), 0)
        col = lax.broadcasted_iota(jnp.int32, (2 * NSTATE, 2 * NSTATE), 1)
        one = (row == col).astype(BF16)
        out_ref[2 * sz.channels : sz.dt, :] = nt(one, state_ref[...].astype(BF16)).astype(BF16)

    return pl.pallas_call(
        kernel,
        out_shape=jax.ShapeDtypeStruct((sz.cols, sz.width), BF16),
        grid=(sz.width // cols,),
        in_specs=[
            pl.BlockSpec((sz.master, 1, cols), lambda i: (0, 0, i)),
            pl.BlockSpec((cols, 2 * NSTATE), lambda i: (i, 0)),
            pl.BlockSpec((sz.grad_rows, sz.cols), lambda i: (0, 0)),
        ],
        out_specs=pl.BlockSpec((sz.cols, cols), lambda i: (0, i)),
        scratch_shapes=[pltpu.VMEM((sz.master_pad, cols), BF16)],
        compiler_params=pltpu.CompilerParams(vmem_limit_bytes=VMEM_LIMIT),
        name="prepare_weights",
    )(proj_in_t, proj_state, order)


def pack_params(sz, head_part, shared_part):
    heads = sz.heads
    pad = ((0, 0), (0, sz.channels - heads * HDIM))
    taps = head_part[:, : CONV * HDIM].reshape(heads, CONV, HDIM).transpose(1, 0, 2)
    taps = jnp.pad(taps.reshape(CONV, heads * HDIM), pad)
    bias = head_part[:, (CONV + 1) * HDIM : (CONV + 2) * HDIM].reshape(1, -1)
    gain = head_part[:, CONV * HDIM : (CONV + 1) * HDIM].reshape(1, -1)
    skip = jnp.repeat(head_part[:, -1], HDIM).reshape(1, -1)
    state_taps = shared_part[: CONV * 2 * NSTATE].reshape(CONV, 2 * NSTATE)
    state_bias = shared_part[CONV * 2 * NSTATE : (CONV + 1) * 2 * NSTATE].reshape(1, -1)
    in_gain = shared_part[(CONV + 1) * 2 * NSTATE :].reshape(1, -1)

    def row(value):
        return jnp.pad(value, ((0, 0), (0, sz.width - value.shape[1])))

    rows = [
        row(jnp.concatenate([taps, state_taps], axis=1)),
        row(jnp.concatenate([jnp.pad(bias, pad), state_bias], axis=1)),
        row(gain),
        row(skip),
        row(head_part[:, -3].reshape(1, -1)),
        row(-jnp.exp(head_part[:, -2]).reshape(1, -1)),
        in_gain,
        jnp.zeros((16 - GAIN_ROW - 1, sz.width), F32),
    ]
    return jnp.concatenate(rows, axis=0)


def to_columns(tile, rows):
    row = lax.broadcasted_iota(jnp.int32, (rows, LANES), 0)
    lane = lax.broadcasted_iota(jnp.int32, (rows, LANES), 1)
    return nt((row == lane).astype(F32), tile, HIGH)


def forward_core(sz, layer, resets, gathered, weights, weight_out, pack, rows):
    block, chunk, chans = STRETCH, CHUNK, sz.channels
    subs = block // chunk
    shards = block // rows

    def kernel(
        reset_ref, h_ref, w_ref, wo_ref, pk_ref, part_ref, sq_ref, p_ref, y_ref, s_ref,
        conv_ref, state_ref,
    ):
        c = pl.program_id(0)
        keep = 1.0 - reset_ref[c]

        @pl.when(c == 0)
        def _():
            conv_ref[...] = jnp.zeros_like(conv_ref)
            state_ref[...] = jnp.zeros_like(state_ref)

        p_ref[...] = nt(h_ref[...], w_ref[...])
        inner = p_ref[:, chans : 2 * chans]
        state_raw = p_ref[:, 2 * chans : sz.dt].astype(BF16).astype(F32)
        conv_ref[0:8, :] = conv_ref[block : block + 8, :] * keep
        conv_ref[8 : 8 + block, :chans] = inner
        conv_ref[8 : 8 + block, chans:] = state_raw
        pre = pk_ref[CONV : CONV + 1, : sz.conv] + pk_ref[0:1, : sz.conv] * conv_ref[8 : 8 + block, :]
        for tap in range(1, CONV):
            pre = pre + pk_ref[tap : tap + 1, : sz.conv] * conv_ref[8 - tap : 8 - tap + block, :]
        act = pre * sigmoid(pre)
        step = softplus(p_ref[:, sz.dt :] + pk_ref[7:8, :LANES])
        decay = step * pk_ref[8:9, :LANES]
        mask = lower_mask(chunk)
        lower = mask.astype(F32)
        lane = lax.broadcasted_iota(jnp.int32, (chunk, LANES), 1)
        for sub in range(subs):
            span = slice(sub * chunk, (sub + 1) * chunk)
            if sub == 0:
                state_ref[...] = state_ref[...] * keep
            s_ref[sub] = state_ref[...]
            dt = step[span]
            log_decay = nn(lower, decay[span], HIGH)
            flat = step_rows(log_decay, dt)
            writer = act[span, chans : chans + NSTATE]
            reader = act[span, chans + NSTATE :]
            cross = nt3(reader, writer)
            for pair in range(sz.padded // 2):
                cols = slice(pair * LANES, (pair + 1) * LANES)
                x = act[span, cols]
                total = jnp.zeros((chunk, LANES), F32)
                for side in range(2):
                    head = 2 * pair + side
                    gap = log_decay[:, head : head + 1] - flat[head : head + 1, :]
                    weight = cross * jnp.exp(jnp.where(mask, gap, -1e30)) * flat[8 + head : 9 + head, :]
                    part = jnp.where((lane < HDIM) == (side == 0), x, 0.0)
                    total = total + nn3(weight, part)
                logs = halves(log_decay[:, 2 * pair : 2 * pair + 1], log_decay[:, 2 * pair + 1 : 2 * pair + 2])
                dts = halves(dt[:, 2 * pair : 2 * pair + 1], dt[:, 2 * pair + 1 : 2 * pair + 2])
                old = state_ref[:, cols]
                total = total + jnp.exp(logs) * nn3(reader, old)
                last = logs[chunk - 1 : chunk, :]
                moved_in = x * jnp.exp(last - logs) * dts
                state_ref[:, cols] = jnp.exp(last) * old + tn3(writer, moved_in)
                y_ref[span, cols] = total + pk_ref[6:7, cols] * x
        z = p_ref[:, :chans]
        gated = y_ref[...] * z * sigmoid(z)
        square = nt(jnp.ones((8, chans), F32), gated * gated, HIGH)
        for k in range(shards):
            sq_ref[k] = square[:, k * rows : (k + 1) * rows]
        high, low = split(gated * pk_ref[5:6, :chans])
        part_ref[...] = (nn(high, wo_ref[...]) + nn(low, wo_ref[...])).astype(BF16)

    width = sz.width
    return pl.pallas_call(
        kernel,
        grid=(sz.blocks,),
        out_shape=[
            jax.ShapeDtypeStruct((sz.tokens, width), BF16),
            jax.ShapeDtypeStruct((sz.tokens // rows, 8, rows), F32),
            jax.ShapeDtypeStruct((sz.tokens, sz.cols), F32),
            jax.ShapeDtypeStruct((sz.tokens, chans), F32),
            jax.ShapeDtypeStruct((sz.tokens // chunk, NSTATE, chans), F32),
        ],
        in_specs=[
            pl.BlockSpec(memory_space=pltpu.SMEM),
            pl.BlockSpec((block, width), lambda c: (c, 0)),
            pl.BlockSpec((None, sz.cols, width), lambda c: (layer, 0, 0)),
            pl.BlockSpec((None, chans, width), lambda c: (layer, 0, 0)),
            pl.BlockSpec((None, 16, width), lambda c: (layer, 0, 0)),
        ],
        out_specs=[
            pl.BlockSpec((block, width), lambda c: (c, 0)),
            pl.BlockSpec((shards, 8, rows), lambda c: (c, 0, 0)),
            pl.BlockSpec((block, sz.cols), lambda c: (c, 0)),
            pl.BlockSpec((block, chans), lambda c: (c, 0)),
            pl.BlockSpec((subs, NSTATE, chans), lambda c: (c, 0, 0)),
        ],
        scratch_shapes=[
            pltpu.VMEM((block + 8, sz.conv), F32),
            pltpu.VMEM((NSTATE, chans), F32),
        ],
        compiler_params=pltpu.CompilerParams(vmem_limit_bytes=VMEM_LIMIT),
        name="forward_core",
    )(resets, gathered, weights, weight_out, pack)


def backward_core(sz, layer, resets, grads, proj, mixed, states, stats, weights, weight_out, pack, order, rows):
    block, chunk, chans = STRETCH, CHUNK, sz.channels
    subs = block // chunk
    blocks = sz.blocks

    def kernel(
        reset_ref, g_ref, p_ref, halo_ref, y_ref, s_ref, st_ref, w_ref, wo_ref, pk_ref, order_ref, sum_ref,
        gh_ref, gt_ref, q_ref, acc_ref,
        conv_ref, dpre_ref, dact_ref, dlog_ref, ddt_ref, dstate_ref,
    ):
        i = pl.program_id(0)
        c = blocks - 1 - i
        keep = 1.0 - reset_ref[c]
        after = 1.0 - reset_ref[jnp.minimum(c + 1, blocks - 1)]

        @pl.when(i == 0)
        def _():
            dpre_ref[...] = jnp.zeros_like(dpre_ref)
            dstate_ref[...] = jnp.zeros_like(dstate_ref)
            acc_ref[...] = jnp.zeros_like(acc_ref)

        conv_ref[0:8, :chans] = halo_ref[:, chans : 2 * chans] * keep
        conv_ref[0:8, chans:] = halo_ref[:, 2 * chans : sz.dt].astype(BF16).astype(F32) * keep
        conv_ref[8 : 8 + block, :chans] = p_ref[:, chans : 2 * chans]
        conv_ref[8 : 8 + block, chans:] = p_ref[:, 2 * chans : sz.dt].astype(BF16).astype(F32)
        pre = pk_ref[CONV : CONV + 1, : sz.conv] + pk_ref[0:1, : sz.conv] * conv_ref[8 : 8 + block, :]
        for tap in range(1, CONV):
            pre = pre + pk_ref[tap : tap + 1, : sz.conv] * conv_ref[8 - tap : 8 - tap + block, :]
        gate = sigmoid(pre)
        act = pre * gate
        slope = gate * (1.0 + pre * (1.0 - gate))
        step_in = p_ref[:, sz.dt :] + pk_ref[7:8, :LANES]
        step = softplus(step_in)
        rate = pk_ref[8:9, :LANES]
        decay = step * rate
        z = p_ref[:, :chans]
        zgate = sigmoid(z)
        zsilu = z * zgate
        y = y_ref[...]
        gated = y * zsilu
        gain = pk_ref[5:6, :chans]
        skip = pk_ref[6:7, :chans]
        columns = [to_columns(st_ref[k], rows) for k in range(block // rows)]
        columns = jnp.concatenate(columns, axis=0)
        scale = columns[:, 0:1]
        along = columns[:, 1:2]
        grad_q = nt(g_ref[...], wo_ref[...])
        q_ref[...] = (gated * scale * gain).astype(BF16)
        acc_ref[5:6, :chans] += jnp.sum(grad_q * gated * scale, axis=0, keepdims=True)
        dgated = grad_q * gain * scale - gated * (scale * scale * along * (1.0 / (HEADS * HDIM)))
        dy = dgated * zsilu
        dz = dgated * y * zgate * (1.0 + z * (1.0 - zgate))
        x_all = act[:, :chans]
        acc_ref[6:7, :chans] += jnp.sum(dy * x_all, axis=0, keepdims=True)
        scan_dot = nn(dy * (y - skip * x_all), sum_ref[...], HIGH)
        mask = lower_mask(chunk)
        lower = mask.astype(F32)
        lane = lax.broadcasted_iota(jnp.int32, (chunk, LANES), 1)
        for sub in reversed(range(subs)):
            span = slice(sub * chunk, (sub + 1) * chunk)
            dt = step[span]
            log_decay = nn(lower, decay[span], HIGH)
            flat = step_rows(log_decay, dt)
            writer = act[span, chans : chans + NSTATE]
            reader = act[span, chans + NSTATE :]
            cross = nt3(reader, writer)
            cross_grad = jnp.zeros((chunk, chunk), F32)
            dreader = jnp.zeros((chunk, NSTATE), F32)
            dwriter = jnp.zeros((chunk, NSTATE), F32)
            fall = jnp.zeros((LANES, chunk), F32)
            row = lax.broadcasted_iota(jnp.int32, (LANES, chunk), 0)
            reach = []
            carried = []
            for pair in range(sz.padded // 2):
                cols = slice(pair * LANES, (pair + 1) * LANES)
                x = act[span, cols]
                g = dy[span, cols]
                logs = halves(log_decay[:, 2 * pair : 2 * pair + 1], log_decay[:, 2 * pair + 1 : 2 * pair + 2])
                dts = halves(dt[:, 2 * pair : 2 * pair + 1], dt[:, 2 * pair + 1 : 2 * pair + 2])
                last = logs[chunk - 1 : chunk, :]
                old = s_ref[sub, :, cols]
                dnew = dstate_ref[:, cols]
                faded = g * jnp.exp(logs)
                tail = jnp.exp(last - logs)
                dreader = dreader + nt3(faded, old)
                ahead = nn3(writer, dnew)
                dx = g * skip[:, cols] + ahead * tail * dts
                dwriter = dwriter + nt3(x * tail * dts, dnew)
                reach.append(x * ahead * tail)
                carried.append(jnp.sum(old * dnew, axis=0, keepdims=True) * jnp.exp(last))
                dstate_ref[:, cols] = jnp.exp(last) * dnew + tn3(reader, faded)
                for side in range(2):
                    head = 2 * pair + side
                    own = (lane < HDIM) == (side == 0)
                    g_own = jnp.where(own, g, 0.0)
                    gap = log_decay[:, head : head + 1] - flat[head : head + 1, :]
                    decays = jnp.exp(jnp.where(mask, gap, -1e30))
                    steps = flat[8 + head : 9 + head, :]
                    spread = nt3(g_own, x) * decays
                    weight = cross * decays * steps
                    dx = dx + tn3(weight, g_own)
                    cross_grad = cross_grad + spread * steps
                    sums = jnp.sum(spread * cross, axis=0, keepdims=True)
                    fall = fall + jnp.where(row == head, sums, 0.0)
                dact_ref[span, cols] = dx
            dact_ref[span, chans : chans + NSTATE] = dwriter + tn3(cross_grad, reader)
            dact_ref[span, chans + NSTATE :] = dreader + nn3(cross_grad, writer)
            reach = nn(jnp.concatenate(reach, axis=1), sum_ref[...], HIGH)
            carried = nn(jnp.concatenate(carried, axis=1), sum_ref[...], HIGH)
            direct = jnp.transpose(fall) + reach
            given = dt * reach
            dlog = scan_dot[span] - dt * direct
            ends = jnp.sum(given, axis=0, keepdims=True) + carried
            at_end = lax.broadcasted_iota(jnp.int32, (chunk, LANES), 0) == chunk - 1
            dlog = dlog + jnp.where(at_end, ends, 0.0)
            ddecay = tn(lower, dlog, HIGH)
            ddt_ref[span, :] = direct + ddecay * rate
            acc_ref[8:9, :LANES] += jnp.sum(ddecay * dt, axis=0, keepdims=True)
        dstate_ref[...] = dstate_ref[...] * keep
        ddt_raw = ddt_ref[...] * sigmoid(step_in)
        acc_ref[7:8, :LANES] += jnp.sum(ddt_raw, axis=0, keepdims=True)
        dpre_ref[block : block + 8, :] = dpre_ref[0:8, :] * after
        dpre_ref[0:block, :] = dact_ref[...] * slope
        raw = conv_ref[8 : 8 + block, :]
        acc_ref[CONV : CONV + 1, : sz.conv] += jnp.sum(dpre_ref[0:block, :], axis=0, keepdims=True)
        draw = jnp.zeros((block, sz.conv), F32)
        for tap in range(CONV):
            later = dpre_ref[tap : tap + block, :]
            draw = draw + pk_ref[tap : tap + 1, : sz.conv] * later
            acc_ref[tap : tap + 1, : sz.conv] += jnp.sum(raw * later, axis=0, keepdims=True)
        low = jnp.concatenate(
            [dz.astype(BF16), draw.astype(BF16), ddt_raw.astype(BF16)], axis=1
        )
        gh_ref[...] = nn(low, w_ref[...]).astype(BF16)
        gt_ref[...] = nt(order_ref[...], low).astype(BF16)

    width = sz.width
    back = blocks - 1
    per = block // 8
    return pl.pallas_call(
        kernel,
        grid=(blocks,),
        out_shape=[
            jax.ShapeDtypeStruct((sz.tokens, width), BF16),
            jax.ShapeDtypeStruct((sz.grad_rows, sz.tokens), BF16),
            jax.ShapeDtypeStruct((sz.tokens, chans), BF16),
            jax.ShapeDtypeStruct((16, width), F32),
        ],
        in_specs=[
            pl.BlockSpec(memory_space=pltpu.SMEM),
            pl.BlockSpec((block, width), lambda i: (back - i, 0)),
            pl.BlockSpec((block, sz.cols), lambda i: (back - i, 0)),
            pl.BlockSpec((8, sz.cols), lambda i: (jnp.maximum((back - i) * per - 1, 0), 0)),
            pl.BlockSpec((block, chans), lambda i: (back - i, 0)),
            pl.BlockSpec((subs, NSTATE, chans), lambda i: (back - i, 0, 0)),
            pl.BlockSpec((block // rows, 8, LANES), lambda i: (back - i, 0, 0)),
            pl.BlockSpec((None, sz.cols, width), lambda i: (layer, 0, 0)),
            pl.BlockSpec((None, chans, width), lambda i: (layer, 0, 0)),
            pl.BlockSpec((None, 16, width), lambda i: (layer, 0, 0)),
            pl.BlockSpec((sz.grad_rows, sz.cols), lambda i: (0, 0)),
            pl.BlockSpec((chans, LANES), lambda i: (0, 0)),
        ],
        out_specs=[
            pl.BlockSpec((block, width), lambda i: (back - i, 0)),
            pl.BlockSpec((sz.grad_rows, block), lambda i: (0, back - i)),
            pl.BlockSpec((block, chans), lambda i: (back - i, 0)),
            pl.BlockSpec((16, width), lambda i: (0, 0)),
        ],
        scratch_shapes=[
            pltpu.VMEM((block + 8, sz.conv), F32),
            pltpu.VMEM((block + 8, sz.conv), F32),
            pltpu.VMEM((block, sz.conv), F32),
            pltpu.VMEM((chunk, LANES), F32),
            pltpu.VMEM((block, LANES), F32),
            pltpu.VMEM((NSTATE, chans), F32),
        ],
        compiler_params=pltpu.CompilerParams(vmem_limit_bytes=VMEM_LIMIT),
        name="backward_core",
    )(resets, grads, proj, proj, mixed, states, stats, weights, weight_out, pack, order, sz.head_sum())


def weight_grads(sz, grads_t, gathered, scaled, out_grads):
    cols = 256

    split_row = sz.master_pad

    def kernel(gt_ref, h_ref, q_ref, g_ref, in_ref, state_ref, out_ref):
        in_ref[...] = nn(gt_ref[:split_row, :], h_ref[...]).astype(BF16)
        state_ref[...] = nn(gt_ref[split_row:, :], h_ref[...])
        out_ref[...] = tn(q_ref[...], g_ref[...]).astype(BF16)

    tokens, width, chans = sz.tokens, sz.width, sz.channels
    return pl.pallas_call(
        kernel,
        grid=(width // cols,),
        out_shape=[
            jax.ShapeDtypeStruct((sz.master_pad, width), BF16),
            jax.ShapeDtypeStruct((2 * NSTATE, width), F32),
            jax.ShapeDtypeStruct((chans, width), BF16),
        ],
        in_specs=[
            pl.BlockSpec((sz.grad_rows, tokens), lambda i: (0, 0)),
            pl.BlockSpec((tokens, cols), lambda i: (0, i)),
            pl.BlockSpec((tokens, chans), lambda i: (0, 0)),
            pl.BlockSpec((tokens, cols), lambda i: (0, i)),
        ],
        out_specs=[
            pl.BlockSpec((sz.master_pad, cols), lambda i: (0, i)),
            pl.BlockSpec((2 * NSTATE, cols), lambda i: (0, i)),
            pl.BlockSpec((chans, cols), lambda i: (0, i)),
        ],
        compiler_params=pltpu.CompilerParams(vmem_limit_bytes=VMEM_LIMIT),
        name="weight_grads",
    )(grads_t, gathered, scaled, out_grads)


def adam_update(weight, moment, second, gradient, rate, decay):
    moment_new = BETA_ONE * moment + (1.0 - BETA_ONE) * gradient
    second_new = BETA_TWO * second + (1.0 - BETA_TWO) * gradient * gradient
    corrected = moment_new / (1.0 - BETA_ONE**ADAM_STEP)
    corrected_sq = second_new / (1.0 - BETA_TWO**ADAM_STEP)
    weight_new = weight - rate * (corrected / (jnp.sqrt(corrected_sq) + ADAM_EPS) + decay * weight)
    return (weight_new, moment_new, second_new)


def adam_in(sz, clip, grad, weight, moment, second):
    block = LANES
    width = sz.width

    def kernel(clip_ref, g_ref, w_ref, m_ref, v_ref, wn_ref, mn_ref, vn_ref, low_ref):
        scale = clip_ref[0]

        def body(i, carry):
            made = []
            for half in range(2):
                span = pl.ds(pl.multiple_of(i * 16 + half * 8, 8), 8)
                new = adam_update(
                    w_ref[span, 0, :], m_ref[span, 0, :], v_ref[span, 0, :],
                    scale * g_ref[span, :], LEARN_MATRIX, WEIGHT_DECAY,
                )
                wn_ref[span, 0, :] = new[0]
                mn_ref[span, 0, :] = new[1]
                vn_ref[span, 0, :] = new[2]
                made.append(new[0])
            low_ref[pl.ds(pl.multiple_of(i * 16, 16), 16), :] = jnp.concatenate(made, axis=0).astype(BF16)
            return carry

        lax.fori_loop(0, block // 16, body, 0)

    view = pl.BlockSpec((block, 1, width), lambda i: (i, 0, 0))
    flat = pl.BlockSpec((block, width), lambda i: (i, 0))
    shape = jax.ShapeDtypeStruct((sz.master, 1, width), F32)
    return pl.pallas_call(
        kernel,
        grid=(sz.master_pad // block,),
        out_shape=[shape, shape, shape, jax.ShapeDtypeStruct((sz.master, width), BF16)],
        in_specs=[pl.BlockSpec(memory_space=pltpu.SMEM), flat, view, view, view],
        out_specs=[view, view, view, flat],
        compiler_params=pltpu.CompilerParams(vmem_limit_bytes=VMEM_LIMIT),
        name="adam_in",
    )(clip, grad, weight, moment, second)


def adam_plain(clip, grad, weight, moment, second, transposed):
    rows, width = weight.shape
    block = min(256 if transposed else 64, rows)

    def kernel(clip_ref, g_ref, w_ref, m_ref, v_ref, wn_ref, mn_ref, vn_ref, low_ref):
        if transposed:
            row = lax.broadcasted_iota(jnp.int32, (width, width), 0)
            col = lax.broadcasted_iota(jnp.int32, (width, width), 1)
            grad_value = tn(g_ref[...], (row == col).astype(BF16))
        else:
            grad_value = g_ref[...]
        new = adam_update(
            w_ref[...], m_ref[...], v_ref[...], clip_ref[0] * grad_value, LEARN_MATRIX, WEIGHT_DECAY
        )
        wn_ref[...], mn_ref[...], vn_ref[...] = new
        low_ref[...] = new[0].astype(BF16)

    flat = pl.BlockSpec((block, width), lambda i: (i, 0))
    turned = pl.BlockSpec((width, block), lambda i: (0, i))
    shape = jax.ShapeDtypeStruct((rows, width), F32)
    return pl.pallas_call(
        kernel,
        grid=(rows // block,),
        out_shape=[shape, shape, shape, jax.ShapeDtypeStruct((rows, width), BF16)],
        in_specs=[
            pl.BlockSpec(memory_space=pltpu.SMEM), turned if transposed else flat, flat, flat, flat
        ],
        out_specs=[flat] * 4,
        compiler_params=pltpu.CompilerParams(vmem_limit_bytes=VMEM_LIMIT),
        name="adam_plain",
    )(clip, grad, weight, moment, second)


def columns_first(array):
    return jnp.transpose(array, (2, 0, 1))


def shards(
    inputs,
    cotangent,
    valid_lengths,
    proj_in,
    proj_in_m,
    proj_in_v,
    proj_state,
    proj_state_m,
    proj_state_v,
    proj_out,
    proj_out_m,
    proj_out_v,
    head_params,
    head_m,
    head_v,
    shared_params,
    shared_m,
    shared_v,
):
    section = lax.axis_index("section")
    head_idx = lax.axis_index("head")
    count = lax.axis_size("head")
    rows, width = inputs.shape[1], inputs.shape[2]
    heads = head_params.shape[1]
    tokens = rows * count
    sz = Sizes(heads, tokens, width)
    order = sz.order()
    start_block, seq_length, resets = seq_layout(
        lax.dynamic_index_in_dim(valid_lengths, section, 0, keepdims=False)
    )
    token = head_idx * rows + lax.broadcasted_iota(jnp.int32, (rows, LANES), 0)
    live = jnp.zeros((rows, LANES), F32)
    for block in range(sz.blocks):
        inside = (token // STRETCH == block) & (token - start_block[block] * STRETCH < seq_length[block])
        live = jnp.where(inside, 1.0, live)
    first = lax.dynamic_index_in_dim(inputs, section, 0, keepdims=False)
    cot = lax.dynamic_index_in_dim(cotangent, section, 0, keepdims=False)
    own_weights = prepare_weights(sz, columns_first(proj_in), proj_state[0], order)
    own_out = proj_out[0].astype(BF16)
    own_out = jnp.pad(own_out, ((0, sz.channels - own_out.shape[0]), (0, 0)))
    own_pack = pack_params(sz, head_params[0], shared_params[0])
    weights, weight_out, pack, rows_zero = opening(
        count, sz, own_weights, own_out, own_pack, first, 0
    )
    def run_forward(layer, gathered):
        return forward_core(sz, layer, resets, gathered, weights, weight_out, pack, rows)

    def run_backward(layer, out_grads, kept, stats):
        _, _, proj, mixed, states = kept
        return backward_core(
            sz, layer, resets, out_grads, proj, mixed, states, stats, weights, weight_out, pack, order, rows
        )

    kept_zero = run_forward(0, rows_zero)
    result_zero, branch_zero, total_zero, rows_one = after_forward(
        count, sz, 0, kept_zero[0], kept_zero[1], first, live, pack, None, 1
    )
    kept_one = run_forward(1, rows_one)
    result_one, _, _, out_grads_one, stats_one = after_forward(
        count, sz, 1, kept_one[0], kept_one[1], result_zero, live, pack, cot, 2
    )
    back_one = run_backward(1, out_grads_one, kept_one, stats_one)
    grad_one, low_one, gain_one, out_grads_zero, stats_zero = after_backward(
        count, sz, 1, back_one[0], result_zero, cot, live, pack, (branch_zero, total_zero), 3
    )
    back_zero = run_backward(0, out_grads_zero, kept_zero, stats_zero)
    grad_zero, _, gain_zero = after_backward(
        count, sz, 0, back_zero[0], first, low_one, live, pack, None, 4
    )
    made_zero = list(weight_grads(sz, back_zero[1], rows_zero, back_zero[2], out_grads_zero))
    made_one = list(weight_grads(sz, back_one[1], rows_one, back_one[2], out_grads_one))

    def with_gain(small, gain):
        return jnp.concatenate([small[:GAIN_ROW], gain, small[GAIN_ROW + 1 :]], axis=0)

    lower = [made_zero[0], made_zero[2], made_zero[1], with_gain(back_zero[3], gain_zero)]
    upper = [made_one[0], made_one[2], made_one[1], with_gain(back_one[3], gain_one)]
    grad_in, grad_out, state_sum, small, layer_outs, grad_buffer, squares = trade_sections(
        list(zip(lower, upper)), [(result_zero, result_one), (grad_zero, grad_one)], 2, 5
    )

    state_part = state_sum.astype(BF16)
    chans = heads * HDIM
    shared_len = shared_params.shape[1]
    lines = -(-shared_len // (count * LANES))
    conv_rows = small[: CONV + 1, sz.channels : sz.conv].reshape(-1)
    shared_own = jnp.concatenate([conv_rows, small[GAIN_ROW]])
    shared_own = jnp.pad(shared_own, (0, count * lines * LANES - shared_len))
    shared_own = jnp.pad(shared_own.reshape(count, lines, LANES), ((0, 0), (0, 8 - lines), (0, 0)))
    state_own, shared_parts = scatter_rows(
        count, state_part.reshape(16 * count, -1), shared_own, 6
    )
    shared_piece = jnp.sum(shared_parts, axis=0)
    head_part = head_params[0]
    taps = small[:CONV, :chans].reshape(CONV, heads, HDIM).transpose(1, 0, 2).reshape(heads, -1)
    grad_head = jnp.concatenate(
        [
            taps,
            small[5, :chans].reshape(heads, HDIM),
            small[CONV, :chans].reshape(heads, HDIM),
            small[7, :heads][:, None],
            (small[8, :heads] * -jnp.exp(head_part[:, -2]))[:, None],
            jnp.sum(small[6, :chans].reshape(heads, HDIM), axis=1)[:, None],
        ],
        axis=1,
    )
    local_sq = jnp.sum(squares) + jnp.sum(grad_head * grad_head)
    local_sq = local_sq + jnp.sum(state_own * state_own) + jnp.sum(shared_piece * shared_piece)
    stats = shared_piece.at[7].set(local_sq)
    state_all, all_stats = gather_rows(count, state_own.astype(BF16), stats, 7)
    grad_state = state_all.reshape(state_part.shape)
    grad_shared = all_stats[:, :lines].reshape(-1)[:shared_len]
    section_sq = jnp.sum(all_stats[:, 7, 0])
    norm_sq = section_sq + lax.ppermute(section_sq, "section", [(0, 1), (1, 0)])
    grad_norm = jnp.sqrt(norm_sq)
    threshold = CLIP_COEF * PARAMS**0.5
    clip_scale = threshold / jnp.maximum(grad_norm, threshold)
    clip = clip_scale.reshape(1)
    new_in = adam_in(
        sz, clip, grad_in, columns_first(proj_in), columns_first(proj_in_m), columns_first(proj_in_v)
    )
    new_out = adam_plain(
        clip, grad_out, proj_out[0], proj_out_m[0], proj_out_v[0], False
    )
    new_state = adam_plain(
        clip, grad_state, proj_state[0], proj_state_m[0], proj_state_v[0], True
    )
    new_head = adam_update(
        head_part, head_m[0], head_v[0], clip_scale * grad_head, LEARN_VECTOR, 0.0
    )
    new_shared = adam_update(
        shared_params[0], shared_m[0], shared_v[0], clip_scale * grad_shared, LEARN_VECTOR, 0.0
    )
    back_view = [jnp.transpose(array, (1, 2, 0)) for array in new_in[:3]]
    return (
        layer_outs[None],
        grad_buffer[None],
        grad_norm,
        back_view[0],
        back_view[1],
        back_view[2],
        new_in[3].T[None],
        new_state[0][None],
        new_state[1][None],
        new_state[2][None],
        new_state[3][None],
        new_out[0][None],
        new_out[1][None],
        new_out[2][None],
        new_out[3][None],
        new_head[0][None],
        new_head[1][None],
        new_head[2][None],
        new_shared[0][None],
        new_shared[1][None],
        new_shared[2][None],
    )


def solution(mesh):
    in_specs = (
        P(None, "head", None),
        P(None, "head", None),
        P(),
        P("section", None, "head"),
        P("section", None, "head"),
        P("section", None, "head"),
        P("section", None, None),
        P("section", None, None),
        P("section", None, None),
        P("section", "head", None),
        P("section", "head", None),
        P("section", "head", None),
        P("section", "head", None),
        P("section", "head", None),
        P("section", "head", None),
        P("section", None),
        P("section", None),
        P("section", None),
    )
    out_specs = (
        P("section", None, "head", None),
        P("section", None, "head", None),
        P(),
        P("section", None, "head"),
        P("section", None, "head"),
        P("section", None, "head"),
        P("section", None, "head"),
        P("section", None, None),
        P("section", None, None),
        P("section", None, None),
        P("section", None, None),
        P("section", "head", None),
        P("section", "head", None),
        P("section", "head", None),
        P("section", "head", None),
        P("section", "head", None),
        P("section", "head", None),
        P("section", "head", None),
        P("section", None),
        P("section", None),
        P("section", None),
    )
    return jax.shard_map(shards, mesh=mesh, in_specs=in_specs, out_specs=out_specs, check_vma=False)
```

```python
import itertools

import jax
import jax.numpy as jnp
import numpy as np
from jax import lax
from jax.experimental import pallas as pl
from jax.experimental.pallas import tpu as pltpu
from jax.sharding import PartitionSpec as P

HEADS = 64
HDIM = 64
NSTATE = 128
CONV = 4
STRETCH = 256
ADAM_STEP = 5
PARAMS = 51698560

HIGH = lax.Precision.HIGHEST
EPS_NORM = 1e-05
ADAM_EPS = 1e-08
BETA_ONE = 0.5
BETA_TWO = 0.5
CLIP_COEF = 0.2
LEARN_MATRIX = 0.02
LEARN_VECTOR = 0.2
WEIGHT_DECAY = 0.1

F32 = jnp.float32
BF16 = jnp.bfloat16
MESH = pl.DeviceIdType.MESH
LANES = 128
CHUNK = 128
COLS = HDIM * 2 + 1
GAIN_ROW = 9
VMEM_LIMIT = 56 << 20


def seq_layout(lengths_row):
    block_count = lengths_row.shape[0]
    block_idx = jnp.arange(block_count, dtype=jnp.int32)
    starts = lengths_row > 0
    start_block = lax.cummax(jnp.where(starts, block_idx, 0), axis=0)
    owner_mask = (start_block[:, None] == block_idx[None, :]).astype(jnp.int32)
    seq_length = jnp.sum(owner_mask * lengths_row[None, :], axis=1)
    return (start_block, seq_length, starts.astype(jnp.float32))


def chip_dims(count):
    side = 4 if count % 64 == 0 else 2
    if count % (side * side) != 0:
        return (count, 1, 1)
    return (count // (side * side), side, side)


def place(dims):
    me = lax.axis_index("head")
    return (me // (dims[1] * dims[2]), (me // dims[2]) % dims[1], me % dims[2])


def linear(dims, spot):
    return (spot[0] * dims[1] + spot[1]) * dims[2] + spot[2]


def moved(dims, spot, shifts):
    return tuple(s if d == 0 else (s + d) % n for s, d, n in zip(spot, shifts, dims))


def shift_of(order, offsets):
    out = [0, 0, 0]
    for axis, off in zip(order, offsets):
        out[axis] = off
    return out


def greet_axes(dims, spot):
    barrier = pltpu.get_barrier_semaphore()
    count = 0
    for axis in range(3):
        for off in range(1, dims[axis]):
            peer = linear(dims, moved(dims, spot, shift_of((axis,), (off,))))
            pl.semaphore_signal(
                barrier, inc=1, device_id={"head": peer}, device_id_type=MESH
            )
            count += 1
    if count:
        pl.semaphore_wait(barrier, count)


def greet_all(count, pair=None):
    barrier = pltpu.get_barrier_semaphore()
    me = lax.axis_index("head")
    if pair is not None:
        other = 1 - lax.axis_index(pair)
        pl.semaphore_signal(barrier, inc=1, device_id={pair: other}, device_id_type=MESH)
    for off in range(1, count):
        pl.semaphore_signal(
            barrier, inc=1, device_id={"head": (me + off) % count}, device_id_type=MESH
        )
    expected = count - 1 + (pair is not None)
    if expected:
        pl.semaphore_wait(barrier, expected)


def rows_at(shard, rows):
    return pl.ds(pl.multiple_of(shard * rows, rows), rows)


def column_parts(width, shares):
    tiles = width // LANES
    parts, start, taken = [], 0, 0
    for share, order, group in shares:
        taken += share
        stop = tiles * taken // 16 * LANES
        if stop > start:
            parts.append((start, stop - start, order, group))
            start = stop
    return parts


GATHER = ((2, (2, 1, 0), 0), (2, (1, 2, 0), 0), (6, (0, 2, 1), 0), (6, (0, 1, 2), 0))
GATHER_SMALL = ((8, (0, 2, 1), 0), (8, (0, 1, 2), 0))
SCATTER = (
    (1, (2, 0, 1), 0), (1, (1, 0, 2), 0), (1, (0, 1, 2), 0), (1, (0, 2, 1), 0),
    (3, (2, 1, 0), 0), (3, (1, 2, 0), 0), (3, (2, 1, 0), 1), (3, (1, 2, 0), 1),
)
SCATTER_SMALL = ((8, (2, 1, 0), 0), (8, (1, 2, 0), 0))
SCATTER_PACE = (0.3, 0.9, 0.7, 2.0)


def guarded(preds, action):
    preds = [pred for pred in preds if pred is not None]
    if not preds:
        action()
        return
    cond = preds[0]()
    for pred in preds[1:]:
        cond = jnp.logical_and(cond, pred())
    pl.when(cond)(action)


def gather_steps(dims, parts, rows, own_ref, all_ref, send_sem, recv_sem, between=()):
    spot = place(dims)
    me = linear(dims, spot)
    waits = []
    counter = [0] * len(parts)

    def lined(axis):
        return axis == 0 and dims[0] > 2 and dims[1] == 2

    def above(axis, dist):
        return lambda: spot[axis] + dist < dims[axis]

    def below(axis, dist):
        return lambda: spot[axis] >= dist

    def sources(part, pos):
        axis = parts[part][2][pos]
        if not lined(axis):
            return [(off, None) for off in range(1, dims[axis])]
        out = []
        for dist in range(1, dims[axis]):
            out.append((dist, above(axis, dist)))
            out.append((-dist, below(axis, dist)))
        return out

    def block(part, offsets):
        start, width, order, _ = parts[part]
        shard = linear(dims, moved(dims, spot, shift_of(order, offsets)))
        return shard, all_ref.at[rows_at(shard, rows), pl.ds(start, width)]

    def push(part, offsets, pos, preds, src, came):
        axis = parts[part][2][pos]
        shard, dst = block(part, offsets)
        up, down = (1, above(axis, 1)), (-1, below(axis, 1))
        if lined(axis):
            targets = [up, down] if came == 0 else [down] if came > 0 else [up]
        else:
            targets = [(off, None) for off in range(1, dims[axis])] if came == 0 else []
        for off, pred in targets:
            peer = linear(dims, moved(dims, spot, shift_of((axis,), (off,))))
            number = counter[part]
            counter[part] += 1

            def begin(peer=peer, number=number):
                pltpu.make_async_remote_copy(
                    src_ref=dst if src is None else src,
                    dst_ref=dst,
                    send_sem=send_sem.at[part, number],
                    recv_sem=recv_sem.at[part, shard],
                    device_id={"head": peer},
                    device_id_type=MESH,
                ).start()

            guarded([pred], begin)
            waits.append((preds + [pred], part, number))

    def visit(part, offsets, preds, pos, came):
        def body():
            shard, dst = block(part, offsets)
            pltpu.make_async_remote_copy(
                src_ref=dst,
                dst_ref=dst,
                send_sem=send_sem.at[part, 0],
                recv_sem=recv_sem.at[part, shard],
                device_id={"head": me},
                device_id_type=MESH,
            ).wait_recv()
            push(part, offsets, pos, preds, None, came)
            for later in range(pos + 1, 3):
                push(part, offsets, later, preds, None, 0)

        guarded(preds, body)

    for pos in range(3):
        for part, (start, width, _, _) in enumerate(parts):
            push(part, (0, 0, 0), pos, [], own_ref.at[:, pl.ds(start, width)], 0)
    todo = []
    for part in range(len(parts)):
        first, second, third = (sources(part, pos) for pos in range(3))
        for k, (oa, pa) in enumerate(first):
            todo.append(((0, k, part), part, (oa, 0, 0), [pa], 0, oa))
        for ka, (oa, pa) in enumerate([(0, None)] + first):
            for k, (ob, pb) in enumerate(second):
                todo.append(((1, ka + k, part), part, (oa, ob, 0), [pa, pb], 1, ob))
            for kb, (ob, pb) in enumerate([(0, None)] + second):
                for k, (oc, pc) in enumerate(third):
                    todo.append(
                        ((2, ka + kb + k, part), part, (oa, ob, oc), [pa, pb, pc], 2, oc)
                    )
    todo.sort(key=lambda entry: (sum(abs(off) for off in entry[2]), entry[0]))
    between = list(between)
    for _, part, offsets, preds, pos, came in todo:
        if between:
            between.pop(0)()
        visit(part, offsets, preds, pos, came)
    for work in between:
        work()
    for preds, part, number in waits:

        def settle(part=part, number=number):
            start, width, _, _ = parts[part]
            ref = own_ref.at[:, pl.ds(start, width)]
            pltpu.make_async_remote_copy(
                src_ref=ref,
                dst_ref=ref,
                send_sem=send_sem.at[part, number],
                recv_sem=recv_sem.at[part, 0],
                device_id={"head": me},
                device_id_type=MESH,
            ).wait_send()

        guarded(preds, settle)


def gather_sends(dims):
    return 3 * dims[0] * dims[1] * dims[2]


def scatter_steps(dims, parts, rows, in_ref, out_ref, box_ref, send_sem, recv_sem):
    spot = place(dims)
    me = linear(dims, spot)
    sends = []

    def size(part, pos):
        return dims[parts[part][2][pos]]

    def slot_one(part, ea, ob, oc):
        return ((ea - 1) * size(part, 1) + ob) * size(part, 2) + oc

    def slot_two(part, eb, oc):
        base = (size(part, 0) - 1) * size(part, 1) * size(part, 2)
        return base + (eb - 1) * size(part, 2) + oc

    def slot_three(part, ec):
        return slot_two(part, size(part, 1), 0) + ec - 1

    def cols(part):
        return pl.ds(parts[part][0], parts[part][1])

    def mine(part, offsets):
        shard = linear(dims, moved(dims, spot, shift_of(parts[part][2], offsets)))
        return in_ref.at[rows_at(shard, rows), cols(part)]

    def send(part, src, pos, off, slot):
        peer = linear(dims, moved(dims, spot, shift_of((parts[part][2][pos],), (off,))))
        copy = pltpu.make_async_remote_copy(
            src_ref=src,
            dst_ref=box_ref.at[slot, :, cols(part)],
            send_sem=send_sem.at[part, slot],
            recv_sem=recv_sem.at[part, slot],
            device_id={"head": peer},
            device_id_type=MESH,
        )
        copy.start()
        sends.append(copy)

    def arrived(part, slot):
        ref = box_ref.at[slot, :, cols(part)]
        pltpu.make_async_remote_copy(
            src_ref=ref,
            dst_ref=ref,
            send_sem=send_sem.at[part, slot],
            recv_sem=recv_sem.at[part, slot],
            device_id={"head": me},
            device_id_type=MESH,
        ).wait_recv()
        return ref[...].astype(F32)

    def combined(part, ob, oc, stages):
        total = mine(part, (0, ob, oc))[...].astype(F32)
        for ea in range(1, size(part, 0)):
            total = total + arrived(part, slot_one(part, ea, ob, oc))
        for eb in range(1, size(part, 1)) if stages > 1 else ():
            total = total + arrived(part, slot_two(part, eb, oc))
        for ec in range(1, size(part, 2)) if stages > 2 else ():
            total = total + arrived(part, slot_three(part, ec))
        return total

    def put_by(part, ob, oc, total):
        if size(part, 0) > 1:
            hold = box_ref.at[slot_one(part, 1, ob, oc), :, cols(part)]
        elif size(part, 1) > 1 and ob == 0:
            hold = box_ref.at[slot_two(part, 1, oc), :, cols(part)]
        else:
            return mine(part, (0, ob, oc))
        hold[...] = total.astype(box_ref.dtype)
        return hold

    def first(part, ob, oc, off):
        slot = slot_one(part, size(part, 0) - off, ob, oc)
        send(part, mine(part, (off, ob, oc)), 0, off, slot)

    def second(part, ob, oc, _):
        hold = put_by(part, ob, oc, combined(part, ob, oc, 1))
        send(part, hold, 1, ob, slot_two(part, size(part, 1) - ob, oc))

    def third(part, _, oc, __):
        hold = put_by(part, 0, oc, combined(part, 0, oc, 2))
        send(part, hold, 2, oc, slot_three(part, size(part, 2) - oc))

    def last(part, _, __, ___):
        out_ref[:, cols(part)] = combined(part, 0, 0, 3)

    lag, rest, turn, end = SCATTER_PACE
    program = []
    for part, (_, _, _, group) in enumerate(parts):
        for ob, oc in itertools.product(range(size(part, 1)), range(size(part, 2))):
            for off in range(1, size(part, 0)):
                rank = (0.0 if ob else rest) + group * lag
                program.append((rank, oc == 0, off, part, first, ob, oc))
            if ob:
                program.append((turn + group * lag, oc == 0, 0, part, second, ob, oc))
        for oc in range(1, size(part, 2)):
            program.append((end + group * lag, False, 0, part, third, 0, oc))
        program.append((3.0 + group * lag, True, 0, part, last, 0, 0))
    program.sort(key=lambda step: step[:4])
    for _, _, off, part, action, ob, oc in program:
        action(part, ob, oc, off)
    return sends


class PlaneScatter:
    def __init__(self, dims, rows, width):
        self.dims, self.rows, self.half = dims, rows, width // 2
        self.orders = ((2, 1), (1, 2))
        self.width = width
        depth = dims[0]
        most = max(dims[1], dims[2])
        self.one = depth * (most - 1) * most
        self.two = depth * (most - 1)
        self.slots = max(self.one + self.two + depth, 1)

    def scratch(self):
        return [
            pltpu.VMEM((self.slots, self.rows, self.width), BF16),
            DMA((2, self.slots)),
            DMA((2, self.slots)),
        ]

    def bind(self, part_ref, out_ref, box_ref, send_sem, recv_sem):
        self.part_ref, self.out_ref, self.box_ref = part_ref, out_ref, box_ref
        self.send_sem, self.recv_sem = send_sem, recv_sem
        self.spot = place(self.dims)
        self.me = linear(self.dims, self.spot)

    def sizes(self, part):
        a, b = self.orders[part]
        return self.dims[a], self.dims[b]

    def slot_one(self, part, plane, ea, ob):
        size_a, size_b = self.sizes(part)
        return (plane * (size_a - 1) + ea - 1) * size_b + ob

    def slot_two(self, part, plane, eb):
        return self.one + plane * (self.sizes(part)[1] - 1) + eb - 1

    def slot_three(self, plane):
        return self.one + self.two + plane

    def cols(self, part):
        return pl.ds(part * self.half, self.half)

    def mine(self, part, plane, oa, ob):
        shift = shift_of(self.orders[part], (oa, ob))
        spot = moved(self.dims, (plane, self.spot[1], self.spot[2]), shift)
        return self.part_ref.at[rows_at(linear(self.dims, spot), self.rows), self.cols(part)]

    def copy(self, part, src, slot, sent, peer):
        return pltpu.make_async_remote_copy(
            src_ref=src,
            dst_ref=self.box_ref.at[slot, :, self.cols(part)],
            send_sem=self.send_sem.at[part, sent],
            recv_sem=self.recv_sem.at[part, slot],
            device_id={"head": peer},
            device_id_type=MESH,
        )

    def peer(self, part, pos, off):
        shift = shift_of((self.orders[part][pos],), (off,))
        return linear(self.dims, moved(self.dims, self.spot, shift))

    def arrived(self, part, slot):
        ref = self.box_ref.at[slot, :, self.cols(part)]
        self.copy(part, ref, slot, slot, self.me).wait_recv()
        return ref[...].astype(F32)

    def first(self, plane):
        for inner in (1, 0):
            for part in range(2):
                size_a, size_b = self.sizes(part)
                for ob in range(size_b):
                    if (ob != 0) != bool(inner):
                        continue
                    for off in range(1, size_a):
                        slot = self.slot_one(part, plane, size_a - off, ob)
                        src = self.mine(part, plane, off, ob)
                        self.copy(part, src, slot, slot, self.peer(part, 0, off)).start()

    def second(self, plane):
        for part in range(2):
            size_a, size_b = self.sizes(part)
            for ob in range(1, size_b):
                hold = self.mine(part, plane, 0, ob)
                total = hold[...].astype(F32)
                for ea in range(1, size_a):
                    total = total + self.arrived(part, self.slot_one(part, plane, ea, ob))
                hold[...] = total.astype(BF16)
                slot = self.slot_two(part, plane, size_b - ob)
                self.copy(part, hold, slot, slot, self.peer(part, 1, ob)).start()

    def third(self, plane):
        depth = self.spot[0]
        for part in range(2):
            size_a, size_b = self.sizes(part)
            hold = self.mine(part, plane, 0, 0)
            total = hold[...].astype(F32)
            for ea in range(1, size_a):
                total = total + self.arrived(part, self.slot_one(part, plane, ea, 0))
            for eb in range(1, size_b):
                total = total + self.arrived(part, self.slot_two(part, plane, eb))

            @pl.when(plane == depth)
            def _(part=part, total=total):
                self.out_ref[:, self.cols(part)] = total

            @pl.when(plane != depth)
            def _(part=part, total=total, hold=hold):
                hold[...] = total.astype(BF16)
                peer = linear(self.dims, (plane, self.spot[1], self.spot[2]))
                self.copy(part, hold, self.slot_three(depth), self.slot_three(plane), peer).start()

    def last(self):
        for part in range(2):
            total = self.out_ref[:, self.cols(part)]
            for off in range(1, self.dims[0]):
                plane = (self.spot[0] + off) % self.dims[0]
                total = total + self.arrived(part, self.slot_three(plane))
            self.out_ref[:, self.cols(part)] = total

    def step(self, number, made, plane_of):
        for back, action in ((0, self.first), (1, self.second), (2, self.third)):
            k = made - 1 - back
            if isinstance(made, int):
                if 0 <= k < number:
                    action(plane_of(k))
            else:
                pl.when(k >= 0)(lambda k=k, action=action: action(plane_of(k)))

    def finish(self, number, plane_of):
        for extra in (1, 2):
            self.step(number, number + extra, plane_of)
        self.last()

    def drain(self):
        ref_of = lambda part: self.box_ref.at[0, :, self.cols(part)]
        for part in range(2):
            size_a, size_b = self.sizes(part)
            for plane in range(self.dims[0]):
                slots = [self.slot_one(part, plane, ea, ob) for ea in range(1, size_a) for ob in range(size_b)]
                slots += [self.slot_two(part, plane, eb) for eb in range(1, size_b)]
                for slot in slots:
                    self.copy(part, ref_of(part), slot, slot, self.me).wait_send()
            for off in range(1, self.dims[0]):
                slot = self.slot_three((self.spot[0] + off) % self.dims[0])
                self.copy(part, ref_of(part), slot, slot, self.me).wait_send()


def start_direct(count, own_ref_of, box_ref, send_sem, recv_sem):
    me = lax.axis_index("head")
    copies = []
    for off in range(1, count):
        peer = (me + off) % count
        copy = pltpu.make_async_remote_copy(
            src_ref=own_ref_of(peer),
            dst_ref=box_ref.at[me],
            send_sem=send_sem.at[off],
            recv_sem=recv_sem.at[count - off],
            device_id={"head": peer},
            device_id_type=MESH,
        )
        copy.start()
        copies.append(copy)
    return copies


def wait_direct(count, box_ref, copies, recv_sem, send_sem):
    me = lax.axis_index("head")
    for off in range(1, count):
        ref = box_ref.at[(me + off) % count]
        pltpu.make_async_remote_copy(
            src_ref=ref,
            dst_ref=ref,
            send_sem=send_sem.at[off],
            recv_sem=recv_sem.at[off],
            device_id={"head": me},
            device_id_type=MESH,
        ).wait_recv()
    for copy in copies:
        copy.wait_send()


VMEM_SPEC = pl.BlockSpec(memory_space=pltpu.VMEM)
ANY_SPEC = pl.BlockSpec(memory_space=pl.ANY)
DMA = pltpu.SemaphoreType.DMA


def params(collective_id):
    return pltpu.CompilerParams(
        collective_id=collective_id, has_side_effects=True, vmem_limit_bytes=VMEM_LIMIT
    )


def gather_scratch(parts, dims, count):
    return [DMA((len(parts), gather_sends(dims))), DMA((len(parts), count)), DMA]


def run_gather(count, parts, own_ref, all_ref, sems, stat=None, between=()):
    dims = chip_dims(count)
    rows = own_ref.shape[0]
    me = lax.axis_index("head")
    send_sem, recv_sem, local_sem = sems
    local = pltpu.make_async_copy(own_ref, all_ref.at[rows_at(me, rows)], local_sem)
    local.start()
    if stat is not None:
        stat_ref, box_ref, small_send, small_recv = stat
        copies = start_direct(count, lambda peer: stat_ref, box_ref, small_send, small_recv)
        box_ref[me] = stat_ref[...]
    gather_steps(dims, parts, rows, own_ref, all_ref, send_sem, recv_sem, between)
    if stat is not None:
        wait_direct(count, box_ref, copies, small_recv, small_send)
    local.wait()


def scatter_scratch(parts, count, rows, width):
    slots = max(count - 1, 1)
    return [pltpu.VMEM((slots, rows, width), BF16), DMA((len(parts), slots)), DMA((len(parts), slots))]


def finish_sums(count, sz, state_part, small, squares, pack, head_sum, collective_id):
    dims = chip_dims(count)
    width = state_part.shape[1]
    rows = state_part.shape[0] // count
    back, parts = column_parts(width, SCATTER_SMALL), column_parts(width, GATHER_SMALL)
    chans, state = sz.channels, 2 * NSTATE
    pieces = sz.width // LANES
    threshold = CLIP_COEF * PARAMS**0.5

    def kernel(*refs):
        refs = list(refs)
        take = lambda number: [refs.pop(0) for _ in range(number)]
        in_ref, small_ref, squares_ref, pks_ref, sum_ref = take(5)
        all_ref, stats_ref, norm_ref = take(3)
        share_ref, sums_ref, out_ref, own_ref, stat_ref, mine_ref, got_ref = take(7)
        scatter_refs, ag_sems = take(3), take(3)
        small_send, small_recv, stat_send, stat_recv, pair_send, pair_recv = take(6)
        me = lax.axis_index("head")
        section = lax.axis_index("section")
        share_ref[...] = jnp.zeros_like(share_ref)
        share_ref[0:1, :] = small_ref[GAIN_ROW : GAIN_ROW + 1, :]
        share_ref[1 : CONV + 2, :state] = small_ref[: CONV + 1, chans : chans + state]

        def piece(peer):
            return share_ref.at[:, pl.ds(pl.multiple_of((peer % pieces) * LANES, LANES), LANES)]

        greet_all(count, "section")
        copies = start_direct(count, piece, sums_ref, small_send, small_recv)
        sums_ref[me] = piece(me)[...]
        sends = scatter_steps(dims, back, rows, in_ref, out_ref, *scatter_refs)
        wait_direct(count, sums_ref, copies, small_recv, small_send)
        shared = jnp.sum(sums_ref[...], axis=0)
        shared_sq = jnp.where(me < pieces, jnp.sum(shared * shared), 0.0)
        state_own = out_ref[...]
        own_ref[...] = state_own.astype(BF16)
        taps = small_ref[: CONV + 2, :chans]
        skip = nn(small_ref[6:7, :chans], sum_ref[...], HIGH)
        bias = small_ref[7:8, :LANES]
        rate = small_ref[8:9, :LANES] * pks_ref[section, 8:9, :LANES]
        lane = lax.broadcasted_iota(jnp.int32, (1, LANES), 1)
        of_heads = jnp.where(lane < sz.heads, bias * bias + rate * rate + skip * skip, 0.0)
        if chans > sz.heads * HDIM:
            taps = taps[:, : sz.heads * HDIM]
        total = jnp.sum(squares_ref[...]) + jnp.sum(taps * taps) + jnp.sum(of_heads)
        total = total + jnp.sum(state_own * state_own) + shared_sq
        row = lax.broadcasted_iota(jnp.int32, (8, LANES), 0)
        stat_ref[...] = jnp.where(row == 7, total, shared)
        run_gather(count, parts, own_ref, all_ref, ag_sems, (stat_ref, stats_ref, stat_send, stat_recv))
        section_sq = stats_ref[0, 7:8, :]
        for k in range(1, count):
            section_sq = section_sq + stats_ref[k, 7:8, :]
        mine_ref[...] = jnp.broadcast_to(section_sq, (8, LANES))
        pair = pltpu.make_async_remote_copy(
            src_ref=mine_ref,
            dst_ref=got_ref,
            send_sem=pair_send,
            recv_sem=pair_recv,
            device_id={"section": 1 - section},
            device_id_type=MESH,
        )
        pair.start()
        pair.wait()
        norm = jnp.sqrt(mine_ref[...] + got_ref[...])
        norm_ref[...] = jnp.where(row == 0, norm, threshold / jnp.maximum(norm, threshold))
        for copy in sends:
            copy.wait_send()

    return pl.pallas_call(
        kernel,
        out_shape=[
            jax.ShapeDtypeStruct(state_part.shape, BF16),
            jax.ShapeDtypeStruct((count, 8, LANES), F32),
            jax.ShapeDtypeStruct((8, LANES), F32),
        ],
        in_specs=[VMEM_SPEC] * 5,
        out_specs=[ANY_SPEC, VMEM_SPEC, VMEM_SPEC],
        scratch_shapes=[
            pltpu.VMEM((8, sz.width), F32),
            pltpu.VMEM((count, 8, LANES), F32),
            pltpu.VMEM((rows, width), F32),
            pltpu.VMEM((rows, width), BF16),
        ]
        + [pltpu.VMEM((8, LANES), F32)] * 3
        + scatter_scratch(back, count, rows, width)
        + gather_scratch(parts, dims, count)
        + [DMA((count,))] * 4
        + [DMA, DMA],
        compiler_params=params(collective_id),
        name="finish_sums",
    )(state_part, small, squares, pack, head_sum)


def norm_rows(value, gain):
    mean = jnp.mean(value * value, axis=1, keepdims=True)
    return value * lax.rsqrt(mean + EPS_NORM) * gain


def norm_rows_back(value, gain, grad):
    width = value.shape[1]
    scale = lax.rsqrt(jnp.mean(value * value, axis=1, keepdims=True) + EPS_NORM)
    scaled = grad * gain
    dot = jnp.sum(scaled * value, axis=1, keepdims=True)
    back = scaled * scale - value * (scale * scale * scale * dot * (1.0 / width))
    return back, jnp.sum(grad * value * scale, axis=0, keepdims=True)


def write_pack(sz, pack_ref, head_ref, shared_ref):
    chans, state = sz.channels, 2 * NSTATE
    pack_ref[...] = jnp.zeros_like(pack_ref)
    lane = lax.broadcasted_iota(jnp.int32, (1, LANES), 1)
    bias_row = jnp.zeros((1, LANES), F32)
    rate_row = jnp.zeros((1, LANES), F32)
    rates = -jnp.exp(head_ref[:, (CONV + 2) * HDIM :])
    for head in range(sz.heads):
        cols = slice(head * HDIM, (head + 1) * HDIM)
        for tap in range(CONV):
            pack_ref[tap : tap + 1, cols] = head_ref[head : head + 1, tap * HDIM : (tap + 1) * HDIM]
        pack_ref[5:6, cols] = head_ref[head : head + 1, CONV * HDIM : (CONV + 1) * HDIM]
        pack_ref[CONV : CONV + 1, cols] = head_ref[head : head + 1, (CONV + 1) * HDIM : (CONV + 2) * HDIM]
        last = (CONV + 2) * HDIM
        pack_ref[6:7, cols] = jnp.broadcast_to(head_ref[head : head + 1, last + 2 : last + 3], (1, HDIM))
        bias_row = jnp.where(lane == head, head_ref[head : head + 1, last : last + 1], bias_row)
        rate_row = jnp.where(lane == head, rates[head : head + 1, 1:2], rate_row)
    pack_ref[7:8, :LANES] = bias_row
    pack_ref[8:9, :LANES] = rate_row
    for tap in range(CONV + 1):
        pack_ref[tap : tap + 1, chans : chans + state] = shared_ref[:, tap * state : (tap + 1) * state]
    pack_ref[GAIN_ROW : GAIN_ROW + 1, :] = shared_ref[:, (CONV + 1) * state :]


def opening(count, sz, proj_in_t, proj_state, proj_out, head_part, shared_part, order, first, collective_id):
    dims = chip_dims(count)
    rows, width = first.shape
    parts = column_parts(width, GATHER)
    cols = 256
    steps = width // cols
    full = sz.master // 16 * 16
    own_rows = proj_out.shape[0]

    def kernel(*refs):
        refs = list(refs)
        take = lambda number: [refs.pop(0) for _ in range(number)]
        in_hbm, state_hbm, out_hbm, order_hbm, head_ref, shared_ref, x_ref = take(7)
        ws_ref, wos_ref, pks_ref, all_ref = take(4)
        own_ref, in_ref, state_ref, out_ref, order_ref, low_ref, w_ref, wo_ref = take(8)
        ag_sems = take(3)
        load_sem, pair_send, pair_recv, pair_local = take(4)
        section = lax.axis_index("section")
        other = 1 - section
        loads = [
            pltpu.make_async_copy(src, dst, load_sem.at[k])
            for k, (src, dst) in enumerate(
                ((order_hbm, order_ref), (in_hbm, in_ref), (state_hbm, state_ref), (out_hbm, out_ref))
            )
        ]
        for copy in loads:
            copy.start()
        write_pack(sz, pks_ref.at[section], head_ref, shared_ref)
        greet_all(count, "section")
        sent = []

        def share(src, dst, k):
            copy = pltpu.make_async_remote_copy(
                src_ref=src,
                dst_ref=dst,
                send_sem=pair_send.at[k],
                recv_sem=pair_recv.at[k],
                device_id={"section": other},
                device_id_type=MESH,
            )
            copy.start()
            return copy

        pack_copy = share(pks_ref.at[section], pks_ref.at[section], 0)
        pack_copy.wait()
        gain = pks_ref[0, GAIN_ROW : GAIN_ROW + 1, :]
        own_ref[...] = norm_rows(x_ref[...].astype(F32), gain).astype(BF16)

        def keep(src, dst, k):
            local = pltpu.make_async_copy(src, dst, pair_local.at[k])
            local.start()
            sent.extend([share(src, dst, k), local])

        def low_out():
            for copy in loads:
                copy.wait()
            if own_rows < sz.channels:
                wo_ref[...] = jnp.zeros_like(wo_ref)
            wo_ref[:own_rows, :] = out_ref[...].astype(BF16)
            keep(wo_ref, wos_ref.at[section], 1)

        def low_in(step):
            span = slice(step * cols, (step + 1) * cols)
            low_ref[:full, :] = in_ref[:full, 0, span].astype(BF16)
            if full < sz.master_pad:
                low_ref[full:, :] = jnp.zeros((sz.master_pad - full, cols), BF16)
            if full < sz.master:
                low_ref[full : full + 16, :] = jnp.concatenate(
                    [in_ref[full : sz.master, 0, span], jnp.zeros((full + 16 - sz.master, cols), F32)], axis=0
                ).astype(BF16)
            w_ref[:, span] = tn(order_ref[: sz.master_pad, :], low_ref[...]).astype(BF16)
            row = lax.broadcasted_iota(jnp.int32, (2 * NSTATE, 2 * NSTATE), 0)
            col = lax.broadcasted_iota(jnp.int32, (2 * NSTATE, 2 * NSTATE), 1)
            one = (row == col).astype(BF16)
            w_ref[2 * sz.channels : sz.dt, span] = nt(one, state_ref[span, :].astype(BF16)).astype(BF16)
            keep(w_ref.at[:, span], ws_ref.at[section, :, span], 2 + step)

        work = [low_out] + [lambda step=step: low_in(step) for step in range(steps)]
        run_gather(count, parts, own_ref, all_ref, ag_sems, None, work)
        for copy in sent:
            copy.wait()

    return pl.pallas_call(
        kernel,
        out_shape=[
            jax.ShapeDtypeStruct((2, sz.cols, width), BF16),
            jax.ShapeDtypeStruct((2, sz.channels, width), BF16),
            jax.ShapeDtypeStruct((2, 16, width), F32),
            jax.ShapeDtypeStruct((count * rows, width), BF16),
        ],
        in_specs=[ANY_SPEC] * 4 + [VMEM_SPEC] * 3,
        out_specs=[ANY_SPEC, ANY_SPEC, VMEM_SPEC, ANY_SPEC],
        scratch_shapes=[
            pltpu.VMEM((rows, width), BF16),
            pltpu.VMEM(proj_in_t.shape, F32),
            pltpu.VMEM(proj_state.shape, F32),
            pltpu.VMEM(proj_out.shape, F32),
            pltpu.VMEM(order.shape, BF16),
            pltpu.VMEM((sz.master_pad, cols), BF16),
            pltpu.VMEM((sz.cols, width), BF16),
            pltpu.VMEM((sz.channels, width), BF16),
        ]
        + gather_scratch(parts, dims, count)
        + [DMA((4,)), DMA((2 + steps,)), DMA((2 + steps,)), DMA((2 + steps,))],
        compiler_params=params(collective_id),
        name="opening",
    )(proj_in_t, proj_state, proj_out, order, head_part, shared_part, first)


def column_of(tile, rows):
    row = lax.broadcasted_iota(jnp.int32, (rows, rows), 0)
    lane = lax.broadcasted_iota(jnp.int32, (rows, rows), 1)
    return nt((row == lane).astype(F32), tile, HIGH)[:, 0:1]


def write_stats(stat_ref, squares, out_grad, branch, rows):
    dot = nt(jnp.ones((8, branch.shape[1]), F32), out_grad * branch, HIGH)
    scale = lax.rsqrt(squares / (HEADS * HDIM) + EPS_NORM)
    row = lax.broadcasted_iota(jnp.int32, (8, rows), 0)
    stat_ref[...] = jnp.zeros_like(stat_ref)
    stat_ref[:, :rows] = jnp.where(row == 0, scale, jnp.where(row == 1, dot, 0.0))


def greet_other():
    barrier = pltpu.get_barrier_semaphore()
    other = 1 - lax.axis_index("section")
    pl.semaphore_signal(barrier, inc=1, device_id={"section": other}, device_id_type=MESH)
    pl.semaphore_wait(barrier, 1)
    return other


def add_up(out_ref, mine_ref, got_ref, squares_ref):
    rows, width = out_ref.shape
    step = 16 if rows % 16 == 0 else rows

    def body(i, carry):
        span = pl.ds(pl.multiple_of(i * step, step), step)
        total = mine_ref[span, :].astype(F32) + got_ref[span, :].astype(F32)
        out_ref[span, :] = total
        if squares_ref is not None:
            part = total * total
            for k in range(0, step, 8):
                squares_ref[...] += part[k : k + 8]
        return carry

    lax.fori_loop(0, rows // step, body, 0)


def trade_sections(sums, stacks, squared, collective_id):
    pairs = sums + stacks
    number, summed = len(pairs), len(sums)

    def kernel(*refs):
        ins, outs = refs[: 2 * number], refs[2 * number : 3 * number]
        squares_ref = refs[3 * number]
        boxes = refs[3 * number + 1 : 3 * number + 1 + summed]
        send_sem, recv_sem = refs[3 * number + 1 + summed :]
        squares_ref[...] = jnp.zeros_like(squares_ref)
        section = lax.axis_index("section")
        other = greet_other()

        def go(mine, theirs):
            copies = []
            for k in range(number):
                copy = pltpu.make_async_remote_copy(
                    src_ref=theirs[k],
                    dst_ref=boxes[k] if k < summed else outs[k].at[section],
                    send_sem=send_sem.at[k],
                    recv_sem=recv_sem.at[k],
                    device_id={"section": other},
                    device_id_type=MESH,
                )
                copy.start()
                copies.append(copy)
            for k in range(summed, number):
                outs[k][section] = mine[k][...]
            for k in range(number):
                copies[k].wait()
                if k < summed:
                    add_up(outs[k], mine[k], boxes[k], squares_ref if k < squared else None)

        pl.when(section == 0)(lambda: go(ins[0::2], ins[1::2]))
        pl.when(section == 1)(lambda: go(ins[1::2], ins[0::2]))

    shapes = [jax.ShapeDtypeStruct(a.shape, F32) for a, _ in sums]
    shapes += [jax.ShapeDtypeStruct((2,) + a.shape, a.dtype) for a, _ in stacks]
    shapes.append(jax.ShapeDtypeStruct((8, sums[0][0].shape[1]), F32))
    return pl.pallas_call(
        kernel,
        out_shape=shapes,
        in_specs=[VMEM_SPEC] * (2 * number),
        out_specs=[VMEM_SPEC] * len(shapes),
        scratch_shapes=[pltpu.VMEM(a.shape, a.dtype) for a, _ in sums] + [DMA((number,))] * 2,
        compiler_params=pltpu.CompilerParams(
            collective_id=collective_id, has_side_effects=True, vmem_limit_bytes=VMEM_LIMIT
        ),
        name="trade_sections",
    )(*[a for pair in pairs for a in pair])


class Sizes:
    def __init__(self, heads, tokens, width):
        self.heads = heads
        self.padded = heads + heads % 2
        self.channels = self.padded * HDIM
        self.conv = self.channels + 2 * NSTATE
        self.cols = 2 * self.channels + 2 * NSTATE + LANES
        self.dt = 2 * self.channels + 2 * NSTATE
        self.master = heads * COLS
        self.master_pad = -(-self.master // LANES) * LANES
        self.grad_rows = self.master_pad + 2 * NSTATE
        self.tokens = tokens
        self.width = width
        self.blocks = tokens // STRETCH

    def order(self):
        table = np.zeros((self.grad_rows, self.cols), np.float32)
        for head in range(self.heads):
            for j in range(HDIM):
                table[head * COLS + j, head * HDIM + j] = 1
                table[head * COLS + HDIM + j, self.channels + head * HDIM + j] = 1
            table[head * COLS + 2 * HDIM, self.dt + head] = 1
        for j in range(2 * NSTATE):
            table[self.master_pad + j, 2 * self.channels + j] = 1
        return jnp.asarray(table, BF16)

    def head_sum(self):
        table = np.zeros((self.channels, LANES), np.float32)
        for head in range(self.padded):
            table[head * HDIM : (head + 1) * HDIM, head] = 1
        return jnp.asarray(table, F32)


def nt(left, right, precision=None):
    return lax.dot_general(
        left, right, (((1,), (1,)), ((), ())), precision=precision, preferred_element_type=F32
    )


def tn(left, right, precision=None):
    return lax.dot_general(
        left, right, (((0,), (0,)), ((), ())), precision=precision, preferred_element_type=F32
    )


def nn(left, right, precision=None):
    return jnp.dot(left, right, precision=precision, preferred_element_type=F32)


def split(value):
    high = value.astype(BF16)
    return high, (value - high.astype(F32)).astype(BF16)


def fine(dot, left, right, left_axis, right_axis):
    left_high, left_low = split(left)
    right_high, right_low = split(right)
    return dot(
        jnp.concatenate([left_high, left_low, left_high], axis=left_axis),
        jnp.concatenate([right_high, right_high, right_low], axis=right_axis),
    )


def nt3(left, right):
    return fine(nt, left, right, 1, 1)


def tn3(left, right):
    return fine(tn, left, right, 0, 0)


def nn3(left, right):
    return fine(nn, left, right, 1, 0)


def softplus(value):
    return jnp.maximum(value, 0.0) + jnp.log1p(jnp.exp(-jnp.abs(value)))


def sigmoid(value):
    return 1.0 / (1.0 + jnp.exp(-value))


def halves(left, right):
    rows = left.shape[0]
    lane = lax.broadcasted_iota(jnp.int32, (rows, LANES), 1)
    return jnp.where(lane < HDIM, left, right)


def lower_mask(size):
    row = lax.broadcasted_iota(jnp.int32, (size, size), 0)
    col = lax.broadcasted_iota(jnp.int32, (size, size), 1)
    return row >= col


def step_rows(log_decay, step):
    lane = lax.broadcasted_iota(jnp.int32, log_decay.shape, 1)
    both = jnp.where(lane < 8, log_decay, pltpu.roll(step, 8, 1))
    return jnp.transpose(jnp.where(lane < 16, both, 0.0))


def to_columns(tile, rows):
    row = lax.broadcasted_iota(jnp.int32, (rows, LANES), 0)
    lane = lax.broadcasted_iota(jnp.int32, (rows, LANES), 1)
    return nt((row == lane).astype(F32), tile, HIGH)


def forward_phase(count, sz, layer, resets, gathered, weights, weight_out, pack, residual, live, cotangent, collective_id):
    block, chunk, chans = STRETCH, CHUNK, sz.channels
    dims = chip_dims(count)
    rows, width = residual.shape
    subs = block // chunk
    shards = block // rows
    blocks = sz.blocks
    planes = dims[0]
    per = blocks // planes
    parts = column_parts(width, GATHER)
    scatter = PlaneScatter(dims, rows, width)
    turn = cotangent is not None

    def kernel(*refs):
        refs = list(refs)
        take = lambda number: [refs.pop(0) for _ in range(number)]
        reset_ref, rows_ref, ws_ref, wos_ref, pks_ref, u_ref, live_ref = take(7)
        cot_ref = refs.pop(0) if turn else None
        result_ref, branch_ref, total_ref, next_ref, p_out, y_out, s_out = take(7)
        stats_ref = refs.pop(0) if turn else None
        conv_ref, state_ref, w_ref, wo_ref, h_buf, p_buf, y_buf, s_buf, part_ref, sq_ref = take(10)
        load_sem, store_sem, weight_sem = take(3)
        sums_ref, own_ref = take(2)
        scatter_refs = take(3)
        ag_sems = take(3)
        small_send, small_recv = take(2)
        pk_ref = pks_ref.at[layer]

        def load(c):
            span = pl.ds(pl.multiple_of(c * block, block), block)
            return pltpu.make_async_copy(rows_ref.at[span, :], h_buf.at[c % 2], load_sem.at[c % 2])

        def stores(c):
            slot = c % 2
            span = pl.ds(pl.multiple_of(c * block, block), block)
            return [
                pltpu.make_async_copy(p_buf.at[slot], p_out.at[span, :], store_sem.at[0, slot]),
                pltpu.make_async_copy(y_buf.at[slot], y_out.at[span, :], store_sem.at[1, slot]),
                pltpu.make_async_copy(s_buf.at[slot], s_out.at[pl.ds(c * subs, subs)], store_sem.at[2, slot]),
            ]

        load(0).start()
        weight_copies = [
            pltpu.make_async_copy(ws_ref.at[layer], w_ref, weight_sem.at[0]),
            pltpu.make_async_copy(wos_ref.at[layer], wo_ref, weight_sem.at[1]),
        ]
        for copy in weight_copies:
            copy.start()
        greet_all(count)
        conv_ref[...] = jnp.zeros_like(conv_ref)
        state_ref[...] = jnp.zeros_like(state_ref)
        scatter.bind(part_ref, branch_ref, *scatter_refs)
        for copy in weight_copies:
            copy.wait()

        def one_block(c, carry):
            slot = c % 2
            keep = 1.0 - reset_ref[c]
            span_all = pl.ds(pl.multiple_of(c * block, block), block)
            pl.when(c + 1 < blocks)(lambda: load(c + 1).start())
            load(c).wait()

            @pl.when(c >= 2)
            def _():
                for copy in stores(c - 2):
                    copy.wait()

            h_ref, p_ref, y_ref, s_ref = (buf.at[slot] for buf in (h_buf, p_buf, y_buf, s_buf))
            p_ref[...] = nt(h_ref[...], w_ref[...])
            inner = p_ref[:, chans : 2 * chans]
            state_raw = p_ref[:, 2 * chans : sz.dt].astype(BF16).astype(F32)
            conv_ref[0:8, :] = conv_ref[block : block + 8, :] * keep
            conv_ref[8 : 8 + block, :chans] = inner
            conv_ref[8 : 8 + block, chans:] = state_raw
            pre = pk_ref[CONV : CONV + 1, : sz.conv] + pk_ref[0:1, : sz.conv] * conv_ref[8 : 8 + block, :]
            for tap in range(1, CONV):
                pre = pre + pk_ref[tap : tap + 1, : sz.conv] * conv_ref[8 - tap : 8 - tap + block, :]
            act = pre * sigmoid(pre)
            step = softplus(p_ref[:, sz.dt :] + pk_ref[7:8, :LANES])
            decay = step * pk_ref[8:9, :LANES]
            mask = lower_mask(chunk)
            lower = mask.astype(F32)
            lane = lax.broadcasted_iota(jnp.int32, (chunk, LANES), 1)
            for sub in range(subs):
                span = slice(sub * chunk, (sub + 1) * chunk)
                if sub == 0:
                    state_ref[...] = state_ref[...] * keep
                s_ref[sub] = state_ref[...]
                dt = step[span]
                log_decay = nn(lower, decay[span], HIGH)
                flat = step_rows(log_decay, dt)
                writer = act[span, chans : chans + NSTATE]
                reader = act[span, chans + NSTATE :]
                cross = nt3(reader, writer)
                for pair in range(sz.padded // 2):
                    cols = slice(pair * LANES, (pair + 1) * LANES)
                    x = act[span, cols]
                    total = jnp.zeros((chunk, LANES), F32)
                    for side in range(2):
                        head = 2 * pair + side
                        gap = log_decay[:, head : head + 1] - flat[head : head + 1, :]
                        weight = cross * jnp.exp(jnp.where(mask, gap, -1e30)) * flat[8 + head : 9 + head, :]
                        part = jnp.where((lane < HDIM) == (side == 0), x, 0.0)
                        total = total + nn3(weight, part)
                    logs = halves(log_decay[:, 2 * pair : 2 * pair + 1], log_decay[:, 2 * pair + 1 : 2 * pair + 2])
                    dts = halves(dt[:, 2 * pair : 2 * pair + 1], dt[:, 2 * pair + 1 : 2 * pair + 2])
                    old = state_ref[:, cols]
                    total = total + jnp.exp(logs) * nn3(reader, old)
                    last = logs[chunk - 1 : chunk, :]
                    moved_in = x * jnp.exp(last - logs) * dts
                    state_ref[:, cols] = jnp.exp(last) * old + tn3(writer, moved_in)
                    y_ref[span, cols] = total + pk_ref[6:7, cols] * x
            z = p_ref[:, :chans]
            gated = y_ref[...] * z * sigmoid(z)
            square = nt(jnp.ones((8, chans), F32), gated * gated, HIGH)
            for k in range(shards):
                sq_ref[c * shards + k] = square[:, k * rows : (k + 1) * rows]
            high, low = split(gated * pk_ref[5:6, :chans])
            part_ref[span_all, :] = (nn(high, wo_ref[...]) + nn(low, wo_ref[...])).astype(BF16)
            for copy in stores(c):
                copy.start()
            if per == 1:
                scatter.step(planes, c + 1, lambda k: k)
            else:
                pl.when(c % per == per - 1)(lambda: scatter.step(planes, c // per + 1, lambda k: k))
            return carry

        lax.fori_loop(0, blocks, one_block, 0)
        me = lax.axis_index("head")
        copies = start_direct(count, lambda peer: sq_ref.at[peer], sums_ref, small_send, small_recv)
        sums_ref[me] = sq_ref[me]
        scatter.finish(planes, lambda k: k)
        wait_direct(count, sums_ref, copies, small_recv, small_send)
        total = jnp.sum(sums_ref[...], axis=0)
        total_ref[...] = total
        scale = lax.rsqrt(column_of(total, rows) / (HEADS * HDIM) + EPS_NORM)
        branch = branch_ref[...] * scale
        branch_ref[...] = branch
        live_col = live_ref[:, 0:1]
        result = (u_ref[...].astype(F32) + live_col * branch).astype(BF16)
        result_ref[...] = result
        stat = None
        if turn:
            stat_ref, stat_send, stat_recv = refs
            out_grad = (live_col * cot_ref[...].astype(F32)).astype(BF16)
            own_ref[...] = out_grad
            write_stats(stat_ref, total, out_grad.astype(F32), branch, rows)
            stat = (stat_ref, stats_ref, stat_send, stat_recv)
        else:
            gain = pks_ref[layer + 1, GAIN_ROW : GAIN_ROW + 1, :]
            own_ref[...] = norm_rows(result.astype(F32), gain).astype(BF16)
        run_gather(count, parts, own_ref, next_ref, ag_sems, stat)
        for c in range(max(blocks - 2, 0), blocks):
            for copy in stores(c):
                copy.wait()
        scatter.drain()

    tokens = sz.tokens
    out_shape = [
        jax.ShapeDtypeStruct((rows, width), BF16),
        jax.ShapeDtypeStruct((rows, width), F32),
        jax.ShapeDtypeStruct((8, rows), F32),
        jax.ShapeDtypeStruct((tokens, width), BF16),
        jax.ShapeDtypeStruct((tokens, sz.cols), F32),
        jax.ShapeDtypeStruct((tokens, chans), F32),
        jax.ShapeDtypeStruct((tokens // chunk, NSTATE, chans), F32),
    ]
    out_specs = [VMEM_SPEC] * 3 + [ANY_SPEC] * 4
    scratch = [
        pltpu.VMEM((block + 8, sz.conv), F32),
        pltpu.VMEM((NSTATE, chans), F32),
        pltpu.VMEM((sz.cols, width), BF16),
        pltpu.VMEM((chans, width), BF16),
        pltpu.VMEM((2, block, width), BF16),
        pltpu.VMEM((2, block, sz.cols), F32),
        pltpu.VMEM((2, block, chans), F32),
        pltpu.VMEM((2, subs, NSTATE, chans), F32),
        pltpu.VMEM((tokens, width), BF16),
        pltpu.VMEM((count, 8, rows), F32),
        DMA((2,)),
        DMA((3, 2)),
        DMA((2,)),
        pltpu.VMEM((count, 8, rows), F32),
        pltpu.VMEM((rows, width), BF16),
    ]
    scratch += scatter.scratch() + gather_scratch(parts, dims, count) + [DMA((count,))] * 2
    operands = [resets, gathered, weights, weight_out, pack, residual, live]
    in_specs = [pl.BlockSpec(memory_space=pltpu.SMEM)] + [ANY_SPEC] * 3 + [VMEM_SPEC] * 3
    if turn:
        out_shape.append(jax.ShapeDtypeStruct((count, 8, LANES), F32))
        out_specs.append(VMEM_SPEC)
        scratch += [pltpu.VMEM((8, LANES), F32)] + [DMA((count,))] * 2
        operands.append(cotangent)
        in_specs.append(VMEM_SPEC)
    return pl.pallas_call(
        kernel,
        out_shape=out_shape,
        in_specs=in_specs,
        out_specs=out_specs,
        scratch_shapes=scratch,
        compiler_params=params(collective_id),
        name="forward_phase",
    )(*operands)


def backward_phase(
    count, sz, layer, resets, out_grads, proj, mixed, states, stats, weights, weight_out, pack, order,
    residual, upstream, live, below, upper, collective_id,
):
    block, chunk, chans = STRETCH, CHUNK, sz.channels
    dims = chip_dims(count)
    rows, width = residual.shape
    subs = block // chunk
    blocks = sz.blocks
    planes = dims[0]
    per = blocks // planes
    parts = column_parts(width, GATHER)
    scatter = PlaneScatter(dims, rows, width)
    more = below is not None
    close = upper is not None
    cols = 256
    steps = width // cols

    def kernel(*refs):
        refs = list(refs)
        take = lambda number: [refs.pop(0) for _ in range(number)]
        reset_ref, g_all, p_all, y_all, s_all, ws_ref, wos_ref, orders_ref = take(8)
        st_ref, pks_ref, sum_ref, u_ref, up_ref, live_ref = take(6)
        if more:
            lower_ref, lower_total = take(2)
        if close:
            gt_upper, q_upper, h_upper, g_upper, h_own = take(5)
            acc_upper, result_own, result_upper, grad_upper = take(4)
            sum_in, sum_out, sum_state, sum_small, outs_ref, grads_ref, squares_ref = take(7)
        else:
            grad_ref, low_grad_ref, acc_ref, gt_out, q_out = take(5)
        if more:
            next_ref, stats_ref = take(2)
        conv_ref, dpre_ref, dact_ref, ddt_ref, dstate_ref = take(5)
        w_ref, wo_ref, order_ref, g_buf, p_buf, halo_buf, y_buf, s_buf, gt_buf, q_buf, part_ref = take(11)
        load_sem, store_sem, weight_sem = take(3)
        scatter_refs = take(3)
        pk_ref = pks_ref.at[layer]
        if close:
            grad_ref, acc_ref, gt_full, q_full, gt_one, q_one, h_cols, g_cols = take(8)
            send_state, box_in, box_out, box_state, box_small, state_own = take(6)
            send_in, send_out = w_ref.at[: sz.master_pad, :], wo_ref
            col_sem, whole_sem, trade_send, trade_recv, few_send, few_recv = take(6)
            section = lax.axis_index("section")
            other = 1 - section
            whole = [
                pltpu.make_async_copy(gt_upper, gt_one, whole_sem.at[0]),
                pltpu.make_async_copy(q_upper, q_one, whole_sem.at[1]),
            ]

        def loads(c):
            slot = c % 2
            span = pl.ds(pl.multiple_of(c * block, block), block)
            before = pl.multiple_of(jnp.maximum(c * block - 8, 0), 8)
            return [
                pltpu.make_async_copy(g_all.at[span, :], g_buf.at[slot], load_sem.at[0, slot]),
                pltpu.make_async_copy(p_all.at[span, :], p_buf.at[slot], load_sem.at[1, slot]),
                pltpu.make_async_copy(p_all.at[pl.ds(before, 8), :], halo_buf.at[slot], load_sem.at[2, slot]),
                pltpu.make_async_copy(y_all.at[span, :], y_buf.at[slot], load_sem.at[3, slot]),
                pltpu.make_async_copy(s_all.at[pl.ds(c * subs, subs)], s_buf.at[slot], load_sem.at[4, slot]),
            ]

        def stores(c):
            slot = c % 2
            span = pl.ds(pl.multiple_of(c * block, block), block)
            if close:
                return []
            return [
                pltpu.make_async_copy(gt_buf.at[slot], gt_out.at[:, span], store_sem.at[0, slot]),
                pltpu.make_async_copy(q_buf.at[slot], q_out.at[span, :], store_sem.at[1, slot]),
            ]

        for copy in loads(blocks - 1):
            copy.start()
        weight_copies = [
            pltpu.make_async_copy(wos_ref.at[layer], wo_ref, weight_sem.at[0]),
            pltpu.make_async_copy(ws_ref.at[layer], w_ref, weight_sem.at[1]),
            pltpu.make_async_copy(orders_ref, order_ref, weight_sem.at[2]),
        ]
        for copy in weight_copies:
            copy.start()
        if close:
            for copy in whole:
                copy.start()
            greet_all(count, "section")
        else:
            greet_all(count)
        dpre_ref[...] = jnp.zeros_like(dpre_ref)
        dstate_ref[...] = jnp.zeros_like(dstate_ref)
        acc_ref[...] = jnp.zeros_like(acc_ref)
        scatter.bind(part_ref, grad_ref, *scatter_refs)
        for copy in weight_copies:
            copy.wait()

        def one_block(i, carry):
            c = blocks - 1 - i
            slot = c % 2
            keep = 1.0 - reset_ref[c]
            after = 1.0 - reset_ref[jnp.minimum(c + 1, blocks - 1)]
            span_all = pl.ds(pl.multiple_of(c * block, block), block)

            @pl.when(c >= 1)
            def _():
                for copy in loads(c - 1):
                    copy.start()

            for copy in loads(c):
                copy.wait()

            if not close:
                @pl.when(i >= 2)
                def _():
                    for copy in stores(c + 2):
                        copy.wait()

            g_ref, p_ref, halo_ref, y_ref, s_ref = (
                buf.at[slot] for buf in (g_buf, p_buf, halo_buf, y_buf, s_buf)
            )
            if close:
                gt_ref, q_ref = gt_full.at[:, span_all], q_full.at[span_all, :]
            else:
                gt_ref, q_ref = gt_buf.at[slot], q_buf.at[slot]
            conv_ref[0:8, :chans] = halo_ref[:, chans : 2 * chans] * keep
            conv_ref[0:8, chans:] = halo_ref[:, 2 * chans : sz.dt].astype(BF16).astype(F32) * keep
            conv_ref[8 : 8 + block, :chans] = p_ref[:, chans : 2 * chans]
            conv_ref[8 : 8 + block, chans:] = p_ref[:, 2 * chans : sz.dt].astype(BF16).astype(F32)
            pre = pk_ref[CONV : CONV + 1, : sz.conv] + pk_ref[0:1, : sz.conv] * conv_ref[8 : 8 + block, :]
            for tap in range(1, CONV):
                pre = pre + pk_ref[tap : tap + 1, : sz.conv] * conv_ref[8 - tap : 8 - tap + block, :]
            gate = sigmoid(pre)
            act = pre * gate
            slope = gate * (1.0 + pre * (1.0 - gate))
            step_in = p_ref[:, sz.dt :] + pk_ref[7:8, :LANES]
            step = softplus(step_in)
            rate = pk_ref[8:9, :LANES]
            decay = step * rate
            z = p_ref[:, :chans]
            zgate = sigmoid(z)
            zsilu = z * zgate
            y = y_ref[...]
            gated = y * zsilu
            gain = pk_ref[5:6, :chans]
            skip = pk_ref[6:7, :chans]
            columns = [to_columns(st_ref[c * (block // rows) + k], rows) for k in range(block // rows)]
            columns = jnp.concatenate(columns, axis=0)
            scale = columns[:, 0:1]
            along = columns[:, 1:2]
            grad_q = nt(g_ref[...], wo_ref[...])
            q_ref[...] = (gated * scale * gain).astype(BF16)
            acc_ref[5:6, :chans] += jnp.sum(grad_q * gated * scale, axis=0, keepdims=True)
            dgated = grad_q * gain * scale - gated * (scale * scale * along * (1.0 / (HEADS * HDIM)))
            dy = dgated * zsilu
            dz = dgated * y * zgate * (1.0 + z * (1.0 - zgate))
            x_all = act[:, :chans]
            acc_ref[6:7, :chans] += jnp.sum(dy * x_all, axis=0, keepdims=True)
            scan_dot = nn(dy * (y - skip * x_all), sum_ref[...], HIGH)
            mask = lower_mask(chunk)
            lower = mask.astype(F32)
            lane = lax.broadcasted_iota(jnp.int32, (chunk, LANES), 1)
            for sub in reversed(range(subs)):
                span = slice(sub * chunk, (sub + 1) * chunk)
                dt = step[span]
                log_decay = nn(lower, decay[span], HIGH)
                flat = step_rows(log_decay, dt)
                writer = act[span, chans : chans + NSTATE]
                reader = act[span, chans + NSTATE :]
                cross = nt3(reader, writer)
                cross_grad = jnp.zeros((chunk, chunk), F32)
                dreader = jnp.zeros((chunk, NSTATE), F32)
                dwriter = jnp.zeros((chunk, NSTATE), F32)
                fall = jnp.zeros((LANES, chunk), F32)
                row = lax.broadcasted_iota(jnp.int32, (LANES, chunk), 0)
                reach = []
                carried = []
                for pair in range(sz.padded // 2):
                    cols = slice(pair * LANES, (pair + 1) * LANES)
                    x = act[span, cols]
                    g = dy[span, cols]
                    logs = halves(log_decay[:, 2 * pair : 2 * pair + 1], log_decay[:, 2 * pair + 1 : 2 * pair + 2])
                    dts = halves(dt[:, 2 * pair : 2 * pair + 1], dt[:, 2 * pair + 1 : 2 * pair + 2])
                    last = logs[chunk - 1 : chunk, :]
                    old = s_ref[sub, :, cols]
                    dnew = dstate_ref[:, cols]
                    faded = g * jnp.exp(logs)
                    tail = jnp.exp(last - logs)
                    dreader = dreader + nt3(faded, old)
                    ahead = nn3(writer, dnew)
                    dx = g * skip[:, cols] + ahead * tail * dts
                    dwriter = dwriter + nt3(x * tail * dts, dnew)
                    reach.append(x * ahead * tail)
                    carried.append(jnp.sum(old * dnew, axis=0, keepdims=True) * jnp.exp(last))
                    dstate_ref[:, cols] = jnp.exp(last) * dnew + tn3(reader, faded)
                    for side in range(2):
                        head = 2 * pair + side
                        own = (lane < HDIM) == (side == 0)
                        g_own = jnp.where(own, g, 0.0)
                        gap = log_decay[:, head : head + 1] - flat[head : head + 1, :]
                        decays = jnp.exp(jnp.where(mask, gap, -1e30))
                        steps = flat[8 + head : 9 + head, :]
                        spread = nt3(g_own, x) * decays
                        weight = cross * decays * steps
                        dx = dx + tn3(weight, g_own)
                        cross_grad = cross_grad + spread * steps
                        sums = jnp.sum(spread * cross, axis=0, keepdims=True)
                        fall = fall + jnp.where(row == head, sums, 0.0)
                    dact_ref[span, cols] = dx
                dact_ref[span, chans : chans + NSTATE] = dwriter + tn3(cross_grad, reader)
                dact_ref[span, chans + NSTATE :] = dreader + nn3(cross_grad, writer)
                reach = nn(jnp.concatenate(reach, axis=1), sum_ref[...], HIGH)
                carried = nn(jnp.concatenate(carried, axis=1), sum_ref[...], HIGH)
                direct = jnp.transpose(fall) + reach
                given = dt * reach
                dlog = scan_dot[span] - dt * direct
                ends = jnp.sum(given, axis=0, keepdims=True) + carried
                at_end = lax.broadcasted_iota(jnp.int32, (chunk, LANES), 0) == chunk - 1
                dlog = dlog + jnp.where(at_end, ends, 0.0)
                ddecay = tn(lower, dlog, HIGH)
                ddt_ref[span, :] = direct + ddecay * rate
                acc_ref[8:9, :LANES] += jnp.sum(ddecay * dt, axis=0, keepdims=True)
            dstate_ref[...] = dstate_ref[...] * keep
            ddt_raw = ddt_ref[...] * sigmoid(step_in)
            acc_ref[7:8, :LANES] += jnp.sum(ddt_raw, axis=0, keepdims=True)
            dpre_ref[block : block + 8, :] = dpre_ref[0:8, :] * after
            dpre_ref[0:block, :] = dact_ref[...] * slope
            raw = conv_ref[8 : 8 + block, :]
            acc_ref[CONV : CONV + 1, : sz.conv] += jnp.sum(dpre_ref[0:block, :], axis=0, keepdims=True)
            draw = jnp.zeros((block, sz.conv), F32)
            for tap in range(CONV):
                later = dpre_ref[tap : tap + block, :]
                draw = draw + pk_ref[tap : tap + 1, : sz.conv] * later
                acc_ref[tap : tap + 1, : sz.conv] += jnp.sum(raw * later, axis=0, keepdims=True)
            low = jnp.concatenate(
                [dz.astype(BF16), draw.astype(BF16), ddt_raw.astype(BF16)], axis=1
            )
            part_ref[span_all, :] = nn(low, w_ref[...]).astype(BF16)
            gt_ref[...] = nt(order_ref[...], low).astype(BF16)
            for copy in stores(c):
                copy.start()
            if per == 1:
                scatter.step(planes, i + 1, lambda k: planes - 1 - k)
            else:
                pl.when(i % per == per - 1)(
                    lambda: scatter.step(planes, i // per + 1, lambda k: planes - 1 - k)
                )
            return carry

        def input_grads():
            gain = pk_ref[GAIN_ROW : GAIN_ROW + 1, :]
            grad, gain_grad = norm_rows_back(u_ref[...].astype(F32), gain, grad_ref[...])
            grad = grad + up_ref[...].astype(F32)
            grad_ref[...] = grad
            acc_ref[GAIN_ROW : GAIN_ROW + 1, :] = gain_grad
            return grad

        lax.fori_loop(0, blocks, one_block, 0)
        if not close:
            scatter.finish(planes, lambda k: planes - 1 - k)
            grad = input_grads()
            low_grad_ref[...] = grad.astype(BF16)
            if more:
                own_ref, stat_ref, stat_send, stat_recv = take(4)
                out_grad = (live_ref[:, 0:1] * grad.astype(BF16).astype(F32)).astype(BF16)
                own_ref[...] = out_grad
                write_stats(stat_ref, lower_total[...], out_grad.astype(F32), lower_ref[...], rows)
                run_gather(count, parts, own_ref, next_ref, refs, (stat_ref, stats_ref, stat_send, stat_recv))
            for c in range(0, min(2, blocks)):
                for copy in stores(c):
                    copy.wait()
            scatter.drain()
            return

        def at(j):
            return pl.ds(pl.multiple_of(j * cols, cols), cols)

        def columns(which, j):
            slot = j % 2
            h_all, g_from = (h_upper, g_upper) if which else (h_own, g_all)
            return [
                pltpu.make_async_copy(h_all.at[:, at(j)], h_cols.at[slot], col_sem.at[0, slot]),
                pltpu.make_async_copy(g_from.at[:, at(j)], g_cols.at[slot], col_sem.at[1, slot]),
            ]

        def passed(src, dst, send_sem, recv_sem):
            return pltpu.make_async_remote_copy(
                src_ref=src, dst_ref=dst, send_sem=send_sem, recv_sem=recv_sem,
                device_id={"section": other}, device_id_type=MESH,
            )

        def traded(j):
            sets = ((send_in, box_in), (send_out, box_out), (send_state, box_state))
            return [
                passed(src.at[:, at(j)], dst.at[:, at(j)], trade_send.at[k, j], trade_recv.at[k, j])
                for k, (src, dst) in enumerate(sets)
            ]

        def weight_steps(which, begin, end):
            gt, q = (gt_one, q_one) if which else (gt_full, q_full)

            def body(j, carry):
                slot = j % 2
                for copy in columns(which, j):
                    copy.wait()

                @pl.when(j + 1 < steps)
                def _():
                    for copy in columns(which, j + 1):
                        copy.start()

                in_grad = nn(gt[: sz.master_pad, :], h_cols[slot])
                state_grad = nn(gt[sz.master_pad :, :], h_cols[slot])
                out_grad = tn(q[...], g_cols[slot])

                @pl.when(section == which)
                def _():
                    sum_in[:, at(j)] = in_grad
                    sum_out[:, at(j)] = out_grad
                    state_own[:, at(j)] = state_grad

                @pl.when(section != which)
                def _():
                    send_in[:, at(j)] = in_grad.astype(BF16)
                    send_out[:, at(j)] = out_grad.astype(BF16)
                    send_state[:, at(j)] = state_grad
                    for copy in traded(j):
                        copy.start()

                return carry

            lax.fori_loop(begin, end, body, 0)

        def begin_columns(which):
            for copy in columns(which, 0):
                copy.start()

        begin_columns(1)
        for copy in whole:
            copy.wait()
        weight_steps(1, 0, steps // 4)
        scatter.step(planes, planes + 1, lambda k: planes - 1 - k)
        weight_steps(1, steps // 4, steps // 2)
        scatter.step(planes, planes + 2, lambda k: planes - 1 - k)
        weight_steps(1, steps // 2, steps)
        begin_columns(0)
        weight_steps(0, 0, steps // 4)
        scatter.last()
        input_grads()
        few = [(acc_ref, acc_upper, box_small), (result_own, result_upper, outs_ref.at[section])]
        few.append((grad_ref, grad_upper, grads_ref.at[section]))

        def few_copies(theirs):
            return [
                passed(entry[theirs], entry[2], few_send.at[k], few_recv.at[k]) for k, entry in enumerate(few)
            ]

        @pl.when(section == 0)
        def _():
            for copy in few_copies(1):
                copy.start()
            outs_ref[0] = result_own[...]
            grads_ref[0] = grad_ref[...]

        @pl.when(section == 1)
        def _():
            for copy in few_copies(0):
                copy.start()
            outs_ref[1] = result_upper[...]
            grads_ref[1] = grad_upper[...]

        weight_steps(0, steps // 4, steps)
        squares_ref[...] = jnp.zeros_like(squares_ref)

        def add_up(j, carry):
            for copy in traded(j):
                copy.wait_recv()
            total = sum_in[:, at(j)] + box_in[:, at(j)].astype(F32)
            sum_in[:, at(j)] = total
            squares_ref[0:1, at(j)] += jnp.sum(total * total, axis=0, keepdims=True)
            total = sum_out[:, at(j)] + box_out[:, at(j)].astype(F32)
            sum_out[:, at(j)] = total
            squares_ref[1:2, at(j)] += jnp.sum(total * total, axis=0, keepdims=True)
            sum_state[:, at(j)] = (state_own[:, at(j)] + box_state[:, at(j)]).astype(BF16)
            return carry

        lax.fori_loop(0, steps, add_up, 0)
        for copy in few_copies(0):
            copy.wait_recv()
        sum_small[...] = jnp.where(section == 0, acc_ref[...], acc_upper[...]) + box_small[...]

        def settle(j, carry):
            for copy in traded(j):
                copy.wait_send()
            return carry

        lax.fori_loop(0, steps, settle, 0)
        for copy in few_copies(0):
            copy.wait_send()
        scatter.drain()

    tokens = sz.tokens
    state = 2 * NSTATE
    if close:
        out_shape = [
            jax.ShapeDtypeStruct((sz.master_pad, width), F32),
            jax.ShapeDtypeStruct((chans, width), F32),
            jax.ShapeDtypeStruct((state, width), BF16),
            jax.ShapeDtypeStruct((16, width), F32),
            jax.ShapeDtypeStruct((2, rows, width), BF16),
            jax.ShapeDtypeStruct((2, rows, width), F32),
            jax.ShapeDtypeStruct((8, width), F32),
        ]
        out_specs = [VMEM_SPEC] * 7
    else:
        out_shape = [
            jax.ShapeDtypeStruct((rows, width), F32),
            jax.ShapeDtypeStruct((rows, width), BF16),
            jax.ShapeDtypeStruct((16, width), F32),
            jax.ShapeDtypeStruct((sz.grad_rows, tokens), BF16),
            jax.ShapeDtypeStruct((tokens, chans), BF16),
        ]
        out_specs = [VMEM_SPEC] * 3 + [ANY_SPEC] * 2
    scratch = [
        pltpu.VMEM((block + 8, sz.conv), F32),
        pltpu.VMEM((block + 8, sz.conv), F32),
        pltpu.VMEM((block, sz.conv), F32),
        pltpu.VMEM((block, LANES), F32),
        pltpu.VMEM((NSTATE, chans), F32),
        pltpu.VMEM((sz.cols, width), BF16),
        pltpu.VMEM((chans, width), BF16),
        pltpu.VMEM((sz.grad_rows, sz.cols), BF16),
        pltpu.VMEM((2, block, width), BF16),
        pltpu.VMEM((2, block, sz.cols), F32),
        pltpu.VMEM((2, 8, sz.cols), F32),
        pltpu.VMEM((2, block, chans), F32),
        pltpu.VMEM((2, subs, NSTATE, chans), F32),
        pltpu.VMEM((8, LANES) if close else (2, sz.grad_rows, block), BF16),
        pltpu.VMEM((8, LANES) if close else (2, block, chans), BF16),
        pltpu.VMEM((tokens, width), BF16),
        DMA((5, 2)),
        DMA((2, 2)),
        DMA((3,)),
    ]
    scratch += scatter.scratch()
    if close:
        scratch += [
            pltpu.VMEM((rows, width), F32),
            pltpu.VMEM((16, width), F32),
            pltpu.VMEM((sz.grad_rows, tokens), BF16),
            pltpu.VMEM((tokens, chans), BF16),
            pltpu.VMEM((sz.grad_rows, tokens), BF16),
            pltpu.VMEM((tokens, chans), BF16),
            pltpu.VMEM((2, tokens, cols), BF16),
            pltpu.VMEM((2, tokens, cols), BF16),
        ]
        scratch += [
            pltpu.VMEM((state, width), F32),
            pltpu.VMEM((sz.master_pad, width), BF16),
            pltpu.VMEM((chans, width), BF16),
            pltpu.VMEM((state, width), F32),
            pltpu.VMEM((16, width), F32),
            pltpu.VMEM((state, width), F32),
        ]
        scratch += [DMA((2, 2)), DMA((2,)), DMA((3, steps)), DMA((3, steps)), DMA((3,)), DMA((3,))]
    operands = [resets, out_grads, proj, mixed, states, weights, weight_out, order]
    in_specs = [pl.BlockSpec(memory_space=pltpu.SMEM)] + [ANY_SPEC] * 7 + [VMEM_SPEC] * 6
    operands += [stats, pack, sz.head_sum(), residual, upstream, live]
    if more:
        out_shape += [
            jax.ShapeDtypeStruct((tokens, width), BF16),
            jax.ShapeDtypeStruct((count, 8, LANES), F32),
        ]
        out_specs += [ANY_SPEC, VMEM_SPEC]
        scratch += [pltpu.VMEM((rows, width), BF16), pltpu.VMEM((8, LANES), F32)]
        scratch += [DMA((count,))] * 2 + gather_scratch(parts, dims, count)
        operands += list(below)
        in_specs += [VMEM_SPEC] * 2
    if close:
        operands += list(upper)
        in_specs += [ANY_SPEC] * 5 + [VMEM_SPEC] * 4
    return pl.pallas_call(
        kernel,
        out_shape=out_shape,
        in_specs=in_specs,
        out_specs=out_specs,
        scratch_shapes=scratch,
        compiler_params=params(collective_id),
        name="last_phase" if close else "backward_phase",
    )(*operands)


def weight_grads(sz, grads_t, gathered, scaled, out_grads):
    cols = 256

    split_row = sz.master_pad

    def kernel(gt_ref, h_ref, q_ref, g_ref, in_ref, state_ref, out_ref):
        in_ref[...] = nn(gt_ref[:split_row, :], h_ref[...]).astype(BF16)
        state_ref[...] = nn(gt_ref[split_row:, :], h_ref[...])
        out_ref[...] = tn(q_ref[...], g_ref[...]).astype(BF16)

    tokens, width, chans = sz.tokens, sz.width, sz.channels
    return pl.pallas_call(
        kernel,
        grid=(width // cols,),
        out_shape=[
            jax.ShapeDtypeStruct((sz.master_pad, width), BF16),
            jax.ShapeDtypeStruct((2 * NSTATE, width), F32),
            jax.ShapeDtypeStruct((chans, width), BF16),
        ],
        in_specs=[
            pl.BlockSpec((sz.grad_rows, tokens), lambda i: (0, 0)),
            pl.BlockSpec((tokens, cols), lambda i: (0, i)),
            pl.BlockSpec((tokens, chans), lambda i: (0, 0)),
            pl.BlockSpec((tokens, cols), lambda i: (0, i)),
        ],
        out_specs=[
            pl.BlockSpec((sz.master_pad, cols), lambda i: (0, i)),
            pl.BlockSpec((2 * NSTATE, cols), lambda i: (0, i)),
            pl.BlockSpec((chans, cols), lambda i: (0, i)),
        ],
        compiler_params=pltpu.CompilerParams(vmem_limit_bytes=VMEM_LIMIT),
        name="weight_grads",
    )(grads_t, gathered, scaled, out_grads)


def adam_update(weight, moment, second, gradient, rate, decay):
    moment_new = BETA_ONE * moment + (1.0 - BETA_ONE) * gradient
    second_new = BETA_TWO * second + (1.0 - BETA_TWO) * gradient * gradient
    corrected = moment_new / (1.0 - BETA_ONE**ADAM_STEP)
    corrected_sq = second_new / (1.0 - BETA_TWO**ADAM_STEP)
    weight_new = weight - rate * (corrected / (jnp.sqrt(corrected_sq) + ADAM_EPS) + decay * weight)
    return (weight_new, moment_new, second_new)


def adam_in(sz, clip, grad, weight, moment, second):
    block = LANES
    width = sz.width

    def kernel(clip_ref, g_ref, w_ref, m_ref, v_ref, wn_ref, mn_ref, vn_ref, low_ref):
        scale = clip_ref[0]

        def body(i, carry):
            made = []
            for half in range(2):
                span = pl.ds(pl.multiple_of(i * 16 + half * 8, 8), 8)
                new = adam_update(
                    w_ref[span, 0, :], m_ref[span, 0, :], v_ref[span, 0, :],
                    scale * g_ref[span, :], LEARN_MATRIX, WEIGHT_DECAY,
                )
                wn_ref[span, 0, :] = new[0]
                mn_ref[span, 0, :] = new[1]
                vn_ref[span, 0, :] = new[2]
                made.append(new[0])
            low_ref[pl.ds(pl.multiple_of(i * 16, 16), 16), :] = jnp.concatenate(made, axis=0).astype(BF16)
            return carry

        lax.fori_loop(0, block // 16, body, 0)

    view = pl.BlockSpec((block, 1, width), lambda i: (i, 0, 0))
    flat = pl.BlockSpec((block, width), lambda i: (i, 0))
    shape = jax.ShapeDtypeStruct((sz.master, 1, width), F32)
    return pl.pallas_call(
        kernel,
        grid=(sz.master_pad // block,),
        out_shape=[shape, shape, shape, jax.ShapeDtypeStruct((sz.master, width), BF16)],
        in_specs=[pl.BlockSpec(memory_space=pltpu.SMEM), flat, view, view, view],
        out_specs=[view, view, view, flat],
        compiler_params=pltpu.CompilerParams(vmem_limit_bytes=VMEM_LIMIT),
        name="adam_in",
    )(clip, grad, weight, moment, second)


def adam_plain(clip, grad, weight, moment, second, transposed):
    rows, width = weight.shape
    block = min(256 if transposed else 64, rows)

    def kernel(clip_ref, g_ref, w_ref, m_ref, v_ref, wn_ref, mn_ref, vn_ref, low_ref):
        if transposed:
            row = lax.broadcasted_iota(jnp.int32, (width, width), 0)
            col = lax.broadcasted_iota(jnp.int32, (width, width), 1)
            grad_value = tn(g_ref[...], (row == col).astype(BF16))
        else:
            grad_value = g_ref[...]
        new = adam_update(
            w_ref[...], m_ref[...], v_ref[...], clip_ref[0] * grad_value, LEARN_MATRIX, WEIGHT_DECAY
        )
        wn_ref[...], mn_ref[...], vn_ref[...] = new
        low_ref[...] = new[0].astype(BF16)

    flat = pl.BlockSpec((block, width), lambda i: (i, 0))
    turned = pl.BlockSpec((width, block), lambda i: (0, i))
    shape = jax.ShapeDtypeStruct((rows, width), F32)
    return pl.pallas_call(
        kernel,
        grid=(rows // block,),
        out_shape=[shape, shape, shape, jax.ShapeDtypeStruct((rows, width), BF16)],
        in_specs=[
            pl.BlockSpec(memory_space=pltpu.SMEM), turned if transposed else flat, flat, flat, flat
        ],
        out_specs=[flat] * 4,
        compiler_params=pltpu.CompilerParams(vmem_limit_bytes=VMEM_LIMIT),
        name="adam_plain",
    )(clip, grad, weight, moment, second)


def columns_first(array):
    return jnp.transpose(array, (2, 0, 1))


def shards(
    inputs,
    cotangent,
    valid_lengths,
    proj_in,
    proj_in_m,
    proj_in_v,
    proj_state,
    proj_state_m,
    proj_state_v,
    proj_out,
    proj_out_m,
    proj_out_v,
    head_params,
    head_m,
    head_v,
    shared_params,
    shared_m,
    shared_v,
):
    section = lax.axis_index("section")
    head_idx = lax.axis_index("head")
    count = lax.axis_size("head")
    rows, width = inputs.shape[1], inputs.shape[2]
    heads = head_params.shape[1]
    tokens = rows * count
    sz = Sizes(heads, tokens, width)
    order = sz.order()
    start_block, seq_length, resets = seq_layout(
        lax.dynamic_index_in_dim(valid_lengths, section, 0, keepdims=False)
    )
    token = head_idx * rows + lax.broadcasted_iota(jnp.int32, (rows, LANES), 0)
    live = jnp.zeros((rows, LANES), F32)
    for block in range(sz.blocks):
        inside = (token // STRETCH == block) & (token - start_block[block] * STRETCH < seq_length[block])
        live = jnp.where(inside, 1.0, live)
    first = lax.dynamic_index_in_dim(inputs, section, 0, keepdims=False)
    cot = lax.dynamic_index_in_dim(cotangent, section, 0, keepdims=False)
    weights, weight_out, pack, rows_zero = opening(
        count, sz, columns_first(proj_in), proj_state[0], proj_out[0], head_params[0], shared_params, order, first, 0
    )

    def run_forward(layer, gathered, residual, cotangent, collective_id):
        return forward_phase(
            count, sz, layer, resets, gathered, weights, weight_out, pack, residual, live, cotangent, collective_id
        )

    def run_backward(layer, out_grads, kept, stats, residual, upstream, below, upper, collective_id):
        proj, mixed, states = kept[4:7]
        return backward_phase(
            count, sz, layer, resets, out_grads, proj, mixed, states, stats, weights, weight_out, pack, order,
            residual, upstream, live, below, upper, collective_id,
        )

    kept_zero = run_forward(0, rows_zero, first, None, 1)
    result_zero, branch_zero, total_zero, rows_one = kept_zero[:4]
    kept_one = run_forward(1, rows_one, result_zero, cot, 2)
    result_one, out_grads_one, stats_one = kept_one[0], kept_one[3], kept_one[7]
    back_one = run_backward(
        1, out_grads_one, kept_one, stats_one, result_zero, cot, (branch_zero, total_zero), None, 3
    )
    grad_one, low_one, acc_one, grads_t_one, scaled_one, out_grads_zero, stats_zero = back_one
    upper = (
        grads_t_one, scaled_one, rows_one, out_grads_one, rows_zero, acc_one, result_zero, result_one, grad_one
    )
    if tokens * width <= 4 << 20:
        grad_in, grad_out, state_part, small, layer_outs, grad_buffer, squares = run_backward(
            0, out_grads_zero, kept_zero, stats_zero, first, low_one, None, upper, 4
        )
    else:
        grad_zero, _, acc_zero, grads_t_zero, scaled_zero = run_backward(
            0, out_grads_zero, kept_zero, stats_zero, first, low_one, None, None, 4
        )
        lower = weight_grads(sz, grads_t_zero, rows_zero, scaled_zero, out_grads_zero)
        higher = weight_grads(sz, grads_t_one, rows_one, scaled_one, out_grads_one)
        grad_in, grad_out, state_sum, small, layer_outs, grad_buffer, squares = trade_sections(
            [(lower[0], higher[0]), (lower[2], higher[2]), (lower[1], higher[1]), (acc_zero, acc_one)],
            [(result_zero, result_one), (grad_zero, grad_one)],
            2,
            6,
        )
        state_part = state_sum.astype(BF16)

    state_all, all_stats, norms = finish_sums(
        count, sz, state_part.reshape(16 * count, -1), small, squares, pack, sz.head_sum(), 5
    )
    grad_state = state_all.reshape(state_part.shape)
    pieces = width // LANES
    shared_rows = all_stats[:pieces].transpose(1, 0, 2).reshape(8, width)
    grad_shared = jnp.concatenate(
        [shared_rows[1 : CONV + 2, : 2 * NSTATE].reshape(-1), shared_rows[0]]
    )
    grad_norm, clip_scale = norms[0, 0], norms[1, 0]
    clip = norms[1, :1]
    chans = heads * HDIM
    head_part = head_params[0]
    taps = small[:CONV, :chans].reshape(CONV, heads, HDIM).transpose(1, 0, 2).reshape(heads, -1)
    grad_head = jnp.concatenate(
        [
            taps,
            small[5, :chans].reshape(heads, HDIM),
            small[CONV, :chans].reshape(heads, HDIM),
            small[7, :heads][:, None],
            (small[8, :heads] * -jnp.exp(head_part[:, -2]))[:, None],
            jnp.sum(small[6, :chans].reshape(heads, HDIM), axis=1)[:, None],
        ],
        axis=1,
    )
    new_in = adam_in(
        sz, clip, grad_in, columns_first(proj_in), columns_first(proj_in_m), columns_first(proj_in_v)
    )
    new_out = adam_plain(
        clip, grad_out, proj_out[0], proj_out_m[0], proj_out_v[0], False
    )
    new_state = adam_plain(
        clip, grad_state, proj_state[0], proj_state_m[0], proj_state_v[0], True
    )
    new_head = adam_update(
        head_part, head_m[0], head_v[0], clip_scale * grad_head, LEARN_VECTOR, 0.0
    )
    new_shared = adam_update(
        shared_params[0], shared_m[0], shared_v[0], clip_scale * grad_shared, LEARN_VECTOR, 0.0
    )
    back_view = [jnp.transpose(array, (1, 2, 0)) for array in new_in[:3]]
    return (
        layer_outs[None],
        grad_buffer[None],
        grad_norm,
        back_view[0],
        back_view[1],
        back_view[2],
        new_in[3].T[None],
        new_state[0][None],
        new_state[1][None],
        new_state[2][None],
        new_state[3][None],
        new_out[0][None],
        new_out[1][None],
        new_out[2][None],
        new_out[3][None],
        new_head[0][None],
        new_head[1][None],
        new_head[2][None],
        new_shared[0][None],
        new_shared[1][None],
        new_shared[2][None],
    )


def solution(mesh):
    in_specs = (
        P(None, "head", None),
        P(None, "head", None),
        P(),
        P("section", None, "head"),
        P("section", None, "head"),
        P("section", None, "head"),
        P("section", None, None),
        P("section", None, None),
        P("section", None, None),
        P("section", "head", None),
        P("section", "head", None),
        P("section", "head", None),
        P("section", "head", None),
        P("section", "head", None),
        P("section", "head", None),
        P("section", None),
        P("section", None),
        P("section", None),
    )
    out_specs = (
        P("section", None, "head", None),
        P("section", None, "head", None),
        P(),
        P("section", None, "head"),
        P("section", None, "head"),
        P("section", None, "head"),
        P("section", None, "head"),
        P("section", None, None),
        P("section", None, None),
        P("section", None, None),
        P("section", None, None),
        P("section", "head", None),
        P("section", "head", None),
        P("section", "head", None),
        P("section", "head", None),
        P("section", "head", None),
        P("section", "head", None),
        P("section", "head", None),
        P("section", None),
        P("section", None),
        P("section", None),
    )
    return jax.shard_map(shards, mesh=mesh, in_specs=in_specs, out_specs=out_specs, check_vma=False)
```

```python
import itertools

import jax
import jax.numpy as jnp
import numpy as np
from jax import lax
from jax.experimental import pallas as pl
from jax.experimental.pallas import tpu as pltpu
from jax.sharding import PartitionSpec as P

HEADS = 64
HDIM = 64
NSTATE = 128
CONV = 4
STRETCH = 256
ADAM_STEP = 5
PARAMS = 51698560

HIGH = lax.Precision.HIGHEST
EPS_NORM = 1e-05
ADAM_EPS = 1e-08
BETA_ONE = 0.5
BETA_TWO = 0.5
CLIP_COEF = 0.2
LEARN_MATRIX = 0.02
LEARN_VECTOR = 0.2
WEIGHT_DECAY = 0.1

F32 = jnp.float32
BF16 = jnp.bfloat16
MESH = pl.DeviceIdType.MESH
LANES = 128
CHUNK = 128
COLS = HDIM * 2 + 1
GAIN_ROW = 9
VMEM_LIMIT = 58 << 20


def keeps(lengths_ref, micro, block):
    return jnp.where(lengths_ref[micro, block] > 0, 0.0, 1.0)


def live_rows_of(lengths_ref, micro, shard, rows):
    token = shard * rows
    own_block = token // STRETCH
    start, length = jnp.int32(0), lengths_ref[micro, 0]
    for block in range(1, lengths_ref.shape[1]):
        here = lengths_ref[micro, block]
        begins = (here > 0) & (block <= own_block)
        start = jnp.where(begins, block, start)
        length = jnp.where(begins, here, length)
    position = token - start * STRETCH + lax.broadcasted_iota(jnp.int32, (rows, 1), 0)
    return (position < length).astype(F32)


def chip_dims(count):
    side = 4 if count % 64 == 0 else 2
    if count % (side * side) != 0:
        return (count, 1, 1)
    return (count // (side * side), side, side)


def place(dims):
    me = lax.axis_index("head")
    return (me // (dims[1] * dims[2]), (me // dims[2]) % dims[1], me % dims[2])


class Heads:
    def __init__(self, count):
        self.count = count
        self.dims = chip_dims(count)
        self.lined = False

    def spot(self):
        return place(self.dims)

    def device(self, index):
        return {"head": index}


class Team:
    def __init__(self, count):
        self.count = count
        self.chips = chip_dims(count)
        self.paired = self.chips[2] == 2
        self.lined = True
        self.dims = self.chips[:2] + (2,) if self.paired else self.chips

    def spot(self):
        spot = place(self.chips)
        return spot[:2] + (lax.axis_index("section"),) if self.paired else spot

    def device(self, index):
        if not self.paired:
            return {"head": index}
        return {"section": index % 2, "head": index // 2 * 2 + lax.axis_index("head") % 2}

    def micro(self):
        return lax.axis_index("head") % 2 if self.paired else lax.axis_index("section")

    def owner(self, layer):
        if not self.paired:
            return {"section": layer}
        return {"section": layer, "head": lax.axis_index("head") // 2 * 2 + lax.axis_index("section")}

    def user(self, micro):
        if not self.paired:
            return {"section": micro}
        head = lax.axis_index("head")
        return {"section": head % 2, "head": head // 2 * 2 + micro}

    def alone(self, which):
        section = lax.axis_index("section")
        if not self.paired:
            return section == which
        return (lax.axis_index("head") % 2 == section) & (section == which)


def linear(dims, spot):
    return (spot[0] * dims[1] + spot[1]) * dims[2] + spot[2]


def moved(dims, spot, shifts):
    return tuple(s if d == 0 else (s + d) % n for s, d, n in zip(spot, shifts, dims))


def shift_of(order, offsets):
    out = [0, 0, 0]
    for axis, off in zip(order, offsets):
        out[axis] = off
    return out


def greet_all(count, pair=False):
    barrier = pltpu.get_barrier_semaphore()
    me = lax.axis_index("head")
    section = lax.axis_index("section")
    for off in range(1, count):
        peer = (me + off) % count
        pl.semaphore_signal(barrier, inc=1, device_id={"head": peer}, device_id_type=MESH)
        if pair:
            there = {"section": 1 - section, "head": peer}
            pl.semaphore_signal(barrier, inc=1, device_id=there, device_id_type=MESH)
    if pair:
        pl.semaphore_signal(barrier, inc=1, device_id={"section": 1 - section}, device_id_type=MESH)
    pl.semaphore_wait(barrier, 2 * count - 1 if pair else count - 1)


def rows_at(shard, rows):
    return pl.ds(pl.multiple_of(shard * rows, rows), rows)


def column_parts(width, shares):
    tiles = width // LANES
    parts, start, taken = [], 0, 0
    for share, order, group in shares:
        taken += share
        stop = tiles * taken // 16 * LANES
        if stop > start:
            parts.append((start, stop - start, order, group))
            start = stop
    return parts


TEAM_GATHER = ((3, (1, 0, 2), 0), (7, (0, 1, 2), 0), (6, (0, 1, 2), 0))
GATHER = ((2, (2, 1, 0), 0), (2, (1, 2, 0), 0), (6, (0, 2, 1), 0), (6, (0, 1, 2), 0))
GATHER_SMALL = ((8, (0, 2, 1), 0), (8, (0, 1, 2), 0))
SCATTER = (
    (1, (2, 0, 1), 0), (1, (1, 0, 2), 0), (1, (0, 1, 2), 0), (1, (0, 2, 1), 0),
    (3, (2, 1, 0), 0), (3, (1, 2, 0), 0), (3, (2, 1, 0), 1), (3, (1, 2, 0), 1),
)
TEAM_SCATTER_SMALL = ((16, (2, 1, 0), 0),)
SCATTER_SMALL = ((8, (2, 1, 0), 0), (8, (1, 2, 0), 0))
SCATTER_PACE = (0.3, 0.9, 0.7, 2.0)


def guarded(preds, action):
    preds = [pred for pred in preds if pred is not None]
    if not preds:
        action()
        return
    cond = preds[0]()
    for pred in preds[1:]:
        cond = jnp.logical_and(cond, pred())
    pl.when(cond)(action)


def gather_steps(group, parts, rows, own_ref, all_ref, send_sem, recv_sem, between=()):
    dims = group.dims
    spot = group.spot()
    me = linear(dims, spot)
    waits = []
    counter = [0] * len(parts)

    def lined(axis):
        return group.lined and axis == 0 and dims[0] > 2 and dims[1] == 2

    def above(axis, dist):
        return lambda: spot[axis] + dist < dims[axis]

    def below(axis, dist):
        return lambda: spot[axis] >= dist

    def sources(part, pos):
        axis = parts[part][2][pos]
        if not lined(axis):
            return [(off, None) for off in range(1, dims[axis])]
        out = []
        for dist in range(1, dims[axis]):
            out.append((dist, above(axis, dist)))
            out.append((-dist, below(axis, dist)))
        return out

    def block(part, offsets):
        start, width, order, _ = parts[part]
        shard = linear(dims, moved(dims, spot, shift_of(order, offsets)))
        return shard, all_ref.at[rows_at(shard, rows), pl.ds(start, width)]

    def push(part, offsets, pos, preds, src, came):
        axis = parts[part][2][pos]
        shard, dst = block(part, offsets)
        up, down = (1, above(axis, 1)), (-1, below(axis, 1))
        if lined(axis):
            targets = [up, down] if came == 0 else [down] if came > 0 else [up]
        else:
            targets = [(off, None) for off in range(1, dims[axis])] if came == 0 else []
        for off, pred in targets:
            peer = linear(dims, moved(dims, spot, shift_of((axis,), (off,))))
            number = counter[part]
            counter[part] += 1

            def begin(peer=peer, number=number):
                pltpu.make_async_remote_copy(
                    src_ref=dst if src is None else src,
                    dst_ref=dst,
                    send_sem=send_sem.at[part, number],
                    recv_sem=recv_sem.at[part, shard],
                    device_id=group.device(peer),
                    device_id_type=MESH,
                ).start()

            guarded([pred], begin)
            waits.append((preds + [pred], part, number))

    def visit(part, offsets, preds, pos, came):
        def body():
            shard, dst = block(part, offsets)
            pltpu.make_async_remote_copy(
                src_ref=dst,
                dst_ref=dst,
                send_sem=send_sem.at[part, 0],
                recv_sem=recv_sem.at[part, shard],
                device_id=group.device(me),
                device_id_type=MESH,
            ).wait_recv()
            push(part, offsets, pos, preds, None, came)
            for later in range(pos + 1, 3):
                push(part, offsets, later, preds, None, 0)

        guarded(preds, body)

    for pos in range(3):
        for part, (start, width, _, _) in enumerate(parts):
            push(part, (0, 0, 0), pos, [], own_ref.at[:, pl.ds(start, width)], 0)
    todo = []
    for part in range(len(parts)):
        first, second, third = (sources(part, pos) for pos in range(3))
        for k, (oa, pa) in enumerate(first):
            todo.append(((0, k, part), part, (oa, 0, 0), [pa], 0, oa))
        for ka, (oa, pa) in enumerate([(0, None)] + first):
            for k, (ob, pb) in enumerate(second):
                todo.append(((1, ka + k, part), part, (oa, ob, 0), [pa, pb], 1, ob))
            for kb, (ob, pb) in enumerate([(0, None)] + second):
                for k, (oc, pc) in enumerate(third):
                    todo.append(
                        ((2, ka + kb + k, part), part, (oa, ob, oc), [pa, pb, pc], 2, oc)
                    )
    todo.sort(key=lambda entry: (sum(abs(off) for off in entry[2]), entry[0]))
    between = list(between)
    for _, part, offsets, preds, pos, came in todo:
        if between:
            between.pop(0)()
        visit(part, offsets, preds, pos, came)
    for work in between:
        work()
    for preds, part, number in waits:

        def settle(part=part, number=number):
            start, width, _, _ = parts[part]
            ref = own_ref.at[:, pl.ds(start, width)]
            pltpu.make_async_remote_copy(
                src_ref=ref,
                dst_ref=ref,
                send_sem=send_sem.at[part, number],
                recv_sem=recv_sem.at[part, 0],
                device_id=group.device(me),
                device_id_type=MESH,
            ).wait_send()

        guarded(preds, settle)


def gather_sends(dims):
    return 3 * dims[0] * dims[1] * dims[2]


def scatter_steps(group, parts, rows, in_ref, out_ref, box_ref, send_sem, recv_sem, staged=False):
    dims = group.dims
    spot = group.spot()
    me = linear(dims, spot)
    sends = []

    def size(part, pos):
        return dims[parts[part][2][pos]]

    def slot_one(part, ea, ob, oc):
        return ((ea - 1) * size(part, 1) + ob) * size(part, 2) + oc

    def slot_two(part, eb, oc):
        base = (size(part, 0) - 1) * size(part, 1) * size(part, 2)
        return base + (eb - 1) * size(part, 2) + oc

    def slot_three(part, ec):
        return slot_two(part, size(part, 1), 0) + ec - 1

    def cols(part):
        return pl.ds(parts[part][0], parts[part][1])

    def mine(part, offsets):
        shard = linear(dims, moved(dims, spot, shift_of(parts[part][2], offsets)))
        return in_ref.at[rows_at(shard, rows), cols(part)]

    def send(part, src, pos, off, slot):
        peer = linear(dims, moved(dims, spot, shift_of((parts[part][2][pos],), (off,))))
        copy = pltpu.make_async_remote_copy(
            src_ref=src,
            dst_ref=box_ref.at[slot, :, cols(part)],
            send_sem=send_sem.at[part, slot],
            recv_sem=recv_sem.at[part, slot],
            device_id=group.device(peer),
            device_id_type=MESH,
        )
        copy.start()
        sends.append(copy)

    def arrived(part, slot):
        ref = box_ref.at[slot, :, cols(part)]
        pltpu.make_async_remote_copy(
            src_ref=ref,
            dst_ref=ref,
            send_sem=send_sem.at[part, slot],
            recv_sem=recv_sem.at[part, slot],
            device_id=group.device(me),
            device_id_type=MESH,
        ).wait_recv()
        return ref[...].astype(F32)

    def combined(part, ob, oc, stages):
        total = mine(part, (0, ob, oc))[...].astype(F32)
        for ea in range(1, size(part, 0)):
            total = total + arrived(part, slot_one(part, ea, ob, oc))
        for eb in range(1, size(part, 1)) if stages > 1 else ():
            total = total + arrived(part, slot_two(part, eb, oc))
        for ec in range(1, size(part, 2)) if stages > 2 else ():
            total = total + arrived(part, slot_three(part, ec))
        return total

    def put_by(part, ob, oc, total):
        if size(part, 0) > 1:
            hold = box_ref.at[slot_one(part, 1, ob, oc), :, cols(part)]
        elif size(part, 1) > 1 and ob == 0:
            hold = box_ref.at[slot_two(part, 1, oc), :, cols(part)]
        else:
            return mine(part, (0, ob, oc))
        hold[...] = total.astype(box_ref.dtype)
        return hold

    def first(part, ob, oc, off):
        slot = slot_one(part, size(part, 0) - off, ob, oc)
        send(part, mine(part, (off, ob, oc)), 0, off, slot)

    def second(part, ob, oc, _):
        hold = put_by(part, ob, oc, combined(part, ob, oc, 1))
        send(part, hold, 1, ob, slot_two(part, size(part, 1) - ob, oc))

    def third(part, _, oc, __):
        hold = put_by(part, 0, oc, combined(part, 0, oc, 2))
        send(part, hold, 2, oc, slot_three(part, size(part, 2) - oc))

    def last(part, _, __, ___):
        out_ref[:, cols(part)] = combined(part, 0, 0, 3)

    lag, rest, turn, end = SCATTER_PACE
    program = []
    for part, (_, _, _, late) in enumerate(parts):
        for ob, oc in itertools.product(range(size(part, 1)), range(size(part, 2))):
            for off in range(1, size(part, 0)):
                rank = (0.0 if ob else rest) + late * lag
                program.append((rank, oc == 0, off, part, first, ob, oc))
            if ob:
                program.append((turn + late * lag, oc == 0, 0, part, second, ob, oc))
        for oc in range(1, size(part, 2)):
            program.append((end + late * lag, False, 0, part, third, 0, oc))
        program.append((3.0 + late * lag, True, 0, part, last, 0, 0))
    program.sort(key=lambda step: step[:4])

    def run(low, high):
        for rank, _, off, part, action, ob, oc in program:
            if low <= rank < high:
                action(part, ob, oc, off)

    if staged:
        marks = (-1.0, turn, end, 3.0, 9.0)
        return sends, [lambda k=k: run(marks[k], marks[k + 1]) for k in range(4)]
    run(-1.0, 99.0)
    return sends


PIECES = 1


class PlaneScatter:
    def __init__(self, group, rows, width):
        self.group, self.dims, self.rows = group, group.dims, rows
        self.wide = group.paired
        self.orders = ((2, 1),) * PIECES if self.wide else ((2, 1), (1, 2))
        self.half = width // len(self.orders)
        self.width = width
        depth = self.dims[0]
        most = max(self.dims[1], self.dims[2])
        self.one = depth * (most - 1) * most
        self.two = depth * (most - 1)
        self.slots = self.one + self.two + 2 * depth
        self.first_type = F32 if self.wide else BF16

    def scratch(self):
        parts = len(self.orders)
        later = self.two + 2 * self.dims[0]
        return [
            pltpu.VMEM((self.one, self.rows, self.width), self.first_type),
            pltpu.VMEM((later, self.rows, self.width), BF16),
            pltpu.VMEM((self.two + self.dims[0] if self.wide else 1, self.rows, self.width), BF16),
            DMA((parts, self.slots)),
            DMA((parts, self.slots)),
        ]

    def bind(self, part_ref, out_ref, first_ref, later_ref, hold_ref, send_sem, recv_sem):
        self.part_ref, self.out_ref = part_ref, out_ref
        self.first_ref, self.later_ref, self.hold_ref = first_ref, later_ref, hold_ref
        self.send_sem, self.recv_sem = send_sem, recv_sem
        self.spot = self.group.spot()
        self.me = linear(self.dims, self.spot)

    def sizes(self, part):
        a, b = self.orders[part]
        return self.dims[a], self.dims[b]

    def slot_one(self, part, plane, ea, ob):
        size_a, size_b = self.sizes(part)
        return (plane * (size_a - 1) + ea - 1) * size_b + ob

    def slot_two(self, part, plane, eb):
        return self.one + plane * (self.sizes(part)[1] - 1) + eb - 1

    def slot_three(self, plane, below):
        return self.one + self.two + 2 * plane + below

    def cols(self, part):
        return pl.ds(part * self.half, self.half)

    def mine(self, part, plane, oa, ob):
        shift = shift_of(self.orders[part], (oa, ob))
        spot = moved(self.dims, (plane, self.spot[1], self.spot[2]), shift)
        return self.part_ref.at[rows_at(linear(self.dims, spot), self.rows), self.cols(part)]

    def box(self, part, slot, begun):
        if begun:
            return self.first_ref.at[slot, :, self.cols(part)]
        return self.later_ref.at[slot - self.one, :, self.cols(part)]

    def copy(self, part, src, slot, sent, peer, begun=False):
        return remote(
            src,
            self.box(part, slot, begun),
            self.send_sem.at[part, sent],
            self.recv_sem.at[part, slot],
            self.group.device(peer),
        )

    def hold(self, part, plane, oa, ob, slot):
        if self.wide:
            return self.hold_ref.at[slot - self.one, :, self.cols(part)]
        return self.mine(part, plane, oa, ob)

    def peer(self, part, pos, off):
        shift = shift_of((self.orders[part][pos],), (off,))
        return linear(self.dims, moved(self.dims, self.spot, shift))

    def arrived(self, part, slot, begun=False):
        ref = self.box(part, slot, begun)
        self.copy(part, ref, slot, slot, self.me, begun).wait_recv()
        return ref[...].astype(F32)

    def first(self, plane):
        for inner in (1, 0):
            for part in range(len(self.orders)):
                size_a, size_b = self.sizes(part)
                for ob in range(size_b):
                    if (ob != 0) != bool(inner):
                        continue
                    for off in range(1, size_a):
                        slot = self.slot_one(part, plane, size_a - off, ob)
                        src = self.mine(part, plane, off, ob)
                        self.copy(part, src, slot, slot, self.peer(part, 0, off), True).start()

    def second(self, plane):
        for part in range(len(self.orders)):
            size_a, size_b = self.sizes(part)
            for ob in range(1, size_b):
                slot = self.slot_two(part, plane, size_b - ob)
                total = self.mine(part, plane, 0, ob)[...].astype(F32)
                for ea in range(1, size_a):
                    total = total + self.arrived(part, self.slot_one(part, plane, ea, ob), True)
                hold = self.hold(part, plane, 0, ob, slot)
                hold[...] = total.astype(BF16)
                self.copy(part, hold, slot, slot, self.peer(part, 1, ob)).start()

    def third(self, plane, place_in_line):
        depth = self.spot[0]
        above = depth > plane
        place_here = jnp.where(above, self.dims[0] - 1 - depth, depth)

        def own_total(part):
            size_a, size_b = self.sizes(part)
            total = self.mine(part, plane, 0, 0)[...].astype(F32)
            for ea in range(1, size_a):
                total = total + self.arrived(part, self.slot_one(part, plane, ea, 0), True)
            for eb in range(1, size_b):
                total = total + self.arrived(part, self.slot_two(part, plane, eb))
            return total

        if place_in_line == 0:

            @pl.when(plane == depth)
            def _():
                for part in range(len(self.orders)):
                    self.out_ref[:, self.cols(part)] = own_total(part)

        @pl.when((plane != depth) & (place_here == place_in_line))
        def _():
            below = jnp.where(above, 0, 1)
            onward = jnp.where(above, depth - 1, depth + 1)
            peer = linear(self.dims, (onward, self.spot[1], self.spot[2]))
            slot = self.slot_three(plane, below)
            for part in range(len(self.orders)):
                total = own_total(part)
                if place_in_line > 0:
                    total = total + self.arrived(part, slot)
                hold = self.hold(part, plane, 0, 0, self.one + self.two + plane)
                hold[...] = total.astype(BF16)
                self.copy(part, hold, slot, slot, peer).start()

    def last(self):
        depth = self.spot[0]
        for below, there in ((0, depth < self.dims[0] - 1), (1, depth > 0)):

            @pl.when(there)
            def _(below=below):
                for part in range(len(self.orders)):
                    total = self.out_ref[:, self.cols(part)]
                    total = total + self.arrived(part, self.slot_three(depth, below))
                    self.out_ref[:, self.cols(part)] = total

    def step(self, number, made, plane_of):
        actions = [self.first, self.second]
        actions += [lambda plane, k=k: self.third(plane, k) for k in range(max(self.dims[0] - 1, 1))]
        for back, action in enumerate(actions):
            k = made - 1 - back
            if isinstance(made, int):
                if 0 <= k < number:
                    action(plane_of(k))
            else:
                pl.when(k >= 0)(lambda k=k, action=action: action(plane_of(k)))

    def extra_steps(self):
        return 1 + max(self.dims[0] - 1, 1)

    def finish(self, number, plane_of, begun=0):
        for extra in range(1 + begun, self.extra_steps() + 1):
            self.step(number, number + extra, plane_of)
        self.last()

    def drain(self):
        for part in range(len(self.orders)):
            size_a, size_b = self.sizes(part)
            early, late = self.box(part, 0, True), self.box(part, self.one, False)
            for plane in range(self.dims[0]):
                for ea in range(1, size_a):
                    for ob in range(size_b):
                        slot = self.slot_one(part, plane, ea, ob)
                        self.copy(part, early, slot, slot, self.me, True).wait_send()
                for eb in range(1, size_b):
                    slot = self.slot_two(part, plane, eb)
                    self.copy(part, late, slot, slot, self.me).wait_send()
            for off in range(1, self.dims[0]):
                plane = (self.spot[0] + off) % self.dims[0]
                slot = self.slot_three(plane, jnp.where(self.spot[0] > plane, 0, 1))
                self.copy(part, late, slot, slot, self.me).wait_send()


def start_direct(group, own_ref_of, box_ref, send_sem, recv_sem):
    count = group.count
    me = linear(group.dims, group.spot())
    copies = []
    for off in range(1, count):
        peer = (me + off) % count
        copy = pltpu.make_async_remote_copy(
            src_ref=own_ref_of(peer),
            dst_ref=box_ref.at[me],
            send_sem=send_sem.at[off],
            recv_sem=recv_sem.at[count - off],
            device_id=group.device(peer),
            device_id_type=MESH,
        )
        copy.start()
        copies.append(copy)
    return copies


def wait_direct(group, box_ref, copies, recv_sem, send_sem):
    count = group.count
    me = linear(group.dims, group.spot())
    for off in range(1, count):
        ref = box_ref.at[(me + off) % count]
        pltpu.make_async_remote_copy(
            src_ref=ref,
            dst_ref=ref,
            send_sem=send_sem.at[off],
            recv_sem=recv_sem.at[off],
            device_id=group.device(me),
            device_id_type=MESH,
        ).wait_recv()
    for copy in copies:
        copy.wait_send()


def remote(src, dst, send_sem, recv_sem, device):
    return pltpu.make_async_remote_copy(
        src_ref=src, dst_ref=dst, send_sem=send_sem, recv_sem=recv_sem, device_id=device, device_id_type=MESH
    )


class Delivery:
    def __init__(self, src, dst, send_sem, recv_sem, device, alone):
        self.alone = alone
        self.ends = src, dst, send_sem, recv_sem, device

    def near(self):
        return pltpu.make_async_copy(*self.ends[:3])

    def far(self):
        return remote(*self.ends)

    def start(self):
        pl.when(self.alone)(lambda: self.near().start())
        pl.when(jnp.logical_not(self.alone))(lambda: self.far().start())

    def wait_sent(self):
        pl.when(self.alone)(lambda: self.near().wait())
        pl.when(jnp.logical_not(self.alone))(lambda: self.far().wait_send())

    def wait_got(self):
        pl.when(jnp.logical_not(self.alone))(lambda: self.far().wait_recv())


VMEM_SPEC = pl.BlockSpec(memory_space=pltpu.VMEM)
ANY_SPEC = pl.BlockSpec(memory_space=pl.ANY)
DMA = pltpu.SemaphoreType.DMA


def params(collective_id):
    return pltpu.CompilerParams(
        collective_id=collective_id, has_side_effects=True, vmem_limit_bytes=VMEM_LIMIT
    )


def gather_scratch(parts, dims, count):
    return [DMA((len(parts), gather_sends(dims))), DMA((len(parts), count)), DMA]


def run_gather(group, parts, own_ref, all_ref, sems, stat=None, between=()):
    rows = own_ref.shape[0]
    me = linear(group.dims, group.spot())
    send_sem, recv_sem, local_sem = sems
    local = pltpu.make_async_copy(own_ref, all_ref.at[rows_at(me, rows)], local_sem)
    local.start()
    if stat is not None:
        stat_ref, box_ref, small_send, small_recv = stat
        copies = start_direct(group, lambda peer: stat_ref, box_ref, small_send, small_recv)
        box_ref[me] = stat_ref[...]
    gather_steps(group, parts, rows, own_ref, all_ref, send_sem, recv_sem, between)
    if stat is not None:
        wait_direct(group, box_ref, copies, small_recv, small_send)
    local.wait()


def scatter_scratch(parts, count, rows, width):
    slots = max(count - 1, 1)
    return [pltpu.VMEM((slots, rows, width), BF16), DMA((len(parts), slots)), DMA((len(parts), slots))]


def finish_sums(count, sz, states, small, squares, rates, head_sum, collective_id):
    team, heads = Team(count), Heads(count)
    width = states[0].shape[1]
    rows = states[0].shape[0] // count
    layers = len(states)
    back = column_parts(width, TEAM_SCATTER_SMALL if layers > 1 else SCATTER_SMALL)
    parts = column_parts(width, GATHER_SMALL)
    chans, state = sz.channels, 2 * NSTATE
    pieces = sz.width // LANES
    threshold = CLIP_COEF * PARAMS**0.5

    def kernel(*refs):
        refs = list(refs)
        take = lambda number: [refs.pop(0) for _ in range(number)]
        in_refs = take(layers)
        small_ref, squares_ref, rates_ref, sum_ref = take(4)
        all_ref, stats_ref, norm_ref = take(3)
        share_ref, sums_ref, out_ref, own_ref, stat_ref, mine_ref, got_ref = take(7)
        scatter_refs, ag_sems = take(3), take(3)
        if layers > 1:
            both_ref, pieces_ref, piece_send, piece_recv = take(4)
        small_send, small_recv, stat_send, stat_recv, pair_send, pair_recv = take(6)
        me = lax.axis_index("head")
        section = lax.axis_index("section")
        share_ref[...] = jnp.zeros_like(share_ref)
        share_ref[0:1, :] = small_ref[GAIN_ROW : GAIN_ROW + 1, :]
        share_ref[1 : CONV + 2, :state] = small_ref[: CONV + 1, chans : chans + state]

        def piece(peer):
            return share_ref.at[:, pl.ds(pl.multiple_of((peer % pieces) * LANES, LANES), LANES)]

        greet_all(count, True)
        copies = start_direct(heads, piece, sums_ref, small_send, small_recv)
        sums_ref[me] = piece(me)[...]
        if layers > 1:
            for k in range(count):
                for layer in range(layers):
                    to = slice((k * layers + layer) * rows, (k * layers + layer + 1) * rows)
                    both_ref[to, :] = in_refs[layer][k * rows : (k + 1) * rows, :]
            sends = scatter_steps(team, back, rows * layers, both_ref, out_ref, *scatter_refs)
            micro = team.micro()
            passed = [
                Delivery(
                    out_ref.at[pl.ds(layer * rows, rows), :], pieces_ref.at[micro],
                    piece_send.at[layer], piece_recv.at[micro], team.owner(layer), team.alone(layer),
                )
                for layer in range(layers)
            ]
            for copy in passed:
                copy.start()
            for copy in passed:
                copy.wait_sent()
            for m in range(2):
                ref = pieces_ref.at[m]
                Delivery(ref, ref, piece_send.at[0], piece_recv.at[m], team.user(m), team.alone(m)).wait_got()
            state_own = pieces_ref[0] + pieces_ref[1]
        else:
            sends = scatter_steps(heads, back, rows, in_refs[0], out_ref, *scatter_refs)
            state_own = out_ref[...]
        wait_direct(heads, sums_ref, copies, small_recv, small_send)
        shared = jnp.sum(sums_ref[...], axis=0)
        shared_sq = jnp.where(me < pieces, jnp.sum(shared * shared), 0.0)
        own_ref[...] = state_own.astype(BF16)
        taps = small_ref[: CONV + 2, :chans]
        skip = nn(small_ref[6:7, :chans], sum_ref[...], HIGH)
        bias = small_ref[7:8, :LANES]
        rate = small_ref[8:9, :LANES] * rates_ref[...]
        lane = lax.broadcasted_iota(jnp.int32, (1, LANES), 1)
        of_heads = jnp.where(lane < sz.heads, bias * bias + rate * rate + skip * skip, 0.0)
        if chans > sz.heads * HDIM:
            taps = taps[:, : sz.heads * HDIM]
        total = jnp.sum(squares_ref[...]) + jnp.sum(taps * taps) + jnp.sum(of_heads)
        total = total + jnp.sum(state_own * state_own) + shared_sq
        row = lax.broadcasted_iota(jnp.int32, (8, LANES), 0)
        stat_ref[...] = jnp.where(row == 7, total, shared)
        run_gather(heads, parts, own_ref, all_ref, ag_sems, (stat_ref, stats_ref, stat_send, stat_recv))
        section_sq = stats_ref[0, 7:8, :]
        for k in range(1, count):
            section_sq = section_sq + stats_ref[k, 7:8, :]
        mine_ref[...] = jnp.broadcast_to(section_sq, (8, LANES))
        pair = pltpu.make_async_remote_copy(
            src_ref=mine_ref,
            dst_ref=got_ref,
            send_sem=pair_send,
            recv_sem=pair_recv,
            device_id={"section": 1 - section},
            device_id_type=MESH,
        )
        pair.start()
        pair.wait()
        norm = jnp.sqrt(mine_ref[...] + got_ref[...])
        norm_ref[...] = jnp.where(row == 0, norm, threshold / jnp.maximum(norm, threshold))
        for copy in sends:
            copy.wait_send()

    return pl.pallas_call(
        kernel,
        out_shape=[
            jax.ShapeDtypeStruct(states[0].shape, BF16),
            jax.ShapeDtypeStruct((count, 8, LANES), F32),
            jax.ShapeDtypeStruct((8, LANES), F32),
        ],
        in_specs=[VMEM_SPEC] * (4 + layers),
        out_specs=[ANY_SPEC, VMEM_SPEC, VMEM_SPEC],
        scratch_shapes=[
            pltpu.VMEM((8, sz.width), F32),
            pltpu.VMEM((count, 8, LANES), F32),
            pltpu.VMEM((rows * layers, width), F32),
            pltpu.VMEM((rows, width), BF16),
        ]
        + [pltpu.VMEM((8, LANES), F32)] * 3
        + scatter_scratch(back, count, rows * layers, width)
        + gather_scratch(parts, heads.dims, count)
        + (
            [pltpu.VMEM((count * rows * layers, width), BF16), pltpu.VMEM((2, rows, width), F32), DMA((2,)), DMA((2,))]
            if layers > 1
            else []
        )
        + [DMA((count,))] * 4
        + [DMA, DMA],
        compiler_params=params(collective_id),
        name="finish_sums",
    )(*states, small, squares, rates, head_sum)


def norm_rows(value, gain):
    mean = jnp.mean(value * value, axis=1, keepdims=True)
    return value * lax.rsqrt(mean + EPS_NORM) * gain


def norm_rows_back(value, gain, grad):
    width = value.shape[1]
    scale = lax.rsqrt(jnp.mean(value * value, axis=1, keepdims=True) + EPS_NORM)
    scaled = grad * gain
    dot = jnp.sum(scaled * value, axis=1, keepdims=True)
    back = scaled * scale - value * (scale * scale * scale * dot * (1.0 / width))
    return back, jnp.sum(grad * value * scale, axis=0, keepdims=True)


def write_pack(sz, pack_ref, head_ref, shared_ref):
    chans, state = sz.channels, 2 * NSTATE
    pack_ref[...] = jnp.zeros_like(pack_ref)
    lane = lax.broadcasted_iota(jnp.int32, (1, LANES), 1)
    bias_row = jnp.zeros((1, LANES), F32)
    rate_row = jnp.zeros((1, LANES), F32)
    rates = -jnp.exp(head_ref[:, (CONV + 2) * HDIM :])
    for head in range(sz.heads):
        cols = slice(head * HDIM, (head + 1) * HDIM)
        for tap in range(CONV):
            pack_ref[tap : tap + 1, cols] = head_ref[head : head + 1, tap * HDIM : (tap + 1) * HDIM]
        pack_ref[5:6, cols] = head_ref[head : head + 1, CONV * HDIM : (CONV + 1) * HDIM]
        pack_ref[CONV : CONV + 1, cols] = head_ref[head : head + 1, (CONV + 1) * HDIM : (CONV + 2) * HDIM]
        last = (CONV + 2) * HDIM
        pack_ref[6:7, cols] = jnp.broadcast_to(head_ref[head : head + 1, last + 2 : last + 3], (1, HDIM))
        bias_row = jnp.where(lane == head, head_ref[head : head + 1, last : last + 1], bias_row)
        rate_row = jnp.where(lane == head, rates[head : head + 1, 1:2], rate_row)
    pack_ref[7:8, :LANES] = bias_row
    pack_ref[8:9, :LANES] = rate_row
    for tap in range(CONV + 1):
        pack_ref[tap : tap + 1, chans : chans + state] = shared_ref[:, tap * state : (tap + 1) * state]
    pack_ref[GAIN_ROW : GAIN_ROW + 1, :] = shared_ref[:, (CONV + 1) * state :]


def give_weights(team, number, w_ref, wo_ref, ws_ref, wos_ref, zero_ref, sems, sz, steps, cols):
    send, recv = sems
    section = lax.axis_index("section")
    head_rows = (pl.ds(0, 2 * sz.channels), pl.ds(sz.dt, 16))
    state_rows = pl.ds(2 * sz.channels, 2 * NSTATE)

    def for_users(src, dst, k):
        return [
            Delivery(src, dst, send.at[k, micro], recv.at[k], team.user(micro), team.alone(micro))
            for micro in range(2)
        ]

    def block(step):
        span = pl.ds(step * cols, cols)
        out = []
        for k, rows in enumerate(head_rows):
            out += for_users(w_ref.at[rows, span], ws_ref.at[rows, span], 3 * step + k)
        pair = w_ref.at[state_rows, span], ws_ref.at[state_rows, span]
        k = 3 * step + 2
        for there in range(2):
            out.append(
                Delivery(*pair, send.at[k, there], recv.at[k], {"section": there}, section == there)
            )
        return out

    def matrix():
        return for_users(wo_ref, wos_ref, 3 * steps)

    def receive():
        for step in range(steps):
            span = pl.ds(step * cols, cols)
            for k, rows in enumerate(head_rows):
                got = ws_ref.at[rows, span]
                Delivery(got, got, send.at[0, 0], recv.at[3 * step + k], team.owner(number), team.alone(number)).wait_got()
            got = ws_ref.at[state_rows, span]
            Delivery(got, got, send.at[0, 0], recv.at[3 * step + 2], {"section": number}, section == number).wait_got()
        Delivery(wos_ref, wos_ref, send.at[0, 0], recv.at[3 * steps], team.owner(number), team.alone(number)).wait_got()

    def blank(sem):
        return pltpu.make_async_copy(zero_ref, ws_ref.at[pl.ds(sz.dt + 16, LANES - 16), :], sem)

    return block, matrix, receive, blank


def opening(count, sz, proj_in_t, proj_state, proj_out, head_part, shared_part, order, inputs, cotangent, collective_id):
    team = Team(count)
    rows, width = inputs.shape[1:]
    parts = column_parts(width, TEAM_GATHER if team.paired else GATHER)
    cols = 256
    steps = width // cols
    full = sz.master // 16 * 16
    own_rows = proj_out.shape[0]

    def kernel(*refs):
        refs = list(refs)
        take = lambda number: [refs.pop(0) for _ in range(number)]
        in_hbm, state_hbm, out_hbm, order_hbm, head_ref, shared_ref, x_ref, cot_ref = take(8)
        w_own, wo_own, ws_ref, wos_ref, pks_ref, rates_ref, first_ref, cot_own, all_ref = take(9)
        own_ref, in_ref, state_ref, out_ref, order_ref, low_ref, w_ref, wo_ref, zero_ref = take(9)
        ag_sems = take(3)
        load_sem, pack_send, pack_recv, swap_send, swap_recv, give_send, give_recv, local_sem = take(8)
        section = lax.axis_index("section")
        micro = team.micro()
        loads = [
            pltpu.make_async_copy(src, dst, load_sem.at[k])
            for k, (src, dst) in enumerate(
                ((order_hbm, order_ref), (in_hbm, in_ref), (state_hbm, state_ref), (out_hbm, out_ref))
            )
        ]
        for copy in loads:
            copy.start()
        write_pack(sz, own_pack_ref := refs[0], head_ref, shared_ref)
        rates_ref[...] = own_pack_ref[8:9, :LANES]
        zero_ref[...] = jnp.zeros_like(zero_ref)
        greet_all(count, True)
        packs = [
            Delivery(
                own_pack_ref, pks_ref.at[section], pack_send.at[m], pack_recv.at[section], team.user(m), team.alone(m)
            )
            for m in range(2)
        ]
        for copy in packs:
            copy.start()
        straight = micro == section
        if team.paired:
            head = lax.axis_index("head")
            partner = {"section": head % 2, "head": head // 2 * 2 + section}
            swaps = [
                remote(x_ref.at[section], first_ref, swap_send.at[0], swap_recv.at[0], partner),
                remote(cot_ref.at[section], cot_own, swap_send.at[1], swap_recv.at[1], partner),
            ]

            @pl.when(jnp.logical_not(straight))
            def _():
                for copy in swaps:
                    copy.start()

            @pl.when(straight)
            def _():
                first_ref[...] = x_ref[micro]
                cot_own[...] = cot_ref[micro]

        else:
            first_ref[...] = x_ref[micro]
            cot_own[...] = cot_ref[micro]

        block, matrix, receive, blank = give_weights(
            team, 0, w_ref, wo_ref, ws_ref, wos_ref, zero_ref, (give_send, give_recv), sz, steps, cols
        )
        keeps = [
            pltpu.make_async_copy(w_ref, w_own, local_sem.at[0]),
            pltpu.make_async_copy(wo_ref, wo_own, local_sem.at[1]),
        ]

        def lower(copies):
            @pl.when(section == 0)
            def _():
                for copy in copies():
                    copy.start()

        def low_out():
            loads[3].wait()
            if own_rows < sz.channels:
                wo_ref[...] = jnp.zeros_like(wo_ref)
            wo_ref[:own_rows, :] = out_ref[...].astype(BF16)
            keeps[1].start()
            lower(matrix)

        def low_in(step):
            if step == 0:
                for copy in loads[:3]:
                    copy.wait()
                blank(local_sem.at[2]).start()
            span = slice(step * cols, (step + 1) * cols)
            low_ref[:full, :] = in_ref[:full, 0, span].astype(BF16)
            if full < sz.master_pad:
                low_ref[full:, :] = jnp.zeros((sz.master_pad - full, cols), BF16)
            if full < sz.master:
                low_ref[full : full + 16, :] = jnp.concatenate(
                    [in_ref[full : sz.master, 0, span], jnp.zeros((full + 16 - sz.master, cols), F32)], axis=0
                ).astype(BF16)
            w_ref[:, span] = tn(order_ref[: sz.master_pad, :], low_ref[...]).astype(BF16)
            row = lax.broadcasted_iota(jnp.int32, (2 * NSTATE, 2 * NSTATE), 0)
            col = lax.broadcasted_iota(jnp.int32, (2 * NSTATE, 2 * NSTATE), 1)
            one = (row == col).astype(BF16)
            w_ref[2 * sz.channels : sz.dt, span] = nt(one, state_ref[span, :].astype(BF16)).astype(BF16)
            lower(lambda: block(step))

        low_out()
        ahead = 3
        for step in range(ahead):
            low_in(step)
        if team.paired:
            pl.when(jnp.logical_not(straight))(lambda: swaps[0].wait_recv())

        def got_pack(layer):
            ref = pks_ref.at[layer]
            Delivery(ref, ref, pack_send.at[0], pack_recv.at[layer], team.owner(layer), team.alone(layer)).wait_got()

        got_pack(0)
        pl.when(team.alone(0))(lambda: packs[0].near().wait())
        gain = pks_ref[0, GAIN_ROW : GAIN_ROW + 1, :]
        own_ref[...] = norm_rows(first_ref[...].astype(F32), gain).astype(BF16)
        work = [lambda step=step: low_in(step) for step in range(ahead, steps)]
        run_gather(team, parts, own_ref, all_ref, ag_sems, None, work)
        keeps[0].start()
        got_pack(1)
        if team.paired:

            @pl.when(jnp.logical_not(straight))
            def _():
                swaps[1].wait_recv()
                for copy in swaps:
                    copy.wait_send()

        for m, copy in enumerate(packs):
            done = team.alone(0) if m == 0 else jnp.bool_(False)
            pl.when(jnp.logical_not(done))(copy.wait_sent)
        receive()

        @pl.when(section == 0)
        def _():
            for step in range(steps):
                for copy in block(step):
                    copy.wait_sent()
            for copy in matrix():
                copy.wait_sent()

        blank(local_sem.at[2]).wait()
        for copy in keeps:
            copy.wait()

    w_shape = jax.ShapeDtypeStruct((sz.cols, width), BF16)
    wo_shape = jax.ShapeDtypeStruct((sz.channels, width), BF16)
    row_shape = jax.ShapeDtypeStruct((rows, width), BF16)
    return pl.pallas_call(
        kernel,
        out_shape=[
            w_shape, wo_shape, w_shape, wo_shape,
            jax.ShapeDtypeStruct((2, 16, width), F32),
            jax.ShapeDtypeStruct((1, LANES), F32),
            row_shape, row_shape,
            jax.ShapeDtypeStruct((count * rows, width), BF16),
        ],
        in_specs=[ANY_SPEC] * 4 + [VMEM_SPEC] * 4,
        out_specs=[ANY_SPEC] * 4 + [VMEM_SPEC] * 4 + [ANY_SPEC],
        scratch_shapes=[
            pltpu.VMEM((rows, width), BF16),
            pltpu.VMEM(proj_in_t.shape, F32),
            pltpu.VMEM(proj_state.shape, F32),
            pltpu.VMEM(proj_out.shape, F32),
            pltpu.VMEM(order.shape, BF16),
            pltpu.VMEM((sz.master_pad, cols), BF16),
            pltpu.VMEM((sz.cols, width), BF16),
            pltpu.VMEM((sz.channels, width), BF16),
            pltpu.VMEM((LANES - 16, width), BF16),
        ]
        + gather_scratch(parts, team.dims, count)
        + [DMA((4,)), DMA((2,)), DMA((2,)), DMA((2,)), DMA((2,))]
        + [DMA((3 * steps + 1, 2)), DMA((3 * steps + 1,)), DMA((3,))]
        + [pltpu.VMEM((16, width), F32)],
        compiler_params=params(collective_id),
        name="opening",
    )(proj_in_t, proj_state, proj_out, order, head_part, shared_part, inputs, cotangent)


def column_of(tile, rows):
    row = lax.broadcasted_iota(jnp.int32, (rows, rows), 0)
    lane = lax.broadcasted_iota(jnp.int32, (rows, rows), 1)
    return nt((row == lane).astype(F32), tile, HIGH)[:, 0:1]


def write_stats(stat_ref, squares, out_grad, branch, rows):
    dot = nt(jnp.ones((8, branch.shape[1]), F32), out_grad * branch, HIGH)
    scale = lax.rsqrt(squares / (HEADS * HDIM) + EPS_NORM)
    row = lax.broadcasted_iota(jnp.int32, (8, rows), 0)
    stat_ref[...] = jnp.zeros_like(stat_ref)
    stat_ref[:, :rows] = jnp.where(row == 0, scale, jnp.where(row == 1, dot, 0.0))


def greet_other():
    barrier = pltpu.get_barrier_semaphore()
    other = 1 - lax.axis_index("section")
    pl.semaphore_signal(barrier, inc=1, device_id={"section": other}, device_id_type=MESH)
    pl.semaphore_wait(barrier, 1)
    return other


def add_up(out_ref, mine_ref, got_ref, squares_ref):
    rows, width = out_ref.shape
    step = 16 if rows % 16 == 0 else rows

    def body(i, carry):
        span = pl.ds(pl.multiple_of(i * step, step), step)
        total = mine_ref[span, :].astype(F32) + got_ref[span, :].astype(F32)
        out_ref[span, :] = total
        if squares_ref is not None:
            part = total * total
            for k in range(0, step, 8):
                squares_ref[...] += part[k : k + 8]
        return carry

    lax.fori_loop(0, rows // step, body, 0)


def trade_sections(sums, stacks, squared, collective_id):
    pairs = sums + stacks
    number, summed = len(pairs), len(sums)

    def kernel(*refs):
        ins, outs = refs[: 2 * number], refs[2 * number : 3 * number]
        squares_ref = refs[3 * number]
        boxes = refs[3 * number + 1 : 3 * number + 1 + summed]
        send_sem, recv_sem = refs[3 * number + 1 + summed :]
        squares_ref[...] = jnp.zeros_like(squares_ref)
        section = lax.axis_index("section")
        other = greet_other()

        def go(mine, theirs):
            copies = []
            for k in range(number):
                copy = pltpu.make_async_remote_copy(
                    src_ref=theirs[k],
                    dst_ref=boxes[k] if k < summed else outs[k].at[section],
                    send_sem=send_sem.at[k],
                    recv_sem=recv_sem.at[k],
                    device_id={"section": other},
                    device_id_type=MESH,
                )
                copy.start()
                copies.append(copy)
            for k in range(summed, number):
                outs[k][section] = mine[k][...]
            for k in range(number):
                copies[k].wait()
                if k < summed:
                    add_up(outs[k], mine[k], boxes[k], squares_ref if k < squared else None)

        pl.when(section == 0)(lambda: go(ins[0::2], ins[1::2]))
        pl.when(section == 1)(lambda: go(ins[1::2], ins[0::2]))

    shapes = [jax.ShapeDtypeStruct(a.shape, F32) for a, _ in sums]
    shapes += [jax.ShapeDtypeStruct((2,) + a.shape, a.dtype) for a, _ in stacks]
    shapes.append(jax.ShapeDtypeStruct((8, sums[0][0].shape[1]), F32))
    return pl.pallas_call(
        kernel,
        out_shape=shapes,
        in_specs=[VMEM_SPEC] * (2 * number),
        out_specs=[VMEM_SPEC] * len(shapes),
        scratch_shapes=[pltpu.VMEM(a.shape, a.dtype) for a, _ in sums] + [DMA((number,))] * 2,
        compiler_params=pltpu.CompilerParams(
            collective_id=collective_id, has_side_effects=True, vmem_limit_bytes=VMEM_LIMIT
        ),
        name="trade_sections",
    )(*[a for pair in pairs for a in pair])


def fits(sz):
    return Team(sz.count).paired and sz.tokens * sz.width <= 4 << 20


class Sizes:
    def __init__(self, count, heads, tokens, width):
        self.count = count
        self.heads = heads
        self.padded = heads + heads % 2
        self.channels = self.padded * HDIM
        self.conv = self.channels + 2 * NSTATE
        self.cols = 2 * self.channels + 2 * NSTATE + LANES
        self.dt = 2 * self.channels + 2 * NSTATE
        self.master = heads * COLS
        self.master_pad = -(-self.master // LANES) * LANES
        self.grad_rows = self.master_pad + 2 * NSTATE
        self.tokens = tokens
        self.width = width
        self.blocks = tokens // STRETCH

    def order(self):
        table = np.zeros((self.grad_rows, self.cols), np.float32)
        for head in range(self.heads):
            for j in range(HDIM):
                table[head * COLS + j, head * HDIM + j] = 1
                table[head * COLS + HDIM + j, self.channels + head * HDIM + j] = 1
            table[head * COLS + 2 * HDIM, self.dt + head] = 1
        for j in range(2 * NSTATE):
            table[self.master_pad + j, 2 * self.channels + j] = 1
        return jnp.asarray(table, BF16)

    def head_sum(self):
        table = np.zeros((self.channels, LANES), np.float32)
        for head in range(self.padded):
            table[head * HDIM : (head + 1) * HDIM, head] = 1
        return jnp.asarray(table, F32)


def nt(left, right, precision=None):
    return lax.dot_general(
        left, right, (((1,), (1,)), ((), ())), precision=precision, preferred_element_type=F32
    )


def tn(left, right, precision=None):
    return lax.dot_general(
        left, right, (((0,), (0,)), ((), ())), precision=precision, preferred_element_type=F32
    )


def nn(left, right, precision=None):
    return jnp.dot(left, right, precision=precision, preferred_element_type=F32)


def split(value):
    high = value.astype(BF16)
    return high, (value - high.astype(F32)).astype(BF16)


def fine(dot, left, right, left_axis, right_axis):
    left_high, left_low = split(left)
    right_high, right_low = split(right)
    return dot(
        jnp.concatenate([left_high, left_low, left_high], axis=left_axis),
        jnp.concatenate([right_high, right_high, right_low], axis=right_axis),
    )


def nt3(left, right):
    return fine(nt, left, right, 1, 1)


def tn3(left, right):
    return fine(tn, left, right, 0, 0)


def nn3(left, right):
    return fine(nn, left, right, 1, 0)


def softplus(value):
    return jnp.maximum(value, 0.0) + jnp.log1p(jnp.exp(-jnp.abs(value)))


def sigmoid(value):
    return 1.0 / (1.0 + jnp.exp(-value))


def halves(left, right):
    rows = left.shape[0]
    lane = lax.broadcasted_iota(jnp.int32, (rows, LANES), 1)
    return jnp.where(lane < HDIM, left, right)


def lower_mask(size):
    row = lax.broadcasted_iota(jnp.int32, (size, size), 0)
    col = lax.broadcasted_iota(jnp.int32, (size, size), 1)
    return row >= col


def step_rows(log_decay, step):
    lane = lax.broadcasted_iota(jnp.int32, log_decay.shape, 1)
    both = jnp.where(lane < 8, log_decay, pltpu.roll(step, 8, 1))
    return jnp.transpose(jnp.where(lane < 16, both, 0.0))


def to_columns(tile, rows):
    row = lax.broadcasted_iota(jnp.int32, (rows, LANES), 0)
    lane = lax.broadcasted_iota(jnp.int32, (rows, LANES), 1)
    return nt((row == lane).astype(F32), tile, HIGH)


def forward_phase(
    count, sz, layer, lengths, gathered, weights, weight_out, pack, residual, cotangent, own, collective_id
):
    block, chunk, chans = STRETCH, CHUNK, sz.channels
    team = Team(count)
    dims = team.dims
    rows, width = residual.shape
    subs = block // chunk
    shards = block // rows
    blocks = sz.blocks
    planes = dims[0]
    per = blocks // planes
    parts = column_parts(width, TEAM_GATHER if team.paired else GATHER)
    scatter = PlaneScatter(team, rows, width)
    turn = cotangent is not None
    passing = own is not None
    cols = 256
    steps = width // cols

    def kernel(*refs):
        refs = list(refs)
        take = lambda number: [refs.pop(0) for _ in range(number)]
        reset_ref, rows_ref, ws_ref, wos_ref, pks_ref, u_ref = take(6)
        cot_ref = refs.pop(0) if turn else None
        w_own, wo_own = take(2) if passing else (None, None)
        result_ref, branch_ref, total_ref, next_ref, p_out, y_out, s_out = take(7)
        stats_ref = refs.pop(0) if turn else None
        ws_next, wos_next = take(2) if passing else (None, None)
        conv_ref, state_ref, w_ref, wo_ref, h_buf, p_buf, y_buf, s_buf, part_ref, sq_ref = take(10)
        load_sem, store_sem, weight_sem = take(3)
        sums_ref, own_ref = take(2)
        scatter_refs = take(5)
        ag_sems = take(3)
        small_send, small_recv = take(2)
        if passing:
            w_mine, wo_mine, zero_ref, own_sem, give_send, give_recv = take(6)
        pk_ref = pks_ref.at[layer]

        def load(c):
            span = pl.ds(pl.multiple_of(c * block, block), block)
            return pltpu.make_async_copy(rows_ref.at[span, :], h_buf.at[c % 2], load_sem.at[c % 2])

        def stores(c):
            slot = c % 2
            span = pl.ds(pl.multiple_of(c * block, block), block)
            return [
                pltpu.make_async_copy(p_buf.at[slot], p_out.at[span, :], store_sem.at[0, slot]),
                pltpu.make_async_copy(y_buf.at[slot], y_out.at[span, :], store_sem.at[1, slot]),
                pltpu.make_async_copy(s_buf.at[slot], s_out.at[pl.ds(c * subs, subs)], store_sem.at[2, slot]),
            ]

        load(0).start()
        weight_copies = [
            pltpu.make_async_copy(ws_ref, w_ref, weight_sem.at[0]),
            pltpu.make_async_copy(wos_ref, wo_ref, weight_sem.at[1]),
        ]
        for copy in weight_copies:
            copy.start()
        if passing:
            section = lax.axis_index("section")
            own_copies = [
                pltpu.make_async_copy(w_own, w_mine, own_sem.at[0]),
                pltpu.make_async_copy(wo_own, wo_mine, own_sem.at[1]),
            ]
            for copy in own_copies:
                copy.start()
            zero_ref[...] = jnp.zeros_like(zero_ref)
            give_block, give_matrix, receive, blank = give_weights(
                team, 1, w_mine, wo_mine, ws_next, wos_next, zero_ref, (give_send, give_recv), sz, steps, cols
            )
            blank(own_sem.at[2]).start()
        greet_all(count, True)
        if passing:
            for copy in own_copies:
                copy.wait()

            @pl.when(section == 1)
            def _():
                for step in range(steps):
                    for copy in give_block(step):
                        copy.start()
                for copy in give_matrix():
                    copy.start()

        conv_ref[...] = jnp.zeros_like(conv_ref)
        state_ref[...] = jnp.zeros_like(state_ref)
        scatter.bind(part_ref, branch_ref, *scatter_refs)
        for copy in weight_copies:
            copy.wait()

        def one_block(c, carry):
            slot = c % 2
            keep = keeps(reset_ref, team.micro(), c)
            span_all = pl.ds(pl.multiple_of(c * block, block), block)
            pl.when(c + 1 < blocks)(lambda: load(c + 1).start())
            load(c).wait()

            @pl.when(c >= 2)
            def _():
                for copy in stores(c - 2):
                    copy.wait()

            h_ref, p_ref, y_ref, s_ref = (buf.at[slot] for buf in (h_buf, p_buf, y_buf, s_buf))
            p_ref[...] = nt(h_ref[...], w_ref[...])
            inner = p_ref[:, chans : 2 * chans]
            state_raw = p_ref[:, 2 * chans : sz.dt].astype(BF16).astype(F32)
            conv_ref[0:8, :] = conv_ref[block : block + 8, :] * keep
            conv_ref[8 : 8 + block, :chans] = inner
            conv_ref[8 : 8 + block, chans:] = state_raw
            pre = pk_ref[CONV : CONV + 1, : sz.conv] + pk_ref[0:1, : sz.conv] * conv_ref[8 : 8 + block, :]
            for tap in range(1, CONV):
                pre = pre + pk_ref[tap : tap + 1, : sz.conv] * conv_ref[8 - tap : 8 - tap + block, :]
            act = pre * sigmoid(pre)
            step = softplus(p_ref[:, sz.dt :] + pk_ref[7:8, :LANES])
            decay = step * pk_ref[8:9, :LANES]
            mask = lower_mask(chunk)
            lower = mask.astype(F32)
            lane = lax.broadcasted_iota(jnp.int32, (chunk, LANES), 1)
            for sub in range(subs):
                span = slice(sub * chunk, (sub + 1) * chunk)
                if sub == 0:
                    state_ref[...] = state_ref[...] * keep
                s_ref[sub] = state_ref[...]
                dt = step[span]
                log_decay = nn(lower, decay[span], HIGH)
                flat = step_rows(log_decay, dt)
                writer = act[span, chans : chans + NSTATE]
                reader = act[span, chans + NSTATE :]
                cross = nt3(reader, writer)
                for pair in range(sz.padded // 2):
                    cols = slice(pair * LANES, (pair + 1) * LANES)
                    x = act[span, cols]
                    total = jnp.zeros((chunk, LANES), F32)
                    for side in range(2):
                        head = 2 * pair + side
                        gap = log_decay[:, head : head + 1] - flat[head : head + 1, :]
                        weight = cross * jnp.exp(jnp.where(mask, gap, -1e30)) * flat[8 + head : 9 + head, :]
                        part = jnp.where((lane < HDIM) == (side == 0), x, 0.0)
                        total = total + nn3(weight, part)
                    logs = halves(log_decay[:, 2 * pair : 2 * pair + 1], log_decay[:, 2 * pair + 1 : 2 * pair + 2])
                    dts = halves(dt[:, 2 * pair : 2 * pair + 1], dt[:, 2 * pair + 1 : 2 * pair + 2])
                    old = state_ref[:, cols]
                    total = total + jnp.exp(logs) * nn3(reader, old)
                    last = logs[chunk - 1 : chunk, :]
                    moved_in = x * jnp.exp(last - logs) * dts
                    state_ref[:, cols] = jnp.exp(last) * old + tn3(writer, moved_in)
                    y_ref[span, cols] = total + pk_ref[6:7, cols] * x
            z = p_ref[:, :chans]
            gated = y_ref[...] * z * sigmoid(z)
            square = nt(jnp.ones((8, chans), F32), gated * gated, HIGH)
            for k in range(shards):
                sq_ref[c * shards + k] = square[:, k * rows : (k + 1) * rows]
            high, low = split(gated * pk_ref[5:6, :chans])
            part_ref[span_all, :] = (nn(high, wo_ref[...]) + nn(low, wo_ref[...])).astype(part_ref.dtype)
            for copy in stores(c):
                copy.start()
            if per == 1:
                scatter.step(planes, c + 1, lambda k: k)
            else:
                pl.when(c % per == per - 1)(lambda: scatter.step(planes, c // per + 1, lambda k: k))
            return carry

        lax.fori_loop(0, blocks, one_block, 0)
        me = linear(dims, team.spot())
        copies = start_direct(team, lambda peer: sq_ref.at[peer], sums_ref, small_send, small_recv)
        sums_ref[me] = sq_ref[me]
        scatter.finish(planes, lambda k: k)
        wait_direct(team, sums_ref, copies, small_recv, small_send)
        total = jnp.sum(sums_ref[...], axis=0)
        total_ref[...] = total
        scale = lax.rsqrt(column_of(total, rows) / (HEADS * HDIM) + EPS_NORM)
        branch = branch_ref[...] * scale
        branch_ref[...] = branch
        live_col = live_rows_of(reset_ref, team.micro(), me, rows)
        result = (u_ref[...].astype(F32) + live_col * branch).astype(BF16)
        result_ref[...] = result
        stat = None
        if turn:
            stat_ref, stat_send, stat_recv = refs
            out_grad = (live_col * cot_ref[...].astype(F32)).astype(BF16)
            own_ref[...] = out_grad
            write_stats(stat_ref, total, out_grad.astype(F32), branch, rows)
            stat = (stat_ref, stats_ref, stat_send, stat_recv)
        else:
            gain = pks_ref[layer + 1, GAIN_ROW : GAIN_ROW + 1, :]
            own_ref[...] = norm_rows(result.astype(F32), gain).astype(BF16)
        run_gather(team, parts, own_ref, next_ref, ag_sems, stat)
        for c in range(max(blocks - 2, 0), blocks):
            for copy in stores(c):
                copy.wait()
        scatter.drain()
        if passing:
            receive()

            @pl.when(section == 1)
            def _():
                for step in range(steps):
                    for copy in give_block(step):
                        copy.wait_sent()
                for copy in give_matrix():
                    copy.wait_sent()

            blank(own_sem.at[2]).wait()

    tokens = sz.tokens
    out_shape = [
        jax.ShapeDtypeStruct((rows, width), BF16),
        jax.ShapeDtypeStruct((rows, width), F32),
        jax.ShapeDtypeStruct((8, rows), F32),
        jax.ShapeDtypeStruct((tokens, width), BF16),
        jax.ShapeDtypeStruct((tokens, sz.cols), F32),
        jax.ShapeDtypeStruct((tokens, chans), F32),
        jax.ShapeDtypeStruct((tokens // chunk, NSTATE, chans), F32),
    ]
    out_specs = [VMEM_SPEC] * 3 + [ANY_SPEC] * 4
    scratch = [
        pltpu.VMEM((block + 8, sz.conv), F32),
        pltpu.VMEM((NSTATE, chans), F32),
        pltpu.VMEM((sz.cols, width), BF16),
        pltpu.VMEM((chans, width), BF16),
        pltpu.VMEM((2, block, width), BF16),
        pltpu.VMEM((2, block, sz.cols), F32),
        pltpu.VMEM((2, block, chans), F32),
        pltpu.VMEM((2, subs, NSTATE, chans), F32),
        pltpu.VMEM((tokens, width), scatter.first_type),
        pltpu.VMEM((count, 8, rows), F32),
        DMA((2,)),
        DMA((3, 2)),
        DMA((2,)),
        pltpu.VMEM((count, 8, rows), F32),
        pltpu.VMEM((rows, width), BF16),
    ]
    scratch += scatter.scratch() + gather_scratch(parts, dims, count) + [DMA((count,))] * 2
    operands = [lengths, gathered, weights, weight_out, pack, residual]
    in_specs = [pl.BlockSpec(memory_space=pltpu.SMEM)] + [ANY_SPEC] * 3 + [VMEM_SPEC] * 2
    if turn:
        out_shape.append(jax.ShapeDtypeStruct((count, 8, LANES), F32))
        out_specs.append(VMEM_SPEC)
        scratch += [pltpu.VMEM((8, LANES), F32)] + [DMA((count,))] * 2
        operands.append(cotangent)
        in_specs.append(VMEM_SPEC)
    if passing:
        out_shape += [jax.ShapeDtypeStruct(array.shape, array.dtype) for array in own]
        out_specs += [ANY_SPEC] * 2
        scratch += [pltpu.VMEM(array.shape, array.dtype) for array in own]
        scratch += [pltpu.VMEM((LANES - 16, width), BF16), DMA((3,))]
        scratch += [DMA((3 * steps + 1, 2)), DMA((3 * steps + 1,))]
        operands += list(own)
        in_specs += [ANY_SPEC] * 2
    return pl.pallas_call(
        kernel,
        out_shape=out_shape,
        in_specs=in_specs,
        out_specs=out_specs,
        scratch_shapes=scratch,
        compiler_params=params(collective_id),
        name="forward_phase",
    )(*operands)


def backward_phase(
    count, sz, layer, lengths, out_grads, proj, mixed, states, stats, weights, weight_out, pack, order,
    residual, upstream, below, gathered, upper, collective_id,
):
    block, chunk, chans = STRETCH, CHUNK, sz.channels
    team = Team(count)
    dims = team.dims
    rows, width = residual.shape
    subs = block // chunk
    blocks = sz.blocks
    planes = dims[0]
    per = blocks // planes
    parts = column_parts(width, TEAM_GATHER if team.paired else GATHER)
    scatter = PlaneScatter(team, rows, width)
    more = below is not None
    close = upper is not None
    early = more and fits(sz)
    cols = 256
    steps = width // cols

    def kernel(*refs):
        refs = list(refs)
        take = lambda number: [refs.pop(0) for _ in range(number)]
        reset_ref, g_all, p_all, y_all, s_all, ws_ref, wos_ref, orders_ref = take(8)
        st_ref, pks_ref, sum_ref, u_ref, up_ref = take(5)
        if more:
            lower_ref, lower_total = take(2)
        if close:
            h_own, in_upper, out_upper, acc_upper, result_own, result_upper, grad_upper = take(7)
            state_upper, rates_ref = take(2)
            sum_in, sum_out, state_all, sum_small, outs_ref, grads_ref, stats_ref, norm_ref = take(8)
        elif early:
            h_own = refs.pop(0)
            grad_ref, low_grad_ref, acc_ref, in_out, out_out, state_out = take(6)
        else:
            grad_ref, low_grad_ref, acc_ref, gt_out, q_out = take(5)
        if more:
            next_ref, stats_ref = take(2)
        conv_ref, dpre_ref, dact_ref, ddt_ref, dstate_ref = take(5)
        w_ref, wo_ref, order_ref, g_buf, p_buf, halo_buf, y_buf, s_buf, gt_buf, q_buf, part_ref = take(11)
        load_sem, store_sem, weight_sem = take(3)
        scatter_refs = take(5)
        pk_ref = pks_ref.at[layer]
        if close or early:
            gt_full, q_full, h_cols, g_cols, col_sem = take(5)
        if close:
            grad_ref, acc_ref, box_in, box_out, box_small = take(5)
            in_out, out_out = w_ref.at[: sz.master_pad, :], wo_ref
            live_rows = pl.ds(0, -(-sz.master // 16) * 16)
            trade_send, trade_recv, few_send, few_recv = take(4)
            in_buf, out_buf, keep_sem = take(3)
            state_out, squares_ref, state_sums, state_box, pieces_ref, state_own = take(6)
            share_ref, shares_ref, stat_ref, mine_ref, got_ref = take(5)
            state_send, state_recv, piece_send, piece_recv = take(4)
            head_sems = take(3)
            share_send, share_recv, stat_send, stat_recv, pair_send, pair_recv = take(6)
            section = lax.axis_index("section")
            micro = team.micro()

        def g_slot(slot):
            return g_buf.at[pl.ds(pl.multiple_of(slot * block, block), block), :]

        def loads(c):
            slot = c % 2
            span = pl.ds(pl.multiple_of(c * block, block), block)
            before = pl.multiple_of(jnp.maximum(c * block - 8, 0), 8)
            return [
                pltpu.make_async_copy(g_all.at[span, :], g_slot(slot), load_sem.at[0, slot]),
                pltpu.make_async_copy(p_all.at[span, :], p_buf.at[slot], load_sem.at[1, slot]),
                pltpu.make_async_copy(p_all.at[pl.ds(before, 8), :], halo_buf.at[slot], load_sem.at[2, slot]),
                pltpu.make_async_copy(y_all.at[span, :], y_buf.at[slot], load_sem.at[3, slot]),
                pltpu.make_async_copy(s_all.at[pl.ds(c * subs, subs)], s_buf.at[slot], load_sem.at[4, slot]),
            ]

        def stores(c):
            slot = c % 2
            span = pl.ds(pl.multiple_of(c * block, block), block)
            if close or early:
                return []
            return [
                pltpu.make_async_copy(gt_buf.at[slot], gt_out.at[:, span], store_sem.at[0, slot]),
                pltpu.make_async_copy(q_buf.at[slot], q_out.at[span, :], store_sem.at[1, slot]),
            ]

        for copy in loads(blocks - 1):
            copy.start()
        weight_copies = [
            pltpu.make_async_copy(wos_ref, wo_ref, weight_sem.at[0]),
            pltpu.make_async_copy(ws_ref, w_ref, weight_sem.at[1]),
            pltpu.make_async_copy(orders_ref, order_ref, weight_sem.at[2]),
        ]
        for copy in weight_copies:
            copy.start()
        greet_all(count, True)
        dpre_ref[...] = jnp.zeros_like(dpre_ref)
        dstate_ref[...] = jnp.zeros_like(dstate_ref)
        acc_ref[...] = jnp.zeros_like(acc_ref)
        scatter.bind(part_ref, grad_ref, *scatter_refs)
        for copy in weight_copies:
            copy.wait()

        def one_block(i, carry):
            c = blocks - 1 - i
            slot = c % 2
            keep = keeps(reset_ref, team.micro(), c)
            after = keeps(reset_ref, team.micro(), jnp.minimum(c + 1, blocks - 1))
            span_all = pl.ds(pl.multiple_of(c * block, block), block)

            @pl.when(c >= 1)
            def _():
                for copy in loads(c - 1):
                    copy.start()

            for copy in loads(c):
                copy.wait()

            if not (close or early):

                @pl.when(i >= 2)
                def _():
                    for copy in stores(c + 2):
                        copy.wait()

            g_ref = g_slot(slot)
            p_ref, halo_ref, y_ref, s_ref = (buf.at[slot] for buf in (p_buf, halo_buf, y_buf, s_buf))
            if close or early:
                gt_ref, q_ref = gt_full.at[:, span_all], q_full.at[span_all, :]
            else:
                gt_ref, q_ref = gt_buf.at[slot], q_buf.at[slot]
            conv_ref[0:8, :chans] = halo_ref[:, chans : 2 * chans] * keep
            conv_ref[0:8, chans:] = halo_ref[:, 2 * chans : sz.dt].astype(BF16).astype(F32) * keep
            conv_ref[8 : 8 + block, :chans] = p_ref[:, chans : 2 * chans]
            conv_ref[8 : 8 + block, chans:] = p_ref[:, 2 * chans : sz.dt].astype(BF16).astype(F32)
            pre = pk_ref[CONV : CONV + 1, : sz.conv] + pk_ref[0:1, : sz.conv] * conv_ref[8 : 8 + block, :]
            for tap in range(1, CONV):
                pre = pre + pk_ref[tap : tap + 1, : sz.conv] * conv_ref[8 - tap : 8 - tap + block, :]
            gate = sigmoid(pre)
            act = pre * gate
            slope = gate * (1.0 + pre * (1.0 - gate))
            step_in = p_ref[:, sz.dt :] + pk_ref[7:8, :LANES]
            step = softplus(step_in)
            rate = pk_ref[8:9, :LANES]
            decay = step * rate
            z = p_ref[:, :chans]
            zgate = sigmoid(z)
            zsilu = z * zgate
            y = y_ref[...]
            gated = y * zsilu
            gain = pk_ref[5:6, :chans]
            skip = pk_ref[6:7, :chans]
            columns = [to_columns(st_ref[c * (block // rows) + k], rows) for k in range(block // rows)]
            columns = jnp.concatenate(columns, axis=0)
            scale = columns[:, 0:1]
            along = columns[:, 1:2]
            grad_q = nt(g_ref[...], wo_ref[...])
            q_ref[...] = (gated * scale * gain).astype(BF16)
            acc_ref[5:6, :chans] += jnp.sum(grad_q * gated * scale, axis=0, keepdims=True)
            dgated = grad_q * gain * scale - gated * (scale * scale * along * (1.0 / (HEADS * HDIM)))
            dy = dgated * zsilu
            dz = dgated * y * zgate * (1.0 + z * (1.0 - zgate))
            x_all = act[:, :chans]
            acc_ref[6:7, :chans] += jnp.sum(dy * x_all, axis=0, keepdims=True)
            scan_dot = nn(dy * (y - skip * x_all), sum_ref[...], HIGH)
            mask = lower_mask(chunk)
            lower = mask.astype(F32)
            lane = lax.broadcasted_iota(jnp.int32, (chunk, LANES), 1)
            for sub in reversed(range(subs)):
                span = slice(sub * chunk, (sub + 1) * chunk)
                dt = step[span]
                log_decay = nn(lower, decay[span], HIGH)
                flat = step_rows(log_decay, dt)
                writer = act[span, chans : chans + NSTATE]
                reader = act[span, chans + NSTATE :]
                cross = nt3(reader, writer)
                cross_grad = jnp.zeros((chunk, chunk), F32)
                dreader = jnp.zeros((chunk, NSTATE), F32)
                dwriter = jnp.zeros((chunk, NSTATE), F32)
                fall = jnp.zeros((LANES, chunk), F32)
                row = lax.broadcasted_iota(jnp.int32, (LANES, chunk), 0)
                reach = []
                carried = []
                for pair in range(sz.padded // 2):
                    cols = slice(pair * LANES, (pair + 1) * LANES)
                    x = act[span, cols]
                    g = dy[span, cols]
                    logs = halves(log_decay[:, 2 * pair : 2 * pair + 1], log_decay[:, 2 * pair + 1 : 2 * pair + 2])
                    dts = halves(dt[:, 2 * pair : 2 * pair + 1], dt[:, 2 * pair + 1 : 2 * pair + 2])
                    last = logs[chunk - 1 : chunk, :]
                    old = s_ref[sub, :, cols]
                    dnew = dstate_ref[:, cols]
                    faded = g * jnp.exp(logs)
                    tail = jnp.exp(last - logs)
                    dreader = dreader + nt3(faded, old)
                    ahead = nn3(writer, dnew)
                    dx = g * skip[:, cols] + ahead * tail * dts
                    dwriter = dwriter + nt3(x * tail * dts, dnew)
                    reach.append(x * ahead * tail)
                    carried.append(jnp.sum(old * dnew, axis=0, keepdims=True) * jnp.exp(last))
                    dstate_ref[:, cols] = jnp.exp(last) * dnew + tn3(reader, faded)
                    for side in range(2):
                        head = 2 * pair + side
                        own = (lane < HDIM) == (side == 0)
                        g_own = jnp.where(own, g, 0.0)
                        gap = log_decay[:, head : head + 1] - flat[head : head + 1, :]
                        decays = jnp.exp(jnp.where(mask, gap, -1e30))
                        steps = flat[8 + head : 9 + head, :]
                        spread = nt3(g_own, x) * decays
                        weight = cross * decays * steps
                        dx = dx + tn3(weight, g_own)
                        cross_grad = cross_grad + spread * steps
                        sums = jnp.sum(spread * cross, axis=0, keepdims=True)
                        fall = fall + jnp.where(row == head, sums, 0.0)
                    dact_ref[span, cols] = dx
                dact_ref[span, chans : chans + NSTATE] = dwriter + tn3(cross_grad, reader)
                dact_ref[span, chans + NSTATE :] = dreader + nn3(cross_grad, writer)
                reach = nn(jnp.concatenate(reach, axis=1), sum_ref[...], HIGH)
                carried = nn(jnp.concatenate(carried, axis=1), sum_ref[...], HIGH)
                direct = jnp.transpose(fall) + reach
                given = dt * reach
                dlog = scan_dot[span] - dt * direct
                ends = jnp.sum(given, axis=0, keepdims=True) + carried
                at_end = lax.broadcasted_iota(jnp.int32, (chunk, LANES), 0) == chunk - 1
                dlog = dlog + jnp.where(at_end, ends, 0.0)
                ddecay = tn(lower, dlog, HIGH)
                ddt_ref[span, :] = direct + ddecay * rate
                acc_ref[8:9, :LANES] += jnp.sum(ddecay * dt, axis=0, keepdims=True)
            dstate_ref[...] = dstate_ref[...] * keep
            ddt_raw = ddt_ref[...] * sigmoid(step_in)
            acc_ref[7:8, :LANES] += jnp.sum(ddt_raw, axis=0, keepdims=True)
            dpre_ref[block : block + 8, :] = dpre_ref[0:8, :] * after
            dpre_ref[0:block, :] = dact_ref[...] * slope
            raw = conv_ref[8 : 8 + block, :]
            acc_ref[CONV : CONV + 1, : sz.conv] += jnp.sum(dpre_ref[0:block, :], axis=0, keepdims=True)
            draw = jnp.zeros((block, sz.conv), F32)
            for tap in range(CONV):
                later = dpre_ref[tap : tap + block, :]
                draw = draw + pk_ref[tap : tap + 1, : sz.conv] * later
                acc_ref[tap : tap + 1, : sz.conv] += jnp.sum(raw * later, axis=0, keepdims=True)
            low = jnp.concatenate(
                [dz.astype(BF16), draw.astype(BF16), ddt_raw.astype(BF16)], axis=1
            )
            part_ref[span_all, :] = nn(low, w_ref[...]).astype(part_ref.dtype)
            gt_ref[...] = nt(order_ref[...], low).astype(BF16)
            for copy in stores(c):
                copy.start()
            if per == 1:
                scatter.step(planes, i + 1, lambda k: planes - 1 - k)
            else:
                pl.when(i % per == per - 1)(
                    lambda: scatter.step(planes, i // per + 1, lambda k: planes - 1 - k)
                )
            return carry

        def input_grads():
            gain = pk_ref[GAIN_ROW : GAIN_ROW + 1, :]
            grad, gain_grad = norm_rows_back(u_ref[...].astype(F32), gain, grad_ref[...])
            grad = grad + up_ref[...].astype(F32)
            grad_ref[...] = grad
            acc_ref[GAIN_ROW : GAIN_ROW + 1, :] = gain_grad
            return grad

        def at(j):
            return pl.ds(pl.multiple_of(j * cols, cols), cols)

        def columns(j):
            slot = j % 2
            return [
                pltpu.make_async_copy(h_own.at[:, at(j)], h_cols.at[slot], col_sem.at[0, slot]),
                pltpu.make_async_copy(g_all.at[:, at(j)], g_cols.at[slot], col_sem.at[1, slot]),
            ]

        def weight_step(j, then=None):
            slot = j % 2
            for copy in columns(j):
                copy.wait()

            @pl.when(j + 1 < steps)
            def _():
                for copy in columns(j + 1):
                    copy.start()

            in_out[:, at(j)] = nn(gt_full[: sz.master_pad, :], h_cols[slot]).astype(BF16)
            out_out[:, at(j)] = tn(q_full[...], g_cols[slot]).astype(BF16)
            if then is not None:
                then(j)
            state_out[:, at(j)] = nn(gt_full[sz.master_pad :, :], h_cols[slot]).astype(BF16)

        if close:
            def trade(layer, j):
                ins, outs = (in_upper, out_upper) if layer else (in_out, out_out)
                sets = ((ins, box_in, live_rows), (outs, box_out, slice(None)))
                return [
                    Delivery(
                        src.at[cut, at(j)], dst.at[micro, cut, at(j)],
                        trade_send.at[k, layer, j], trade_recv.at[k, micro, j],
                        team.owner(layer), team.alone(layer),
                    )
                    for k, (src, dst, cut) in enumerate(sets)
                ]

            def each(action):
                def body(j, carry):
                    action(j)
                    return carry

                lax.fori_loop(0, steps, body, 0)

            def begin(layer):
                def action(j):
                    for copy in trade(layer, j):
                        copy.start()

                return action

            each(begin(1))
            few = {}
            for layer_now, sources in (
                (0, (acc_ref, result_own, grad_ref)), (1, (acc_upper, result_upper, grad_upper))
            ):
                for k, (src, dst) in enumerate(zip(sources, (box_small, outs_ref, grads_ref))):
                    few[layer_now, k] = Delivery(
                        src, dst.at[micro], few_send.at[k, layer_now], few_recv.at[k, micro],
                        team.owner(layer_now), team.alone(layer_now),
                    )
            late = ((0, 0), (0, 2))
            for key, copy in few.items():
                if key not in late:
                    copy.start()

        lax.fori_loop(0, blocks, one_block, 0)
        if not close:
            if early:
                for copy in columns(0):
                    copy.start()
            scatter.finish(planes, lambda k: planes - 1 - k)
            grad = input_grads()
            low_grad_ref[...] = grad.astype(BF16)
            if more:
                own_ref, stat_ref, stat_send, stat_recv = take(4)
                out_grad = (live_rows_of(reset_ref, team.micro(), linear(dims, team.spot()), rows) * grad.astype(BF16).astype(F32)).astype(BF16)
                own_ref[...] = out_grad
                write_stats(stat_ref, lower_total[...], out_grad.astype(F32), lower_ref[...], rows)
                work = [lambda j=j: weight_step(j) for j in range(steps)] if early else []
                run_gather(team, parts, own_ref, next_ref, refs, (stat_ref, stats_ref, stat_send, stat_recv), work)
            if not early:
                for c in range(0, min(2, blocks)):
                    for copy in stores(c):
                        copy.wait()
            scatter.drain()
            return

        def made(begin_at, end_at):
            def body(j, carry):
                weight_step(j, begin(0))
                return carry

            lax.fori_loop(begin_at, end_at, body, 0)

        for copy in columns(0):
            copy.start()
        order_of = lambda k: planes - 1 - k
        stops = scatter.extra_steps()
        for extra in range(1, stops + 1):
            scatter.step(planes, planes + extra, order_of)
            made(steps * (extra - 1) // stops, steps * extra // stops)
        squares_ref[...] = jnp.zeros_like(squares_ref)
        each_rows = 16
        for k in range(count):
            for layer_now, ref in enumerate((state_out, state_upper)):
                to = (2 * k + layer_now) * each_rows
                g_buf[to : to + each_rows, :] = ref[k * each_rows : (k + 1) * each_rows, :]
        state_sends, stages = scatter_steps(
            team, column_parts(width, TEAM_SCATTER_SMALL), 2 * each_rows, g_buf, state_sums, state_box,
            state_send, state_recv, True,
        )
        stages[0]()
        scatter.last()
        input_grads()
        for key in late:
            few[key].start()
        for stage in stages[1:]:
            stage()
        passed = [
            Delivery(
                state_sums.at[pl.ds(layer_now * each_rows, each_rows), :], pieces_ref.at[micro],
                piece_send.at[layer_now], piece_recv.at[micro], team.owner(layer_now), team.alone(layer_now),
            )
            for layer_now in range(2)
        ]
        for copy in passed:
            copy.start()

        def sent(layer):
            def action(j):
                for copy in trade(layer, j):
                    copy.wait_sent()

            return action

        for copy in few.values():
            copy.wait_sent()
        for copy in passed:
            copy.wait_sent()

        def got(src, sem, m):
            Delivery(src, src, trade_send.at[0, 0, 0], sem, team.user(m), team.alone(m)).wait_got()

        for m in range(2):
            for k, box in enumerate((box_small, outs_ref, grads_ref)):
                got(box.at[m], few_recv.at[k, m], m)
        sum_small[...] = box_small[0] + box_small[1]
        heads = Heads(count)
        pieces = width // LANES
        me = lax.axis_index("head")
        share_ref[...] = jnp.zeros_like(share_ref)
        share_ref[0:1, :] = sum_small[GAIN_ROW : GAIN_ROW + 1, :]
        share_ref[1 : CONV + 2, : 2 * NSTATE] = sum_small[: CONV + 1, chans : sz.conv]

        def piece(peer):
            return share_ref.at[:, pl.ds(pl.multiple_of((peer % pieces) * LANES, LANES), LANES)]

        shares = start_direct(heads, piece, shares_ref, share_send, share_recv)
        shares_ref[me] = piece(me)[...]
        for m in range(2):
            got(pieces_ref.at[m], piece_recv.at[m], m)
        state_total = pieces_ref[0] + pieces_ref[1]
        state_own[...] = state_total.astype(BF16)
        def kept(j):
            slot = j % 2
            return [
                pltpu.make_async_copy(in_buf.at[slot, live_rows, :], sum_in.at[live_rows, at(j)], keep_sem.at[0, slot]),
                pltpu.make_async_copy(out_buf.at[slot], sum_out.at[:, at(j)], keep_sem.at[1, slot]),
            ]

        stat_copies = []

        def begin_norm():
            each(sent(1))
            each(sent(0))

            def add_up(j, carry):
                @pl.when(j >= 2)
                def _():
                    for copy in kept(j - 2):
                        copy.wait()

                for k, (box, total_ref) in enumerate(((box_in, in_buf), (box_out, out_buf))):
                    for m in range(2):
                        cut = slice(None) if k else live_rows
                        got(box.at[m, cut, at(j)], trade_recv.at[k, m, j], m)
                    count_rows = chans if k else -(-sz.master // 16) * 16
                    total = box[0, :count_rows, at(j)].astype(F32) + box[1, :count_rows, at(j)].astype(F32)
                    total_ref[j % 2, :count_rows, :] = total
                    squares_ref[k : k + 1, at(j)] += jnp.sum(total * total, axis=0, keepdims=True)
                for copy in kept(j):
                    copy.start()
                return carry

            lax.fori_loop(0, steps, add_up, 0)
            wait_direct(heads, shares_ref, shares, share_recv, share_send)
            shared = jnp.sum(shares_ref[...], axis=0)
            taps = sum_small[: CONV + 2, : sz.heads * HDIM]
            skip_sums = nn(sum_small[6:7, :chans], sum_ref[...], HIGH)
            bias = sum_small[7:8, :LANES]
            rate = sum_small[8:9, :LANES] * rates_ref[...]
            lane = lax.broadcasted_iota(jnp.int32, (1, LANES), 1)
            of_heads = jnp.where(lane < sz.heads, bias * bias + rate * rate + skip_sums * skip_sums, 0.0)
            total = jnp.sum(squares_ref[...]) + jnp.sum(taps * taps) + jnp.sum(of_heads)
            total = total + jnp.sum(state_total * state_total)
            total = total + jnp.where(me < pieces, jnp.sum(shared * shared), 0.0)
            row = lax.broadcasted_iota(jnp.int32, (8, LANES), 0)
            stat_ref[...] = jnp.where(row == 7, total, shared)
            stat_copies.extend(start_direct(heads, lambda peer: stat_ref, stats_ref, stat_send, stat_recv))
            stats_ref[me] = stat_ref[...]

        run_gather(
            heads, column_parts(width, GATHER_SMALL), state_own, state_all, head_sems, None,
            [lambda: None] * 4 + [begin_norm],
        )
        wait_direct(heads, stats_ref, stat_copies, stat_recv, stat_send)
        row = lax.broadcasted_iota(jnp.int32, (8, LANES), 0)
        section_sq = stats_ref[0, 7:8, :]
        for k in range(1, count):
            section_sq = section_sq + stats_ref[k, 7:8, :]
        mine_ref[...] = jnp.broadcast_to(section_sq, (8, LANES))
        pair = remote(mine_ref, got_ref, pair_send, pair_recv, {"section": 1 - section})
        pair.start()
        pair.wait()
        norm = jnp.sqrt(mine_ref[...] + got_ref[...])
        threshold = CLIP_COEF * PARAMS**0.5
        norm_ref[...] = jnp.where(row == 0, norm, threshold / jnp.maximum(norm, threshold))
        for j in range(max(steps - 2, 0), steps):
            for copy in kept(j):
                copy.wait()
        for copy in state_sends:
            copy.wait_send()
        scatter.drain()

    tokens = sz.tokens
    state = 2 * NSTATE
    if close:
        out_shape = [
            jax.ShapeDtypeStruct((sz.master_pad, width), F32),
            jax.ShapeDtypeStruct((chans, width), F32),
            jax.ShapeDtypeStruct((state, width), BF16),
            jax.ShapeDtypeStruct((16, width), F32),
            jax.ShapeDtypeStruct((2, rows, width), BF16),
            jax.ShapeDtypeStruct((2, rows, width), F32),
            jax.ShapeDtypeStruct((count, 8, LANES), F32),
            jax.ShapeDtypeStruct((8, LANES), F32),
        ]
        out_specs = [ANY_SPEC] * 3 + [VMEM_SPEC] * 5
    elif early:
        out_shape = [
            jax.ShapeDtypeStruct((rows, width), F32),
            jax.ShapeDtypeStruct((rows, width), BF16),
            jax.ShapeDtypeStruct((16, width), F32),
            jax.ShapeDtypeStruct((sz.master_pad, width), BF16),
            jax.ShapeDtypeStruct((chans, width), BF16),
            jax.ShapeDtypeStruct((state, width), BF16),
        ]
        out_specs = [VMEM_SPEC] * 6
    else:
        out_shape = [
            jax.ShapeDtypeStruct((rows, width), F32),
            jax.ShapeDtypeStruct((rows, width), BF16),
            jax.ShapeDtypeStruct((16, width), F32),
            jax.ShapeDtypeStruct((sz.grad_rows, tokens), BF16),
            jax.ShapeDtypeStruct((tokens, chans), BF16),
        ]
        out_specs = [VMEM_SPEC] * 3 + [ANY_SPEC] * 2
    scratch = [
        pltpu.VMEM((block + 8, sz.conv), F32),
        pltpu.VMEM((block + 8, sz.conv), F32),
        pltpu.VMEM((block, sz.conv), F32),
        pltpu.VMEM((block, LANES), F32),
        pltpu.VMEM((NSTATE, chans), F32),
        pltpu.VMEM((sz.cols, width), BF16),
        pltpu.VMEM((chans, width), BF16),
        pltpu.VMEM((sz.grad_rows, sz.cols), BF16),
        pltpu.VMEM((max(2 * block, 2 * 16 * count) if close else 2 * block, width), BF16),
        pltpu.VMEM((2, block, sz.cols), F32),
        pltpu.VMEM((2, 8, sz.cols), F32),
        pltpu.VMEM((2, block, chans), F32),
        pltpu.VMEM((2, subs, NSTATE, chans), F32),
        pltpu.VMEM((8, LANES) if close or early else (2, sz.grad_rows, block), BF16),
        pltpu.VMEM((8, LANES) if close or early else (2, block, chans), BF16),
        pltpu.VMEM((tokens, width), scatter.first_type),
        DMA((5, 2)),
        DMA((2, 2)),
        DMA((3,)),
    ]
    scratch += scatter.scratch()
    if close or early:
        scratch += [
            pltpu.VMEM((sz.grad_rows, tokens), BF16),
            pltpu.VMEM((tokens, chans), BF16),
            pltpu.VMEM((2, tokens, cols), BF16),
            pltpu.VMEM((2, tokens, cols), BF16),
            DMA((2, 2)),
        ]
    if close:
        scratch += [
            pltpu.VMEM((rows, width), F32),
            pltpu.VMEM((16, width), F32),
            pltpu.VMEM((2, sz.master_pad, width), BF16),
            pltpu.VMEM((2, chans, width), BF16),
            pltpu.VMEM((2, 16, width), F32),
            DMA((2, 2, steps)),
            DMA((2, 2, steps)),
            DMA((3, 2)),
            DMA((3, 2)),
            pltpu.VMEM((2, sz.master_pad, cols), F32),
            pltpu.VMEM((2, chans, cols), F32),
            DMA((2, 2)),
            pltpu.VMEM((state, width), BF16),
            pltpu.VMEM((8, width), F32),
            pltpu.VMEM((32, width), F32),
            pltpu.VMEM((count - 1, 32, width), BF16),
            pltpu.VMEM((2, 16, width), F32),
            pltpu.VMEM((16, width), BF16),
            pltpu.VMEM((8, width), F32),
            pltpu.VMEM((count, 8, LANES), F32),
        ]
        scratch += [pltpu.VMEM((8, LANES), F32)] * 3
        scratch += [DMA((1, count - 1)), DMA((1, count - 1)), DMA((2,)), DMA((2,))]
        scratch += gather_scratch(column_parts(width, GATHER_SMALL), Heads(count).dims, count)
        scratch += [DMA((count,))] * 4 + [DMA, DMA]
    operands = [lengths, out_grads, proj, mixed, states, weights, weight_out, order]
    in_specs = [pl.BlockSpec(memory_space=pltpu.SMEM)] + [ANY_SPEC] * 7 + [VMEM_SPEC] * 5
    operands += [stats, pack, sz.head_sum(), residual, upstream]
    if more:
        out_shape += [
            jax.ShapeDtypeStruct((tokens, width), BF16),
            jax.ShapeDtypeStruct((count, 8, LANES), F32),
        ]
        out_specs += [ANY_SPEC, VMEM_SPEC]
        scratch += [pltpu.VMEM((rows, width), BF16), pltpu.VMEM((8, LANES), F32)]
        scratch += [DMA((count,))] * 2 + gather_scratch(parts, dims, count)
        operands += list(below)
        in_specs += [VMEM_SPEC] * 2
    if close:
        operands += list(upper)
        in_specs += [ANY_SPEC] * 3 + [VMEM_SPEC] * 6
    elif early:
        operands.append(gathered)
        in_specs.append(ANY_SPEC)
    return pl.pallas_call(
        kernel,
        out_shape=out_shape,
        in_specs=in_specs,
        out_specs=out_specs,
        scratch_shapes=scratch,
        compiler_params=params(collective_id),
        name="last_phase" if close else "backward_phase",
    )(*operands)


def weight_grads(sz, grads_t, gathered, scaled, out_grads):
    cols = 256

    split_row = sz.master_pad

    def kernel(gt_ref, h_ref, q_ref, g_ref, in_ref, state_ref, out_ref):
        in_ref[...] = nn(gt_ref[:split_row, :], h_ref[...]).astype(BF16)
        state_ref[...] = nn(gt_ref[split_row:, :], h_ref[...])
        out_ref[...] = tn(q_ref[...], g_ref[...]).astype(BF16)

    tokens, width, chans = sz.tokens, sz.width, sz.channels
    return pl.pallas_call(
        kernel,
        grid=(width // cols,),
        out_shape=[
            jax.ShapeDtypeStruct((sz.master_pad, width), BF16),
            jax.ShapeDtypeStruct((2 * NSTATE, width), F32),
            jax.ShapeDtypeStruct((chans, width), BF16),
        ],
        in_specs=[
            pl.BlockSpec((sz.grad_rows, tokens), lambda i: (0, 0)),
            pl.BlockSpec((tokens, cols), lambda i: (0, i)),
            pl.BlockSpec((tokens, chans), lambda i: (0, 0)),
            pl.BlockSpec((tokens, cols), lambda i: (0, i)),
        ],
        out_specs=[
            pl.BlockSpec((sz.master_pad, cols), lambda i: (0, i)),
            pl.BlockSpec((2 * NSTATE, cols), lambda i: (0, i)),
            pl.BlockSpec((chans, cols), lambda i: (0, i)),
        ],
        compiler_params=pltpu.CompilerParams(vmem_limit_bytes=VMEM_LIMIT),
        name="weight_grads",
    )(grads_t, gathered, scaled, out_grads)


def adam_update(weight, moment, second, gradient, rate, decay):
    moment_new = BETA_ONE * moment + (1.0 - BETA_ONE) * gradient
    second_new = BETA_TWO * second + (1.0 - BETA_TWO) * gradient * gradient
    corrected = moment_new * (1.0 / (1.0 - BETA_ONE**ADAM_STEP))
    corrected_sq = second_new * (1.0 / (1.0 - BETA_TWO**ADAM_STEP))
    weight_new = weight - rate * (corrected / (jnp.sqrt(corrected_sq) + ADAM_EPS) + decay * weight)
    return (weight_new, moment_new, second_new)


def adam_in(sz, clip, grad, weight, moment, second):
    block = LANES
    width = sz.width

    def kernel(clip_ref, g_ref, w_ref, m_ref, v_ref, wn_ref, mn_ref, vn_ref, low_ref):
        scale = clip_ref[0]

        def body(i, carry):
            made = []
            for half in range(2):
                span = pl.ds(pl.multiple_of(i * 16 + half * 8, 8), 8)
                new = adam_update(
                    w_ref[span, 0, :], m_ref[span, 0, :], v_ref[span, 0, :],
                    scale * g_ref[span, :], LEARN_MATRIX, WEIGHT_DECAY,
                )
                wn_ref[span, 0, :] = new[0]
                mn_ref[span, 0, :] = new[1]
                vn_ref[span, 0, :] = new[2]
                made.append(new[0])
            low_ref[pl.ds(pl.multiple_of(i * 16, 16), 16), :] = jnp.concatenate(made, axis=0).astype(BF16)
            return carry

        lax.fori_loop(0, block // 16, body, 0)

    view = pl.BlockSpec((block, 1, width), lambda i: (i, 0, 0))
    flat = pl.BlockSpec((block, width), lambda i: (i, 0))
    shape = jax.ShapeDtypeStruct((sz.master, 1, width), F32)
    return pl.pallas_call(
        kernel,
        grid=(sz.master_pad // block,),
        out_shape=[shape, shape, shape, jax.ShapeDtypeStruct((sz.master, width), BF16)],
        in_specs=[pl.BlockSpec(memory_space=pltpu.SMEM), flat, view, view, view],
        out_specs=[view, view, view, flat],
        compiler_params=pltpu.CompilerParams(vmem_limit_bytes=VMEM_LIMIT),
        name="adam_in",
    )(clip, grad, weight, moment, second)


def adam_plain(clip, grad, weight, moment, second, transposed):
    rows, width = weight.shape
    block = min(256 if transposed else 64, rows)

    def kernel(clip_ref, g_ref, w_ref, m_ref, v_ref, wn_ref, mn_ref, vn_ref, low_ref):
        if transposed:
            row = lax.broadcasted_iota(jnp.int32, (width, width), 0)
            col = lax.broadcasted_iota(jnp.int32, (width, width), 1)
            grad_value = tn(g_ref[...], (row == col).astype(BF16))
        else:
            grad_value = g_ref[...]
        new = adam_update(
            w_ref[...], m_ref[...], v_ref[...], clip_ref[0] * grad_value, LEARN_MATRIX, WEIGHT_DECAY
        )
        wn_ref[...], mn_ref[...], vn_ref[...] = new
        low_ref[...] = new[0].astype(BF16)

    flat = pl.BlockSpec((block, width), lambda i: (i, 0))
    turned = pl.BlockSpec((width, block), lambda i: (0, i))
    shape = jax.ShapeDtypeStruct((rows, width), F32)
    return pl.pallas_call(
        kernel,
        grid=(rows // block,),
        out_shape=[shape, shape, shape, jax.ShapeDtypeStruct((rows, width), BF16)],
        in_specs=[
            pl.BlockSpec(memory_space=pltpu.SMEM), turned if transposed else flat, flat, flat, flat
        ],
        out_specs=[flat] * 4,
        compiler_params=pltpu.CompilerParams(vmem_limit_bytes=VMEM_LIMIT),
        name="adam_plain",
    )(clip, grad, weight, moment, second)


def adam_few(sz, norms, small, stats, rates, head, shared):
    state = 2 * NSTATE
    pieces = sz.width // LANES
    conv = (CONV + 1) * state
    last = (CONV + 2) * HDIM

    def kernel(norm_ref, small_ref, stats_ref, rates_ref, *refs):
        ins, outs, (head_grad, shared_grad) = refs[:6], refs[6:12], refs[12:]
        scale = norm_ref[1:2, 0:1]
        lane = lax.broadcasted_iota(jnp.int32, (1, LANES), 1)
        rate_grad = small_ref[8:9, :LANES] * rates_ref[...]
        for head_at in range(sz.heads):
            row = slice(head_at, head_at + 1)
            cols = slice(head_at * HDIM, (head_at + 1) * HDIM)
            for tap in range(CONV):
                head_grad[row, tap * HDIM : (tap + 1) * HDIM] = small_ref[tap : tap + 1, cols]
            head_grad[row, CONV * HDIM : (CONV + 1) * HDIM] = small_ref[5:6, cols]
            head_grad[row, (CONV + 1) * HDIM : last] = small_ref[CONV : CONV + 1, cols]
            head_grad[row, last : last + 1] = small_ref[7:8, head_at : head_at + 1]
            head_grad[row, last + 1 : last + 2] = rate_grad[:, head_at : head_at + 1]
            head_grad[row, last + 2 : last + 3] = jnp.sum(small_ref[6:7, cols], axis=1, keepdims=True)
        for tap in range(CONV + 1):
            for k in range(state // LANES):
                to = tap * state + k * LANES
                shared_grad[:, to : to + LANES] = stats_ref[k, tap + 1 : tap + 2, :]
        for k in range(pieces):
            shared_grad[:, conv + k * LANES : conv + (k + 1) * LANES] = stats_ref[k, 0:1, :]
        for k, grad in enumerate((head_grad, shared_grad)):
            new = adam_update(*(ref[...] for ref in ins[3 * k : 3 * k + 3]), scale * grad[...], LEARN_VECTOR, 0.0)
            for ref, value in zip(outs[3 * k : 3 * k + 3], new):
                ref[...] = value

    arrays = list(head) + list(shared)
    return pl.pallas_call(
        kernel,
        out_shape=[jax.ShapeDtypeStruct(array.shape, F32) for array in arrays],
        in_specs=[VMEM_SPEC] * 10,
        out_specs=[VMEM_SPEC] * 6,
        scratch_shapes=[pltpu.VMEM(head[0].shape, F32), pltpu.VMEM(shared[0].shape, F32)],
        name="adam_few",
    )(norms, small, stats, rates, *arrays)


def columns_first(array):
    return jnp.transpose(array, (2, 0, 1))


def shards(
    inputs,
    cotangent,
    valid_lengths,
    proj_in,
    proj_in_m,
    proj_in_v,
    proj_state,
    proj_state_m,
    proj_state_v,
    proj_out,
    proj_out_m,
    proj_out_v,
    head_params,
    head_m,
    head_v,
    shared_params,
    shared_m,
    shared_v,
):
    count = lax.axis_size("head")
    rows, width = inputs.shape[1], inputs.shape[2]
    heads = head_params.shape[1]
    tokens = rows * count
    sz = Sizes(count, heads, tokens, width)
    order = sz.order()
    own_in, own_out, lower_in, lower_out, pack, rates, first, cot, rows_zero = opening(
        count, sz, columns_first(proj_in), proj_state[0], proj_out[0], head_params[0], shared_params, order,
        inputs, cotangent, 0,
    )

    kept_zero = forward_phase(
        count, sz, 0, valid_lengths, rows_zero, lower_in, lower_out, pack, first, None, (own_in, own_out), 1
    )
    result_zero, branch_zero, total_zero, rows_one = kept_zero[:4]
    upper_in, upper_out = kept_zero[7:]
    kept_one = forward_phase(
        count, sz, 1, valid_lengths, rows_one, upper_in, upper_out, pack, result_zero, cot, None, 2
    )
    result_one, out_grads_one, stats_one = kept_one[0], kept_one[3], kept_one[7]
    back_one = backward_phase(
        count, sz, 1, valid_lengths, out_grads_one, *kept_one[4:7], stats_one, upper_in, upper_out, pack, order,
        result_zero, cot, (branch_zero, total_zero), rows_one, None, 3,
    )
    out_grads_zero, stats_zero = back_one[-2:]
    grad_one, low_one, acc_one = back_one[:3]

    def run_last(upper):
        return backward_phase(
            count, sz, 0, valid_lengths, out_grads_zero, *kept_zero[4:7], stats_zero, lower_in, lower_out, pack, order,
            first, low_one, None, rows_zero, upper, 4,
        )

    if fits(sz):
        in_one, out_one, state_one = back_one[3:6]
        upper = (rows_zero, in_one, out_one, acc_one, result_zero, result_one, grad_one, state_one, rates)
        grad_in, grad_out, grad_state, small, layer_outs, grad_buffer, all_stats, norms = run_last(upper)
    else:
        grads_t_one, scaled_one = back_one[3:5]
        grad_zero, _, acc_zero, grads_t_zero, scaled_zero = run_last(None)
        lower = weight_grads(sz, grads_t_zero, rows_zero, scaled_zero, out_grads_zero)
        higher = weight_grads(sz, grads_t_one, rows_one, scaled_one, out_grads_one)
        grad_in, grad_out, state_sum, small, layer_outs, grad_buffer, squares = trade_sections(
            [(lower[0], higher[0]), (lower[2], higher[2]), (lower[1], higher[1]), (acc_zero, acc_one)],
            [(result_zero, result_one), (grad_zero, grad_one)],
            2,
            6,
        )
        state_part = state_sum.astype(BF16)
        state_all, all_stats, norms = finish_sums(
            count, sz, [state_part.reshape(16 * count, -1)], small, squares, rates, sz.head_sum(), 5
        )
        grad_state = state_all.reshape(state_part.shape)
    grad_norm, clip = norms[0, 0], norms[1, :1]
    few = adam_few(
        sz, norms, small, all_stats, rates,
        (head_params[0], head_m[0], head_v[0]), (shared_params, shared_m, shared_v),
    )
    new_in = adam_in(
        sz, clip, grad_in, columns_first(proj_in), columns_first(proj_in_m), columns_first(proj_in_v)
    )
    new_out = adam_plain(
        clip, grad_out, proj_out[0], proj_out_m[0], proj_out_v[0], False
    )
    new_state = adam_plain(
        clip, grad_state, proj_state[0], proj_state_m[0], proj_state_v[0], True
    )
    back_view = [jnp.transpose(array, (1, 2, 0)) for array in new_in[:3]]
    return (
        layer_outs[None],
        grad_buffer[None],
        grad_norm,
        back_view[0],
        back_view[1],
        back_view[2],
        new_in[3].T[None],
        new_state[0][None],
        new_state[1][None],
        new_state[2][None],
        new_state[3][None],
        new_out[0][None],
        new_out[1][None],
        new_out[2][None],
        new_out[3][None],
        few[0][None],
        few[1][None],
        few[2][None],
        few[3],
        few[4],
        few[5],
    )


def solution(mesh):
    in_specs = (
        P(None, "head", None),
        P(None, "head", None),
        P(),
        P("section", None, "head"),
        P("section", None, "head"),
        P("section", None, "head"),
        P("section", None, None),
        P("section", None, None),
        P("section", None, None),
        P("section", "head", None),
        P("section", "head", None),
        P("section", "head", None),
        P("section", "head", None),
        P("section", "head", None),
        P("section", "head", None),
        P("section", None),
        P("section", None),
        P("section", None),
    )
    out_specs = (
        P("section", None, "head", None),
        P("section", None, "head", None),
        P(),
        P("section", None, "head"),
        P("section", None, "head"),
        P("section", None, "head"),
        P("section", None, "head"),
        P("section", None, None),
        P("section", None, None),
        P("section", None, None),
        P("section", None, None),
        P("section", "head", None),
        P("section", "head", None),
        P("section", "head", None),
        P("section", "head", None),
        P("section", "head", None),
        P("section", "head", None),
        P("section", "head", None),
        P("section", None),
        P("section", None),
        P("section", None),
    )
    return jax.shard_map(shards, mesh=mesh, in_specs=in_specs, out_specs=out_specs, check_vma=False)
```

```python
import itertools

import jax
import jax.numpy as jnp
import numpy as np
from jax import lax
from jax.experimental import pallas as pl
from jax.experimental.pallas import tpu as pltpu
from jax.sharding import PartitionSpec as P

HEADS = 64
HDIM = 64
NSTATE = 128
CONV = 4
STRETCH = 256
ADAM_STEP = 5
PARAMS = 51698560

HIGH = lax.Precision.HIGHEST
EPS_NORM = 1e-05
ADAM_EPS = 1e-08
BETA_ONE = 0.5
BETA_TWO = 0.5
CLIP_COEF = 0.2
LEARN_MATRIX = 0.02
LEARN_VECTOR = 0.2
WEIGHT_DECAY = 0.1

F32 = jnp.float32
BF16 = jnp.bfloat16
MESH = pl.DeviceIdType.MESH
LANES = 128
CHUNK = 128
COLS = HDIM * 2 + 1
GAIN_ROW = 9
VMEM_LIMIT = 58 << 20


def keeps(lengths_ref, micro, block):
    return jnp.where(lengths_ref[micro, block] > 0, 0.0, 1.0)


def live_rows_of(lengths_ref, micro, shard, rows):
    token = shard * rows
    own_block = token // STRETCH
    start, length = jnp.int32(0), lengths_ref[micro, 0]
    for block in range(1, lengths_ref.shape[1]):
        here = lengths_ref[micro, block]
        begins = (here > 0) & (block <= own_block)
        start = jnp.where(begins, block, start)
        length = jnp.where(begins, here, length)
    position = token - start * STRETCH + lax.broadcasted_iota(jnp.int32, (rows, 1), 0)
    return (position < length).astype(F32)


def chip_dims(count):
    side = 4 if count % 64 == 0 else 2
    if count % (side * side) != 0:
        return (count, 1, 1)
    return (count // (side * side), side, side)


def place(dims):
    me = lax.axis_index("head")
    return (me // (dims[1] * dims[2]), (me // dims[2]) % dims[1], me % dims[2])


class Heads:
    def __init__(self, count):
        self.count = count
        self.dims = chip_dims(count)
        self.lined = False

    def spot(self):
        return place(self.dims)

    def device(self, index):
        return {"head": index}


class Team:
    def __init__(self, count):
        self.count = count
        self.chips = chip_dims(count)
        self.paired = self.chips[2] == 2
        self.lined = True
        self.dims = self.chips[:2] + (2,) if self.paired else self.chips

    def spot(self):
        spot = place(self.chips)
        return spot[:2] + (lax.axis_index("section"),) if self.paired else spot

    def device(self, index):
        if not self.paired:
            return {"head": index}
        return {"section": index % 2, "head": index // 2 * 2 + lax.axis_index("head") % 2}

    def micro(self):
        return lax.axis_index("head") % 2 if self.paired else lax.axis_index("section")

    def owner(self, layer):
        if not self.paired:
            return {"section": layer}
        return {"section": layer, "head": lax.axis_index("head") // 2 * 2 + lax.axis_index("section")}

    def user(self, micro):
        if not self.paired:
            return {"section": micro}
        head = lax.axis_index("head")
        return {"section": head % 2, "head": head // 2 * 2 + micro}

    def alone(self, which):
        section = lax.axis_index("section")
        if not self.paired:
            return section == which
        return (lax.axis_index("head") % 2 == section) & (section == which)


def linear(dims, spot):
    return (spot[0] * dims[1] + spot[1]) * dims[2] + spot[2]


def moved(dims, spot, shifts):
    return tuple(s if d == 0 else (s + d) % n for s, d, n in zip(spot, shifts, dims))


def shift_of(order, offsets):
    out = [0, 0, 0]
    for axis, off in zip(order, offsets):
        out[axis] = off
    return out


def greet_all(count, pair=False):
    barrier = pltpu.get_barrier_semaphore()
    me = lax.axis_index("head")
    section = lax.axis_index("section")
    for off in range(1, count):
        peer = (me + off) % count
        pl.semaphore_signal(barrier, inc=1, device_id={"head": peer}, device_id_type=MESH)
        if pair:
            there = {"section": 1 - section, "head": peer}
            pl.semaphore_signal(barrier, inc=1, device_id=there, device_id_type=MESH)
    if pair:
        pl.semaphore_signal(barrier, inc=1, device_id={"section": 1 - section}, device_id_type=MESH)
    pl.semaphore_wait(barrier, 2 * count - 1 if pair else count - 1)


def rows_at(shard, rows):
    return pl.ds(pl.multiple_of(shard * rows, rows), rows)


def column_parts(width, shares):
    tiles = width // LANES
    parts, start, taken = [], 0, 0
    for share, order, group in shares:
        taken += share
        stop = tiles * taken // 16 * LANES
        if stop > start:
            parts.append((start, stop - start, order, group))
            start = stop
    return parts


TEAM_GATHER = ((3, (1, 0, 2), 0), (7, (0, 1, 2), 0), (6, (0, 1, 2), 0))
GATHER = ((2, (2, 1, 0), 0), (2, (1, 2, 0), 0), (6, (0, 2, 1), 0), (6, (0, 1, 2), 0))
GATHER_SMALL = ((8, (0, 2, 1), 0), (8, (0, 1, 2), 0))
SCATTER = (
    (1, (2, 0, 1), 0), (1, (1, 0, 2), 0), (1, (0, 1, 2), 0), (1, (0, 2, 1), 0),
    (3, (2, 1, 0), 0), (3, (1, 2, 0), 0), (3, (2, 1, 0), 1), (3, (1, 2, 0), 1),
)
TEAM_SCATTER_SMALL = ((16, (2, 1, 0), 0),)
SCATTER_SMALL = ((8, (2, 1, 0), 0), (8, (1, 2, 0), 0))
SCATTER_PACE = (0.3, 0.9, 0.7, 2.0)


def guarded(preds, action):
    preds = [pred for pred in preds if pred is not None]
    if not preds:
        action()
        return
    cond = preds[0]()
    for pred in preds[1:]:
        cond = jnp.logical_and(cond, pred())
    pl.when(cond)(action)


def gather_steps(group, parts, rows, own_ref, all_ref, send_sem, recv_sem, between=()):
    dims = group.dims
    spot = group.spot()
    me = linear(dims, spot)
    waits = []
    counter = [0] * len(parts)

    def lined(axis):
        return group.lined and axis == 0 and dims[0] > 2 and dims[1] == 2

    def above(axis, dist):
        return lambda: spot[axis] + dist < dims[axis]

    def below(axis, dist):
        return lambda: spot[axis] >= dist

    def sources(part, pos):
        axis = parts[part][2][pos]
        if not lined(axis):
            return [(off, None) for off in range(1, dims[axis])]
        out = []
        for dist in range(1, dims[axis]):
            out.append((dist, above(axis, dist)))
            out.append((-dist, below(axis, dist)))
        return out

    def block(part, offsets):
        start, width, order, _ = parts[part]
        shard = linear(dims, moved(dims, spot, shift_of(order, offsets)))
        return shard, all_ref.at[rows_at(shard, rows), pl.ds(start, width)]

    def push(part, offsets, pos, preds, src, came):
        axis = parts[part][2][pos]
        shard, dst = block(part, offsets)
        up, down = (1, above(axis, 1)), (-1, below(axis, 1))
        if lined(axis):
            targets = [up, down] if came == 0 else [down] if came > 0 else [up]
        else:
            targets = [(off, None) for off in range(1, dims[axis])] if came == 0 else []
        for off, pred in targets:
            peer = linear(dims, moved(dims, spot, shift_of((axis,), (off,))))
            number = counter[part]
            counter[part] += 1

            def begin(peer=peer, number=number):
                pltpu.make_async_remote_copy(
                    src_ref=dst if src is None else src,
                    dst_ref=dst,
                    send_sem=send_sem.at[part, number],
                    recv_sem=recv_sem.at[part, shard],
                    device_id=group.device(peer),
                    device_id_type=MESH,
                ).start()

            guarded([pred], begin)
            waits.append((preds + [pred], part, number))

    def visit(part, offsets, preds, pos, came):
        def body():
            shard, dst = block(part, offsets)
            pltpu.make_async_remote_copy(
                src_ref=dst,
                dst_ref=dst,
                send_sem=send_sem.at[part, 0],
                recv_sem=recv_sem.at[part, shard],
                device_id=group.device(me),
                device_id_type=MESH,
            ).wait_recv()
            push(part, offsets, pos, preds, None, came)
            for later in range(pos + 1, 3):
                push(part, offsets, later, preds, None, 0)

        guarded(preds, body)

    for pos in range(3):
        for part, (start, width, _, _) in enumerate(parts):
            push(part, (0, 0, 0), pos, [], own_ref.at[:, pl.ds(start, width)], 0)
    todo = []
    for part in range(len(parts)):
        first, second, third = (sources(part, pos) for pos in range(3))
        for k, (oa, pa) in enumerate(first):
            todo.append(((0, k, part), part, (oa, 0, 0), [pa], 0, oa))
        for ka, (oa, pa) in enumerate([(0, None)] + first):
            for k, (ob, pb) in enumerate(second):
                todo.append(((1, ka + k, part), part, (oa, ob, 0), [pa, pb], 1, ob))
            for kb, (ob, pb) in enumerate([(0, None)] + second):
                for k, (oc, pc) in enumerate(third):
                    todo.append(
                        ((2, ka + kb + k, part), part, (oa, ob, oc), [pa, pb, pc], 2, oc)
                    )
    todo.sort(key=lambda entry: (sum(abs(off) for off in entry[2]), entry[0]))
    between = list(between)
    for _, part, offsets, preds, pos, came in todo:
        if between:
            between.pop(0)()
        visit(part, offsets, preds, pos, came)
    for work in between:
        work()
    for preds, part, number in waits:

        def settle(part=part, number=number):
            start, width, _, _ = parts[part]
            ref = own_ref.at[:, pl.ds(start, width)]
            pltpu.make_async_remote_copy(
                src_ref=ref,
                dst_ref=ref,
                send_sem=send_sem.at[part, number],
                recv_sem=recv_sem.at[part, 0],
                device_id=group.device(me),
                device_id_type=MESH,
            ).wait_send()

        guarded(preds, settle)


def gather_sends(dims):
    return 3 * dims[0] * dims[1] * dims[2]


def scatter_steps(group, parts, rows, in_ref, out_ref, box_ref, send_sem, recv_sem, staged=False):
    dims = group.dims
    spot = group.spot()
    me = linear(dims, spot)
    sends = []

    def size(part, pos):
        return dims[parts[part][2][pos]]

    def slot_one(part, ea, ob, oc):
        return ((ea - 1) * size(part, 1) + ob) * size(part, 2) + oc

    def slot_two(part, eb, oc):
        base = (size(part, 0) - 1) * size(part, 1) * size(part, 2)
        return base + (eb - 1) * size(part, 2) + oc

    def slot_three(part, ec):
        return slot_two(part, size(part, 1), 0) + ec - 1

    def cols(part):
        return pl.ds(parts[part][0], parts[part][1])

    def mine(part, offsets):
        shard = linear(dims, moved(dims, spot, shift_of(parts[part][2], offsets)))
        return in_ref.at[rows_at(shard, rows), cols(part)]

    def send(part, src, pos, off, slot):
        peer = linear(dims, moved(dims, spot, shift_of((parts[part][2][pos],), (off,))))
        copy = pltpu.make_async_remote_copy(
            src_ref=src,
            dst_ref=box_ref.at[slot, :, cols(part)],
            send_sem=send_sem.at[part, slot],
            recv_sem=recv_sem.at[part, slot],
            device_id=group.device(peer),
            device_id_type=MESH,
        )
        copy.start()
        sends.append(copy)

    def arrived(part, slot):
        ref = box_ref.at[slot, :, cols(part)]
        pltpu.make_async_remote_copy(
            src_ref=ref,
            dst_ref=ref,
            send_sem=send_sem.at[part, slot],
            recv_sem=recv_sem.at[part, slot],
            device_id=group.device(me),
            device_id_type=MESH,
        ).wait_recv()
        return ref[...].astype(F32)

    def combined(part, ob, oc, stages):
        total = mine(part, (0, ob, oc))[...].astype(F32)
        for ea in range(1, size(part, 0)):
            total = total + arrived(part, slot_one(part, ea, ob, oc))
        for eb in range(1, size(part, 1)) if stages > 1 else ():
            total = total + arrived(part, slot_two(part, eb, oc))
        for ec in range(1, size(part, 2)) if stages > 2 else ():
            total = total + arrived(part, slot_three(part, ec))
        return total

    def put_by(part, ob, oc, total):
        if size(part, 0) > 1:
            hold = box_ref.at[slot_one(part, 1, ob, oc), :, cols(part)]
        elif size(part, 1) > 1 and ob == 0:
            hold = box_ref.at[slot_two(part, 1, oc), :, cols(part)]
        else:
            return mine(part, (0, ob, oc))
        hold[...] = total.astype(box_ref.dtype)
        return hold

    def first(part, ob, oc, off):
        slot = slot_one(part, size(part, 0) - off, ob, oc)
        send(part, mine(part, (off, ob, oc)), 0, off, slot)

    def second(part, ob, oc, _):
        hold = put_by(part, ob, oc, combined(part, ob, oc, 1))
        send(part, hold, 1, ob, slot_two(part, size(part, 1) - ob, oc))

    def third(part, _, oc, __):
        hold = put_by(part, 0, oc, combined(part, 0, oc, 2))
        send(part, hold, 2, oc, slot_three(part, size(part, 2) - oc))

    def last(part, _, __, ___):
        out_ref[:, cols(part)] = combined(part, 0, 0, 3)

    lag, rest, turn, end = SCATTER_PACE
    program = []
    for part, (_, _, _, late) in enumerate(parts):
        for ob, oc in itertools.product(range(size(part, 1)), range(size(part, 2))):
            for off in range(1, size(part, 0)):
                rank = (0.0 if ob else rest) + late * lag
                program.append((rank, oc == 0, off, part, first, ob, oc))
            if ob:
                program.append((turn + late * lag, oc == 0, 0, part, second, ob, oc))
        for oc in range(1, size(part, 2)):
            program.append((end + late * lag, False, 0, part, third, 0, oc))
        program.append((3.0 + late * lag, True, 0, part, last, 0, 0))
    program.sort(key=lambda step: step[:4])

    def run(low, high):
        for rank, _, off, part, action, ob, oc in program:
            if low <= rank < high:
                action(part, ob, oc, off)

    if staged:
        marks = (-1.0, turn, end, 3.0, 9.0)
        return sends, [lambda k=k: run(marks[k], marks[k + 1]) for k in range(4)]
    run(-1.0, 99.0)
    return sends


PIECES = 1


class PlaneScatter:
    def __init__(self, group, rows, width):
        self.group, self.dims, self.rows = group, group.dims, rows
        self.wide = group.paired
        self.orders = ((2, 1),) * PIECES if self.wide else ((2, 1), (1, 2))
        self.half = width // len(self.orders)
        self.width = width
        depth = self.dims[0]
        most = max(self.dims[1], self.dims[2])
        self.one = depth * (most - 1) * most
        self.two = depth * (most - 1)
        self.slots = self.one + self.two + 2 * depth
        self.first_type = F32 if self.wide else BF16

    def scratch(self):
        parts = len(self.orders)
        later = self.two + 2 * self.dims[0]
        return [
            pltpu.VMEM((self.one, self.rows, self.width), self.first_type),
            pltpu.VMEM((later, self.rows, self.width), BF16),
            pltpu.VMEM((self.two + self.dims[0] if self.wide else 1, self.rows, self.width), BF16),
            DMA((parts, self.slots)),
            DMA((parts, self.slots)),
        ]

    def bind(self, part_ref, out_ref, first_ref, later_ref, hold_ref, send_sem, recv_sem):
        self.part_ref, self.out_ref = part_ref, out_ref
        self.first_ref, self.later_ref, self.hold_ref = first_ref, later_ref, hold_ref
        self.send_sem, self.recv_sem = send_sem, recv_sem
        self.spot = self.group.spot()
        self.me = linear(self.dims, self.spot)

    def sizes(self, part):
        a, b = self.orders[part]
        return self.dims[a], self.dims[b]

    def slot_one(self, part, plane, ea, ob):
        size_a, size_b = self.sizes(part)
        return (plane * (size_a - 1) + ea - 1) * size_b + ob

    def slot_two(self, part, plane, eb):
        return self.one + plane * (self.sizes(part)[1] - 1) + eb - 1

    def slot_three(self, plane, below):
        return self.one + self.two + 2 * plane + below

    def cols(self, part):
        return pl.ds(part * self.half, self.half)

    def mine(self, part, plane, oa, ob):
        shift = shift_of(self.orders[part], (oa, ob))
        spot = moved(self.dims, (plane, self.spot[1], self.spot[2]), shift)
        return self.part_ref.at[rows_at(linear(self.dims, spot), self.rows), self.cols(part)]

    def box(self, part, slot, begun):
        if begun:
            return self.first_ref.at[slot, :, self.cols(part)]
        return self.later_ref.at[slot - self.one, :, self.cols(part)]

    def copy(self, part, src, slot, sent, peer, begun=False):
        return remote(
            src,
            self.box(part, slot, begun),
            self.send_sem.at[part, sent],
            self.recv_sem.at[part, slot],
            self.group.device(peer),
        )

    def hold(self, part, plane, oa, ob, slot):
        if self.wide:
            return self.hold_ref.at[slot - self.one, :, self.cols(part)]
        return self.mine(part, plane, oa, ob)

    def peer(self, part, pos, off):
        shift = shift_of((self.orders[part][pos],), (off,))
        return linear(self.dims, moved(self.dims, self.spot, shift))

    def arrived(self, part, slot, begun=False):
        ref = self.box(part, slot, begun)
        self.copy(part, ref, slot, slot, self.me, begun).wait_recv()
        return ref[...].astype(F32)

    def first(self, plane):
        for inner in (1, 0):
            for part in range(len(self.orders)):
                size_a, size_b = self.sizes(part)
                for ob in range(size_b):
                    if (ob != 0) != bool(inner):
                        continue
                    for off in range(1, size_a):
                        slot = self.slot_one(part, plane, size_a - off, ob)
                        src = self.mine(part, plane, off, ob)
                        self.copy(part, src, slot, slot, self.peer(part, 0, off), True).start()

    def second(self, plane):
        for part in range(len(self.orders)):
            size_a, size_b = self.sizes(part)
            for ob in range(1, size_b):
                slot = self.slot_two(part, plane, size_b - ob)
                total = self.mine(part, plane, 0, ob)[...].astype(F32)
                for ea in range(1, size_a):
                    total = total + self.arrived(part, self.slot_one(part, plane, ea, ob), True)
                hold = self.hold(part, plane, 0, ob, slot)
                hold[...] = total.astype(BF16)
                self.copy(part, hold, slot, slot, self.peer(part, 1, ob)).start()

    def third(self, plane, place_in_line):
        depth = self.spot[0]
        above = depth > plane
        place_here = jnp.where(above, self.dims[0] - 1 - depth, depth)

        def own_total(part):
            size_a, size_b = self.sizes(part)
            total = self.mine(part, plane, 0, 0)[...].astype(F32)
            for ea in range(1, size_a):
                total = total + self.arrived(part, self.slot_one(part, plane, ea, 0), True)
            for eb in range(1, size_b):
                total = total + self.arrived(part, self.slot_two(part, plane, eb))
            return total

        if place_in_line == 0:

            @pl.when(plane == depth)
            def _():
                for part in range(len(self.orders)):
                    self.out_ref[:, self.cols(part)] = own_total(part)

        @pl.when((plane != depth) & (place_here == place_in_line))
        def _():
            below = jnp.where(above, 0, 1)
            onward = jnp.where(above, depth - 1, depth + 1)
            peer = linear(self.dims, (onward, self.spot[1], self.spot[2]))
            slot = self.slot_three(plane, below)
            for part in range(len(self.orders)):
                total = own_total(part)
                if place_in_line > 0:
                    total = total + self.arrived(part, slot)
                hold = self.hold(part, plane, 0, 0, self.one + self.two + plane)
                hold[...] = total.astype(BF16)
                self.copy(part, hold, slot, slot, peer).start()

    def last(self):
        depth = self.spot[0]
        for below, there in ((0, depth < self.dims[0] - 1), (1, depth > 0)):

            @pl.when(there)
            def _(below=below):
                for part in range(len(self.orders)):
                    total = self.out_ref[:, self.cols(part)]
                    total = total + self.arrived(part, self.slot_three(depth, below))
                    self.out_ref[:, self.cols(part)] = total

    def step(self, number, made, plane_of):
        actions = [self.first, self.second]
        actions += [lambda plane, k=k: self.third(plane, k) for k in range(max(self.dims[0] - 1, 1))]
        for back, action in enumerate(actions):
            k = made - 1 - back
            if isinstance(made, int):
                if 0 <= k < number:
                    action(plane_of(k))
            else:
                pl.when(k >= 0)(lambda k=k, action=action: action(plane_of(k)))

    def extra_steps(self):
        return 1 + max(self.dims[0] - 1, 1)

    def finish(self, number, plane_of, begun=0):
        for extra in range(1 + begun, self.extra_steps() + 1):
            self.step(number, number + extra, plane_of)
        self.last()

    def drain(self):
        for part in range(len(self.orders)):
            size_a, size_b = self.sizes(part)
            early, late = self.box(part, 0, True), self.box(part, self.one, False)
            for plane in range(self.dims[0]):
                for ea in range(1, size_a):
                    for ob in range(size_b):
                        slot = self.slot_one(part, plane, ea, ob)
                        self.copy(part, early, slot, slot, self.me, True).wait_send()
                for eb in range(1, size_b):
                    slot = self.slot_two(part, plane, eb)
                    self.copy(part, late, slot, slot, self.me).wait_send()
            for off in range(1, self.dims[0]):
                plane = (self.spot[0] + off) % self.dims[0]
                slot = self.slot_three(plane, jnp.where(self.spot[0] > plane, 0, 1))
                self.copy(part, late, slot, slot, self.me).wait_send()


def start_direct(group, own_ref_of, box_ref, send_sem, recv_sem):
    count = group.count
    me = linear(group.dims, group.spot())
    copies = []
    for off in range(1, count):
        peer = (me + off) % count
        copy = pltpu.make_async_remote_copy(
            src_ref=own_ref_of(peer),
            dst_ref=box_ref.at[me],
            send_sem=send_sem.at[off],
            recv_sem=recv_sem.at[count - off],
            device_id=group.device(peer),
            device_id_type=MESH,
        )
        copy.start()
        copies.append(copy)
    return copies


def wait_direct(group, box_ref, copies, recv_sem, send_sem):
    count = group.count
    me = linear(group.dims, group.spot())
    for off in range(1, count):
        ref = box_ref.at[(me + off) % count]
        pltpu.make_async_remote_copy(
            src_ref=ref,
            dst_ref=ref,
            send_sem=send_sem.at[off],
            recv_sem=recv_sem.at[off],
            device_id=group.device(me),
            device_id_type=MESH,
        ).wait_recv()
    for copy in copies:
        copy.wait_send()


def remote(src, dst, send_sem, recv_sem, device):
    return pltpu.make_async_remote_copy(
        src_ref=src, dst_ref=dst, send_sem=send_sem, recv_sem=recv_sem, device_id=device, device_id_type=MESH
    )


class Delivery:
    def __init__(self, src, dst, send_sem, recv_sem, device, alone):
        self.alone = alone
        self.ends = src, dst, send_sem, recv_sem, device

    def near(self):
        return pltpu.make_async_copy(*self.ends[:3])

    def far(self):
        return remote(*self.ends)

    def start(self):
        pl.when(self.alone)(lambda: self.near().start())
        pl.when(jnp.logical_not(self.alone))(lambda: self.far().start())

    def wait_sent(self):
        pl.when(self.alone)(lambda: self.near().wait())
        pl.when(jnp.logical_not(self.alone))(lambda: self.far().wait_send())

    def wait_got(self):
        pl.when(jnp.logical_not(self.alone))(lambda: self.far().wait_recv())


VMEM_SPEC = pl.BlockSpec(memory_space=pltpu.VMEM)
ANY_SPEC = pl.BlockSpec(memory_space=pl.ANY)
DMA = pltpu.SemaphoreType.DMA


def params(collective_id):
    return pltpu.CompilerParams(
        collective_id=collective_id, has_side_effects=True, vmem_limit_bytes=VMEM_LIMIT
    )


def gather_scratch(parts, dims, count):
    return [DMA((len(parts), gather_sends(dims))), DMA((len(parts), count)), DMA]


def run_gather(group, parts, own_ref, all_ref, sems, stat=None, between=()):
    rows = own_ref.shape[0]
    me = linear(group.dims, group.spot())
    send_sem, recv_sem, local_sem = sems
    local = pltpu.make_async_copy(own_ref, all_ref.at[rows_at(me, rows)], local_sem)
    local.start()
    if stat is not None:
        stat_ref, box_ref, small_send, small_recv = stat
        copies = start_direct(group, lambda peer: stat_ref, box_ref, small_send, small_recv)
        box_ref[me] = stat_ref[...]
    gather_steps(group, parts, rows, own_ref, all_ref, send_sem, recv_sem, between)
    if stat is not None:
        wait_direct(group, box_ref, copies, small_recv, small_send)
    local.wait()


def scatter_scratch(parts, count, rows, width):
    slots = max(count - 1, 1)
    return [pltpu.VMEM((slots, rows, width), BF16), DMA((len(parts), slots)), DMA((len(parts), slots))]


def finish_sums(count, sz, states, small, squares, rates, head_sum, collective_id):
    team, heads = Team(count), Heads(count)
    width = states[0].shape[1]
    rows = states[0].shape[0] // count
    layers = len(states)
    back = column_parts(width, TEAM_SCATTER_SMALL if layers > 1 else SCATTER_SMALL)
    parts = column_parts(width, GATHER_SMALL)
    chans, state = sz.channels, 2 * NSTATE
    pieces = sz.width // LANES
    threshold = CLIP_COEF * PARAMS**0.5

    def kernel(*refs):
        refs = list(refs)
        take = lambda number: [refs.pop(0) for _ in range(number)]
        in_refs = take(layers)
        small_ref, squares_ref, rates_ref, sum_ref = take(4)
        all_ref, stats_ref, norm_ref = take(3)
        share_ref, sums_ref, out_ref, own_ref, stat_ref, mine_ref, got_ref = take(7)
        scatter_refs, ag_sems = take(3), take(3)
        if layers > 1:
            both_ref, pieces_ref, piece_send, piece_recv = take(4)
        small_send, small_recv, stat_send, stat_recv, pair_send, pair_recv = take(6)
        me = lax.axis_index("head")
        section = lax.axis_index("section")
        share_ref[...] = jnp.zeros_like(share_ref)
        share_ref[0:1, :] = small_ref[GAIN_ROW : GAIN_ROW + 1, :]
        share_ref[1 : CONV + 2, :state] = small_ref[: CONV + 1, chans : chans + state]

        def piece(peer):
            return share_ref.at[:, pl.ds(pl.multiple_of((peer % pieces) * LANES, LANES), LANES)]

        greet_all(count, True)
        copies = start_direct(heads, piece, sums_ref, small_send, small_recv)
        sums_ref[me] = piece(me)[...]
        if layers > 1:
            for k in range(count):
                for layer in range(layers):
                    to = slice((k * layers + layer) * rows, (k * layers + layer + 1) * rows)
                    both_ref[to, :] = in_refs[layer][k * rows : (k + 1) * rows, :]
            sends = scatter_steps(team, back, rows * layers, both_ref, out_ref, *scatter_refs)
            micro = team.micro()
            passed = [
                Delivery(
                    out_ref.at[pl.ds(layer * rows, rows), :], pieces_ref.at[micro],
                    piece_send.at[layer], piece_recv.at[micro], team.owner(layer), team.alone(layer),
                )
                for layer in range(layers)
            ]
            for copy in passed:
                copy.start()
            for copy in passed:
                copy.wait_sent()
            for m in range(2):
                ref = pieces_ref.at[m]
                Delivery(ref, ref, piece_send.at[0], piece_recv.at[m], team.user(m), team.alone(m)).wait_got()
            state_own = pieces_ref[0] + pieces_ref[1]
        else:
            sends = scatter_steps(heads, back, rows, in_refs[0], out_ref, *scatter_refs)
            state_own = out_ref[...]
        wait_direct(heads, sums_ref, copies, small_recv, small_send)
        shared = jnp.sum(sums_ref[...], axis=0)
        shared_sq = jnp.where(me < pieces, jnp.sum(shared * shared), 0.0)
        own_ref[...] = state_own.astype(BF16)
        taps = small_ref[: CONV + 2, :chans]
        skip = nn(small_ref[6:7, :chans], sum_ref[...], HIGH)
        bias = small_ref[7:8, :LANES]
        rate = small_ref[8:9, :LANES] * rates_ref[...]
        lane = lax.broadcasted_iota(jnp.int32, (1, LANES), 1)
        of_heads = jnp.where(lane < sz.heads, bias * bias + rate * rate + skip * skip, 0.0)
        if chans > sz.heads * HDIM:
            taps = taps[:, : sz.heads * HDIM]
        total = jnp.sum(squares_ref[...]) + jnp.sum(taps * taps) + jnp.sum(of_heads)
        total = total + jnp.sum(state_own * state_own) + shared_sq
        row = lax.broadcasted_iota(jnp.int32, (8, LANES), 0)
        stat_ref[...] = jnp.where(row == 7, total, shared)
        run_gather(heads, parts, own_ref, all_ref, ag_sems, (stat_ref, stats_ref, stat_send, stat_recv))
        section_sq = stats_ref[0, 7:8, :]
        for k in range(1, count):
            section_sq = section_sq + stats_ref[k, 7:8, :]
        mine_ref[...] = jnp.broadcast_to(section_sq, (8, LANES))
        pair = pltpu.make_async_remote_copy(
            src_ref=mine_ref,
            dst_ref=got_ref,
            send_sem=pair_send,
            recv_sem=pair_recv,
            device_id={"section": 1 - section},
            device_id_type=MESH,
        )
        pair.start()
        pair.wait()
        norm = jnp.sqrt(mine_ref[...] + got_ref[...])
        norm_ref[...] = jnp.where(row == 0, norm, threshold / jnp.maximum(norm, threshold))
        for copy in sends:
            copy.wait_send()

    return pl.pallas_call(
        kernel,
        out_shape=[
            jax.ShapeDtypeStruct(states[0].shape, BF16),
            jax.ShapeDtypeStruct((count, 8, LANES), F32),
            jax.ShapeDtypeStruct((8, LANES), F32),
        ],
        in_specs=[VMEM_SPEC] * (4 + layers),
        out_specs=[ANY_SPEC, VMEM_SPEC, VMEM_SPEC],
        scratch_shapes=[
            pltpu.VMEM((8, sz.width), F32),
            pltpu.VMEM((count, 8, LANES), F32),
            pltpu.VMEM((rows * layers, width), F32),
            pltpu.VMEM((rows, width), BF16),
        ]
        + [pltpu.VMEM((8, LANES), F32)] * 3
        + scatter_scratch(back, count, rows * layers, width)
        + gather_scratch(parts, heads.dims, count)
        + (
            [pltpu.VMEM((count * rows * layers, width), BF16), pltpu.VMEM((2, rows, width), F32), DMA((2,)), DMA((2,))]
            if layers > 1
            else []
        )
        + [DMA((count,))] * 4
        + [DMA, DMA],
        compiler_params=params(collective_id),
        name="finish_sums",
    )(*states, small, squares, rates, head_sum)


def norm_rows(value, gain):
    mean = jnp.mean(value * value, axis=1, keepdims=True)
    return value * lax.rsqrt(mean + EPS_NORM) * gain


def norm_rows_back(value, gain, grad):
    width = value.shape[1]
    scale = lax.rsqrt(jnp.mean(value * value, axis=1, keepdims=True) + EPS_NORM)
    scaled = grad * gain
    dot = jnp.sum(scaled * value, axis=1, keepdims=True)
    back = scaled * scale - value * (scale * scale * scale * dot * (1.0 / width))
    return back, jnp.sum(grad * value * scale, axis=0, keepdims=True)


def write_pack(sz, pack_ref, head_ref, shared_ref):
    chans, state = sz.channels, 2 * NSTATE
    pack_ref[...] = jnp.zeros_like(pack_ref)
    lane = lax.broadcasted_iota(jnp.int32, (1, LANES), 1)
    bias_row = jnp.zeros((1, LANES), F32)
    rate_row = jnp.zeros((1, LANES), F32)
    rates = -jnp.exp(head_ref[:, (CONV + 2) * HDIM :])
    for head in range(sz.heads):
        cols = slice(head * HDIM, (head + 1) * HDIM)
        for tap in range(CONV):
            pack_ref[tap : tap + 1, cols] = head_ref[head : head + 1, tap * HDIM : (tap + 1) * HDIM]
        pack_ref[5:6, cols] = head_ref[head : head + 1, CONV * HDIM : (CONV + 1) * HDIM]
        pack_ref[CONV : CONV + 1, cols] = head_ref[head : head + 1, (CONV + 1) * HDIM : (CONV + 2) * HDIM]
        last = (CONV + 2) * HDIM
        pack_ref[6:7, cols] = jnp.broadcast_to(head_ref[head : head + 1, last + 2 : last + 3], (1, HDIM))
        bias_row = jnp.where(lane == head, head_ref[head : head + 1, last : last + 1], bias_row)
        rate_row = jnp.where(lane == head, rates[head : head + 1, 1:2], rate_row)
    pack_ref[7:8, :LANES] = bias_row
    pack_ref[8:9, :LANES] = rate_row
    for tap in range(CONV + 1):
        pack_ref[tap : tap + 1, chans : chans + state] = shared_ref[:, tap * state : (tap + 1) * state]
    pack_ref[GAIN_ROW : GAIN_ROW + 1, :] = shared_ref[:, (CONV + 1) * state :]


def give_weights(team, number, w_ref, wo_ref, ws_ref, wos_ref, zero_ref, sems, sz, steps, cols):
    send, recv = sems
    section = lax.axis_index("section")
    head_rows = (pl.ds(0, 2 * sz.channels), pl.ds(sz.dt, 16))
    state_rows = pl.ds(2 * sz.channels, 2 * NSTATE)

    def for_users(src, dst, k):
        return [
            Delivery(src, dst, send.at[k, micro], recv.at[k], team.user(micro), team.alone(micro))
            for micro in range(2)
        ]

    def block(step):
        span = pl.ds(step * cols, cols)
        out = []
        for k, rows in enumerate(head_rows):
            out += for_users(w_ref.at[rows, span], ws_ref.at[rows, span], 3 * step + k)
        pair = w_ref.at[state_rows, span], ws_ref.at[state_rows, span]
        k = 3 * step + 2
        for there in range(2):
            out.append(
                Delivery(*pair, send.at[k, there], recv.at[k], {"section": there}, section == there)
            )
        return out

    def matrix():
        return for_users(wo_ref, wos_ref, 3 * steps)

    def receive():
        for step in range(steps):
            span = pl.ds(step * cols, cols)
            for k, rows in enumerate(head_rows):
                got = ws_ref.at[rows, span]
                Delivery(got, got, send.at[0, 0], recv.at[3 * step + k], team.owner(number), team.alone(number)).wait_got()
            got = ws_ref.at[state_rows, span]
            Delivery(got, got, send.at[0, 0], recv.at[3 * step + 2], {"section": number}, section == number).wait_got()
        Delivery(wos_ref, wos_ref, send.at[0, 0], recv.at[3 * steps], team.owner(number), team.alone(number)).wait_got()

    def blank(sem):
        return pltpu.make_async_copy(zero_ref, ws_ref.at[pl.ds(sz.dt + 16, LANES - 16), :], sem)

    return block, matrix, receive, blank


def opening(count, sz, proj_in_t, proj_state, proj_out, head_part, shared_part, order, inputs, cotangent, collective_id):
    team = Team(count)
    rows, width = inputs.shape[1:]
    parts = column_parts(width, TEAM_GATHER if team.paired else GATHER)
    cols = 256
    steps = width // cols
    full = sz.master // 16 * 16
    own_rows = proj_out.shape[0]

    def kernel(*refs):
        refs = list(refs)
        take = lambda number: [refs.pop(0) for _ in range(number)]
        in_hbm, state_hbm, out_hbm, order_hbm, head_ref, shared_ref, x_ref, cot_ref = take(8)
        w_own, wo_own, ws_ref, wos_ref, pks_ref, rates_ref, first_ref, cot_own, all_ref = take(9)
        own_ref, in_ref, state_ref, out_ref, order_ref, low_ref, w_ref, wo_ref, zero_ref = take(9)
        ag_sems = take(3)
        load_sem, pack_send, pack_recv, swap_send, swap_recv, give_send, give_recv, local_sem = take(8)
        relay_ref, relay_sem = take(2)
        section = lax.axis_index("section")
        other = 1 - section
        micro = team.micro()
        loads = [
            pltpu.make_async_copy(src, dst, load_sem.at[k])
            for k, (src, dst) in enumerate(
                ((order_hbm, order_ref), (in_hbm, in_ref), (state_hbm, state_ref), (out_hbm, out_ref))
            )
        ]
        for copy in loads:
            copy.start()
        write_pack(sz, own_pack_ref := refs[0], head_ref, shared_ref)
        rates_ref[...] = own_pack_ref[8:9, :LANES]
        zero_ref[...] = jnp.zeros_like(zero_ref)
        greet_all(count, True)
        packs = [
            Delivery(
                own_pack_ref, pks_ref.at[section], pack_send.at[m], pack_recv.at[section], team.user(m), team.alone(m)
            )
            for m in range(2)
        ]
        for copy in packs:
            copy.start()
        straight = micro == section
        if team.paired:
            head = lax.axis_index("head")
            partner = {"section": head % 2, "head": head // 2 * 2 + section}
            swaps = [
                remote(x_ref.at[section], first_ref, swap_send.at[0], swap_recv.at[0], partner),
                remote(cot_ref.at[section], cot_own, swap_send.at[1], swap_recv.at[1], partner),
            ]

            @pl.when(jnp.logical_not(straight))
            def _():
                for copy in swaps:
                    copy.start()

            @pl.when(straight)
            def _():
                first_ref[...] = x_ref[micro]
                cot_own[...] = cot_ref[micro]

        else:
            first_ref[...] = x_ref[micro]
            cot_own[...] = cot_ref[micro]

        block, matrix, receive, blank = give_weights(
            team, 0, w_ref, wo_ref, ws_ref, wos_ref, zero_ref, (give_send, give_recv), sz, steps, cols
        )
        keeps = [
            pltpu.make_async_copy(w_ref, w_own, local_sem.at[0]),
            pltpu.make_async_copy(wo_ref, wo_own, local_sem.at[1]),
        ]

        def lower(copies):
            @pl.when(section == 0)
            def _():
                for copy in copies():
                    copy.start()

        x = lax.axis_index("head") % 2
        far = {"section": x, "head": lax.axis_index("head") // 2 * 2 + 1 - x}

        def by_way():
            return remote(wo_ref, relay_ref, relay_sem.at[0], relay_sem.at[1], {"section": other})

        def on_from():
            return remote(relay_ref, wos_ref, relay_sem.at[2], give_recv.at[3 * steps], far)

        def matrix_near():
            there = {"section": x}
            return Delivery(wo_ref, wos_ref, give_send.at[3 * steps, 0], give_recv.at[3 * steps], there, section == x)

        def pass_on():
            @pl.when(section == 1)
            def _():
                by_way().wait_recv()
                on_from().start()

        def low_out():
            loads[3].wait()
            if own_rows < sz.channels:
                wo_ref[...] = jnp.zeros_like(wo_ref)
            wo_ref[:own_rows, :] = out_ref[...].astype(BF16)
            keeps[1].start()
            if team.paired:
                lower(lambda: [by_way(), matrix_near()])
            else:
                lower(matrix)

        def low_in(step):
            if step == 0:
                for copy in loads[:3]:
                    copy.wait()
                blank(local_sem.at[2]).start()
            span = slice(step * cols, (step + 1) * cols)
            low_ref[:full, :] = in_ref[:full, 0, span].astype(BF16)
            if full < sz.master_pad:
                low_ref[full:, :] = jnp.zeros((sz.master_pad - full, cols), BF16)
            if full < sz.master:
                low_ref[full : full + 16, :] = jnp.concatenate(
                    [in_ref[full : sz.master, 0, span], jnp.zeros((full + 16 - sz.master, cols), F32)], axis=0
                ).astype(BF16)
            w_ref[:, span] = tn(order_ref[: sz.master_pad, :], low_ref[...]).astype(BF16)
            row = lax.broadcasted_iota(jnp.int32, (2 * NSTATE, 2 * NSTATE), 0)
            col = lax.broadcasted_iota(jnp.int32, (2 * NSTATE, 2 * NSTATE), 1)
            one = (row == col).astype(BF16)
            w_ref[2 * sz.channels : sz.dt, span] = nt(one, state_ref[span, :].astype(BF16)).astype(BF16)
            lower(lambda: block(step))

        low_out()
        ahead = 3
        for step in range(ahead):
            low_in(step)
        if team.paired:
            pass_on()
        if team.paired:
            pl.when(jnp.logical_not(straight))(lambda: swaps[0].wait_recv())

        def got_pack(layer):
            ref = pks_ref.at[layer]
            Delivery(ref, ref, pack_send.at[0], pack_recv.at[layer], team.owner(layer), team.alone(layer)).wait_got()

        got_pack(0)
        pl.when(team.alone(0))(lambda: packs[0].near().wait())
        gain = pks_ref[0, GAIN_ROW : GAIN_ROW + 1, :]
        own_ref[...] = norm_rows(first_ref[...].astype(F32), gain).astype(BF16)
        work = [lambda step=step: low_in(step) for step in range(ahead, steps)]
        run_gather(team, parts, own_ref, all_ref, ag_sems, None, work)
        keeps[0].start()
        got_pack(1)
        if team.paired:

            @pl.when(jnp.logical_not(straight))
            def _():
                swaps[1].wait_recv()
                for copy in swaps:
                    copy.wait_send()

        for m, copy in enumerate(packs):
            done = team.alone(0) if m == 0 else jnp.bool_(False)
            pl.when(jnp.logical_not(done))(copy.wait_sent)
        receive()

        @pl.when(section == 0)
        def _():
            for step in range(steps):
                for copy in block(step):
                    copy.wait_sent()
            if team.paired:
                matrix_near().wait_sent()
                by_way().wait_send()
            else:
                for copy in matrix():
                    copy.wait_sent()

        if team.paired:
            pl.when(section == 1)(lambda: on_from().wait_send())
        blank(local_sem.at[2]).wait()
        for copy in keeps:
            copy.wait()

    w_shape = jax.ShapeDtypeStruct((sz.cols, width), BF16)
    wo_shape = jax.ShapeDtypeStruct((sz.channels, width), BF16)
    row_shape = jax.ShapeDtypeStruct((rows, width), BF16)
    return pl.pallas_call(
        kernel,
        out_shape=[
            w_shape, wo_shape, w_shape, wo_shape,
            jax.ShapeDtypeStruct((2, 16, width), F32),
            jax.ShapeDtypeStruct((1, LANES), F32),
            row_shape, row_shape,
            jax.ShapeDtypeStruct((count * rows, width), BF16),
        ],
        in_specs=[ANY_SPEC] * 4 + [VMEM_SPEC] * 4,
        out_specs=[ANY_SPEC] * 4 + [VMEM_SPEC] * 4 + [ANY_SPEC],
        scratch_shapes=[
            pltpu.VMEM((rows, width), BF16),
            pltpu.VMEM(proj_in_t.shape, F32),
            pltpu.VMEM(proj_state.shape, F32),
            pltpu.VMEM(proj_out.shape, F32),
            pltpu.VMEM(order.shape, BF16),
            pltpu.VMEM((sz.master_pad, cols), BF16),
            pltpu.VMEM((sz.cols, width), BF16),
            pltpu.VMEM((sz.channels, width), BF16),
            pltpu.VMEM((LANES - 16, width), BF16),
        ]
        + gather_scratch(parts, team.dims, count)
        + [DMA((4,)), DMA((2,)), DMA((2,)), DMA((2,)), DMA((2,))]
        + [DMA((3 * steps + 1, 2)), DMA((3 * steps + 1,)), DMA((3,))]
        + [pltpu.VMEM((sz.channels, width), BF16), DMA((3,))]
        + [pltpu.VMEM((16, width), F32)],
        compiler_params=params(collective_id),
        name="opening",
    )(proj_in_t, proj_state, proj_out, order, head_part, shared_part, inputs, cotangent)


def column_of(tile, rows):
    row = lax.broadcasted_iota(jnp.int32, (rows, rows), 0)
    lane = lax.broadcasted_iota(jnp.int32, (rows, rows), 1)
    return nt((row == lane).astype(F32), tile, HIGH)[:, 0:1]


def write_stats(stat_ref, squares, out_grad, branch, rows):
    dot = nt(jnp.ones((8, branch.shape[1]), F32), out_grad * branch, HIGH)
    scale = lax.rsqrt(squares / (HEADS * HDIM) + EPS_NORM)
    row = lax.broadcasted_iota(jnp.int32, (8, rows), 0)
    stat_ref[...] = jnp.zeros_like(stat_ref)
    stat_ref[:, :rows] = jnp.where(row == 0, scale, jnp.where(row == 1, dot, 0.0))


def greet_other():
    barrier = pltpu.get_barrier_semaphore()
    other = 1 - lax.axis_index("section")
    pl.semaphore_signal(barrier, inc=1, device_id={"section": other}, device_id_type=MESH)
    pl.semaphore_wait(barrier, 1)
    return other


def add_up(out_ref, mine_ref, got_ref, squares_ref):
    rows, width = out_ref.shape
    step = 16 if rows % 16 == 0 else rows

    def body(i, carry):
        span = pl.ds(pl.multiple_of(i * step, step), step)
        total = mine_ref[span, :].astype(F32) + got_ref[span, :].astype(F32)
        out_ref[span, :] = total
        if squares_ref is not None:
            part = total * total
            for k in range(0, step, 8):
                squares_ref[...] += part[k : k + 8]
        return carry

    lax.fori_loop(0, rows // step, body, 0)


def trade_sections(sums, stacks, squared, collective_id):
    pairs = sums + stacks
    number, summed = len(pairs), len(sums)

    def kernel(*refs):
        ins, outs = refs[: 2 * number], refs[2 * number : 3 * number]
        squares_ref = refs[3 * number]
        boxes = refs[3 * number + 1 : 3 * number + 1 + summed]
        send_sem, recv_sem = refs[3 * number + 1 + summed :]
        squares_ref[...] = jnp.zeros_like(squares_ref)
        section = lax.axis_index("section")
        other = greet_other()

        def go(mine, theirs):
            copies = []
            for k in range(number):
                copy = pltpu.make_async_remote_copy(
                    src_ref=theirs[k],
                    dst_ref=boxes[k] if k < summed else outs[k].at[section],
                    send_sem=send_sem.at[k],
                    recv_sem=recv_sem.at[k],
                    device_id={"section": other},
                    device_id_type=MESH,
                )
                copy.start()
                copies.append(copy)
            for k in range(summed, number):
                outs[k][section] = mine[k][...]
            for k in range(number):
                copies[k].wait()
                if k < summed:
                    add_up(outs[k], mine[k], boxes[k], squares_ref if k < squared else None)

        pl.when(section == 0)(lambda: go(ins[0::2], ins[1::2]))
        pl.when(section == 1)(lambda: go(ins[1::2], ins[0::2]))

    shapes = [jax.ShapeDtypeStruct(a.shape, F32) for a, _ in sums]
    shapes += [jax.ShapeDtypeStruct((2,) + a.shape, a.dtype) for a, _ in stacks]
    shapes.append(jax.ShapeDtypeStruct((8, sums[0][0].shape[1]), F32))
    return pl.pallas_call(
        kernel,
        out_shape=shapes,
        in_specs=[VMEM_SPEC] * (2 * number),
        out_specs=[VMEM_SPEC] * len(shapes),
        scratch_shapes=[pltpu.VMEM(a.shape, a.dtype) for a, _ in sums] + [DMA((number,))] * 2,
        compiler_params=pltpu.CompilerParams(
            collective_id=collective_id, has_side_effects=True, vmem_limit_bytes=VMEM_LIMIT
        ),
        name="trade_sections",
    )(*[a for pair in pairs for a in pair])


def fits(sz):
    return Team(sz.count).paired and sz.tokens * sz.width <= 4 << 20


class Sizes:
    def __init__(self, count, heads, tokens, width):
        self.count = count
        self.heads = heads
        self.padded = heads + heads % 2
        self.channels = self.padded * HDIM
        self.conv = self.channels + 2 * NSTATE
        self.cols = 2 * self.channels + 2 * NSTATE + LANES
        self.dt = 2 * self.channels + 2 * NSTATE
        self.master = heads * COLS
        self.master_pad = -(-self.master // LANES) * LANES
        self.grad_rows = self.master_pad + 2 * NSTATE
        self.tokens = tokens
        self.width = width
        self.blocks = tokens // STRETCH

    def order(self):
        table = np.zeros((self.grad_rows, self.cols), np.float32)
        for head in range(self.heads):
            for j in range(HDIM):
                table[head * COLS + j, head * HDIM + j] = 1
                table[head * COLS + HDIM + j, self.channels + head * HDIM + j] = 1
            table[head * COLS + 2 * HDIM, self.dt + head] = 1
        for j in range(2 * NSTATE):
            table[self.master_pad + j, 2 * self.channels + j] = 1
        return jnp.asarray(table, BF16)

    def head_sum(self):
        table = np.zeros((self.channels, LANES), np.float32)
        for head in range(self.padded):
            table[head * HDIM : (head + 1) * HDIM, head] = 1
        return jnp.asarray(table, F32)


def nt(left, right, precision=None):
    return lax.dot_general(
        left, right, (((1,), (1,)), ((), ())), precision=precision, preferred_element_type=F32
    )


def tn(left, right, precision=None):
    return lax.dot_general(
        left, right, (((0,), (0,)), ((), ())), precision=precision, preferred_element_type=F32
    )


def nn(left, right, precision=None):
    return jnp.dot(left, right, precision=precision, preferred_element_type=F32)


def split(value):
    high = value.astype(BF16)
    return high, (value - high.astype(F32)).astype(BF16)


def fine(dot, left, right, left_axis, right_axis):
    left_high, left_low = split(left)
    right_high, right_low = split(right)
    return dot(
        jnp.concatenate([left_high, left_low, left_high], axis=left_axis),
        jnp.concatenate([right_high, right_high, right_low], axis=right_axis),
    )


def exact(dot, ones, value, axis, ones_first=True):
    ones = ones.astype(BF16)
    high, low = split(value)
    ones_axis = {(nn, True): 1, (nn, False): 0, (nt, True): 1, (nt, False): 1, (tn, True): 0}[dot, ones_first]
    both = jnp.concatenate([ones, ones], axis=ones_axis)
    halves_of = jnp.concatenate([high, low], axis=axis)
    return dot(both, halves_of) if ones_first else dot(halves_of, both)


def nt3(left, right):
    return fine(nt, left, right, 1, 1)


def tn3(left, right):
    return fine(tn, left, right, 0, 0)


def nn3(left, right):
    return fine(nn, left, right, 1, 0)


def softplus(value):
    return jnp.maximum(value, 0.0) + jnp.log1p(jnp.exp(-jnp.abs(value)))


def sigmoid(value):
    return 1.0 / (1.0 + jnp.exp(-value))


def halves(left, right):
    rows = left.shape[0]
    lane = lax.broadcasted_iota(jnp.int32, (rows, LANES), 1)
    return jnp.where(lane < HDIM, left, right)


def lower_mask(size):
    row = lax.broadcasted_iota(jnp.int32, (size, size), 0)
    col = lax.broadcasted_iota(jnp.int32, (size, size), 1)
    return row >= col


def step_rows(log_decay, step):
    lane = lax.broadcasted_iota(jnp.int32, log_decay.shape, 1)
    both = jnp.where(lane < 8, log_decay, pltpu.roll(step, 8, 1))
    return jnp.transpose(jnp.where(lane < 16, both, 0.0))


def to_columns(tile, rows):
    row = lax.broadcasted_iota(jnp.int32, (rows, LANES), 0)
    lane = lax.broadcasted_iota(jnp.int32, (rows, LANES), 1)
    return exact(nt, (row == lane).astype(F32), tile, 1)


def forward_phase(
    count, sz, layer, lengths, gathered, weights, weight_out, pack, residual, cotangent, own, collective_id
):
    block, chunk, chans = STRETCH, CHUNK, sz.channels
    team = Team(count)
    dims = team.dims
    rows, width = residual.shape
    subs = block // chunk
    shards = block // rows
    blocks = sz.blocks
    planes = dims[0]
    per = blocks // planes
    parts = column_parts(width, TEAM_GATHER if team.paired else GATHER)
    scatter = PlaneScatter(team, rows, width)
    turn = cotangent is not None
    passing = own is not None
    cols = 256
    steps = width // cols

    def kernel(*refs):
        refs = list(refs)
        take = lambda number: [refs.pop(0) for _ in range(number)]
        reset_ref, rows_ref, ws_ref, wos_ref, pks_ref, u_ref = take(6)
        cot_ref = refs.pop(0) if turn else None
        w_own, wo_own = take(2) if passing else (None, None)
        result_ref, branch_ref, total_ref, next_ref, p_out, y_out, s_out = take(7)
        stats_ref = refs.pop(0) if turn else None
        ws_next, wos_next = take(2) if passing else (None, None)
        conv_ref, state_ref, w_ref, wo_ref, h_buf, p_buf, y_buf, s_buf, part_ref, sq_ref = take(10)
        load_sem, store_sem, weight_sem = take(3)
        sums_ref, own_ref = take(2)
        scatter_refs = take(5)
        ag_sems = take(3)
        small_send, small_recv = take(2)
        if passing:
            w_mine, wo_mine, zero_ref, own_sem, give_send, give_recv = take(6)
        pk_ref = pks_ref.at[layer]

        def load(c):
            span = pl.ds(pl.multiple_of(c * block, block), block)
            return pltpu.make_async_copy(rows_ref.at[span, :], h_buf.at[c % 2], load_sem.at[c % 2])

        def stores(c):
            slot = c % 2
            span = pl.ds(pl.multiple_of(c * block, block), block)
            return [
                pltpu.make_async_copy(p_buf.at[slot], p_out.at[span, :], store_sem.at[0, slot]),
                pltpu.make_async_copy(y_buf.at[slot], y_out.at[span, :], store_sem.at[1, slot]),
                pltpu.make_async_copy(s_buf.at[slot], s_out.at[pl.ds(c * subs, subs)], store_sem.at[2, slot]),
            ]

        load(0).start()
        weight_copies = [
            pltpu.make_async_copy(ws_ref, w_ref, weight_sem.at[0]),
            pltpu.make_async_copy(wos_ref, wo_ref, weight_sem.at[1]),
        ]
        for copy in weight_copies:
            copy.start()
        if passing:
            section = lax.axis_index("section")
            own_copies = [
                pltpu.make_async_copy(w_own, w_mine, own_sem.at[0]),
                pltpu.make_async_copy(wo_own, wo_mine, own_sem.at[1]),
            ]
            for copy in own_copies:
                copy.start()
            zero_ref[...] = jnp.zeros_like(zero_ref)
            give_block, give_matrix, receive, blank = give_weights(
                team, 1, w_mine, wo_mine, ws_next, wos_next, zero_ref, (give_send, give_recv), sz, steps, cols
            )
            blank(own_sem.at[2]).start()
        greet_all(count, True)
        if passing:
            for copy in own_copies:
                copy.wait()

            @pl.when(section == 1)
            def _():
                for step in range(steps):
                    for copy in give_block(step):
                        copy.start()
                for copy in give_matrix():
                    copy.start()

        conv_ref[...] = jnp.zeros_like(conv_ref)
        state_ref[...] = jnp.zeros_like(state_ref)
        scatter.bind(part_ref, branch_ref, *scatter_refs)
        for copy in weight_copies:
            copy.wait()

        def one_block(c, carry):
            slot = c % 2
            keep = keeps(reset_ref, team.micro(), c)
            span_all = pl.ds(pl.multiple_of(c * block, block), block)
            pl.when(c + 1 < blocks)(lambda: load(c + 1).start())
            load(c).wait()

            @pl.when(c >= 2)
            def _():
                for copy in stores(c - 2):
                    copy.wait()

            h_ref, p_ref, y_ref, s_ref = (buf.at[slot] for buf in (h_buf, p_buf, y_buf, s_buf))
            p_ref[...] = nt(h_ref[...], w_ref[...])
            inner = p_ref[:, chans : 2 * chans]
            state_raw = p_ref[:, 2 * chans : sz.dt].astype(BF16).astype(F32)
            conv_ref[0:8, :] = conv_ref[block : block + 8, :] * keep
            conv_ref[8 : 8 + block, :chans] = inner
            conv_ref[8 : 8 + block, chans:] = state_raw
            pre = pk_ref[CONV : CONV + 1, : sz.conv] + pk_ref[0:1, : sz.conv] * conv_ref[8 : 8 + block, :]
            for tap in range(1, CONV):
                pre = pre + pk_ref[tap : tap + 1, : sz.conv] * conv_ref[8 - tap : 8 - tap + block, :]
            act = pre * sigmoid(pre)
            step = softplus(p_ref[:, sz.dt :] + pk_ref[7:8, :LANES])
            decay = step * pk_ref[8:9, :LANES]
            mask = lower_mask(chunk)
            lower = mask.astype(F32)
            lane = lax.broadcasted_iota(jnp.int32, (chunk, LANES), 1)
            for sub in range(subs):
                span = slice(sub * chunk, (sub + 1) * chunk)
                if sub == 0:
                    state_ref[...] = state_ref[...] * keep
                s_ref[sub] = state_ref[...]
                dt = step[span]
                log_decay = exact(nn, lower, decay[span], 0)
                flat = step_rows(log_decay, dt)
                writer = act[span, chans : chans + NSTATE]
                reader = act[span, chans + NSTATE :]
                cross = nt3(reader, writer)
                for pair in range(sz.padded // 2):
                    cols = slice(pair * LANES, (pair + 1) * LANES)
                    x = act[span, cols]
                    total = jnp.zeros((chunk, LANES), F32)
                    for side in range(2):
                        head = 2 * pair + side
                        gap = log_decay[:, head : head + 1] - flat[head : head + 1, :]
                        weight = cross * jnp.exp(jnp.where(mask, gap, -1e30)) * flat[8 + head : 9 + head, :]
                        part = jnp.where((lane < HDIM) == (side == 0), x, 0.0)
                        total = total + nn3(weight, part)
                    logs = halves(log_decay[:, 2 * pair : 2 * pair + 1], log_decay[:, 2 * pair + 1 : 2 * pair + 2])
                    dts = halves(dt[:, 2 * pair : 2 * pair + 1], dt[:, 2 * pair + 1 : 2 * pair + 2])
                    old = state_ref[:, cols]
                    total = total + jnp.exp(logs) * nn3(reader, old)
                    last = logs[chunk - 1 : chunk, :]
                    moved_in = x * jnp.exp(last - logs) * dts
                    state_ref[:, cols] = jnp.exp(last) * old + tn3(writer, moved_in)
                    y_ref[span, cols] = total + pk_ref[6:7, cols] * x
            z = p_ref[:, :chans]
            gated = y_ref[...] * z * sigmoid(z)
            square = exact(nt, jnp.ones((8, chans), F32), gated * gated, 1)
            for k in range(shards):
                sq_ref[c * shards + k] = square[:, k * rows : (k + 1) * rows]
            high, low = split(gated * pk_ref[5:6, :chans])
            part_ref[span_all, :] = (nn(high, wo_ref[...]) + nn(low, wo_ref[...])).astype(part_ref.dtype)
            for copy in stores(c):
                copy.start()
            if per == 1:
                scatter.step(planes, c + 1, lambda k: k)
            else:
                pl.when(c % per == per - 1)(lambda: scatter.step(planes, c // per + 1, lambda k: k))
            return carry

        lax.fori_loop(0, blocks, one_block, 0)
        me = linear(dims, team.spot())
        copies = start_direct(team, lambda peer: sq_ref.at[peer], sums_ref, small_send, small_recv)
        sums_ref[me] = sq_ref[me]
        scatter.finish(planes, lambda k: k)
        wait_direct(team, sums_ref, copies, small_recv, small_send)
        total = jnp.sum(sums_ref[...], axis=0)
        total_ref[...] = total
        scale = lax.rsqrt(column_of(total, rows) / (HEADS * HDIM) + EPS_NORM)
        branch = branch_ref[...] * scale
        branch_ref[...] = branch
        live_col = live_rows_of(reset_ref, team.micro(), me, rows)
        result = (u_ref[...].astype(F32) + live_col * branch).astype(BF16)
        result_ref[...] = result
        stat = None
        if turn:
            stat_ref, stat_send, stat_recv = refs
            out_grad = (live_col * cot_ref[...].astype(F32)).astype(BF16)
            own_ref[...] = out_grad
            write_stats(stat_ref, total, out_grad.astype(F32), branch, rows)
            stat = (stat_ref, stats_ref, stat_send, stat_recv)
        else:
            gain = pks_ref[layer + 1, GAIN_ROW : GAIN_ROW + 1, :]
            own_ref[...] = norm_rows(result.astype(F32), gain).astype(BF16)
        run_gather(team, parts, own_ref, next_ref, ag_sems, stat)
        for c in range(max(blocks - 2, 0), blocks):
            for copy in stores(c):
                copy.wait()
        scatter.drain()
        if passing:
            receive()

            @pl.when(section == 1)
            def _():
                for step in range(steps):
                    for copy in give_block(step):
                        copy.wait_sent()
                for copy in give_matrix():
                    copy.wait_sent()

            blank(own_sem.at[2]).wait()

    tokens = sz.tokens
    out_shape = [
        jax.ShapeDtypeStruct((rows, width), BF16),
        jax.ShapeDtypeStruct((rows, width), F32),
        jax.ShapeDtypeStruct((8, rows), F32),
        jax.ShapeDtypeStruct((tokens, width), BF16),
        jax.ShapeDtypeStruct((tokens, sz.cols), F32),
        jax.ShapeDtypeStruct((tokens, chans), F32),
        jax.ShapeDtypeStruct((tokens // chunk, NSTATE, chans), F32),
    ]
    out_specs = [VMEM_SPEC] * 3 + [ANY_SPEC] * 4
    scratch = [
        pltpu.VMEM((block + 8, sz.conv), F32),
        pltpu.VMEM((NSTATE, chans), F32),
        pltpu.VMEM((sz.cols, width), BF16),
        pltpu.VMEM((chans, width), BF16),
        pltpu.VMEM((2, block, width), BF16),
        pltpu.VMEM((2, block, sz.cols), F32),
        pltpu.VMEM((2, block, chans), F32),
        pltpu.VMEM((2, subs, NSTATE, chans), F32),
        pltpu.VMEM((tokens, width), scatter.first_type),
        pltpu.VMEM((count, 8, rows), F32),
        DMA((2,)),
        DMA((3, 2)),
        DMA((2,)),
        pltpu.VMEM((count, 8, rows), F32),
        pltpu.VMEM((rows, width), BF16),
    ]
    scratch += scatter.scratch() + gather_scratch(parts, dims, count) + [DMA((count,))] * 2
    operands = [lengths, gathered, weights, weight_out, pack, residual]
    in_specs = [pl.BlockSpec(memory_space=pltpu.SMEM)] + [ANY_SPEC] * 3 + [VMEM_SPEC] * 2
    if turn:
        out_shape.append(jax.ShapeDtypeStruct((count, 8, LANES), F32))
        out_specs.append(VMEM_SPEC)
        scratch += [pltpu.VMEM((8, LANES), F32)] + [DMA((count,))] * 2
        operands.append(cotangent)
        in_specs.append(VMEM_SPEC)
    if passing:
        out_shape += [jax.ShapeDtypeStruct(array.shape, array.dtype) for array in own]
        out_specs += [ANY_SPEC] * 2
        scratch += [pltpu.VMEM(array.shape, array.dtype) for array in own]
        scratch += [pltpu.VMEM((LANES - 16, width), BF16), DMA((3,))]
        scratch += [DMA((3 * steps + 1, 2)), DMA((3 * steps + 1,))]
        operands += list(own)
        in_specs += [ANY_SPEC] * 2
    return pl.pallas_call(
        kernel,
        out_shape=out_shape,
        in_specs=in_specs,
        out_specs=out_specs,
        scratch_shapes=scratch,
        compiler_params=params(collective_id),
        name="forward_phase",
    )(*operands)


def backward_phase(
    count, sz, layer, lengths, out_grads, proj, mixed, states, stats, weights, weight_out, pack, order,
    residual, upstream, below, gathered, upper, collective_id,
):
    block, chunk, chans = STRETCH, CHUNK, sz.channels
    team = Team(count)
    dims = team.dims
    rows, width = residual.shape
    subs = block // chunk
    blocks = sz.blocks
    planes = dims[0]
    per = blocks // planes
    parts = column_parts(width, TEAM_GATHER if team.paired else GATHER)
    scatter = PlaneScatter(team, rows, width)
    more = below is not None
    close = upper is not None
    early = more and fits(sz)
    cols = 256
    steps = width // cols
    ranges = steps

    def kernel(*refs):
        refs = list(refs)
        take = lambda number: [refs.pop(0) for _ in range(number)]
        reset_ref, g_all, p_all, y_all, s_all, ws_ref, wos_ref, orders_ref = take(8)
        st_ref, pks_ref, sum_ref, u_ref, up_ref = take(5)
        if more:
            lower_ref, lower_total = take(2)
        if close:
            h_own, in_upper, out_upper, acc_upper, result_own, result_upper, grad_upper = take(7)
            state_upper, rates_ref = take(2)
            sum_in, sum_out, state_all, sum_small, outs_ref, grads_ref, stats_ref, norm_ref = take(8)
        elif early:
            h_own = refs.pop(0)
            grad_ref, low_grad_ref, acc_ref, in_out, out_out, state_out = take(6)
        else:
            grad_ref, low_grad_ref, acc_ref, gt_out, q_out = take(5)
        if more:
            next_ref, stats_ref = take(2)
        conv_ref, dpre_ref, dact_ref, ddt_ref, dstate_ref = take(5)
        w_ref, wo_ref, order_ref, g_buf, p_buf, halo_buf, y_buf, s_buf, gt_buf, q_buf, part_ref = take(11)
        load_sem, store_sem, weight_sem = take(3)
        scatter_refs = take(5)
        pk_ref = pks_ref.at[layer]
        if close or early:
            gt_full, q_full, h_cols, g_cols, col_sem = take(5)
        if close:
            grad_ref, acc_ref, box_in, box_out, box_small = take(5)
            in_out, out_out = w_ref.at[: sz.master_pad, :], wo_ref
            live_rows = pl.ds(0, -(-sz.master // 16) * 16)
            trade_send, trade_recv, few_send, few_recv = take(4)
            in_buf, out_buf, keep_sem = take(3)
            state_out, squares_ref, state_sums, state_box, pieces_ref, state_own = take(6)
            share_ref, shares_ref, stat_ref, mine_ref, got_ref = take(5)
            state_send, state_recv, piece_send, piece_recv = take(4)
            head_sems = take(3)
            share_send, share_recv, stat_send, stat_recv, pair_send, pair_recv = take(6)
            section = lax.axis_index("section")
            micro = team.micro()

        def g_slot(slot):
            return g_buf.at[pl.ds(pl.multiple_of(slot * block, block), block), :]

        def loads(c):
            slot = c % 2
            span = pl.ds(pl.multiple_of(c * block, block), block)
            before = pl.multiple_of(jnp.maximum(c * block - 8, 0), 8)
            return [
                pltpu.make_async_copy(g_all.at[span, :], g_slot(slot), load_sem.at[0, slot]),
                pltpu.make_async_copy(p_all.at[span, :], p_buf.at[slot], load_sem.at[1, slot]),
                pltpu.make_async_copy(p_all.at[pl.ds(before, 8), :], halo_buf.at[slot], load_sem.at[2, slot]),
                pltpu.make_async_copy(y_all.at[span, :], y_buf.at[slot], load_sem.at[3, slot]),
                pltpu.make_async_copy(s_all.at[pl.ds(c * subs, subs)], s_buf.at[slot], load_sem.at[4, slot]),
            ]

        def stores(c):
            slot = c % 2
            span = pl.ds(pl.multiple_of(c * block, block), block)
            if close or early:
                return []
            return [
                pltpu.make_async_copy(gt_buf.at[slot], gt_out.at[:, span], store_sem.at[0, slot]),
                pltpu.make_async_copy(q_buf.at[slot], q_out.at[span, :], store_sem.at[1, slot]),
            ]

        for copy in loads(blocks - 1):
            copy.start()
        weight_copies = [
            pltpu.make_async_copy(wos_ref, wo_ref, weight_sem.at[0]),
            pltpu.make_async_copy(ws_ref, w_ref, weight_sem.at[1]),
            pltpu.make_async_copy(orders_ref, order_ref, weight_sem.at[2]),
        ]
        for copy in weight_copies:
            copy.start()
        greet_all(count, True)
        dpre_ref[...] = jnp.zeros_like(dpre_ref)
        dstate_ref[...] = jnp.zeros_like(dstate_ref)
        acc_ref[...] = jnp.zeros_like(acc_ref)
        scatter.bind(part_ref, grad_ref, *scatter_refs)
        for copy in weight_copies:
            copy.wait()

        def one_block(i, carry):
            c = blocks - 1 - i
            slot = c % 2
            keep = keeps(reset_ref, team.micro(), c)
            after = keeps(reset_ref, team.micro(), jnp.minimum(c + 1, blocks - 1))
            span_all = pl.ds(pl.multiple_of(c * block, block), block)

            @pl.when(c >= 1)
            def _():
                for copy in loads(c - 1):
                    copy.start()

            for copy in loads(c):
                copy.wait()

            if not (close or early):

                @pl.when(i >= 2)
                def _():
                    for copy in stores(c + 2):
                        copy.wait()

            g_ref = g_slot(slot)
            p_ref, halo_ref, y_ref, s_ref = (buf.at[slot] for buf in (p_buf, halo_buf, y_buf, s_buf))
            if close or early:
                gt_ref, q_ref = gt_full.at[:, span_all], q_full.at[span_all, :]
            else:
                gt_ref, q_ref = gt_buf.at[slot], q_buf.at[slot]
            conv_ref[0:8, :chans] = halo_ref[:, chans : 2 * chans] * keep
            conv_ref[0:8, chans:] = halo_ref[:, 2 * chans : sz.dt].astype(BF16).astype(F32) * keep
            conv_ref[8 : 8 + block, :chans] = p_ref[:, chans : 2 * chans]
            conv_ref[8 : 8 + block, chans:] = p_ref[:, 2 * chans : sz.dt].astype(BF16).astype(F32)
            pre = pk_ref[CONV : CONV + 1, : sz.conv] + pk_ref[0:1, : sz.conv] * conv_ref[8 : 8 + block, :]
            for tap in range(1, CONV):
                pre = pre + pk_ref[tap : tap + 1, : sz.conv] * conv_ref[8 - tap : 8 - tap + block, :]
            gate = sigmoid(pre)
            act = pre * gate
            slope = gate * (1.0 + pre * (1.0 - gate))
            step_in = p_ref[:, sz.dt :] + pk_ref[7:8, :LANES]
            step = softplus(step_in)
            rate = pk_ref[8:9, :LANES]
            decay = step * rate
            z = p_ref[:, :chans]
            zgate = sigmoid(z)
            zsilu = z * zgate
            y = y_ref[...]
            gated = y * zsilu
            gain = pk_ref[5:6, :chans]
            skip = pk_ref[6:7, :chans]
            columns = [to_columns(st_ref[c * (block // rows) + k], rows) for k in range(block // rows)]
            columns = jnp.concatenate(columns, axis=0)
            scale = columns[:, 0:1]
            along = columns[:, 1:2]
            grad_q = nt(g_ref[...], wo_ref[...])
            q_ref[...] = (gated * scale * gain).astype(BF16)
            acc_ref[5:6, :chans] += jnp.sum(grad_q * gated * scale, axis=0, keepdims=True)
            dgated = grad_q * gain * scale - gated * (scale * scale * along * (1.0 / (HEADS * HDIM)))
            dy = dgated * zsilu
            dz = dgated * y * zgate * (1.0 + z * (1.0 - zgate))
            x_all = act[:, :chans]
            acc_ref[6:7, :chans] += jnp.sum(dy * x_all, axis=0, keepdims=True)
            scan_dot = exact(nn, sum_ref[...], dy * (y - skip * x_all), 1, False)
            mask = lower_mask(chunk)
            lower = mask.astype(F32)
            lane = lax.broadcasted_iota(jnp.int32, (chunk, LANES), 1)
            for sub in reversed(range(subs)):
                span = slice(sub * chunk, (sub + 1) * chunk)
                dt = step[span]
                log_decay = exact(nn, lower, decay[span], 0)
                flat = step_rows(log_decay, dt)
                writer = act[span, chans : chans + NSTATE]
                reader = act[span, chans + NSTATE :]
                cross = nt3(reader, writer)
                cross_grad = jnp.zeros((chunk, chunk), F32)
                dreader = jnp.zeros((chunk, NSTATE), F32)
                dwriter = jnp.zeros((chunk, NSTATE), F32)
                fall = jnp.zeros((LANES, chunk), F32)
                row = lax.broadcasted_iota(jnp.int32, (LANES, chunk), 0)
                reach = []
                carried = []
                for pair in range(sz.padded // 2):
                    cols = slice(pair * LANES, (pair + 1) * LANES)
                    x = act[span, cols]
                    g = dy[span, cols]
                    logs = halves(log_decay[:, 2 * pair : 2 * pair + 1], log_decay[:, 2 * pair + 1 : 2 * pair + 2])
                    dts = halves(dt[:, 2 * pair : 2 * pair + 1], dt[:, 2 * pair + 1 : 2 * pair + 2])
                    last = logs[chunk - 1 : chunk, :]
                    old = s_ref[sub, :, cols]
                    dnew = dstate_ref[:, cols]
                    faded = g * jnp.exp(logs)
                    tail = jnp.exp(last - logs)
                    dreader = dreader + nt3(faded, old)
                    ahead = nn3(writer, dnew)
                    dx = g * skip[:, cols] + ahead * tail * dts
                    dwriter = dwriter + nt3(x * tail * dts, dnew)
                    reach.append(x * ahead * tail)
                    carried.append(jnp.sum(old * dnew, axis=0, keepdims=True) * jnp.exp(last))
                    dstate_ref[:, cols] = jnp.exp(last) * dnew + tn3(reader, faded)
                    for side in range(2):
                        head = 2 * pair + side
                        own = (lane < HDIM) == (side == 0)
                        g_own = jnp.where(own, g, 0.0)
                        gap = log_decay[:, head : head + 1] - flat[head : head + 1, :]
                        decays = jnp.exp(jnp.where(mask, gap, -1e30))
                        steps = flat[8 + head : 9 + head, :]
                        spread = nt3(g_own, x) * decays
                        weight = cross * decays * steps
                        dx = dx + tn3(weight, g_own)
                        cross_grad = cross_grad + spread * steps
                        sums = jnp.sum(spread * cross, axis=0, keepdims=True)
                        fall = fall + jnp.where(row == head, sums, 0.0)
                    dact_ref[span, cols] = dx
                dact_ref[span, chans : chans + NSTATE] = dwriter + tn3(cross_grad, reader)
                dact_ref[span, chans + NSTATE :] = dreader + nn3(cross_grad, writer)
                reach = exact(nn, sum_ref[...], jnp.concatenate(reach, axis=1), 1, False)
                carried = exact(nn, sum_ref[...], jnp.broadcast_to(jnp.concatenate(carried, axis=1), (8, chans)), 1, False)[0:1]
                direct = jnp.transpose(fall) + reach
                given = dt * reach
                dlog = scan_dot[span] - dt * direct
                ends = jnp.sum(given, axis=0, keepdims=True) + carried
                at_end = lax.broadcasted_iota(jnp.int32, (chunk, LANES), 0) == chunk - 1
                dlog = dlog + jnp.where(at_end, ends, 0.0)
                ddecay = exact(tn, lower, dlog, 0)
                ddt_ref[span, :] = direct + ddecay * rate
                acc_ref[8:9, :LANES] += jnp.sum(ddecay * dt, axis=0, keepdims=True)
            dstate_ref[...] = dstate_ref[...] * keep
            ddt_raw = ddt_ref[...] * sigmoid(step_in)
            acc_ref[7:8, :LANES] += jnp.sum(ddt_raw, axis=0, keepdims=True)
            dpre_ref[block : block + 8, :] = dpre_ref[0:8, :] * after
            dpre_ref[0:block, :] = dact_ref[...] * slope
            raw = conv_ref[8 : 8 + block, :]
            acc_ref[CONV : CONV + 1, : sz.conv] += jnp.sum(dpre_ref[0:block, :], axis=0, keepdims=True)
            draw = jnp.zeros((block, sz.conv), F32)
            for tap in range(CONV):
                later = dpre_ref[tap : tap + block, :]
                draw = draw + pk_ref[tap : tap + 1, : sz.conv] * later
                acc_ref[tap : tap + 1, : sz.conv] += jnp.sum(raw * later, axis=0, keepdims=True)
            low = jnp.concatenate(
                [dz.astype(BF16), draw.astype(BF16), ddt_raw.astype(BF16)], axis=1
            )
            part_ref[span_all, :] = nn(low, w_ref[...]).astype(part_ref.dtype)
            gt_ref[...] = nt(order_ref[...], low).astype(BF16)
            for copy in stores(c):
                copy.start()
            if per == 1:
                scatter.step(planes, i + 1, lambda k: planes - 1 - k)
            else:
                pl.when(i % per == per - 1)(
                    lambda: scatter.step(planes, i // per + 1, lambda k: planes - 1 - k)
                )
            if close:
                share = -(-ranges // blocks)
                for k in range(share):
                    j = i * share + k
                    pl.when(j < ranges)(lambda j=j: begin(1)(j))
            return carry

        def input_grads():
            gain = pk_ref[GAIN_ROW : GAIN_ROW + 1, :]
            grad, gain_grad = norm_rows_back(u_ref[...].astype(F32), gain, grad_ref[...])
            grad = grad + up_ref[...].astype(F32)
            grad_ref[...] = grad
            acc_ref[GAIN_ROW : GAIN_ROW + 1, :] = gain_grad
            return grad

        def at(j):
            return pl.ds(pl.multiple_of(j * cols, cols), cols)

        def columns(j):
            slot = j % 2
            return [
                pltpu.make_async_copy(h_own.at[:, at(j)], h_cols.at[slot], col_sem.at[0, slot]),
                pltpu.make_async_copy(g_all.at[:, at(j)], g_cols.at[slot], col_sem.at[1, slot]),
            ]

        def weight_step(j, then=None):
            slot = j % 2
            for copy in columns(j):
                copy.wait()

            @pl.when(j + 1 < steps)
            def _():
                for copy in columns(j + 1):
                    copy.start()

            in_out[:, at(j)] = nn(gt_full[: sz.master_pad, :], h_cols[slot]).astype(BF16)
            out_out[:, at(j)] = tn(q_full[...], g_cols[slot]).astype(BF16)
            if then is not None:
                then(j)
            state_out[:, at(j)] = nn(gt_full[sz.master_pad :, :], h_cols[slot]).astype(BF16)

        if close:
            def trade(layer, j):
                ins, outs = (in_upper, out_upper) if layer else (in_out, out_out)
                sets = ((ins, box_in, live_rows), (outs, box_out, slice(None)))
                return [
                    Delivery(
                        src.at[cut, at(j)], dst.at[micro, cut, at(j)],
                        trade_send.at[k, layer, j], trade_recv.at[k, micro, j],
                        team.owner(layer), team.alone(layer),
                    )
                    for k, (src, dst, cut) in enumerate(sets)
                ]

            def each(action):
                def body(j, carry):
                    action(j)
                    return carry

                lax.fori_loop(0, steps, body, 0)

            def begin(layer):
                def action(j):
                    for copy in trade(layer, j):
                        copy.start()

                return action

            few = {}
            for layer_now, sources in (
                (0, (acc_ref, result_own, grad_ref)), (1, (acc_upper, result_upper, grad_upper))
            ):
                for k, (src, dst) in enumerate(zip(sources, (box_small, outs_ref, grads_ref))):
                    few[layer_now, k] = Delivery(
                        src, dst.at[micro], few_send.at[k, layer_now], few_recv.at[k, micro],
                        team.owner(layer_now), team.alone(layer_now),
                    )
            late = ((0, 0), (0, 2))
            for key, copy in few.items():
                if key not in late:
                    copy.start()

        lax.fori_loop(0, blocks, one_block, 0)
        if not close:
            if early:
                for copy in columns(0):
                    copy.start()
            scatter.finish(planes, lambda k: planes - 1 - k)
            grad = input_grads()
            low_grad_ref[...] = grad.astype(BF16)
            if more:
                own_ref, stat_ref, stat_send, stat_recv = take(4)
                out_grad = (live_rows_of(reset_ref, team.micro(), linear(dims, team.spot()), rows) * grad.astype(BF16).astype(F32)).astype(BF16)
                own_ref[...] = out_grad
                write_stats(stat_ref, lower_total[...], out_grad.astype(F32), lower_ref[...], rows)
                work = [lambda j=j: weight_step(j) for j in range(steps)] if early else []
                run_gather(team, parts, own_ref, next_ref, refs, (stat_ref, stats_ref, stat_send, stat_recv), work)
            if not early:
                for c in range(0, min(2, blocks)):
                    for copy in stores(c):
                        copy.wait()
            scatter.drain()
            return

        def made(begin_at, end_at):
            def body(j, carry):
                weight_step(j, begin(0))
                return carry

            lax.fori_loop(begin_at, end_at, body, 0)

        for copy in columns(0):
            copy.start()
        order_of = lambda k: planes - 1 - k
        stops = scatter.extra_steps()
        for extra in range(1, stops + 1):
            scatter.step(planes, planes + extra, order_of)
            made(steps * (extra - 1) // stops, steps * extra // stops)
        squares_ref[...] = jnp.zeros_like(squares_ref)
        each_rows = 16
        for k in range(count):
            for layer_now, ref in enumerate((state_out, state_upper)):
                to = (2 * k + layer_now) * each_rows
                g_buf[to : to + each_rows, :] = ref[k * each_rows : (k + 1) * each_rows, :]
        state_sends, stages = scatter_steps(
            team, column_parts(width, TEAM_SCATTER_SMALL), 2 * each_rows, g_buf, state_sums, state_box,
            state_send, state_recv, True,
        )
        stages[0]()
        scatter.last()
        input_grads()
        for key in late:
            few[key].start()
        for stage in stages[1:]:
            stage()
        passed = [
            Delivery(
                state_sums.at[pl.ds(layer_now * each_rows, each_rows), :], pieces_ref.at[micro],
                piece_send.at[layer_now], piece_recv.at[micro], team.owner(layer_now), team.alone(layer_now),
            )
            for layer_now in range(2)
        ]
        for copy in passed:
            copy.start()

        def sent(layer):
            def action(j):
                for copy in trade(layer, j):
                    copy.wait_sent()

            return action

        for copy in few.values():
            copy.wait_sent()
        for copy in passed:
            copy.wait_sent()

        def got(src, sem, m):
            Delivery(src, src, trade_send.at[0, 0, 0], sem, team.user(m), team.alone(m)).wait_got()

        for m in range(2):
            for k, box in enumerate((box_small, outs_ref, grads_ref)):
                got(box.at[m], few_recv.at[k, m], m)
        sum_small[...] = box_small[0] + box_small[1]
        heads = Heads(count)
        pieces = width // LANES
        me = lax.axis_index("head")
        share_ref[...] = jnp.zeros_like(share_ref)
        share_ref[0:1, :] = sum_small[GAIN_ROW : GAIN_ROW + 1, :]
        share_ref[1 : CONV + 2, : 2 * NSTATE] = sum_small[: CONV + 1, chans : sz.conv]

        def piece(peer):
            return share_ref.at[:, pl.ds(pl.multiple_of((peer % pieces) * LANES, LANES), LANES)]

        shares = start_direct(heads, piece, shares_ref, share_send, share_recv)
        shares_ref[me] = piece(me)[...]
        for m in range(2):
            got(pieces_ref.at[m], piece_recv.at[m], m)
        state_total = pieces_ref[0] + pieces_ref[1]
        state_own[...] = state_total.astype(BF16)
        def kept(j):
            slot = j % 2
            return [
                pltpu.make_async_copy(in_buf.at[slot, live_rows, :], sum_in.at[live_rows, at(j)], keep_sem.at[0, slot]),
                pltpu.make_async_copy(out_buf.at[slot], sum_out.at[:, at(j)], keep_sem.at[1, slot]),
            ]

        stat_copies = []

        def begin_norm():
            each(sent(1))
            each(sent(0))

            def add_up(j, carry):
                @pl.when(j >= 2)
                def _():
                    for copy in kept(j - 2):
                        copy.wait()

                for k, (box, total_ref) in enumerate(((box_in, in_buf), (box_out, out_buf))):
                    for m in range(2):
                        cut = slice(None) if k else live_rows
                        got(box.at[m, cut, at(j)], trade_recv.at[k, m, j], m)
                    count_rows = chans if k else -(-sz.master // 16) * 16
                    total = box[0, :count_rows, at(j)].astype(F32) + box[1, :count_rows, at(j)].astype(F32)
                    total_ref[j % 2, :count_rows, :] = total
                    squares_ref[k : k + 1, at(j)] += jnp.sum(total * total, axis=0, keepdims=True)
                for copy in kept(j):
                    copy.start()
                return carry

            lax.fori_loop(0, steps, add_up, 0)
            wait_direct(heads, shares_ref, shares, share_recv, share_send)
            shared = jnp.sum(shares_ref[...], axis=0)
            taps = sum_small[: CONV + 2, : sz.heads * HDIM]
            skip_sums = nn(sum_small[6:7, :chans], sum_ref[...], HIGH)
            bias = sum_small[7:8, :LANES]
            rate = sum_small[8:9, :LANES] * rates_ref[...]
            lane = lax.broadcasted_iota(jnp.int32, (1, LANES), 1)
            of_heads = jnp.where(lane < sz.heads, bias * bias + rate * rate + skip_sums * skip_sums, 0.0)
            total = jnp.sum(squares_ref[...]) + jnp.sum(taps * taps) + jnp.sum(of_heads)
            total = total + jnp.sum(state_total * state_total)
            total = total + jnp.where(me < pieces, jnp.sum(shared * shared), 0.0)
            row = lax.broadcasted_iota(jnp.int32, (8, LANES), 0)
            stat_ref[...] = jnp.where(row == 7, total, shared)
            stat_copies.extend(start_direct(heads, lambda peer: stat_ref, stats_ref, stat_send, stat_recv))
            stats_ref[me] = stat_ref[...]

        run_gather(
            heads, column_parts(width, GATHER_SMALL), state_own, state_all, head_sems, None,
            [lambda: None] * 4 + [begin_norm],
        )
        wait_direct(heads, stats_ref, stat_copies, stat_recv, stat_send)
        row = lax.broadcasted_iota(jnp.int32, (8, LANES), 0)
        section_sq = stats_ref[0, 7:8, :]
        for k in range(1, count):
            section_sq = section_sq + stats_ref[k, 7:8, :]
        mine_ref[...] = jnp.broadcast_to(section_sq, (8, LANES))
        pair = remote(mine_ref, got_ref, pair_send, pair_recv, {"section": 1 - section})
        pair.start()
        pair.wait()
        norm = jnp.sqrt(mine_ref[...] + got_ref[...])
        threshold = CLIP_COEF * PARAMS**0.5
        norm_ref[...] = jnp.where(row == 0, norm, threshold / jnp.maximum(norm, threshold))
        for j in range(max(steps - 2, 0), steps):
            for copy in kept(j):
                copy.wait()
        for copy in state_sends:
            copy.wait_send()
        scatter.drain()

    tokens = sz.tokens
    state = 2 * NSTATE
    if close:
        out_shape = [
            jax.ShapeDtypeStruct((sz.master_pad, width), F32),
            jax.ShapeDtypeStruct((chans, width), F32),
            jax.ShapeDtypeStruct((state, width), BF16),
            jax.ShapeDtypeStruct((16, width), F32),
            jax.ShapeDtypeStruct((2, rows, width), BF16),
            jax.ShapeDtypeStruct((2, rows, width), F32),
            jax.ShapeDtypeStruct((count, 8, LANES), F32),
            jax.ShapeDtypeStruct((8, LANES), F32),
        ]
        out_specs = [ANY_SPEC] * 3 + [VMEM_SPEC] * 5
    elif early:
        out_shape = [
            jax.ShapeDtypeStruct((rows, width), F32),
            jax.ShapeDtypeStruct((rows, width), BF16),
            jax.ShapeDtypeStruct((16, width), F32),
            jax.ShapeDtypeStruct((sz.master_pad, width), BF16),
            jax.ShapeDtypeStruct((chans, width), BF16),
            jax.ShapeDtypeStruct((state, width), BF16),
        ]
        out_specs = [VMEM_SPEC] * 6
    else:
        out_shape = [
            jax.ShapeDtypeStruct((rows, width), F32),
            jax.ShapeDtypeStruct((rows, width), BF16),
            jax.ShapeDtypeStruct((16, width), F32),
            jax.ShapeDtypeStruct((sz.grad_rows, tokens), BF16),
            jax.ShapeDtypeStruct((tokens, chans), BF16),
        ]
        out_specs = [VMEM_SPEC] * 3 + [ANY_SPEC] * 2
    scratch = [
        pltpu.VMEM((block + 8, sz.conv), F32),
        pltpu.VMEM((block + 8, sz.conv), F32),
        pltpu.VMEM((block, sz.conv), F32),
        pltpu.VMEM((block, LANES), F32),
        pltpu.VMEM((NSTATE, chans), F32),
        pltpu.VMEM((sz.cols, width), BF16),
        pltpu.VMEM((chans, width), BF16),
        pltpu.VMEM((sz.grad_rows, sz.cols), BF16),
        pltpu.VMEM((max(2 * block, 2 * 16 * count) if close else 2 * block, width), BF16),
        pltpu.VMEM((2, block, sz.cols), F32),
        pltpu.VMEM((2, 8, sz.cols), F32),
        pltpu.VMEM((2, block, chans), F32),
        pltpu.VMEM((2, subs, NSTATE, chans), F32),
        pltpu.VMEM((8, LANES) if close or early else (2, sz.grad_rows, block), BF16),
        pltpu.VMEM((8, LANES) if close or early else (2, block, chans), BF16),
        pltpu.VMEM((tokens, width), scatter.first_type),
        DMA((5, 2)),
        DMA((2, 2)),
        DMA((3,)),
    ]
    scratch += scatter.scratch()
    if close or early:
        scratch += [
            pltpu.VMEM((sz.grad_rows, tokens), BF16),
            pltpu.VMEM((tokens, chans), BF16),
            pltpu.VMEM((2, tokens, cols), BF16),
            pltpu.VMEM((2, tokens, cols), BF16),
            DMA((2, 2)),
        ]
    if close:
        scratch += [
            pltpu.VMEM((rows, width), F32),
            pltpu.VMEM((16, width), F32),
            pltpu.VMEM((2, sz.master_pad, width), BF16),
            pltpu.VMEM((2, chans, width), BF16),
            pltpu.VMEM((2, 16, width), F32),
            DMA((2, 2, steps)),
            DMA((2, 2, steps)),
            DMA((3, 2)),
            DMA((3, 2)),
            pltpu.VMEM((2, sz.master_pad, cols), F32),
            pltpu.VMEM((2, chans, cols), F32),
            DMA((2, 2)),
            pltpu.VMEM((state, width), BF16),
            pltpu.VMEM((8, width), F32),
            pltpu.VMEM((32, width), F32),
            pltpu.VMEM((count - 1, 32, width), BF16),
            pltpu.VMEM((2, 16, width), F32),
            pltpu.VMEM((16, width), BF16),
            pltpu.VMEM((8, width), F32),
            pltpu.VMEM((count, 8, LANES), F32),
        ]
        scratch += [pltpu.VMEM((8, LANES), F32)] * 3
        scratch += [DMA((1, count - 1)), DMA((1, count - 1)), DMA((2,)), DMA((2,))]
        scratch += gather_scratch(column_parts(width, GATHER_SMALL), Heads(count).dims, count)
        scratch += [DMA((count,))] * 4 + [DMA, DMA]
    operands = [lengths, out_grads, proj, mixed, states, weights, weight_out, order]
    in_specs = [pl.BlockSpec(memory_space=pltpu.SMEM)] + [ANY_SPEC] * 7 + [VMEM_SPEC] * 5
    operands += [stats, pack, sz.head_sum(), residual, upstream]
    if more:
        out_shape += [
            jax.ShapeDtypeStruct((tokens, width), BF16),
            jax.ShapeDtypeStruct((count, 8, LANES), F32),
        ]
        out_specs += [ANY_SPEC, VMEM_SPEC]
        scratch += [pltpu.VMEM((rows, width), BF16), pltpu.VMEM((8, LANES), F32)]
        scratch += [DMA((count,))] * 2 + gather_scratch(parts, dims, count)
        operands += list(below)
        in_specs += [VMEM_SPEC] * 2
    if close:
        operands += list(upper)
        in_specs += [ANY_SPEC] * 3 + [VMEM_SPEC] * 6
    elif early:
        operands.append(gathered)
        in_specs.append(ANY_SPEC)
    return pl.pallas_call(
        kernel,
        out_shape=out_shape,
        in_specs=in_specs,
        out_specs=out_specs,
        scratch_shapes=scratch,
        compiler_params=params(collective_id),
        name="last_phase" if close else "backward_phase",
    )(*operands)


def weight_grads(sz, grads_t, gathered, scaled, out_grads):
    cols = 256

    split_row = sz.master_pad

    def kernel(gt_ref, h_ref, q_ref, g_ref, in_ref, state_ref, out_ref):
        in_ref[...] = nn(gt_ref[:split_row, :], h_ref[...]).astype(BF16)
        state_ref[...] = nn(gt_ref[split_row:, :], h_ref[...])
        out_ref[...] = tn(q_ref[...], g_ref[...]).astype(BF16)

    tokens, width, chans = sz.tokens, sz.width, sz.channels
    return pl.pallas_call(
        kernel,
        grid=(width // cols,),
        out_shape=[
            jax.ShapeDtypeStruct((sz.master_pad, width), BF16),
            jax.ShapeDtypeStruct((2 * NSTATE, width), F32),
            jax.ShapeDtypeStruct((chans, width), BF16),
        ],
        in_specs=[
            pl.BlockSpec((sz.grad_rows, tokens), lambda i: (0, 0)),
            pl.BlockSpec((tokens, cols), lambda i: (0, i)),
            pl.BlockSpec((tokens, chans), lambda i: (0, 0)),
            pl.BlockSpec((tokens, cols), lambda i: (0, i)),
        ],
        out_specs=[
            pl.BlockSpec((sz.master_pad, cols), lambda i: (0, i)),
            pl.BlockSpec((2 * NSTATE, cols), lambda i: (0, i)),
            pl.BlockSpec((chans, cols), lambda i: (0, i)),
        ],
        compiler_params=pltpu.CompilerParams(vmem_limit_bytes=VMEM_LIMIT),
        name="weight_grads",
    )(grads_t, gathered, scaled, out_grads)


def adam_update(weight, moment, second, gradient, rate, decay):
    moment_new = BETA_ONE * moment + (1.0 - BETA_ONE) * gradient
    second_new = BETA_TWO * second + (1.0 - BETA_TWO) * gradient * gradient
    corrected = moment_new * (1.0 / (1.0 - BETA_ONE**ADAM_STEP))
    corrected_sq = second_new * (1.0 / (1.0 - BETA_TWO**ADAM_STEP))
    weight_new = weight - rate * (corrected / (jnp.sqrt(corrected_sq) + ADAM_EPS) + decay * weight)
    return (weight_new, moment_new, second_new)


def adam_in(sz, clip, grad, weight, moment, second):
    block = LANES
    width = sz.width

    def kernel(clip_ref, g_ref, w_ref, m_ref, v_ref, wn_ref, mn_ref, vn_ref, low_ref):
        scale = clip_ref[0]

        def body(i, carry):
            made = []
            for half in range(2):
                span = pl.ds(pl.multiple_of(i * 16 + half * 8, 8), 8)
                new = adam_update(
                    w_ref[span, 0, :], m_ref[span, 0, :], v_ref[span, 0, :],
                    scale * g_ref[span, :], LEARN_MATRIX, WEIGHT_DECAY,
                )
                wn_ref[span, 0, :] = new[0]
                mn_ref[span, 0, :] = new[1]
                vn_ref[span, 0, :] = new[2]
                made.append(new[0])
            low_ref[pl.ds(pl.multiple_of(i * 16, 16), 16), :] = jnp.concatenate(made, axis=0).astype(BF16)
            return carry

        lax.fori_loop(0, block // 16, body, 0)

    view = pl.BlockSpec((block, 1, width), lambda i: (i, 0, 0))
    flat = pl.BlockSpec((block, width), lambda i: (i, 0))
    shape = jax.ShapeDtypeStruct((sz.master, 1, width), F32)
    return pl.pallas_call(
        kernel,
        grid=(sz.master_pad // block,),
        out_shape=[shape, shape, shape, jax.ShapeDtypeStruct((sz.master, width), BF16)],
        in_specs=[pl.BlockSpec(memory_space=pltpu.SMEM), flat, view, view, view],
        out_specs=[view, view, view, flat],
        compiler_params=pltpu.CompilerParams(vmem_limit_bytes=VMEM_LIMIT),
        name="adam_in",
    )(clip, grad, weight, moment, second)


def adam_plain(clip, grad, weight, moment, second, transposed):
    rows, width = weight.shape
    block = min(256 if transposed else 64, rows)

    def kernel(clip_ref, g_ref, w_ref, m_ref, v_ref, wn_ref, mn_ref, vn_ref, low_ref):
        if transposed:
            row = lax.broadcasted_iota(jnp.int32, (width, width), 0)
            col = lax.broadcasted_iota(jnp.int32, (width, width), 1)
            grad_value = tn(g_ref[...], (row == col).astype(BF16))
        else:
            grad_value = g_ref[...]
        new = adam_update(
            w_ref[...], m_ref[...], v_ref[...], clip_ref[0] * grad_value, LEARN_MATRIX, WEIGHT_DECAY
        )
        wn_ref[...], mn_ref[...], vn_ref[...] = new
        low_ref[...] = new[0].astype(BF16)

    flat = pl.BlockSpec((block, width), lambda i: (i, 0))
    turned = pl.BlockSpec((width, block), lambda i: (0, i))
    shape = jax.ShapeDtypeStruct((rows, width), F32)
    return pl.pallas_call(
        kernel,
        grid=(rows // block,),
        out_shape=[shape, shape, shape, jax.ShapeDtypeStruct((rows, width), BF16)],
        in_specs=[
            pl.BlockSpec(memory_space=pltpu.SMEM), turned if transposed else flat, flat, flat, flat
        ],
        out_specs=[flat] * 4,
        compiler_params=pltpu.CompilerParams(vmem_limit_bytes=VMEM_LIMIT),
        name="adam_plain",
    )(clip, grad, weight, moment, second)


def adam_few(sz, norms, small, stats, rates, head, shared):
    state = 2 * NSTATE
    pieces = sz.width // LANES
    conv = (CONV + 1) * state
    last = (CONV + 2) * HDIM

    def kernel(norm_ref, small_ref, stats_ref, rates_ref, *refs):
        ins, outs, (head_grad, shared_grad) = refs[:6], refs[6:12], refs[12:]
        scale = norm_ref[1:2, 0:1]
        lane = lax.broadcasted_iota(jnp.int32, (1, LANES), 1)
        rate_grad = small_ref[8:9, :LANES] * rates_ref[...]
        for head_at in range(sz.heads):
            row = slice(head_at, head_at + 1)
            cols = slice(head_at * HDIM, (head_at + 1) * HDIM)
            for tap in range(CONV):
                head_grad[row, tap * HDIM : (tap + 1) * HDIM] = small_ref[tap : tap + 1, cols]
            head_grad[row, CONV * HDIM : (CONV + 1) * HDIM] = small_ref[5:6, cols]
            head_grad[row, (CONV + 1) * HDIM : last] = small_ref[CONV : CONV + 1, cols]
            head_grad[row, last : last + 1] = small_ref[7:8, head_at : head_at + 1]
            head_grad[row, last + 1 : last + 2] = rate_grad[:, head_at : head_at + 1]
            head_grad[row, last + 2 : last + 3] = jnp.sum(small_ref[6:7, cols], axis=1, keepdims=True)
        for tap in range(CONV + 1):
            for k in range(state // LANES):
                to = tap * state + k * LANES
                shared_grad[:, to : to + LANES] = stats_ref[k, tap + 1 : tap + 2, :]
        for k in range(pieces):
            shared_grad[:, conv + k * LANES : conv + (k + 1) * LANES] = stats_ref[k, 0:1, :]
        for k, grad in enumerate((head_grad, shared_grad)):
            new = adam_update(*(ref[...] for ref in ins[3 * k : 3 * k + 3]), scale * grad[...], LEARN_VECTOR, 0.0)
            for ref, value in zip(outs[3 * k : 3 * k + 3], new):
                ref[...] = value

    arrays = list(head) + list(shared)
    return pl.pallas_call(
        kernel,
        out_shape=[jax.ShapeDtypeStruct(array.shape, F32) for array in arrays],
        in_specs=[VMEM_SPEC] * 10,
        out_specs=[VMEM_SPEC] * 6,
        scratch_shapes=[pltpu.VMEM(head[0].shape, F32), pltpu.VMEM(shared[0].shape, F32)],
        name="adam_few",
    )(norms, small, stats, rates, *arrays)


def columns_first(array):
    return jnp.transpose(array, (2, 0, 1))


def shards(
    inputs,
    cotangent,
    valid_lengths,
    proj_in,
    proj_in_m,
    proj_in_v,
    proj_state,
    proj_state_m,
    proj_state_v,
    proj_out,
    proj_out_m,
    proj_out_v,
    head_params,
    head_m,
    head_v,
    shared_params,
    shared_m,
    shared_v,
):
    count = lax.axis_size("head")
    rows, width = inputs.shape[1], inputs.shape[2]
    heads = head_params.shape[1]
    tokens = rows * count
    sz = Sizes(count, heads, tokens, width)
    order = sz.order()
    own_in, own_out, lower_in, lower_out, pack, rates, first, cot, rows_zero = opening(
        count, sz, columns_first(proj_in), proj_state[0], proj_out[0], head_params[0], shared_params, order,
        inputs, cotangent, 0,
    )

    kept_zero = forward_phase(
        count, sz, 0, valid_lengths, rows_zero, lower_in, lower_out, pack, first, None, (own_in, own_out), 1
    )
    result_zero, branch_zero, total_zero, rows_one = kept_zero[:4]
    upper_in, upper_out = kept_zero[7:]
    kept_one = forward_phase(
        count, sz, 1, valid_lengths, rows_one, upper_in, upper_out, pack, result_zero, cot, None, 2
    )
    result_one, out_grads_one, stats_one = kept_one[0], kept_one[3], kept_one[7]
    back_one = backward_phase(
        count, sz, 1, valid_lengths, out_grads_one, *kept_one[4:7], stats_one, upper_in, upper_out, pack, order,
        result_zero, cot, (branch_zero, total_zero), rows_one, None, 3,
    )
    out_grads_zero, stats_zero = back_one[-2:]
    grad_one, low_one, acc_one = back_one[:3]

    def run_last(upper):
        return backward_phase(
            count, sz, 0, valid_lengths, out_grads_zero, *kept_zero[4:7], stats_zero, lower_in, lower_out, pack, order,
            first, low_one, None, rows_zero, upper, 4,
        )

    if fits(sz):
        in_one, out_one, state_one = back_one[3:6]
        upper = (rows_zero, in_one, out_one, acc_one, result_zero, result_one, grad_one, state_one, rates)
        grad_in, grad_out, grad_state, small, layer_outs, grad_buffer, all_stats, norms = run_last(upper)
    else:
        grads_t_one, scaled_one = back_one[3:5]
        grad_zero, _, acc_zero, grads_t_zero, scaled_zero = run_last(None)
        lower = weight_grads(sz, grads_t_zero, rows_zero, scaled_zero, out_grads_zero)
        higher = weight_grads(sz, grads_t_one, rows_one, scaled_one, out_grads_one)
        grad_in, grad_out, state_sum, small, layer_outs, grad_buffer, squares = trade_sections(
            [(lower[0], higher[0]), (lower[2], higher[2]), (lower[1], higher[1]), (acc_zero, acc_one)],
            [(result_zero, result_one), (grad_zero, grad_one)],
            2,
            6,
        )
        state_part = state_sum.astype(BF16)
        state_all, all_stats, norms = finish_sums(
            count, sz, [state_part.reshape(16 * count, -1)], small, squares, rates, sz.head_sum(), 5
        )
        grad_state = state_all.reshape(state_part.shape)
    grad_norm, clip = norms[0, 0], norms[1, :1]
    few = adam_few(
        sz, norms, small, all_stats, rates,
        (head_params[0], head_m[0], head_v[0]), (shared_params, shared_m, shared_v),
    )
    new_in = adam_in(
        sz, clip, grad_in, columns_first(proj_in), columns_first(proj_in_m), columns_first(proj_in_v)
    )
    new_out = adam_plain(
        clip, grad_out, proj_out[0], proj_out_m[0], proj_out_v[0], False
    )
    new_state = adam_plain(
        clip, grad_state, proj_state[0], proj_state_m[0], proj_state_v[0], True
    )
    back_view = [jnp.transpose(array, (1, 2, 0)) for array in new_in[:3]]
    return (
        layer_outs[None],
        grad_buffer[None],
        grad_norm,
        back_view[0],
        back_view[1],
        back_view[2],
        new_in[3].T[None],
        new_state[0][None],
        new_state[1][None],
        new_state[2][None],
        new_state[3][None],
        new_out[0][None],
        new_out[1][None],
        new_out[2][None],
        new_out[3][None],
        few[0][None],
        few[1][None],
        few[2][None],
        few[3],
        few[4],
        few[5],
    )


def solution(mesh):
    in_specs = (
        P(None, "head", None),
        P(None, "head", None),
        P(),
        P("section", None, "head"),
        P("section", None, "head"),
        P("section", None, "head"),
        P("section", None, None),
        P("section", None, None),
        P("section", None, None),
        P("section", "head", None),
        P("section", "head", None),
        P("section", "head", None),
        P("section", "head", None),
        P("section", "head", None),
        P("section", "head", None),
        P("section", None),
        P("section", None),
        P("section", None),
    )
    out_specs = (
        P("section", None, "head", None),
        P("section", None, "head", None),
        P(),
        P("section", None, "head"),
        P("section", None, "head"),
        P("section", None, "head"),
        P("section", None, "head"),
        P("section", None, None),
        P("section", None, None),
        P("section", None, None),
        P("section", None, None),
        P("section", "head", None),
        P("section", "head", None),
        P("section", "head", None),
        P("section", "head", None),
        P("section", "head", None),
        P("section", "head", None),
        P("section", "head", None),
        P("section", None),
        P("section", None),
        P("section", None),
    )
    return jax.shard_map(shards, mesh=mesh, in_specs=in_specs, out_specs=out_specs, check_vma=False)
```

```python
import itertools

import jax
import jax.numpy as jnp
import numpy as np
from jax import lax
from jax.experimental import pallas as pl
from jax.experimental.pallas import tpu as pltpu
from jax.sharding import PartitionSpec as P

HEADS = 64
HDIM = 64
NSTATE = 128
CONV = 4
STRETCH = 256
ADAM_STEP = 5
PARAMS = 51698560

HIGH = lax.Precision.HIGHEST
EPS_NORM = 1e-05
ADAM_EPS = 1e-08
BETA_ONE = 0.5
BETA_TWO = 0.5
CLIP_COEF = 0.2
LEARN_MATRIX = 0.02
LEARN_VECTOR = 0.2
WEIGHT_DECAY = 0.1

F32 = jnp.float32
BF16 = jnp.bfloat16
MESH = pl.DeviceIdType.MESH
LANES = 128
CHUNK = 128
COLS = HDIM * 2 + 1
GAIN_ROW = 9
VMEM_LIMIT = 58 << 20


def keeps(lengths_ref, micro, block):
    return jnp.where(lengths_ref[micro, block] > 0, 0.0, 1.0)


def live_rows_of(lengths_ref, micro, shard, rows):
    token = shard * rows
    own_block = token // STRETCH
    start, length = jnp.int32(0), lengths_ref[micro, 0]
    for block in range(1, lengths_ref.shape[1]):
        here = lengths_ref[micro, block]
        begins = (here > 0) & (block <= own_block)
        start = jnp.where(begins, block, start)
        length = jnp.where(begins, here, length)
    position = token - start * STRETCH + lax.broadcasted_iota(jnp.int32, (rows, 1), 0)
    return (position < length).astype(F32)


def chip_dims(count):
    side = 4 if count % 64 == 0 else 2
    if count % (side * side) != 0:
        return (count, 1, 1)
    return (count // (side * side), side, side)


def place(dims):
    me = lax.axis_index("head")
    return (me // (dims[1] * dims[2]), (me // dims[2]) % dims[1], me % dims[2])


class Heads:
    def __init__(self, count):
        self.count = count
        self.dims = chip_dims(count)
        self.lined = False

    def spot(self):
        return place(self.dims)

    def device(self, index):
        return {"head": index}


class Team:
    def __init__(self, count):
        self.count = count
        self.chips = chip_dims(count)
        self.paired = self.chips[2] == 2
        self.lined = True
        self.dims = self.chips[:2] + (2,) if self.paired else self.chips

    def spot(self):
        spot = place(self.chips)
        return spot[:2] + (lax.axis_index("section"),) if self.paired else spot

    def device(self, index):
        if not self.paired:
            return {"head": index}
        return {"section": index % 2, "head": index // 2 * 2 + lax.axis_index("head") % 2}

    def micro(self):
        return lax.axis_index("head") % 2 if self.paired else lax.axis_index("section")

    def owner(self, layer):
        if not self.paired:
            return {"section": layer}
        return {"section": layer, "head": lax.axis_index("head") // 2 * 2 + lax.axis_index("section")}

    def user(self, micro):
        if not self.paired:
            return {"section": micro}
        head = lax.axis_index("head")
        return {"section": head % 2, "head": head // 2 * 2 + micro}

    def alone(self, which):
        section = lax.axis_index("section")
        if not self.paired:
            return section == which
        return (lax.axis_index("head") % 2 == section) & (section == which)


def linear(dims, spot):
    return (spot[0] * dims[1] + spot[1]) * dims[2] + spot[2]


def moved(dims, spot, shifts):
    return tuple(s if d == 0 else (s + d) % n for s, d, n in zip(spot, shifts, dims))


def shift_of(order, offsets):
    out = [0, 0, 0]
    for axis, off in zip(order, offsets):
        out[axis] = off
    return out


def greet_all(count, pair=False):
    barrier = pltpu.get_barrier_semaphore()
    me = lax.axis_index("head")
    section = lax.axis_index("section")
    for off in range(1, count):
        peer = (me + off) % count
        pl.semaphore_signal(barrier, inc=1, device_id={"head": peer}, device_id_type=MESH)
        if pair:
            there = {"section": 1 - section, "head": peer}
            pl.semaphore_signal(barrier, inc=1, device_id=there, device_id_type=MESH)
    if pair:
        pl.semaphore_signal(barrier, inc=1, device_id={"section": 1 - section}, device_id_type=MESH)
    pl.semaphore_wait(barrier, 2 * count - 1 if pair else count - 1)


def rows_at(shard, rows):
    return pl.ds(pl.multiple_of(shard * rows, rows), rows)


def column_parts(width, shares):
    tiles = width // LANES
    parts, start, taken = [], 0, 0
    for share, order, group in shares:
        taken += share
        stop = tiles * taken // 16 * LANES
        if stop > start:
            parts.append((start, stop - start, order, group))
            start = stop
    return parts


TEAM_GATHER = ((3, (1, 0, 2), 0), (7, (0, 1, 2), 0), (6, (0, 1, 2), 0))
GATHER = ((2, (2, 1, 0), 0), (2, (1, 2, 0), 0), (6, (0, 2, 1), 0), (6, (0, 1, 2), 0))
GATHER_SMALL = ((8, (0, 2, 1), 0), (8, (0, 1, 2), 0))
SCATTER = (
    (1, (2, 0, 1), 0), (1, (1, 0, 2), 0), (1, (0, 1, 2), 0), (1, (0, 2, 1), 0),
    (3, (2, 1, 0), 0), (3, (1, 2, 0), 0), (3, (2, 1, 0), 1), (3, (1, 2, 0), 1),
)
TEAM_SCATTER_SMALL = ((16, (2, 1, 0), 0),)
SCATTER_SMALL = ((8, (2, 1, 0), 0), (8, (1, 2, 0), 0))
SCATTER_PACE = (0.3, 0.9, 0.7, 2.0)


def guarded(preds, action):
    preds = [pred for pred in preds if pred is not None]
    if not preds:
        action()
        return
    cond = preds[0]()
    for pred in preds[1:]:
        cond = jnp.logical_and(cond, pred())
    pl.when(cond)(action)


def gather_steps(group, parts, rows, own_ref, all_ref, send_sem, recv_sem, between=()):
    dims = group.dims
    spot = group.spot()
    me = linear(dims, spot)
    waits = []
    counter = [0] * len(parts)

    def lined(axis):
        return group.lined and axis == 0 and dims[0] > 2 and dims[1] == 2

    def above(axis, dist):
        return lambda: spot[axis] + dist < dims[axis]

    def below(axis, dist):
        return lambda: spot[axis] >= dist

    def sources(part, pos):
        axis = parts[part][2][pos]
        if not lined(axis):
            return [(off, None) for off in range(1, dims[axis])]
        out = []
        for dist in range(1, dims[axis]):
            out.append((dist, above(axis, dist)))
            out.append((-dist, below(axis, dist)))
        return out

    def block(part, offsets):
        start, width, order, _ = parts[part]
        shard = linear(dims, moved(dims, spot, shift_of(order, offsets)))
        return shard, all_ref.at[rows_at(shard, rows), pl.ds(start, width)]

    def push(part, offsets, pos, preds, src, came):
        axis = parts[part][2][pos]
        shard, dst = block(part, offsets)
        up, down = (1, above(axis, 1)), (-1, below(axis, 1))
        if lined(axis):
            targets = [up, down] if came == 0 else [down] if came > 0 else [up]
        else:
            targets = [(off, None) for off in range(1, dims[axis])] if came == 0 else []
        for off, pred in targets:
            peer = linear(dims, moved(dims, spot, shift_of((axis,), (off,))))
            number = counter[part]
            counter[part] += 1

            def begin(peer=peer, number=number):
                pltpu.make_async_remote_copy(
                    src_ref=dst if src is None else src,
                    dst_ref=dst,
                    send_sem=send_sem.at[part, number],
                    recv_sem=recv_sem.at[part, shard],
                    device_id=group.device(peer),
                    device_id_type=MESH,
                ).start()

            guarded([pred], begin)
            waits.append((preds + [pred], part, number))

    def visit(part, offsets, preds, pos, came):
        def body():
            shard, dst = block(part, offsets)
            pltpu.make_async_remote_copy(
                src_ref=dst,
                dst_ref=dst,
                send_sem=send_sem.at[part, 0],
                recv_sem=recv_sem.at[part, shard],
                device_id=group.device(me),
                device_id_type=MESH,
            ).wait_recv()
            push(part, offsets, pos, preds, None, came)
            for later in range(pos + 1, 3):
                push(part, offsets, later, preds, None, 0)

        guarded(preds, body)

    for pos in range(3):
        for part, (start, width, _, _) in enumerate(parts):
            push(part, (0, 0, 0), pos, [], own_ref.at[:, pl.ds(start, width)], 0)
    todo = []
    for part in range(len(parts)):
        first, second, third = (sources(part, pos) for pos in range(3))
        for k, (oa, pa) in enumerate(first):
            todo.append(((0, k, part), part, (oa, 0, 0), [pa], 0, oa))
        for ka, (oa, pa) in enumerate([(0, None)] + first):
            for k, (ob, pb) in enumerate(second):
                todo.append(((1, ka + k, part), part, (oa, ob, 0), [pa, pb], 1, ob))
            for kb, (ob, pb) in enumerate([(0, None)] + second):
                for k, (oc, pc) in enumerate(third):
                    todo.append(
                        ((2, ka + kb + k, part), part, (oa, ob, oc), [pa, pb, pc], 2, oc)
                    )
    todo.sort(key=lambda entry: (sum(abs(off) for off in entry[2]), entry[0]))
    between = list(between)
    for _, part, offsets, preds, pos, came in todo:
        if between:
            between.pop(0)()
        visit(part, offsets, preds, pos, came)
    for work in between:
        work()
    for preds, part, number in waits:

        def settle(part=part, number=number):
            start, width, _, _ = parts[part]
            ref = own_ref.at[:, pl.ds(start, width)]
            pltpu.make_async_remote_copy(
                src_ref=ref,
                dst_ref=ref,
                send_sem=send_sem.at[part, number],
                recv_sem=recv_sem.at[part, 0],
                device_id=group.device(me),
                device_id_type=MESH,
            ).wait_send()

        guarded(preds, settle)


def gather_sends(dims):
    return 3 * dims[0] * dims[1] * dims[2]


def scatter_steps(group, parts, rows, in_ref, out_ref, box_ref, send_sem, recv_sem, staged=False):
    dims = group.dims
    spot = group.spot()
    me = linear(dims, spot)
    sends = []

    def size(part, pos):
        return dims[parts[part][2][pos]]

    def slot_one(part, ea, ob, oc):
        return ((ea - 1) * size(part, 1) + ob) * size(part, 2) + oc

    def slot_two(part, eb, oc):
        base = (size(part, 0) - 1) * size(part, 1) * size(part, 2)
        return base + (eb - 1) * size(part, 2) + oc

    def slot_three(part, ec):
        return slot_two(part, size(part, 1), 0) + ec - 1

    def cols(part):
        return pl.ds(parts[part][0], parts[part][1])

    def mine(part, offsets):
        shard = linear(dims, moved(dims, spot, shift_of(parts[part][2], offsets)))
        return in_ref.at[rows_at(shard, rows), cols(part)]

    def send(part, src, pos, off, slot):
        peer = linear(dims, moved(dims, spot, shift_of((parts[part][2][pos],), (off,))))
        copy = pltpu.make_async_remote_copy(
            src_ref=src,
            dst_ref=box_ref.at[slot, :, cols(part)],
            send_sem=send_sem.at[part, slot],
            recv_sem=recv_sem.at[part, slot],
            device_id=group.device(peer),
            device_id_type=MESH,
        )
        copy.start()
        sends.append(copy)

    def arrived(part, slot):
        ref = box_ref.at[slot, :, cols(part)]
        pltpu.make_async_remote_copy(
            src_ref=ref,
            dst_ref=ref,
            send_sem=send_sem.at[part, slot],
            recv_sem=recv_sem.at[part, slot],
            device_id=group.device(me),
            device_id_type=MESH,
        ).wait_recv()
        return ref[...].astype(F32)

    def combined(part, ob, oc, stages):
        total = mine(part, (0, ob, oc))[...].astype(F32)
        for ea in range(1, size(part, 0)):
            total = total + arrived(part, slot_one(part, ea, ob, oc))
        for eb in range(1, size(part, 1)) if stages > 1 else ():
            total = total + arrived(part, slot_two(part, eb, oc))
        for ec in range(1, size(part, 2)) if stages > 2 else ():
            total = total + arrived(part, slot_three(part, ec))
        return total

    def put_by(part, ob, oc, total):
        if size(part, 0) > 1:
            hold = box_ref.at[slot_one(part, 1, ob, oc), :, cols(part)]
        elif size(part, 1) > 1 and ob == 0:
            hold = box_ref.at[slot_two(part, 1, oc), :, cols(part)]
        else:
            return mine(part, (0, ob, oc))
        hold[...] = total.astype(box_ref.dtype)
        return hold

    def first(part, ob, oc, off):
        slot = slot_one(part, size(part, 0) - off, ob, oc)
        send(part, mine(part, (off, ob, oc)), 0, off, slot)

    def second(part, ob, oc, _):
        hold = put_by(part, ob, oc, combined(part, ob, oc, 1))
        send(part, hold, 1, ob, slot_two(part, size(part, 1) - ob, oc))

    def third(part, _, oc, __):
        hold = put_by(part, 0, oc, combined(part, 0, oc, 2))
        send(part, hold, 2, oc, slot_three(part, size(part, 2) - oc))

    def last(part, _, __, ___):
        out_ref[:, cols(part)] = combined(part, 0, 0, 3)

    lag, rest, turn, end = SCATTER_PACE
    program = []
    for part, (_, _, _, late) in enumerate(parts):
        for ob, oc in itertools.product(range(size(part, 1)), range(size(part, 2))):
            for off in range(1, size(part, 0)):
                rank = (0.0 if ob else rest) + late * lag
                program.append((rank, oc == 0, off, part, first, ob, oc))
            if ob:
                program.append((turn + late * lag, oc == 0, 0, part, second, ob, oc))
        for oc in range(1, size(part, 2)):
            program.append((end + late * lag, False, 0, part, third, 0, oc))
        program.append((3.0 + late * lag, True, 0, part, last, 0, 0))
    program.sort(key=lambda step: step[:4])

    def run(low, high):
        for rank, _, off, part, action, ob, oc in program:
            if low <= rank < high:
                action(part, ob, oc, off)

    if staged:
        marks = (-1.0, turn, end, 3.0, 9.0)
        return sends, [lambda k=k: run(marks[k], marks[k + 1]) for k in range(4)]
    run(-1.0, 99.0)
    return sends


PIECES = 1


class PlaneScatter:
    def __init__(self, group, rows, width):
        self.group, self.dims, self.rows = group, group.dims, rows
        self.wide = group.paired
        self.orders = ((2, 1),) * PIECES if self.wide else ((2, 1), (1, 2))
        self.half = width // len(self.orders)
        self.width = width
        depth = self.dims[0]
        most = max(self.dims[1], self.dims[2])
        self.one = depth * (most - 1) * most
        self.two = depth * (most - 1)
        self.slots = self.one + self.two + 2 * depth
        self.first_type = F32 if self.wide else BF16

    def scratch(self):
        parts = len(self.orders)
        later = self.two + 2 * self.dims[0]
        return [
            pltpu.VMEM((self.one, self.rows, self.width), self.first_type),
            pltpu.VMEM((later, self.rows, self.width), BF16),
            pltpu.VMEM((self.two + self.dims[0] if self.wide else 1, self.rows, self.width), BF16),
            DMA((parts, self.slots)),
            DMA((parts, self.slots)),
        ]

    def bind(self, part_ref, out_ref, first_ref, later_ref, hold_ref, send_sem, recv_sem):
        self.part_ref, self.out_ref = part_ref, out_ref
        self.first_ref, self.later_ref, self.hold_ref = first_ref, later_ref, hold_ref
        self.send_sem, self.recv_sem = send_sem, recv_sem
        self.spot = self.group.spot()
        self.me = linear(self.dims, self.spot)

    def sizes(self, part):
        a, b = self.orders[part]
        return self.dims[a], self.dims[b]

    def slot_one(self, part, plane, ea, ob):
        size_a, size_b = self.sizes(part)
        return (plane * (size_a - 1) + ea - 1) * size_b + ob

    def slot_two(self, part, plane, eb):
        return self.one + plane * (self.sizes(part)[1] - 1) + eb - 1

    def slot_three(self, plane, below):
        return self.one + self.two + 2 * plane + below

    def cols(self, part):
        return pl.ds(part * self.half, self.half)

    def mine(self, part, plane, oa, ob):
        shift = shift_of(self.orders[part], (oa, ob))
        spot = moved(self.dims, (plane, self.spot[1], self.spot[2]), shift)
        return self.part_ref.at[rows_at(linear(self.dims, spot), self.rows), self.cols(part)]

    def box(self, part, slot, begun):
        if begun:
            return self.first_ref.at[slot, :, self.cols(part)]
        return self.later_ref.at[slot - self.one, :, self.cols(part)]

    def copy(self, part, src, slot, sent, peer, begun=False):
        return remote(
            src,
            self.box(part, slot, begun),
            self.send_sem.at[part, sent],
            self.recv_sem.at[part, slot],
            self.group.device(peer),
        )

    def hold(self, part, plane, oa, ob, slot):
        if self.wide:
            return self.hold_ref.at[slot - self.one, :, self.cols(part)]
        return self.mine(part, plane, oa, ob)

    def peer(self, part, pos, off):
        shift = shift_of((self.orders[part][pos],), (off,))
        return linear(self.dims, moved(self.dims, self.spot, shift))

    def arrived(self, part, slot, begun=False):
        ref = self.box(part, slot, begun)
        self.copy(part, ref, slot, slot, self.me, begun).wait_recv()
        return ref[...].astype(F32)

    def first(self, plane):
        for inner in (1, 0):
            for part in range(len(self.orders)):
                size_a, size_b = self.sizes(part)
                for ob in range(size_b):
                    if (ob != 0) != bool(inner):
                        continue
                    for off in range(1, size_a):
                        slot = self.slot_one(part, plane, size_a - off, ob)
                        src = self.mine(part, plane, off, ob)
                        self.copy(part, src, slot, slot, self.peer(part, 0, off), True).start()

    def second(self, plane):
        for part in range(len(self.orders)):
            size_a, size_b = self.sizes(part)
            for ob in range(1, size_b):
                slot = self.slot_two(part, plane, size_b - ob)
                total = self.mine(part, plane, 0, ob)[...].astype(F32)
                for ea in range(1, size_a):
                    total = total + self.arrived(part, self.slot_one(part, plane, ea, ob), True)
                hold = self.hold(part, plane, 0, ob, slot)
                hold[...] = total.astype(BF16)
                self.copy(part, hold, slot, slot, self.peer(part, 1, ob)).start()

    def third(self, plane, place_in_line):
        depth = self.spot[0]
        above = depth > plane
        place_here = jnp.where(above, self.dims[0] - 1 - depth, depth)

        def own_total(part):
            size_a, size_b = self.sizes(part)
            total = self.mine(part, plane, 0, 0)[...].astype(F32)
            for ea in range(1, size_a):
                total = total + self.arrived(part, self.slot_one(part, plane, ea, 0), True)
            for eb in range(1, size_b):
                total = total + self.arrived(part, self.slot_two(part, plane, eb))
            return total

        if place_in_line == 0:

            @pl.when(plane == depth)
            def _():
                for part in range(len(self.orders)):
                    self.out_ref[:, self.cols(part)] = own_total(part)

        @pl.when((plane != depth) & (place_here == place_in_line))
        def _():
            below = jnp.where(above, 0, 1)
            onward = jnp.where(above, depth - 1, depth + 1)
            peer = linear(self.dims, (onward, self.spot[1], self.spot[2]))
            slot = self.slot_three(plane, below)
            for part in range(len(self.orders)):
                total = own_total(part)
                if place_in_line > 0:
                    total = total + self.arrived(part, slot)
                hold = self.hold(part, plane, 0, 0, self.one + self.two + plane)
                hold[...] = total.astype(BF16)
                self.copy(part, hold, slot, slot, peer).start()

    def last(self):
        depth = self.spot[0]
        for below, there in ((0, depth < self.dims[0] - 1), (1, depth > 0)):

            @pl.when(there)
            def _(below=below):
                for part in range(len(self.orders)):
                    total = self.out_ref[:, self.cols(part)]
                    total = total + self.arrived(part, self.slot_three(depth, below))
                    self.out_ref[:, self.cols(part)] = total

    def step(self, number, made, plane_of):
        actions = [self.first, self.second]
        actions += [lambda plane, k=k: self.third(plane, k) for k in range(max(self.dims[0] - 1, 1))]
        for back, action in enumerate(actions):
            k = made - 1 - back
            if isinstance(made, int):
                if 0 <= k < number:
                    action(plane_of(k))
            else:
                pl.when(k >= 0)(lambda k=k, action=action: action(plane_of(k)))

    def extra_steps(self):
        return 1 + max(self.dims[0] - 1, 1)

    def finish(self, number, plane_of, begun=0):
        for extra in range(1 + begun, self.extra_steps() + 1):
            self.step(number, number + extra, plane_of)
        self.last()

    def drain(self):
        for part in range(len(self.orders)):
            size_a, size_b = self.sizes(part)
            early, late = self.box(part, 0, True), self.box(part, self.one, False)
            for plane in range(self.dims[0]):
                for ea in range(1, size_a):
                    for ob in range(size_b):
                        slot = self.slot_one(part, plane, ea, ob)
                        self.copy(part, early, slot, slot, self.me, True).wait_send()
                for eb in range(1, size_b):
                    slot = self.slot_two(part, plane, eb)
                    self.copy(part, late, slot, slot, self.me).wait_send()
            for off in range(1, self.dims[0]):
                plane = (self.spot[0] + off) % self.dims[0]
                slot = self.slot_three(plane, jnp.where(self.spot[0] > plane, 0, 1))
                self.copy(part, late, slot, slot, self.me).wait_send()


def start_direct(group, own_ref_of, box_ref, send_sem, recv_sem):
    count = group.count
    me = linear(group.dims, group.spot())
    copies = []
    for off in range(1, count):
        peer = (me + off) % count
        copy = pltpu.make_async_remote_copy(
            src_ref=own_ref_of(peer),
            dst_ref=box_ref.at[me],
            send_sem=send_sem.at[off],
            recv_sem=recv_sem.at[count - off],
            device_id=group.device(peer),
            device_id_type=MESH,
        )
        copy.start()
        copies.append(copy)
    return copies


def wait_direct(group, box_ref, copies, recv_sem, send_sem):
    count = group.count
    me = linear(group.dims, group.spot())
    for off in range(1, count):
        ref = box_ref.at[(me + off) % count]
        pltpu.make_async_remote_copy(
            src_ref=ref,
            dst_ref=ref,
            send_sem=send_sem.at[off],
            recv_sem=recv_sem.at[off],
            device_id=group.device(me),
            device_id_type=MESH,
        ).wait_recv()
    for copy in copies:
        copy.wait_send()


def remote(src, dst, send_sem, recv_sem, device):
    return pltpu.make_async_remote_copy(
        src_ref=src, dst_ref=dst, send_sem=send_sem, recv_sem=recv_sem, device_id=device, device_id_type=MESH
    )


class Delivery:
    def __init__(self, src, dst, send_sem, recv_sem, device, alone):
        self.alone = alone
        self.ends = src, dst, send_sem, recv_sem, device

    def near(self):
        return pltpu.make_async_copy(*self.ends[:3])

    def far(self):
        return remote(*self.ends)

    def start(self):
        pl.when(self.alone)(lambda: self.near().start())
        pl.when(jnp.logical_not(self.alone))(lambda: self.far().start())

    def wait_sent(self):
        pl.when(self.alone)(lambda: self.near().wait())
        pl.when(jnp.logical_not(self.alone))(lambda: self.far().wait_send())

    def wait_got(self):
        pl.when(jnp.logical_not(self.alone))(lambda: self.far().wait_recv())


VMEM_SPEC = pl.BlockSpec(memory_space=pltpu.VMEM)
ANY_SPEC = pl.BlockSpec(memory_space=pl.ANY)
DMA = pltpu.SemaphoreType.DMA


def params(collective_id):
    return pltpu.CompilerParams(
        collective_id=collective_id, has_side_effects=True, vmem_limit_bytes=VMEM_LIMIT
    )


def gather_scratch(parts, dims, count):
    return [DMA((len(parts), gather_sends(dims))), DMA((len(parts), count)), DMA]


def run_gather(group, parts, own_ref, all_ref, sems, stat=None, between=()):
    rows = own_ref.shape[0]
    me = linear(group.dims, group.spot())
    send_sem, recv_sem, local_sem = sems
    local = pltpu.make_async_copy(own_ref, all_ref.at[rows_at(me, rows)], local_sem)
    local.start()
    if stat is not None:
        stat_ref, box_ref, small_send, small_recv = stat
        copies = start_direct(group, lambda peer: stat_ref, box_ref, small_send, small_recv)
        box_ref[me] = stat_ref[...]
    gather_steps(group, parts, rows, own_ref, all_ref, send_sem, recv_sem, between)
    if stat is not None:
        wait_direct(group, box_ref, copies, small_recv, small_send)
    local.wait()


def scatter_scratch(parts, count, rows, width):
    slots = max(count - 1, 1)
    return [pltpu.VMEM((slots, rows, width), BF16), DMA((len(parts), slots)), DMA((len(parts), slots))]


def finish_sums(count, sz, states, small, squares, rates, head_sum, collective_id):
    team, heads = Team(count), Heads(count)
    width = states[0].shape[1]
    rows = states[0].shape[0] // count
    layers = len(states)
    back = column_parts(width, TEAM_SCATTER_SMALL if layers > 1 else SCATTER_SMALL)
    parts = column_parts(width, GATHER_SMALL)
    chans, state = sz.channels, 2 * NSTATE
    pieces = sz.width // LANES
    threshold = CLIP_COEF * PARAMS**0.5

    def kernel(*refs):
        refs = list(refs)
        take = lambda number: [refs.pop(0) for _ in range(number)]
        in_refs = take(layers)
        small_ref, squares_ref, rates_ref, sum_ref = take(4)
        all_ref, stats_ref, norm_ref = take(3)
        share_ref, sums_ref, out_ref, own_ref, stat_ref, mine_ref, got_ref = take(7)
        scatter_refs, ag_sems = take(3), take(3)
        if layers > 1:
            both_ref, pieces_ref, piece_send, piece_recv = take(4)
        small_send, small_recv, stat_send, stat_recv, pair_send, pair_recv = take(6)
        me = lax.axis_index("head")
        section = lax.axis_index("section")
        share_ref[...] = jnp.zeros_like(share_ref)
        share_ref[0:1, :] = small_ref[GAIN_ROW : GAIN_ROW + 1, :]
        share_ref[1 : CONV + 2, :state] = small_ref[: CONV + 1, chans : chans + state]

        def piece(peer):
            return share_ref.at[:, pl.ds(pl.multiple_of((peer % pieces) * LANES, LANES), LANES)]

        greet_all(count, True)
        copies = start_direct(heads, piece, sums_ref, small_send, small_recv)
        sums_ref[me] = piece(me)[...]
        if layers > 1:
            for k in range(count):
                for layer in range(layers):
                    to = slice((k * layers + layer) * rows, (k * layers + layer + 1) * rows)
                    both_ref[to, :] = in_refs[layer][k * rows : (k + 1) * rows, :]
            sends = scatter_steps(team, back, rows * layers, both_ref, out_ref, *scatter_refs)
            micro = team.micro()
            passed = [
                Delivery(
                    out_ref.at[pl.ds(layer * rows, rows), :], pieces_ref.at[micro],
                    piece_send.at[layer], piece_recv.at[micro], team.owner(layer), team.alone(layer),
                )
                for layer in range(layers)
            ]
            for copy in passed:
                copy.start()
            for copy in passed:
                copy.wait_sent()
            for m in range(2):
                ref = pieces_ref.at[m]
                Delivery(ref, ref, piece_send.at[0], piece_recv.at[m], team.user(m), team.alone(m)).wait_got()
            state_own = pieces_ref[0] + pieces_ref[1]
        else:
            sends = scatter_steps(heads, back, rows, in_refs[0], out_ref, *scatter_refs)
            state_own = out_ref[...]
        wait_direct(heads, sums_ref, copies, small_recv, small_send)
        shared = jnp.sum(sums_ref[...], axis=0)
        shared_sq = jnp.where(me < pieces, jnp.sum(shared * shared), 0.0)
        own_ref[...] = state_own.astype(BF16)
        taps = small_ref[: CONV + 2, :chans]
        skip = nn(small_ref[6:7, :chans], sum_ref[...], HIGH)
        bias = small_ref[7:8, :LANES]
        rate = small_ref[8:9, :LANES] * rates_ref[...]
        lane = lax.broadcasted_iota(jnp.int32, (1, LANES), 1)
        of_heads = jnp.where(lane < sz.heads, bias * bias + rate * rate + skip * skip, 0.0)
        if chans > sz.heads * HDIM:
            taps = taps[:, : sz.heads * HDIM]
        total = jnp.sum(squares_ref[...]) + jnp.sum(taps * taps) + jnp.sum(of_heads)
        total = total + jnp.sum(state_own * state_own) + shared_sq
        row = lax.broadcasted_iota(jnp.int32, (8, LANES), 0)
        stat_ref[...] = jnp.where(row == 7, total, shared)
        run_gather(heads, parts, own_ref, all_ref, ag_sems, (stat_ref, stats_ref, stat_send, stat_recv))
        section_sq = stats_ref[0, 7:8, :]
        for k in range(1, count):
            section_sq = section_sq + stats_ref[k, 7:8, :]
        mine_ref[...] = jnp.broadcast_to(section_sq, (8, LANES))
        pair = pltpu.make_async_remote_copy(
            src_ref=mine_ref,
            dst_ref=got_ref,
            send_sem=pair_send,
            recv_sem=pair_recv,
            device_id={"section": 1 - section},
            device_id_type=MESH,
        )
        pair.start()
        pair.wait()
        norm = jnp.sqrt(mine_ref[...] + got_ref[...])
        norm_ref[...] = jnp.where(row == 0, norm, threshold / jnp.maximum(norm, threshold))
        for copy in sends:
            copy.wait_send()

    return pl.pallas_call(
        kernel,
        out_shape=[
            jax.ShapeDtypeStruct(states[0].shape, BF16),
            jax.ShapeDtypeStruct((count, 8, LANES), F32),
            jax.ShapeDtypeStruct((8, LANES), F32),
        ],
        in_specs=[VMEM_SPEC] * (4 + layers),
        out_specs=[ANY_SPEC, VMEM_SPEC, VMEM_SPEC],
        scratch_shapes=[
            pltpu.VMEM((8, sz.width), F32),
            pltpu.VMEM((count, 8, LANES), F32),
            pltpu.VMEM((rows * layers, width), F32),
            pltpu.VMEM((rows, width), BF16),
        ]
        + [pltpu.VMEM((8, LANES), F32)] * 3
        + scatter_scratch(back, count, rows * layers, width)
        + gather_scratch(parts, heads.dims, count)
        + (
            [pltpu.VMEM((count * rows * layers, width), BF16), pltpu.VMEM((2, rows, width), F32), DMA((2,)), DMA((2,))]
            if layers > 1
            else []
        )
        + [DMA((count,))] * 4
        + [DMA, DMA],
        compiler_params=params(collective_id),
        name="finish_sums",
    )(*states, small, squares, rates, head_sum)


def norm_rows(value, gain):
    mean = jnp.mean(value * value, axis=1, keepdims=True)
    return value * lax.rsqrt(mean + EPS_NORM) * gain


def norm_rows_back(value, gain, grad):
    width = value.shape[1]
    scale = lax.rsqrt(jnp.mean(value * value, axis=1, keepdims=True) + EPS_NORM)
    scaled = grad * gain
    dot = jnp.sum(scaled * value, axis=1, keepdims=True)
    back = scaled * scale - value * (scale * scale * scale * dot * (1.0 / width))
    return back, jnp.sum(grad * value * scale, axis=0, keepdims=True)


def write_pack(sz, pack_ref, head_ref, shared_ref):
    chans, state = sz.channels, 2 * NSTATE
    pack_ref[...] = jnp.zeros_like(pack_ref)
    lane = lax.broadcasted_iota(jnp.int32, (1, LANES), 1)
    bias_row = jnp.zeros((1, LANES), F32)
    rate_row = jnp.zeros((1, LANES), F32)
    rates = -jnp.exp(head_ref[:, (CONV + 2) * HDIM :])
    for head in range(sz.heads):
        cols = slice(head * HDIM, (head + 1) * HDIM)
        for tap in range(CONV):
            pack_ref[tap : tap + 1, cols] = head_ref[head : head + 1, tap * HDIM : (tap + 1) * HDIM]
        pack_ref[5:6, cols] = head_ref[head : head + 1, CONV * HDIM : (CONV + 1) * HDIM]
        pack_ref[CONV : CONV + 1, cols] = head_ref[head : head + 1, (CONV + 1) * HDIM : (CONV + 2) * HDIM]
        last = (CONV + 2) * HDIM
        pack_ref[6:7, cols] = jnp.broadcast_to(head_ref[head : head + 1, last + 2 : last + 3], (1, HDIM))
        bias_row = jnp.where(lane == head, head_ref[head : head + 1, last : last + 1], bias_row)
        rate_row = jnp.where(lane == head, rates[head : head + 1, 1:2], rate_row)
    pack_ref[7:8, :LANES] = bias_row
    pack_ref[8:9, :LANES] = rate_row
    for tap in range(CONV + 1):
        pack_ref[tap : tap + 1, chans : chans + state] = shared_ref[:, tap * state : (tap + 1) * state]
    pack_ref[GAIN_ROW : GAIN_ROW + 1, :] = shared_ref[:, (CONV + 1) * state :]


def give_weights(team, number, w_ref, wo_ref, ws_ref, wos_ref, zero_ref, sems, sz, steps, cols):
    send, recv = sems
    section = lax.axis_index("section")
    head_rows = (pl.ds(0, 2 * sz.channels), pl.ds(sz.dt, 16))
    state_rows = pl.ds(2 * sz.channels, 2 * NSTATE)

    def for_users(src, dst, k):
        return [
            Delivery(src, dst, send.at[k, micro], recv.at[k], team.user(micro), team.alone(micro))
            for micro in range(2)
        ]

    def block(step):
        span = pl.ds(step * cols, cols)
        out = []
        for k, rows in enumerate(head_rows):
            out += for_users(w_ref.at[rows, span], ws_ref.at[rows, span], 3 * step + k)
        pair = w_ref.at[state_rows, span], ws_ref.at[state_rows, span]
        k = 3 * step + 2
        for there in range(2):
            out.append(
                Delivery(*pair, send.at[k, there], recv.at[k], {"section": there}, section == there)
            )
        return out

    def matrix():
        return for_users(wo_ref, wos_ref, 3 * steps)

    def receive():
        for step in range(steps):
            span = pl.ds(step * cols, cols)
            for k, rows in enumerate(head_rows):
                got = ws_ref.at[rows, span]
                Delivery(got, got, send.at[0, 0], recv.at[3 * step + k], team.owner(number), team.alone(number)).wait_got()
            got = ws_ref.at[state_rows, span]
            Delivery(got, got, send.at[0, 0], recv.at[3 * step + 2], {"section": number}, section == number).wait_got()
        Delivery(wos_ref, wos_ref, send.at[0, 0], recv.at[3 * steps], team.owner(number), team.alone(number)).wait_got()

    def blank(sem):
        return pltpu.make_async_copy(zero_ref, ws_ref.at[pl.ds(sz.dt + 16, LANES - 16), :], sem)

    return block, matrix, receive, blank


def opening(count, sz, proj_in_t, proj_state, proj_out, head_part, shared_part, order, inputs, cotangent, collective_id):
    team = Team(count)
    rows, width = inputs.shape[1:]
    parts = column_parts(width, TEAM_GATHER if team.paired else GATHER)
    cols = 256
    steps = width // cols
    full = sz.master // 16 * 16
    own_rows = proj_out.shape[0]

    def kernel(*refs):
        refs = list(refs)
        take = lambda number: [refs.pop(0) for _ in range(number)]
        in_hbm, state_hbm, out_hbm, order_hbm, head_ref, shared_ref, x_ref, cot_ref = take(8)
        w_own, wo_own, ws_ref, wos_ref, pks_ref, rates_ref, first_ref, cot_own, all_ref = take(9)
        own_ref, in_ref, state_ref, out_ref, order_ref, low_ref, w_ref, wo_ref, zero_ref = take(9)
        ag_sems = take(3)
        load_sem, pack_send, pack_recv, swap_send, swap_recv, give_send, give_recv, local_sem = take(8)
        relay_ref, relay_sem = take(2)
        section = lax.axis_index("section")
        other = 1 - section
        micro = team.micro()
        loads = [
            pltpu.make_async_copy(src, dst, load_sem.at[k])
            for k, (src, dst) in enumerate(
                ((order_hbm, order_ref), (in_hbm, in_ref), (state_hbm, state_ref), (out_hbm, out_ref))
            )
        ]
        for copy in loads:
            copy.start()
        write_pack(sz, own_pack_ref := refs[0], head_ref, shared_ref)
        rates_ref[...] = own_pack_ref[8:9, :LANES]
        zero_ref[...] = jnp.zeros_like(zero_ref)
        greet_all(count, True)
        packs = [
            Delivery(
                own_pack_ref, pks_ref.at[section], pack_send.at[m], pack_recv.at[section], team.user(m), team.alone(m)
            )
            for m in range(2)
        ]
        for copy in packs:
            copy.start()
        straight = micro == section
        if team.paired:
            head = lax.axis_index("head")
            partner = {"section": head % 2, "head": head // 2 * 2 + section}
            swaps = [
                remote(x_ref.at[section], first_ref, swap_send.at[0], swap_recv.at[0], partner),
                remote(cot_ref.at[section], cot_own, swap_send.at[1], swap_recv.at[1], partner),
            ]

            @pl.when(jnp.logical_not(straight))
            def _():
                for copy in swaps:
                    copy.start()

            @pl.when(straight)
            def _():
                first_ref[...] = x_ref[micro]
                cot_own[...] = cot_ref[micro]

        else:
            first_ref[...] = x_ref[micro]
            cot_own[...] = cot_ref[micro]

        block, matrix, receive, blank = give_weights(
            team, 0, w_ref, wo_ref, ws_ref, wos_ref, zero_ref, (give_send, give_recv), sz, steps, cols
        )
        keeps = [
            pltpu.make_async_copy(w_ref, w_own, local_sem.at[0]),
            pltpu.make_async_copy(wo_ref, wo_own, local_sem.at[1]),
        ]

        def lower(copies):
            @pl.when(section == 0)
            def _():
                for copy in copies():
                    copy.start()

        x = lax.axis_index("head") % 2
        far = {"section": x, "head": lax.axis_index("head") // 2 * 2 + 1 - x}

        def by_way():
            return remote(wo_ref, relay_ref, relay_sem.at[0], relay_sem.at[1], {"section": other})

        def on_from():
            return remote(relay_ref, wos_ref, relay_sem.at[2], give_recv.at[3 * steps], far)

        def matrix_near():
            there = {"section": x}
            return Delivery(wo_ref, wos_ref, give_send.at[3 * steps, 0], give_recv.at[3 * steps], there, section == x)

        def pass_on():
            @pl.when(section == 1)
            def _():
                by_way().wait_recv()
                on_from().start()

        def low_out():
            loads[3].wait()
            if own_rows < sz.channels:
                wo_ref[...] = jnp.zeros_like(wo_ref)
            wo_ref[:own_rows, :] = out_ref[...].astype(BF16)
            keeps[1].start()
            if team.paired:
                lower(lambda: [by_way(), matrix_near()])
            else:
                lower(matrix)

        def low_in(step):
            if step == 0:
                for copy in loads[:3]:
                    copy.wait()
                blank(local_sem.at[2]).start()
            span = slice(step * cols, (step + 1) * cols)
            low_ref[:full, :] = in_ref[:full, 0, span].astype(BF16)
            if full < sz.master_pad:
                low_ref[full:, :] = jnp.zeros((sz.master_pad - full, cols), BF16)
            if full < sz.master:
                low_ref[full : full + 16, :] = jnp.concatenate(
                    [in_ref[full : sz.master, 0, span], jnp.zeros((full + 16 - sz.master, cols), F32)], axis=0
                ).astype(BF16)
            w_ref[:, span] = tn(order_ref[: sz.master_pad, :], low_ref[...]).astype(BF16)
            row = lax.broadcasted_iota(jnp.int32, (2 * NSTATE, 2 * NSTATE), 0)
            col = lax.broadcasted_iota(jnp.int32, (2 * NSTATE, 2 * NSTATE), 1)
            one = (row == col).astype(BF16)
            w_ref[2 * sz.channels : sz.dt, span] = nt(one, state_ref[span, :].astype(BF16)).astype(BF16)
            lower(lambda: block(step))

        low_out()
        ahead = 3
        for step in range(ahead):
            low_in(step)
        if team.paired:
            pass_on()
        if team.paired:
            pl.when(jnp.logical_not(straight))(lambda: swaps[0].wait_recv())

        def got_pack(layer):
            ref = pks_ref.at[layer]
            Delivery(ref, ref, pack_send.at[0], pack_recv.at[layer], team.owner(layer), team.alone(layer)).wait_got()

        got_pack(0)
        pl.when(team.alone(0))(lambda: packs[0].near().wait())
        gain = pks_ref[0, GAIN_ROW : GAIN_ROW + 1, :]
        own_ref[...] = norm_rows(first_ref[...].astype(F32), gain).astype(BF16)
        work = [lambda step=step: low_in(step) for step in range(ahead, steps)]
        run_gather(team, parts, own_ref, all_ref, ag_sems, None, work)
        keeps[0].start()
        got_pack(1)
        if team.paired:

            @pl.when(jnp.logical_not(straight))
            def _():
                swaps[1].wait_recv()
                for copy in swaps:
                    copy.wait_send()

        for m, copy in enumerate(packs):
            done = team.alone(0) if m == 0 else jnp.bool_(False)
            pl.when(jnp.logical_not(done))(copy.wait_sent)
        receive()

        @pl.when(section == 0)
        def _():
            for step in range(steps):
                for copy in block(step):
                    copy.wait_sent()
            if team.paired:
                matrix_near().wait_sent()
                by_way().wait_send()
            else:
                for copy in matrix():
                    copy.wait_sent()

        if team.paired:
            pl.when(section == 1)(lambda: on_from().wait_send())
        blank(local_sem.at[2]).wait()
        for copy in keeps:
            copy.wait()

    w_shape = jax.ShapeDtypeStruct((sz.cols, width), BF16)
    wo_shape = jax.ShapeDtypeStruct((sz.channels, width), BF16)
    row_shape = jax.ShapeDtypeStruct((rows, width), BF16)
    return pl.pallas_call(
        kernel,
        out_shape=[
            w_shape, wo_shape, w_shape, wo_shape,
            jax.ShapeDtypeStruct((2, 16, width), F32),
            jax.ShapeDtypeStruct((1, LANES), F32),
            row_shape, row_shape,
            jax.ShapeDtypeStruct((count * rows, width), BF16),
        ],
        in_specs=[ANY_SPEC] * 4 + [VMEM_SPEC] * 4,
        out_specs=[ANY_SPEC] * 4 + [VMEM_SPEC] * 4 + [ANY_SPEC],
        scratch_shapes=[
            pltpu.VMEM((rows, width), BF16),
            pltpu.VMEM(proj_in_t.shape, F32),
            pltpu.VMEM(proj_state.shape, F32),
            pltpu.VMEM(proj_out.shape, F32),
            pltpu.VMEM(order.shape, BF16),
            pltpu.VMEM((sz.master_pad, cols), BF16),
            pltpu.VMEM((sz.cols, width), BF16),
            pltpu.VMEM((sz.channels, width), BF16),
            pltpu.VMEM((LANES - 16, width), BF16),
        ]
        + gather_scratch(parts, team.dims, count)
        + [DMA((4,)), DMA((2,)), DMA((2,)), DMA((2,)), DMA((2,))]
        + [DMA((3 * steps + 1, 2)), DMA((3 * steps + 1,)), DMA((3,))]
        + [pltpu.VMEM((sz.channels, width), BF16), DMA((3,))]
        + [pltpu.VMEM((16, width), F32)],
        compiler_params=params(collective_id),
        name="opening",
    )(proj_in_t, proj_state, proj_out, order, head_part, shared_part, inputs, cotangent)


def column_of(tile, rows):
    row = lax.broadcasted_iota(jnp.int32, (rows, rows), 0)
    lane = lax.broadcasted_iota(jnp.int32, (rows, rows), 1)
    return nt((row == lane).astype(F32), tile, HIGH)[:, 0:1]


def write_stats(stat_ref, squares, out_grad, branch, rows):
    dot = nt(jnp.ones((8, branch.shape[1]), F32), out_grad * branch, HIGH)
    scale = lax.rsqrt(squares / (HEADS * HDIM) + EPS_NORM)
    row = lax.broadcasted_iota(jnp.int32, (8, rows), 0)
    stat_ref[...] = jnp.zeros_like(stat_ref)
    stat_ref[:, :rows] = jnp.where(row == 0, scale, jnp.where(row == 1, dot, 0.0))


def greet_other():
    barrier = pltpu.get_barrier_semaphore()
    other = 1 - lax.axis_index("section")
    pl.semaphore_signal(barrier, inc=1, device_id={"section": other}, device_id_type=MESH)
    pl.semaphore_wait(barrier, 1)
    return other


def add_up(out_ref, mine_ref, got_ref, squares_ref):
    rows, width = out_ref.shape
    step = 16 if rows % 16 == 0 else rows

    def body(i, carry):
        span = pl.ds(pl.multiple_of(i * step, step), step)
        total = mine_ref[span, :].astype(F32) + got_ref[span, :].astype(F32)
        out_ref[span, :] = total
        if squares_ref is not None:
            part = total * total
            for k in range(0, step, 8):
                squares_ref[...] += part[k : k + 8]
        return carry

    lax.fori_loop(0, rows // step, body, 0)


def trade_sections(sums, stacks, squared, collective_id):
    pairs = sums + stacks
    number, summed = len(pairs), len(sums)

    def kernel(*refs):
        ins, outs = refs[: 2 * number], refs[2 * number : 3 * number]
        squares_ref = refs[3 * number]
        boxes = refs[3 * number + 1 : 3 * number + 1 + summed]
        send_sem, recv_sem = refs[3 * number + 1 + summed :]
        squares_ref[...] = jnp.zeros_like(squares_ref)
        section = lax.axis_index("section")
        other = greet_other()

        def go(mine, theirs):
            copies = []
            for k in range(number):
                copy = pltpu.make_async_remote_copy(
                    src_ref=theirs[k],
                    dst_ref=boxes[k] if k < summed else outs[k].at[section],
                    send_sem=send_sem.at[k],
                    recv_sem=recv_sem.at[k],
                    device_id={"section": other},
                    device_id_type=MESH,
                )
                copy.start()
                copies.append(copy)
            for k in range(summed, number):
                outs[k][section] = mine[k][...]
            for k in range(number):
                copies[k].wait()
                if k < summed:
                    add_up(outs[k], mine[k], boxes[k], squares_ref if k < squared else None)

        pl.when(section == 0)(lambda: go(ins[0::2], ins[1::2]))
        pl.when(section == 1)(lambda: go(ins[1::2], ins[0::2]))

    shapes = [jax.ShapeDtypeStruct(a.shape, F32) for a, _ in sums]
    shapes += [jax.ShapeDtypeStruct((2,) + a.shape, a.dtype) for a, _ in stacks]
    shapes.append(jax.ShapeDtypeStruct((8, sums[0][0].shape[1]), F32))
    return pl.pallas_call(
        kernel,
        out_shape=shapes,
        in_specs=[VMEM_SPEC] * (2 * number),
        out_specs=[VMEM_SPEC] * len(shapes),
        scratch_shapes=[pltpu.VMEM(a.shape, a.dtype) for a, _ in sums] + [DMA((number,))] * 2,
        compiler_params=pltpu.CompilerParams(
            collective_id=collective_id, has_side_effects=True, vmem_limit_bytes=VMEM_LIMIT
        ),
        name="trade_sections",
    )(*[a for pair in pairs for a in pair])


def fits(sz):
    return Team(sz.count).paired and sz.tokens * sz.width <= 4 << 20


class Sizes:
    def __init__(self, count, heads, tokens, width):
        self.count = count
        self.heads = heads
        self.padded = heads + heads % 2
        self.channels = self.padded * HDIM
        self.conv = self.channels + 2 * NSTATE
        self.cols = 2 * self.channels + 2 * NSTATE + LANES
        self.dt = 2 * self.channels + 2 * NSTATE
        self.master = heads * COLS
        self.master_pad = -(-self.master // LANES) * LANES
        self.grad_rows = self.master_pad + 2 * NSTATE
        self.tokens = tokens
        self.width = width
        self.blocks = tokens // STRETCH

    def order(self):
        table = np.zeros((self.grad_rows, self.cols), np.float32)
        for head in range(self.heads):
            for j in range(HDIM):
                table[head * COLS + j, head * HDIM + j] = 1
                table[head * COLS + HDIM + j, self.channels + head * HDIM + j] = 1
            table[head * COLS + 2 * HDIM, self.dt + head] = 1
        for j in range(2 * NSTATE):
            table[self.master_pad + j, 2 * self.channels + j] = 1
        return jnp.asarray(table, BF16)

    def head_sum(self):
        table = np.zeros((self.channels, LANES), np.float32)
        for head in range(self.padded):
            table[head * HDIM : (head + 1) * HDIM, head] = 1
        return jnp.asarray(table, F32)


def nt(left, right, precision=None):
    return lax.dot_general(
        left, right, (((1,), (1,)), ((), ())), precision=precision, preferred_element_type=F32
    )


def tn(left, right, precision=None):
    return lax.dot_general(
        left, right, (((0,), (0,)), ((), ())), precision=precision, preferred_element_type=F32
    )


def nn(left, right, precision=None):
    return jnp.dot(left, right, precision=precision, preferred_element_type=F32)


def split(value):
    high = value.astype(BF16)
    return high, (value - high.astype(F32)).astype(BF16)


def fine(dot, left, right, left_axis, right_axis):
    left_high, left_low = split(left)
    right_high, right_low = split(right)
    return dot(
        jnp.concatenate([left_high, left_low, left_high], axis=left_axis),
        jnp.concatenate([right_high, right_high, right_low], axis=right_axis),
    )


def exact(dot, ones, value, axis, ones_first=True):
    ones = ones.astype(BF16)
    high, low = split(value)
    ones_axis = {(nn, True): 1, (nn, False): 0, (nt, True): 1, (nt, False): 1, (tn, True): 0}[dot, ones_first]
    both = jnp.concatenate([ones, ones], axis=ones_axis)
    halves_of = jnp.concatenate([high, low], axis=axis)
    return dot(both, halves_of) if ones_first else dot(halves_of, both)


def nt3(left, right):
    return fine(nt, left, right, 1, 1)


def tn3(left, right):
    return fine(tn, left, right, 0, 0)


def nn3(left, right):
    return fine(nn, left, right, 1, 0)


def softplus(value):
    return jnp.maximum(value, 0.0) + jnp.log1p(jnp.exp(-jnp.abs(value)))


def sigmoid(value):
    return 1.0 / (1.0 + jnp.exp(-value))


def halves(left, right):
    rows = left.shape[0]
    lane = lax.broadcasted_iota(jnp.int32, (rows, LANES), 1)
    return jnp.where(lane < HDIM, left, right)


def lower_mask(size):
    row = lax.broadcasted_iota(jnp.int32, (size, size), 0)
    col = lax.broadcasted_iota(jnp.int32, (size, size), 1)
    return row >= col


def step_rows(log_decay, step):
    lane = lax.broadcasted_iota(jnp.int32, log_decay.shape, 1)
    both = jnp.where(lane < 8, log_decay, pltpu.roll(step, 8, 1))
    return jnp.transpose(jnp.where(lane < 16, both, 0.0))


def to_columns(tile, rows):
    row = lax.broadcasted_iota(jnp.int32, (rows, LANES), 0)
    lane = lax.broadcasted_iota(jnp.int32, (rows, LANES), 1)
    return exact(nt, (row == lane).astype(F32), tile, 1)


def forward_phase(
    count, sz, layer, lengths, gathered, weights, weight_out, pack, residual, cotangent, own, collective_id
):
    block, chunk, chans = STRETCH, CHUNK, sz.channels
    team = Team(count)
    dims = team.dims
    rows, width = residual.shape
    subs = block // chunk
    shards = block // rows
    blocks = sz.blocks
    planes = dims[0]
    per = blocks // planes
    parts = column_parts(width, TEAM_GATHER if team.paired else GATHER)
    scatter = PlaneScatter(team, rows, width)
    turn = cotangent is not None
    passing = own is not None
    cols = 256
    steps = width // cols

    def kernel(*refs):
        refs = list(refs)
        take = lambda number: [refs.pop(0) for _ in range(number)]
        reset_ref, rows_ref, ws_ref, wos_ref, pks_ref, u_ref = take(6)
        cot_ref = refs.pop(0) if turn else None
        w_own, wo_own = take(2) if passing else (None, None)
        result_ref, branch_ref, total_ref, next_ref, p_out, y_out, s_out = take(7)
        stats_ref = refs.pop(0) if turn else None
        ws_next, wos_next = take(2) if passing else (None, None)
        conv_ref, state_ref, w_ref, wo_ref, h_buf, p_buf, y_buf, s_buf, part_ref, sq_ref = take(10)
        load_sem, store_sem, weight_sem = take(3)
        sums_ref, own_ref = take(2)
        scatter_refs = take(5)
        ag_sems = take(3)
        small_send, small_recv = take(2)
        if passing:
            w_mine, wo_mine, zero_ref, own_sem, give_send, give_recv = take(6)
        pk_ref = pks_ref.at[layer]

        def load(c):
            span = pl.ds(pl.multiple_of(c * block, block), block)
            return pltpu.make_async_copy(rows_ref.at[span, :], h_buf.at[c % 2], load_sem.at[c % 2])

        def stores(c):
            slot = c % 2
            span = pl.ds(pl.multiple_of(c * block, block), block)
            return [
                pltpu.make_async_copy(p_buf.at[slot], p_out.at[span, :], store_sem.at[0, slot]),
                pltpu.make_async_copy(y_buf.at[slot], y_out.at[span, :], store_sem.at[1, slot]),
                pltpu.make_async_copy(s_buf.at[slot], s_out.at[pl.ds(c * subs, subs)], store_sem.at[2, slot]),
            ]

        load(0).start()
        weight_copies = [
            pltpu.make_async_copy(ws_ref, w_ref, weight_sem.at[0]),
            pltpu.make_async_copy(wos_ref, wo_ref, weight_sem.at[1]),
        ]
        for copy in weight_copies:
            copy.start()
        if passing:
            section = lax.axis_index("section")
            own_copies = [
                pltpu.make_async_copy(w_own, w_mine, own_sem.at[0]),
                pltpu.make_async_copy(wo_own, wo_mine, own_sem.at[1]),
            ]
            for copy in own_copies:
                copy.start()
            zero_ref[...] = jnp.zeros_like(zero_ref)
            give_block, give_matrix, receive, blank = give_weights(
                team, 1, w_mine, wo_mine, ws_next, wos_next, zero_ref, (give_send, give_recv), sz, steps, cols
            )
            blank(own_sem.at[2]).start()
        greet_all(count, True)
        if passing:
            for copy in own_copies:
                copy.wait()

            @pl.when(section == 1)
            def _():
                for step in range(steps):
                    for copy in give_block(step):
                        copy.start()
                for copy in give_matrix():
                    copy.start()

        conv_ref[...] = jnp.zeros_like(conv_ref)
        state_ref[...] = jnp.zeros_like(state_ref)
        scatter.bind(part_ref, branch_ref, *scatter_refs)
        for copy in weight_copies:
            copy.wait()

        def one_block(c, carry):
            slot = c % 2
            keep = keeps(reset_ref, team.micro(), c)
            span_all = pl.ds(pl.multiple_of(c * block, block), block)
            pl.when(c + 1 < blocks)(lambda: load(c + 1).start())
            load(c).wait()

            @pl.when(c >= 2)
            def _():
                for copy in stores(c - 2):
                    copy.wait()

            h_ref, p_ref, y_ref, s_ref = (buf.at[slot] for buf in (h_buf, p_buf, y_buf, s_buf))
            p_ref[...] = nt(h_ref[...], w_ref[...])
            inner = p_ref[:, chans : 2 * chans]
            state_raw = p_ref[:, 2 * chans : sz.dt].astype(BF16).astype(F32)
            conv_ref[0:8, :] = conv_ref[block : block + 8, :] * keep
            conv_ref[8 : 8 + block, :chans] = inner
            conv_ref[8 : 8 + block, chans:] = state_raw
            pre = pk_ref[CONV : CONV + 1, : sz.conv] + pk_ref[0:1, : sz.conv] * conv_ref[8 : 8 + block, :]
            for tap in range(1, CONV):
                pre = pre + pk_ref[tap : tap + 1, : sz.conv] * conv_ref[8 - tap : 8 - tap + block, :]
            act = pre * sigmoid(pre)
            step = softplus(p_ref[:, sz.dt :] + pk_ref[7:8, :LANES])
            decay = step * pk_ref[8:9, :LANES]
            mask = lower_mask(chunk)
            lower = mask.astype(F32)
            lane = lax.broadcasted_iota(jnp.int32, (chunk, LANES), 1)
            for sub in range(subs):
                span = slice(sub * chunk, (sub + 1) * chunk)
                if sub == 0:
                    state_ref[...] = state_ref[...] * keep
                s_ref[sub] = state_ref[...]
                dt = step[span]
                log_decay = exact(nn, lower, decay[span], 0)
                flat = step_rows(log_decay, dt)
                writer = act[span, chans : chans + NSTATE]
                reader = act[span, chans + NSTATE :]
                cross = nt3(reader, writer)
                for pair in range(sz.padded // 2):
                    cols = slice(pair * LANES, (pair + 1) * LANES)
                    x = act[span, cols]
                    total = jnp.zeros((chunk, LANES), F32)
                    for side in range(2):
                        head = 2 * pair + side
                        gap = log_decay[:, head : head + 1] - flat[head : head + 1, :]
                        weight = cross * jnp.exp(jnp.where(mask, gap, -1e30)) * flat[8 + head : 9 + head, :]
                        part = jnp.where((lane < HDIM) == (side == 0), x, 0.0)
                        total = total + nn3(weight, part)
                    logs = halves(log_decay[:, 2 * pair : 2 * pair + 1], log_decay[:, 2 * pair + 1 : 2 * pair + 2])
                    dts = halves(dt[:, 2 * pair : 2 * pair + 1], dt[:, 2 * pair + 1 : 2 * pair + 2])
                    old = state_ref[:, cols]
                    total = total + jnp.exp(logs) * nn3(reader, old)
                    last = logs[chunk - 1 : chunk, :]
                    moved_in = x * jnp.exp(last - logs) * dts
                    state_ref[:, cols] = jnp.exp(last) * old + tn3(writer, moved_in)
                    y_ref[span, cols] = total + pk_ref[6:7, cols] * x
            z = p_ref[:, :chans]
            gated = y_ref[...] * z * sigmoid(z)
            square = exact(nt, jnp.ones((8, chans), F32), gated * gated, 1)
            for k in range(shards):
                sq_ref[c * shards + k] = square[:, k * rows : (k + 1) * rows]
            high, low = split(gated * pk_ref[5:6, :chans])
            part_ref[span_all, :] = (nn(high, wo_ref[...]) + nn(low, wo_ref[...])).astype(part_ref.dtype)
            for copy in stores(c):
                copy.start()
            if per == 1:
                scatter.step(planes, c + 1, lambda k: k)
            else:
                pl.when(c % per == per - 1)(lambda: scatter.step(planes, c // per + 1, lambda k: k))
            return carry

        lax.fori_loop(0, blocks, one_block, 0)
        me = linear(dims, team.spot())
        copies = start_direct(team, lambda peer: sq_ref.at[peer], sums_ref, small_send, small_recv)
        sums_ref[me] = sq_ref[me]
        scatter.finish(planes, lambda k: k)
        wait_direct(team, sums_ref, copies, small_recv, small_send)
        total = jnp.sum(sums_ref[...], axis=0)
        total_ref[...] = total
        scale = lax.rsqrt(column_of(total, rows) / (HEADS * HDIM) + EPS_NORM)
        branch = branch_ref[...] * scale
        branch_ref[...] = branch
        live_col = live_rows_of(reset_ref, team.micro(), me, rows)
        result = (u_ref[...].astype(F32) + live_col * branch).astype(BF16)
        result_ref[...] = result
        stat = None
        if turn:
            stat_ref, stat_send, stat_recv = refs
            out_grad = (live_col * cot_ref[...].astype(F32)).astype(BF16)
            own_ref[...] = out_grad
            write_stats(stat_ref, total, out_grad.astype(F32), branch, rows)
            stat = (stat_ref, stats_ref, stat_send, stat_recv)
        else:
            gain = pks_ref[layer + 1, GAIN_ROW : GAIN_ROW + 1, :]
            own_ref[...] = norm_rows(result.astype(F32), gain).astype(BF16)
        run_gather(team, parts, own_ref, next_ref, ag_sems, stat)
        for c in range(max(blocks - 2, 0), blocks):
            for copy in stores(c):
                copy.wait()
        scatter.drain()
        if passing:
            receive()

            @pl.when(section == 1)
            def _():
                for step in range(steps):
                    for copy in give_block(step):
                        copy.wait_sent()
                for copy in give_matrix():
                    copy.wait_sent()

            blank(own_sem.at[2]).wait()

    tokens = sz.tokens
    out_shape = [
        jax.ShapeDtypeStruct((rows, width), BF16),
        jax.ShapeDtypeStruct((rows, width), F32),
        jax.ShapeDtypeStruct((8, rows), F32),
        jax.ShapeDtypeStruct((tokens, width), BF16),
        jax.ShapeDtypeStruct((tokens, sz.cols), F32),
        jax.ShapeDtypeStruct((tokens, chans), F32),
        jax.ShapeDtypeStruct((tokens // chunk, NSTATE, chans), F32),
    ]
    out_specs = [VMEM_SPEC] * 3 + [ANY_SPEC] * 4
    scratch = [
        pltpu.VMEM((block + 8, sz.conv), F32),
        pltpu.VMEM((NSTATE, chans), F32),
        pltpu.VMEM((sz.cols, width), BF16),
        pltpu.VMEM((chans, width), BF16),
        pltpu.VMEM((2, block, width), BF16),
        pltpu.VMEM((2, block, sz.cols), F32),
        pltpu.VMEM((2, block, chans), F32),
        pltpu.VMEM((2, subs, NSTATE, chans), F32),
        pltpu.VMEM((tokens, width), scatter.first_type),
        pltpu.VMEM((count, 8, rows), F32),
        DMA((2,)),
        DMA((3, 2)),
        DMA((2,)),
        pltpu.VMEM((count, 8, rows), F32),
        pltpu.VMEM((rows, width), BF16),
    ]
    scratch += scatter.scratch() + gather_scratch(parts, dims, count) + [DMA((count,))] * 2
    operands = [lengths, gathered, weights, weight_out, pack, residual]
    in_specs = [pl.BlockSpec(memory_space=pltpu.SMEM)] + [ANY_SPEC] * 3 + [VMEM_SPEC] * 2
    if turn:
        out_shape.append(jax.ShapeDtypeStruct((count, 8, LANES), F32))
        out_specs.append(VMEM_SPEC)
        scratch += [pltpu.VMEM((8, LANES), F32)] + [DMA((count,))] * 2
        operands.append(cotangent)
        in_specs.append(VMEM_SPEC)
    if passing:
        out_shape += [jax.ShapeDtypeStruct(array.shape, array.dtype) for array in own]
        out_specs += [ANY_SPEC] * 2
        scratch += [pltpu.VMEM(array.shape, array.dtype) for array in own]
        scratch += [pltpu.VMEM((LANES - 16, width), BF16), DMA((3,))]
        scratch += [DMA((3 * steps + 1, 2)), DMA((3 * steps + 1,))]
        operands += list(own)
        in_specs += [ANY_SPEC] * 2
    return pl.pallas_call(
        kernel,
        out_shape=out_shape,
        in_specs=in_specs,
        out_specs=out_specs,
        scratch_shapes=scratch,
        compiler_params=params(collective_id),
        name="forward_phase",
    )(*operands)


def backward_phase(
    count, sz, layer, lengths, out_grads, proj, mixed, states, stats, weights, weight_out, pack, order,
    residual, upstream, below, gathered, upper, collective_id,
):
    block, chunk, chans = STRETCH, CHUNK, sz.channels
    team = Team(count)
    dims = team.dims
    rows, width = residual.shape
    subs = block // chunk
    blocks = sz.blocks
    planes = dims[0]
    per = blocks // planes
    parts = column_parts(width, TEAM_GATHER if team.paired else GATHER)
    scatter = PlaneScatter(team, rows, width)
    more = below is not None
    close = upper is not None
    early = more and fits(sz)
    cols = 256
    steps = width // cols
    ranges = steps

    def kernel(*refs):
        refs = list(refs)
        take = lambda number: [refs.pop(0) for _ in range(number)]
        reset_ref, g_all, p_all, y_all, s_all, ws_ref, wos_ref, orders_ref = take(8)
        st_ref, pks_ref, sum_ref, u_ref, up_ref = take(5)
        if more:
            lower_ref, lower_total = take(2)
        if close:
            h_own, in_upper, out_upper, acc_upper, result_own, result_upper, grad_upper = take(7)
            state_upper, rates_ref = take(2)
            sum_in, sum_out, state_all, sum_small, outs_ref, grads_ref, stats_ref, norm_ref = take(8)
        elif early:
            h_own = refs.pop(0)
            grad_ref, low_grad_ref, acc_ref, in_out, out_out, state_out = take(6)
        else:
            grad_ref, low_grad_ref, acc_ref, gt_out, q_out = take(5)
        if more:
            next_ref, stats_ref = take(2)
        conv_ref, dpre_ref, dact_ref, ddt_ref, dstate_ref = take(5)
        w_ref, wo_ref, order_ref, g_buf, p_buf, halo_buf, y_buf, s_buf, gt_buf, q_buf, part_ref = take(11)
        load_sem, store_sem, weight_sem = take(3)
        scatter_refs = take(5)
        pk_ref = pks_ref.at[layer]
        if close or early:
            gt_full, q_full, h_cols, g_cols, col_sem = take(5)
        if close:
            grad_ref, acc_ref, box_in, box_out, box_small = take(5)
            in_out, out_out = w_ref.at[: sz.master_pad, :], wo_ref
            live_rows = pl.ds(0, -(-sz.master // 16) * 16)
            trade_send, trade_recv, few_send, few_recv = take(4)
            in_buf, out_buf, keep_sem = take(3)
            state_out, squares_ref, state_sums, state_box, pieces_ref, state_own = take(6)
            share_ref, shares_ref, stat_ref, mine_ref, got_ref = take(5)
            state_send, state_recv, piece_send, piece_recv = take(4)
            head_sems = take(3)
            share_send, share_recv, stat_send, stat_recv, pair_send, pair_recv = take(6)
            section = lax.axis_index("section")
            micro = team.micro()

        def g_slot(slot):
            return g_buf.at[pl.ds(pl.multiple_of(slot * block, block), block), :]

        def loads(c):
            slot = c % 2
            span = pl.ds(pl.multiple_of(c * block, block), block)
            before = pl.multiple_of(jnp.maximum(c * block - 8, 0), 8)
            return [
                pltpu.make_async_copy(g_all.at[span, :], g_slot(slot), load_sem.at[0, slot]),
                pltpu.make_async_copy(p_all.at[span, :], p_buf.at[slot], load_sem.at[1, slot]),
                pltpu.make_async_copy(p_all.at[pl.ds(before, 8), :], halo_buf.at[slot], load_sem.at[2, slot]),
                pltpu.make_async_copy(y_all.at[span, :], y_buf.at[slot], load_sem.at[3, slot]),
                pltpu.make_async_copy(s_all.at[pl.ds(c * subs, subs)], s_buf.at[slot], load_sem.at[4, slot]),
            ]

        def stores(c):
            slot = c % 2
            span = pl.ds(pl.multiple_of(c * block, block), block)
            if close or early:
                return []
            return [
                pltpu.make_async_copy(gt_buf.at[slot], gt_out.at[:, span], store_sem.at[0, slot]),
                pltpu.make_async_copy(q_buf.at[slot], q_out.at[span, :], store_sem.at[1, slot]),
            ]

        for copy in loads(blocks - 1):
            copy.start()
        weight_copies = [
            pltpu.make_async_copy(wos_ref, wo_ref, weight_sem.at[0]),
            pltpu.make_async_copy(ws_ref, w_ref, weight_sem.at[1]),
            pltpu.make_async_copy(orders_ref, order_ref, weight_sem.at[2]),
        ]
        for copy in weight_copies:
            copy.start()
        greet_all(count, True)
        dpre_ref[...] = jnp.zeros_like(dpre_ref)
        dstate_ref[...] = jnp.zeros_like(dstate_ref)
        acc_ref[...] = jnp.zeros_like(acc_ref)
        scatter.bind(part_ref, grad_ref, *scatter_refs)
        for copy in weight_copies:
            copy.wait()

        def one_block(i, carry):
            c = blocks - 1 - i
            slot = c % 2
            keep = keeps(reset_ref, team.micro(), c)
            after = keeps(reset_ref, team.micro(), jnp.minimum(c + 1, blocks - 1))
            span_all = pl.ds(pl.multiple_of(c * block, block), block)

            @pl.when(c >= 1)
            def _():
                for copy in loads(c - 1):
                    copy.start()

            for copy in loads(c):
                copy.wait()

            if not (close or early):

                @pl.when(i >= 2)
                def _():
                    for copy in stores(c + 2):
                        copy.wait()

            g_ref = g_slot(slot)
            p_ref, halo_ref, y_ref, s_ref = (buf.at[slot] for buf in (p_buf, halo_buf, y_buf, s_buf))
            if close or early:
                gt_ref, q_ref = gt_full.at[:, span_all], q_full.at[span_all, :]
            else:
                gt_ref, q_ref = gt_buf.at[slot], q_buf.at[slot]
            conv_ref[0:8, :chans] = halo_ref[:, chans : 2 * chans] * keep
            conv_ref[0:8, chans:] = halo_ref[:, 2 * chans : sz.dt].astype(BF16).astype(F32) * keep
            conv_ref[8 : 8 + block, :chans] = p_ref[:, chans : 2 * chans]
            conv_ref[8 : 8 + block, chans:] = p_ref[:, 2 * chans : sz.dt].astype(BF16).astype(F32)
            pre = pk_ref[CONV : CONV + 1, : sz.conv] + pk_ref[0:1, : sz.conv] * conv_ref[8 : 8 + block, :]
            for tap in range(1, CONV):
                pre = pre + pk_ref[tap : tap + 1, : sz.conv] * conv_ref[8 - tap : 8 - tap + block, :]
            gate = sigmoid(pre)
            act = pre * gate
            slope = gate * (1.0 + pre * (1.0 - gate))
            step_in = p_ref[:, sz.dt :] + pk_ref[7:8, :LANES]
            step = softplus(step_in)
            rate = pk_ref[8:9, :LANES]
            decay = step * rate
            z = p_ref[:, :chans]
            zgate = sigmoid(z)
            zsilu = z * zgate
            y = y_ref[...]
            gated = y * zsilu
            gain = pk_ref[5:6, :chans]
            skip = pk_ref[6:7, :chans]
            columns = [to_columns(st_ref[c * (block // rows) + k], rows) for k in range(block // rows)]
            columns = jnp.concatenate(columns, axis=0)
            scale = columns[:, 0:1]
            along = columns[:, 1:2]
            grad_q = nt(g_ref[...], wo_ref[...])
            q_ref[...] = (gated * scale * gain).astype(BF16)
            acc_ref[5:6, :chans] += jnp.sum(grad_q * gated * scale, axis=0, keepdims=True)
            dgated = grad_q * gain * scale - gated * (scale * scale * along * (1.0 / (HEADS * HDIM)))
            dy = dgated * zsilu
            dz = dgated * y * zgate * (1.0 + z * (1.0 - zgate))
            x_all = act[:, :chans]
            acc_ref[6:7, :chans] += jnp.sum(dy * x_all, axis=0, keepdims=True)
            scan_dot = exact(nn, sum_ref[...], dy * (y - skip * x_all), 1, False)
            mask = lower_mask(chunk)
            lower = mask.astype(F32)
            lane = lax.broadcasted_iota(jnp.int32, (chunk, LANES), 1)
            for sub in reversed(range(subs)):
                span = slice(sub * chunk, (sub + 1) * chunk)
                dt = step[span]
                log_decay = exact(nn, lower, decay[span], 0)
                flat = step_rows(log_decay, dt)
                writer = act[span, chans : chans + NSTATE]
                reader = act[span, chans + NSTATE :]
                cross = nt3(reader, writer)
                cross_grad = jnp.zeros((chunk, chunk), F32)
                dreader = jnp.zeros((chunk, NSTATE), F32)
                dwriter = jnp.zeros((chunk, NSTATE), F32)
                fall = jnp.zeros((LANES, chunk), F32)
                row = lax.broadcasted_iota(jnp.int32, (LANES, chunk), 0)
                reach = []
                carried = []
                for pair in range(sz.padded // 2):
                    cols = slice(pair * LANES, (pair + 1) * LANES)
                    x = act[span, cols]
                    g = dy[span, cols]
                    logs = halves(log_decay[:, 2 * pair : 2 * pair + 1], log_decay[:, 2 * pair + 1 : 2 * pair + 2])
                    dts = halves(dt[:, 2 * pair : 2 * pair + 1], dt[:, 2 * pair + 1 : 2 * pair + 2])
                    last = logs[chunk - 1 : chunk, :]
                    old = s_ref[sub, :, cols]
                    dnew = dstate_ref[:, cols]
                    faded = g * jnp.exp(logs)
                    tail = jnp.exp(last - logs)
                    dreader = dreader + nt3(faded, old)
                    ahead = nn3(writer, dnew)
                    dx = g * skip[:, cols] + ahead * tail * dts
                    dwriter = dwriter + nt3(x * tail * dts, dnew)
                    reach.append(x * ahead * tail)
                    carried.append(jnp.sum(old * dnew, axis=0, keepdims=True) * jnp.exp(last))
                    dstate_ref[:, cols] = jnp.exp(last) * dnew + tn3(reader, faded)
                    for side in range(2):
                        head = 2 * pair + side
                        own = (lane < HDIM) == (side == 0)
                        g_own = jnp.where(own, g, 0.0)
                        gap = log_decay[:, head : head + 1] - flat[head : head + 1, :]
                        decays = jnp.exp(jnp.where(mask, gap, -1e30))
                        steps = flat[8 + head : 9 + head, :]
                        spread = nt3(g_own, x) * decays
                        weight = cross * decays * steps
                        dx = dx + tn3(weight, g_own)
                        cross_grad = cross_grad + spread * steps
                        sums = jnp.sum(spread * cross, axis=0, keepdims=True)
                        fall = fall + jnp.where(row == head, sums, 0.0)
                    dact_ref[span, cols] = dx
                dact_ref[span, chans : chans + NSTATE] = dwriter + tn3(cross_grad, reader)
                dact_ref[span, chans + NSTATE :] = dreader + nn3(cross_grad, writer)
                reach = exact(nn, sum_ref[...], jnp.concatenate(reach, axis=1), 1, False)
                carried = exact(nn, sum_ref[...], jnp.broadcast_to(jnp.concatenate(carried, axis=1), (8, chans)), 1, False)[0:1]
                direct = jnp.transpose(fall) + reach
                given = dt * reach
                dlog = scan_dot[span] - dt * direct
                ends = jnp.sum(given, axis=0, keepdims=True) + carried
                at_end = lax.broadcasted_iota(jnp.int32, (chunk, LANES), 0) == chunk - 1
                dlog = dlog + jnp.where(at_end, ends, 0.0)
                ddecay = exact(tn, lower, dlog, 0)
                ddt_ref[span, :] = direct + ddecay * rate
                acc_ref[8:9, :LANES] += jnp.sum(ddecay * dt, axis=0, keepdims=True)
            dstate_ref[...] = dstate_ref[...] * keep
            ddt_raw = ddt_ref[...] * sigmoid(step_in)
            acc_ref[7:8, :LANES] += jnp.sum(ddt_raw, axis=0, keepdims=True)
            dpre_ref[block : block + 8, :] = dpre_ref[0:8, :] * after
            dpre_ref[0:block, :] = dact_ref[...] * slope
            raw = conv_ref[8 : 8 + block, :]
            acc_ref[CONV : CONV + 1, : sz.conv] += jnp.sum(dpre_ref[0:block, :], axis=0, keepdims=True)
            draw = jnp.zeros((block, sz.conv), F32)
            for tap in range(CONV):
                later = dpre_ref[tap : tap + block, :]
                draw = draw + pk_ref[tap : tap + 1, : sz.conv] * later
                acc_ref[tap : tap + 1, : sz.conv] += jnp.sum(raw * later, axis=0, keepdims=True)
            low = jnp.concatenate(
                [dz.astype(BF16), draw.astype(BF16), ddt_raw.astype(BF16)], axis=1
            )
            part_ref[span_all, :] = nn(low, w_ref[...]).astype(part_ref.dtype)
            gt_ref[...] = nt(order_ref[...], low).astype(BF16)
            for copy in stores(c):
                copy.start()
            if per == 1:
                scatter.step(planes, i + 1, lambda k: planes - 1 - k)
            else:
                pl.when(i % per == per - 1)(
                    lambda: scatter.step(planes, i // per + 1, lambda k: planes - 1 - k)
                )
            if close:
                share = -(-ranges // blocks)
                for k in range(share):
                    j = i * share + k
                    pl.when(j < ranges)(lambda j=j: begin(1)(j))
            return carry

        def input_grads():
            gain = pk_ref[GAIN_ROW : GAIN_ROW + 1, :]
            grad, gain_grad = norm_rows_back(u_ref[...].astype(F32), gain, grad_ref[...])
            grad = grad + up_ref[...].astype(F32)
            grad_ref[...] = grad
            acc_ref[GAIN_ROW : GAIN_ROW + 1, :] = gain_grad
            return grad

        def at(j):
            return pl.ds(pl.multiple_of(j * cols, cols), cols)

        def columns(j):
            slot = j % 2
            return [
                pltpu.make_async_copy(h_own.at[:, at(j)], h_cols.at[slot], col_sem.at[0, slot]),
                pltpu.make_async_copy(g_all.at[:, at(j)], g_cols.at[slot], col_sem.at[1, slot]),
            ]

        def weight_step(j, then=None):
            slot = j % 2
            for copy in columns(j):
                copy.wait()

            @pl.when(j + 1 < steps)
            def _():
                for copy in columns(j + 1):
                    copy.start()

            in_out[:, at(j)] = nn(gt_full[: sz.master_pad, :], h_cols[slot]).astype(BF16)
            out_out[:, at(j)] = tn(q_full[...], g_cols[slot]).astype(BF16)
            if then is not None:
                then(j)
            state_out[:, at(j)] = nn(gt_full[sz.master_pad :, :], h_cols[slot]).astype(BF16)

        if close:
            def trade(layer, j):
                ins, outs = (in_upper, out_upper) if layer else (in_out, out_out)
                sets = ((ins, box_in, live_rows), (outs, box_out, slice(None)))
                return [
                    Delivery(
                        src.at[cut, at(j)], dst.at[micro, cut, at(j)],
                        trade_send.at[k, layer, j], trade_recv.at[k, micro, j],
                        team.owner(layer), team.alone(layer),
                    )
                    for k, (src, dst, cut) in enumerate(sets)
                ]

            def each(action):
                def body(j, carry):
                    action(j)
                    return carry

                lax.fori_loop(0, steps, body, 0)

            def begin(layer):
                def action(j):
                    for copy in trade(layer, j):
                        copy.start()

                return action

            few = {}
            for layer_now, sources in (
                (0, (acc_ref, result_own, grad_ref)), (1, (acc_upper, result_upper, grad_upper))
            ):
                for k, (src, dst) in enumerate(zip(sources, (box_small, outs_ref, grads_ref))):
                    few[layer_now, k] = Delivery(
                        src, dst.at[micro], few_send.at[k, layer_now], few_recv.at[k, micro],
                        team.owner(layer_now), team.alone(layer_now),
                    )
            late = ((0, 0), (0, 2))
            for key, copy in few.items():
                if key not in late:
                    copy.start()

        lax.fori_loop(0, blocks, one_block, 0)
        if not close:
            if early:
                for copy in columns(0):
                    copy.start()
            scatter.finish(planes, lambda k: planes - 1 - k)
            grad = input_grads()
            low_grad_ref[...] = grad.astype(BF16)
            if more:
                own_ref, stat_ref, stat_send, stat_recv = take(4)
                out_grad = (live_rows_of(reset_ref, team.micro(), linear(dims, team.spot()), rows) * grad.astype(BF16).astype(F32)).astype(BF16)
                own_ref[...] = out_grad
                write_stats(stat_ref, lower_total[...], out_grad.astype(F32), lower_ref[...], rows)
                work = [lambda j=j: weight_step(j) for j in range(steps)] if early else []
                run_gather(team, parts, own_ref, next_ref, refs, (stat_ref, stats_ref, stat_send, stat_recv), work)
            if not early:
                for c in range(0, min(2, blocks)):
                    for copy in stores(c):
                        copy.wait()
            scatter.drain()
            return

        def made(begin_at, end_at):
            def body(j, carry):
                weight_step(j, begin(0))
                return carry

            lax.fori_loop(begin_at, end_at, body, 0)

        for copy in columns(0):
            copy.start()
        order_of = lambda k: planes - 1 - k
        stops = scatter.extra_steps()
        for extra in range(1, stops + 1):
            scatter.step(planes, planes + extra, order_of)
            made(steps * (extra - 1) // stops, steps * extra // stops)
        squares_ref[...] = jnp.zeros_like(squares_ref)
        each_rows = 16
        for k in range(count):
            for layer_now, ref in enumerate((state_out, state_upper)):
                to = (2 * k + layer_now) * each_rows
                g_buf[to : to + each_rows, :] = ref[k * each_rows : (k + 1) * each_rows, :]
        state_sends, stages = scatter_steps(
            team, column_parts(width, TEAM_SCATTER_SMALL), 2 * each_rows, g_buf, state_sums, state_box,
            state_send, state_recv, True,
        )
        stages[0]()
        scatter.last()
        input_grads()
        for key in late:
            few[key].start()
        for stage in stages[1:]:
            stage()
        passed = [
            Delivery(
                state_sums.at[pl.ds(layer_now * each_rows, each_rows), :], pieces_ref.at[micro],
                piece_send.at[layer_now], piece_recv.at[micro], team.owner(layer_now), team.alone(layer_now),
            )
            for layer_now in range(2)
        ]
        for copy in passed:
            copy.start()

        def sent(layer):
            def action(j):
                for copy in trade(layer, j):
                    copy.wait_sent()

            return action

        for copy in few.values():
            copy.wait_sent()
        for copy in passed:
            copy.wait_sent()

        def got(src, sem, m):
            Delivery(src, src, trade_send.at[0, 0, 0], sem, team.user(m), team.alone(m)).wait_got()

        for m in range(2):
            for k, box in enumerate((box_small, outs_ref, grads_ref)):
                got(box.at[m], few_recv.at[k, m], m)
        sum_small[...] = box_small[0] + box_small[1]
        heads = Heads(count)
        pieces = width // LANES
        me = lax.axis_index("head")
        share_ref[...] = jnp.zeros_like(share_ref)
        share_ref[0:1, :] = sum_small[GAIN_ROW : GAIN_ROW + 1, :]
        share_ref[1 : CONV + 2, : 2 * NSTATE] = sum_small[: CONV + 1, chans : sz.conv]

        def piece(peer):
            return share_ref.at[:, pl.ds(pl.multiple_of((peer % pieces) * LANES, LANES), LANES)]

        shares = start_direct(heads, piece, shares_ref, share_send, share_recv)
        shares_ref[me] = piece(me)[...]
        for m in range(2):
            got(pieces_ref.at[m], piece_recv.at[m], m)
        state_total = pieces_ref[0] + pieces_ref[1]
        state_own[...] = state_total.astype(BF16)
        def kept(j):
            slot = j % 2
            return [
                pltpu.make_async_copy(in_buf.at[slot, live_rows, :], sum_in.at[live_rows, at(j)], keep_sem.at[0, slot]),
                pltpu.make_async_copy(out_buf.at[slot], sum_out.at[:, at(j)], keep_sem.at[1, slot]),
            ]

        stat_copies = []

        def begin_norm():
            each(sent(1))
            each(sent(0))

            def add_up(j, carry):
                @pl.when(j >= 2)
                def _():
                    for copy in kept(j - 2):
                        copy.wait()

                for k, (box, total_ref) in enumerate(((box_in, in_buf), (box_out, out_buf))):
                    for m in range(2):
                        cut = slice(None) if k else live_rows
                        got(box.at[m, cut, at(j)], trade_recv.at[k, m, j], m)
                    count_rows = chans if k else -(-sz.master // 16) * 16
                    total = box[0, :count_rows, at(j)].astype(F32) + box[1, :count_rows, at(j)].astype(F32)
                    total_ref[j % 2, :count_rows, :] = total
                    squares_ref[k : k + 1, at(j)] += jnp.sum(total * total, axis=0, keepdims=True)
                for copy in kept(j):
                    copy.start()
                return carry

            lax.fori_loop(0, steps, add_up, 0)
            wait_direct(heads, shares_ref, shares, share_recv, share_send)
            shared = jnp.sum(shares_ref[...], axis=0)
            taps = sum_small[: CONV + 2, : sz.heads * HDIM]
            skip_sums = nn(sum_small[6:7, :chans], sum_ref[...], HIGH)
            bias = sum_small[7:8, :LANES]
            rate = sum_small[8:9, :LANES] * rates_ref[...]
            lane = lax.broadcasted_iota(jnp.int32, (1, LANES), 1)
            of_heads = jnp.where(lane < sz.heads, bias * bias + rate * rate + skip_sums * skip_sums, 0.0)
            total = jnp.sum(squares_ref[...]) + jnp.sum(taps * taps) + jnp.sum(of_heads)
            total = total + jnp.sum(state_total * state_total)
            total = total + jnp.where(me < pieces, jnp.sum(shared * shared), 0.0)
            row = lax.broadcasted_iota(jnp.int32, (8, LANES), 0)
            stat_ref[...] = jnp.where(row == 7, total, shared)
            stat_copies.extend(start_direct(heads, lambda peer: stat_ref, stats_ref, stat_send, stat_recv))
            stats_ref[me] = stat_ref[...]

        run_gather(
            heads, column_parts(width, GATHER_SMALL), state_own, state_all, head_sems, None,
            [lambda: None] * 4 + [begin_norm],
        )
        wait_direct(heads, stats_ref, stat_copies, stat_recv, stat_send)
        row = lax.broadcasted_iota(jnp.int32, (8, LANES), 0)
        section_sq = stats_ref[0, 7:8, :]
        for k in range(1, count):
            section_sq = section_sq + stats_ref[k, 7:8, :]
        mine_ref[...] = jnp.broadcast_to(section_sq, (8, LANES))
        pair = remote(mine_ref, got_ref, pair_send, pair_recv, {"section": 1 - section})
        pair.start()
        pair.wait()
        norm = jnp.sqrt(mine_ref[...] + got_ref[...])
        threshold = CLIP_COEF * PARAMS**0.5
        norm_ref[...] = jnp.where(row == 0, norm, threshold / jnp.maximum(norm, threshold))
        for j in range(max(steps - 2, 0), steps):
            for copy in kept(j):
                copy.wait()
        for copy in state_sends:
            copy.wait_send()
        scatter.drain()

    tokens = sz.tokens
    state = 2 * NSTATE
    if close:
        out_shape = [
            jax.ShapeDtypeStruct((sz.master_pad, width), F32),
            jax.ShapeDtypeStruct((chans, width), F32),
            jax.ShapeDtypeStruct((state, width), BF16),
            jax.ShapeDtypeStruct((16, width), F32),
            jax.ShapeDtypeStruct((2, rows, width), BF16),
            jax.ShapeDtypeStruct((2, rows, width), F32),
            jax.ShapeDtypeStruct((count, 8, LANES), F32),
            jax.ShapeDtypeStruct((8, LANES), F32),
        ]
        out_specs = [ANY_SPEC] * 3 + [VMEM_SPEC] * 5
    elif early:
        out_shape = [
            jax.ShapeDtypeStruct((rows, width), F32),
            jax.ShapeDtypeStruct((rows, width), BF16),
            jax.ShapeDtypeStruct((16, width), F32),
            jax.ShapeDtypeStruct((sz.master_pad, width), BF16),
            jax.ShapeDtypeStruct((chans, width), BF16),
            jax.ShapeDtypeStruct((state, width), BF16),
        ]
        out_specs = [VMEM_SPEC] * 6
    else:
        out_shape = [
            jax.ShapeDtypeStruct((rows, width), F32),
            jax.ShapeDtypeStruct((rows, width), BF16),
            jax.ShapeDtypeStruct((16, width), F32),
            jax.ShapeDtypeStruct((sz.grad_rows, tokens), BF16),
            jax.ShapeDtypeStruct((tokens, chans), BF16),
        ]
        out_specs = [VMEM_SPEC] * 3 + [ANY_SPEC] * 2
    scratch = [
        pltpu.VMEM((block + 8, sz.conv), F32),
        pltpu.VMEM((block + 8, sz.conv), F32),
        pltpu.VMEM((block, sz.conv), F32),
        pltpu.VMEM((block, LANES), F32),
        pltpu.VMEM((NSTATE, chans), F32),
        pltpu.VMEM((sz.cols, width), BF16),
        pltpu.VMEM((chans, width), BF16),
        pltpu.VMEM((sz.grad_rows, sz.cols), BF16),
        pltpu.VMEM((max(2 * block, 2 * 16 * count) if close else 2 * block, width), BF16),
        pltpu.VMEM((2, block, sz.cols), F32),
        pltpu.VMEM((2, 8, sz.cols), F32),
        pltpu.VMEM((2, block, chans), F32),
        pltpu.VMEM((2, subs, NSTATE, chans), F32),
        pltpu.VMEM((8, LANES) if close or early else (2, sz.grad_rows, block), BF16),
        pltpu.VMEM((8, LANES) if close or early else (2, block, chans), BF16),
        pltpu.VMEM((tokens, width), scatter.first_type),
        DMA((5, 2)),
        DMA((2, 2)),
        DMA((3,)),
    ]
    scratch += scatter.scratch()
    if close or early:
        scratch += [
            pltpu.VMEM((sz.grad_rows, tokens), BF16),
            pltpu.VMEM((tokens, chans), BF16),
            pltpu.VMEM((2, tokens, cols), BF16),
            pltpu.VMEM((2, tokens, cols), BF16),
            DMA((2, 2)),
        ]
    if close:
        scratch += [
            pltpu.VMEM((rows, width), F32),
            pltpu.VMEM((16, width), F32),
            pltpu.VMEM((2, sz.master_pad, width), BF16),
            pltpu.VMEM((2, chans, width), BF16),
            pltpu.VMEM((2, 16, width), F32),
            DMA((2, 2, steps)),
            DMA((2, 2, steps)),
            DMA((3, 2)),
            DMA((3, 2)),
            pltpu.VMEM((2, sz.master_pad, cols), F32),
            pltpu.VMEM((2, chans, cols), F32),
            DMA((2, 2)),
            pltpu.VMEM((state, width), BF16),
            pltpu.VMEM((8, width), F32),
            pltpu.VMEM((32, width), F32),
            pltpu.VMEM((count - 1, 32, width), BF16),
            pltpu.VMEM((2, 16, width), F32),
            pltpu.VMEM((16, width), BF16),
            pltpu.VMEM((8, width), F32),
            pltpu.VMEM((count, 8, LANES), F32),
        ]
        scratch += [pltpu.VMEM((8, LANES), F32)] * 3
        scratch += [DMA((1, count - 1)), DMA((1, count - 1)), DMA((2,)), DMA((2,))]
        scratch += gather_scratch(column_parts(width, GATHER_SMALL), Heads(count).dims, count)
        scratch += [DMA((count,))] * 4 + [DMA, DMA]
    operands = [lengths, out_grads, proj, mixed, states, weights, weight_out, order]
    in_specs = [pl.BlockSpec(memory_space=pltpu.SMEM)] + [ANY_SPEC] * 7 + [VMEM_SPEC] * 5
    operands += [stats, pack, sz.head_sum(), residual, upstream]
    if more:
        out_shape += [
            jax.ShapeDtypeStruct((tokens, width), BF16),
            jax.ShapeDtypeStruct((count, 8, LANES), F32),
        ]
        out_specs += [ANY_SPEC, VMEM_SPEC]
        scratch += [pltpu.VMEM((rows, width), BF16), pltpu.VMEM((8, LANES), F32)]
        scratch += [DMA((count,))] * 2 + gather_scratch(parts, dims, count)
        operands += list(below)
        in_specs += [VMEM_SPEC] * 2
    if close:
        operands += list(upper)
        in_specs += [ANY_SPEC] * 3 + [VMEM_SPEC] * 6
    elif early:
        operands.append(gathered)
        in_specs.append(ANY_SPEC)
    return pl.pallas_call(
        kernel,
        out_shape=out_shape,
        in_specs=in_specs,
        out_specs=out_specs,
        scratch_shapes=scratch,
        compiler_params=params(collective_id),
        name="last_phase" if close else "backward_phase",
    )(*operands)


def weight_grads(sz, grads_t, gathered, scaled, out_grads):
    cols = 256

    split_row = sz.master_pad

    def kernel(gt_ref, h_ref, q_ref, g_ref, in_ref, state_ref, out_ref):
        in_ref[...] = nn(gt_ref[:split_row, :], h_ref[...]).astype(BF16)
        state_ref[...] = nn(gt_ref[split_row:, :], h_ref[...])
        out_ref[...] = tn(q_ref[...], g_ref[...]).astype(BF16)

    tokens, width, chans = sz.tokens, sz.width, sz.channels
    return pl.pallas_call(
        kernel,
        grid=(width // cols,),
        out_shape=[
            jax.ShapeDtypeStruct((sz.master_pad, width), BF16),
            jax.ShapeDtypeStruct((2 * NSTATE, width), F32),
            jax.ShapeDtypeStruct((chans, width), BF16),
        ],
        in_specs=[
            pl.BlockSpec((sz.grad_rows, tokens), lambda i: (0, 0)),
            pl.BlockSpec((tokens, cols), lambda i: (0, i)),
            pl.BlockSpec((tokens, chans), lambda i: (0, 0)),
            pl.BlockSpec((tokens, cols), lambda i: (0, i)),
        ],
        out_specs=[
            pl.BlockSpec((sz.master_pad, cols), lambda i: (0, i)),
            pl.BlockSpec((2 * NSTATE, cols), lambda i: (0, i)),
            pl.BlockSpec((chans, cols), lambda i: (0, i)),
        ],
        compiler_params=pltpu.CompilerParams(vmem_limit_bytes=VMEM_LIMIT),
        name="weight_grads",
    )(grads_t, gathered, scaled, out_grads)


def adam_update(weight, moment, second, gradient, rate, decay):
    moment_new = BETA_ONE * moment + (1.0 - BETA_ONE) * gradient
    second_new = BETA_TWO * second + (1.0 - BETA_TWO) * gradient * gradient
    corrected = moment_new * (1.0 / (1.0 - BETA_ONE**ADAM_STEP))
    corrected_sq = second_new * (1.0 / (1.0 - BETA_TWO**ADAM_STEP))
    weight_new = weight - rate * (corrected / (jnp.sqrt(corrected_sq) + ADAM_EPS) + decay * weight)
    return (weight_new, moment_new, second_new)


def adam_in(sz, clip, grad, weight, moment, second):
    block = LANES
    width = sz.width

    def kernel(clip_ref, g_ref, w_ref, m_ref, v_ref, wn_ref, mn_ref, vn_ref, low_ref):
        scale = clip_ref[0]

        def body(i, carry):
            made = []
            for half in range(2):
                span = pl.ds(pl.multiple_of(i * 16 + half * 8, 8), 8)
                new = adam_update(
                    w_ref[span, 0, :], m_ref[span, 0, :], v_ref[span, 0, :],
                    scale * g_ref[span, :], LEARN_MATRIX, WEIGHT_DECAY,
                )
                wn_ref[span, 0, :] = new[0]
                mn_ref[span, 0, :] = new[1]
                vn_ref[span, 0, :] = new[2]
                made.append(new[0])
            low_ref[pl.ds(pl.multiple_of(i * 16, 16), 16), :] = jnp.concatenate(made, axis=0).astype(BF16)
            return carry

        lax.fori_loop(0, block // 16, body, 0)

    view = pl.BlockSpec((block, 1, width), lambda i: (i, 0, 0))
    flat = pl.BlockSpec((block, width), lambda i: (i, 0))
    shape = jax.ShapeDtypeStruct((sz.master, 1, width), F32)
    return pl.pallas_call(
        kernel,
        grid=(sz.master_pad // block,),
        out_shape=[shape, shape, shape, jax.ShapeDtypeStruct((sz.master, width), BF16)],
        in_specs=[pl.BlockSpec(memory_space=pltpu.SMEM), flat, view, view, view],
        out_specs=[view, view, view, flat],
        compiler_params=pltpu.CompilerParams(vmem_limit_bytes=VMEM_LIMIT),
        name="adam_in",
    )(clip, grad, weight, moment, second)


def adam_plain(clip, grad, weight, moment, second, transposed):
    rows, width = weight.shape
    block = min(512 if transposed else 64, rows)

    def kernel(clip_ref, g_ref, w_ref, m_ref, v_ref, wn_ref, mn_ref, vn_ref, low_ref):
        if transposed:
            row = lax.broadcasted_iota(jnp.int32, (width, width), 0)
            col = lax.broadcasted_iota(jnp.int32, (width, width), 1)
            grad_value = tn(g_ref[...], (row == col).astype(BF16))
        else:
            grad_value = g_ref[...]
        new = adam_update(
            w_ref[...], m_ref[...], v_ref[...], clip_ref[0] * grad_value, LEARN_MATRIX, WEIGHT_DECAY
        )
        wn_ref[...], mn_ref[...], vn_ref[...] = new
        low_ref[...] = new[0].astype(BF16)

    flat = pl.BlockSpec((block, width), lambda i: (i, 0))
    turned = pl.BlockSpec((width, block), lambda i: (0, i))
    shape = jax.ShapeDtypeStruct((rows, width), F32)
    return pl.pallas_call(
        kernel,
        grid=(rows // block,),
        out_shape=[shape, shape, shape, jax.ShapeDtypeStruct((rows, width), BF16)],
        in_specs=[
            pl.BlockSpec(memory_space=pltpu.SMEM), turned if transposed else flat, flat, flat, flat
        ],
        out_specs=[flat] * 4,
        compiler_params=pltpu.CompilerParams(vmem_limit_bytes=VMEM_LIMIT),
        name="adam_plain",
    )(clip, grad, weight, moment, second)


def adam_few(sz, norms, small, stats, rates, head, shared):
    state = 2 * NSTATE
    pieces = sz.width // LANES
    conv = (CONV + 1) * state
    last = (CONV + 2) * HDIM

    def kernel(norm_ref, small_ref, stats_ref, rates_ref, *refs):
        ins, outs, (head_grad, shared_grad) = refs[:6], refs[6:12], refs[12:]
        scale = norm_ref[1:2, 0:1]
        lane = lax.broadcasted_iota(jnp.int32, (1, LANES), 1)
        rate_grad = small_ref[8:9, :LANES] * rates_ref[...]
        for head_at in range(sz.heads):
            row = slice(head_at, head_at + 1)
            cols = slice(head_at * HDIM, (head_at + 1) * HDIM)
            for tap in range(CONV):
                head_grad[row, tap * HDIM : (tap + 1) * HDIM] = small_ref[tap : tap + 1, cols]
            head_grad[row, CONV * HDIM : (CONV + 1) * HDIM] = small_ref[5:6, cols]
            head_grad[row, (CONV + 1) * HDIM : last] = small_ref[CONV : CONV + 1, cols]
            head_grad[row, last : last + 1] = small_ref[7:8, head_at : head_at + 1]
            head_grad[row, last + 1 : last + 2] = rate_grad[:, head_at : head_at + 1]
            head_grad[row, last + 2 : last + 3] = jnp.sum(small_ref[6:7, cols], axis=1, keepdims=True)
        for tap in range(CONV + 1):
            for k in range(state // LANES):
                to = tap * state + k * LANES
                shared_grad[:, to : to + LANES] = stats_ref[k, tap + 1 : tap + 2, :]
        for k in range(pieces):
            shared_grad[:, conv + k * LANES : conv + (k + 1) * LANES] = stats_ref[k, 0:1, :]
        for k, grad in enumerate((head_grad, shared_grad)):
            new = adam_update(*(ref[...] for ref in ins[3 * k : 3 * k + 3]), scale * grad[...], LEARN_VECTOR, 0.0)
            for ref, value in zip(outs[3 * k : 3 * k + 3], new):
                ref[...] = value

    arrays = list(head) + list(shared)
    return pl.pallas_call(
        kernel,
        out_shape=[jax.ShapeDtypeStruct(array.shape, F32) for array in arrays],
        in_specs=[VMEM_SPEC] * 10,
        out_specs=[VMEM_SPEC] * 6,
        scratch_shapes=[pltpu.VMEM(head[0].shape, F32), pltpu.VMEM(shared[0].shape, F32)],
        name="adam_few",
    )(norms, small, stats, rates, *arrays)


def columns_first(array):
    return jnp.transpose(array, (2, 0, 1))


def shards(
    inputs,
    cotangent,
    valid_lengths,
    proj_in,
    proj_in_m,
    proj_in_v,
    proj_state,
    proj_state_m,
    proj_state_v,
    proj_out,
    proj_out_m,
    proj_out_v,
    head_params,
    head_m,
    head_v,
    shared_params,
    shared_m,
    shared_v,
):
    count = lax.axis_size("head")
    rows, width = inputs.shape[1], inputs.shape[2]
    heads = head_params.shape[1]
    tokens = rows * count
    sz = Sizes(count, heads, tokens, width)
    order = sz.order()
    own_in, own_out, lower_in, lower_out, pack, rates, first, cot, rows_zero = opening(
        count, sz, columns_first(proj_in), proj_state[0], proj_out[0], head_params[0], shared_params, order,
        inputs, cotangent, 0,
    )

    kept_zero = forward_phase(
        count, sz, 0, valid_lengths, rows_zero, lower_in, lower_out, pack, first, None, (own_in, own_out), 1
    )
    result_zero, branch_zero, total_zero, rows_one = kept_zero[:4]
    upper_in, upper_out = kept_zero[7:]
    kept_one = forward_phase(
        count, sz, 1, valid_lengths, rows_one, upper_in, upper_out, pack, result_zero, cot, None, 2
    )
    result_one, out_grads_one, stats_one = kept_one[0], kept_one[3], kept_one[7]
    back_one = backward_phase(
        count, sz, 1, valid_lengths, out_grads_one, *kept_one[4:7], stats_one, upper_in, upper_out, pack, order,
        result_zero, cot, (branch_zero, total_zero), rows_one, None, 3,
    )
    out_grads_zero, stats_zero = back_one[-2:]
    grad_one, low_one, acc_one = back_one[:3]

    def run_last(upper):
        return backward_phase(
            count, sz, 0, valid_lengths, out_grads_zero, *kept_zero[4:7], stats_zero, lower_in, lower_out, pack, order,
            first, low_one, None, rows_zero, upper, 4,
        )

    if fits(sz):
        in_one, out_one, state_one = back_one[3:6]
        upper = (rows_zero, in_one, out_one, acc_one, result_zero, result_one, grad_one, state_one, rates)
        grad_in, grad_out, grad_state, small, layer_outs, grad_buffer, all_stats, norms = run_last(upper)
    else:
        grads_t_one, scaled_one = back_one[3:5]
        grad_zero, _, acc_zero, grads_t_zero, scaled_zero = run_last(None)
        lower = weight_grads(sz, grads_t_zero, rows_zero, scaled_zero, out_grads_zero)
        higher = weight_grads(sz, grads_t_one, rows_one, scaled_one, out_grads_one)
        grad_in, grad_out, state_sum, small, layer_outs, grad_buffer, squares = trade_sections(
            [(lower[0], higher[0]), (lower[2], higher[2]), (lower[1], higher[1]), (acc_zero, acc_one)],
            [(result_zero, result_one), (grad_zero, grad_one)],
            2,
            6,
        )
        state_part = state_sum.astype(BF16)
        state_all, all_stats, norms = finish_sums(
            count, sz, [state_part.reshape(16 * count, -1)], small, squares, rates, sz.head_sum(), 5
        )
        grad_state = state_all.reshape(state_part.shape)
    grad_norm, clip = norms[0, 0], norms[1, :1]
    few = adam_few(
        sz, norms, small, all_stats, rates,
        (head_params[0], head_m[0], head_v[0]), (shared_params, shared_m, shared_v),
    )
    new_in = adam_in(
        sz, clip, grad_in, columns_first(proj_in), columns_first(proj_in_m), columns_first(proj_in_v)
    )
    new_out = adam_plain(
        clip, grad_out, proj_out[0], proj_out_m[0], proj_out_v[0], False
    )
    new_state = adam_plain(
        clip, grad_state, proj_state[0], proj_state_m[0], proj_state_v[0], True
    )
    back_view = [jnp.transpose(array, (1, 2, 0)) for array in new_in[:3]]
    return (
        layer_outs[None],
        grad_buffer[None],
        grad_norm,
        back_view[0],
        back_view[1],
        back_view[2],
        new_in[3].T[None],
        new_state[0][None],
        new_state[1][None],
        new_state[2][None],
        new_state[3][None],
        new_out[0][None],
        new_out[1][None],
        new_out[2][None],
        new_out[3][None],
        few[0][None],
        few[1][None],
        few[2][None],
        few[3],
        few[4],
        few[5],
    )


def solution(mesh):
    in_specs = (
        P(None, "head", None),
        P(None, "head", None),
        P(),
        P("section", None, "head"),
        P("section", None, "head"),
        P("section", None, "head"),
        P("section", None, None),
        P("section", None, None),
        P("section", None, None),
        P("section", "head", None),
        P("section", "head", None),
        P("section", "head", None),
        P("section", "head", None),
        P("section", "head", None),
        P("section", "head", None),
        P("section", None),
        P("section", None),
        P("section", None),
    )
    out_specs = (
        P("section", None, "head", None),
        P("section", None, "head", None),
        P(),
        P("section", None, "head"),
        P("section", None, "head"),
        P("section", None, "head"),
        P("section", None, "head"),
        P("section", None, None),
        P("section", None, None),
        P("section", None, None),
        P("section", None, None),
        P("section", "head", None),
        P("section", "head", None),
        P("section", "head", None),
        P("section", "head", None),
        P("section", "head", None),
        P("section", "head", None),
        P("section", "head", None),
        P("section", None),
        P("section", None),
        P("section", None),
    )
    return jax.shard_map(shards, mesh=mesh, in_specs=in_specs, out_specs=out_specs, check_vma=False)
```
